32 devices in a mesh: blk: 8 (over y, x, core), head: 4 (over z).
Axes of the slice: x: 2, y: 2, z: 4, core: 2. Of those that a mesh axis runs over, the one named last changes fastest.
Arguments:
- inputs: bfloat16 [2, 4096, 768], P(None, ('blk', 'head')), may hold values from -6 to 6
- cotangent: bfloat16 [2, 4096, 768], P(None, ('blk', 'head')), may hold values from -6 to 6
- random_blocks: int32 [2, 64, 12, 3], replicated, may hold values from 0 to 63, as said below
- global_blocks: int32 [2, 2], replicated, may hold values from 0 to 63, as said below
- query_weight: bfloat16 [768, 768], P(('blk', 'head')), may hold values from -0.21875 to 0.21875
- query_bias: bfloat16 [768], P(('blk', 'head')), may hold values from -3 to 3
- key_weight: bfloat16 [768, 768], P(('blk', 'head')), may hold values from -0.21875 to 0.21875
- value_weight: bfloat16 [768, 768], P(('blk', 'head')), may hold values from -0.21875 to 0.21875
- value_bias: bfloat16 [768], P(('blk', 'head')), may hold values from -3 to 3
- out_weight: bfloat16 [768, 768], P(('blk', 'head')), may hold values from -0.875 to 0.875
- out_bias: bfloat16 [768], P(('blk', 'head')), may hold values from -3 to 3
- attn_gain: bfloat16 [768], P(('blk', 'head')), may hold values from 0.5 to 1.5
- attn_shift: bfloat16 [768], P(('blk', 'head')), may hold values from -3 to 3
- up_weight: bfloat16 [768, 3072], P(('blk', 'head')), may hold values from -0.21875 to 0.21875
- up_bias: bfloat16 [3072], P(('blk', 'head')), may hold values from -3 to 3
- down_weight: bfloat16 [3072, 768], P(('blk', 'head')), may hold values from -0.109375 to 0.109375
- down_bias: bfloat16 [768], P(('blk', 'head')), may hold values from -3 to 3
- ffn_gain: bfloat16 [768], P(('blk', 'head')), may hold values from 0.5 to 1.5
- ffn_shift: bfloat16 [768], P(('blk', 'head')), may hold values from -3 to 3
Outputs:
- layer_out: bfloat16 [2, 4096, 768], P(None, ('blk', 'head'))
- input_grad: bfloat16 [2, 4096, 768], P(None, ('blk', 'head'))
- grad_query_weight: float32 [768, 768], P(('blk', 'head'))
- grad_query_bias: float32 [768], P(('blk', 'head'))
- grad_key_weight: float32 [768, 768], P(('blk', 'head'))
- grad_value_weight: float32 [768, 768], P(('blk', 'head'))
- grad_value_bias: float32 [768], P(('blk', 'head'))
- grad_out_weight: float32 [768, 768], P(('blk', 'head'))
- grad_out_bias: float32 [768], P(('blk', 'head'))
- grad_attn_gain: float32 [768], P(('blk', 'head'))
- grad_attn_shift: float32 [768], P(('blk', 'head'))
- grad_up_weight: float32 [768, 3072], P(('blk', 'head'))
- grad_up_bias: float32 [3072], P(('blk', 'head'))
- grad_down_weight: float32 [3072, 768], P(('blk', 'head'))
- grad_down_bias: float32 [768], P(('blk', 'head'))
- grad_ffn_gain: float32 [768], P(('blk', 'head'))
- grad_ffn_shift: float32 [768], P(('blk', 'head'))
The draws below stay inside these ranges and needn't reach their ends.
Inputs may be any that keep to these rules, and one draw needn't show every extreme that they name: `random_blocks`: for each micro-batch, each run of 8 query blocks starting at a multiple of 8 and each run of 3 heads starting at a multiple of 3: at most 10 of their 72 entries lie in any one run of 8 key blocks starting at a multiple of 8, and exactly 10 lie in one such run. Entries may name a window or a global block. `global_blocks`: the 2 global blocks of a micro-batch are different; their positions are drawn anew for each micro-batch.
All inputs are finite; a program needn't handle non-finite values.
Results may differ from the reference program's by a relative error of at most 0.014.
Values may be sent and summed in bfloat16 or wider, within the bound.
A program may use at most 256 MiB of HBM per device.

```python
import jax
import jax.numpy as jnp
from jax import lax

D = 768
HEADS = 12
HD = 64
FF = 3072
BLOCK = 64
RAND = 3
GLOB = 2
MICRO = 2
LENGTH = 4096
NBLOCKS = 64
QB = 8
HG = 3
QG = 8
CAP = 10
SHARDS = 8
HGROUPS = 4


def draw_random_blocks(key, part):
    key = jax.random.fold_in(key, 11)
    requests = QB * HG * RAND
    groups = MICRO * SHARDS * HGROUPS
    first_key, second_key, third_key = jax.random.split(key, 3)
    group_keys = jax.random.split(first_key, groups)
    ranked = jax.vmap(lambda group_key: jax.random.permutation(group_key, requests))(group_keys).astype(jnp.int32)
    hot_source = jax.random.randint(second_key, (groups, 1), 0, SHARDS, dtype=jnp.int32)
    spread_source = (ranked - CAP) % (SHARDS - 1)
    spread_source = spread_source + (spread_source >= hot_source).astype(jnp.int32)
    source = jnp.where(ranked < CAP, hot_source, spread_source)
    within = jax.random.randint(third_key, (groups, requests), 0, QB, dtype=jnp.int32)
    chosen = source * QB + within
    chosen = chosen.reshape(MICRO, SHARDS, HGROUPS, QB, HG, RAND).transpose(0, 1, 3, 2, 4, 5)
    return chosen.reshape(MICRO, NBLOCKS, HEADS, RAND).astype(jnp.int32)


def draw_global_blocks(key, part):
    key = jax.random.fold_in(key, 23)
    micro_keys = jax.random.split(key, MICRO)
    picked = jax.vmap(lambda micro_key: jax.random.permutation(micro_key, NBLOCKS)[:GLOB])(micro_keys)
    return picked.astype(jnp.int32)


def block_scale(key, extent, shards, smallest, high):
    gain = 1.0
    for axis_at, parts in shards:
        draws = jax.random.uniform(jax.random.fold_in(jax.random.fold_in(key, 6), axis_at), (parts,), jnp.float32, smallest / len(shards), high / len(shards))
        gain = gain * jnp.repeat(jnp.exp(draws), extent[axis_at] // parts).reshape((-1,) + (1,) * (len(extent) - 1 - axis_at))
    return gain


def normal_values(stream_key, shape, width, bound, pieces=(), kind=jnp.bfloat16):
    array = jax.random.normal(stream_key, shape, jnp.float32) * width
    if len(pieces) > 0:
        array = block_scale(stream_key, shape, pieces, -0.22, 0.18) * array
    return jnp.clip(array, min=-bound, max=bound).astype(kind)


def setup_inputs(seed: int = 0) -> dict:
    streams_of = jax.random.split(jax.random.key(seed), 20)
    return {
        "inputs": normal_values(streams_of[0], (MICRO, LENGTH, D), 1.0, 6.0, ((1, 32),)),
        "cotangent": normal_values(streams_of[1], (MICRO, LENGTH, D), 1.0, 6.0, ((1, 32),)),
        "random_blocks": draw_random_blocks(jax.random.fold_in(streams_of[19], 71), 0),
        "global_blocks": draw_global_blocks(jax.random.fold_in(streams_of[19], 71), 0),
        "query_weight": normal_values(streams_of[4], (D, D), D ** -0.5, 0.21875, ((0, 32),)),
        "query_bias": normal_values(streams_of[5], (D,), 0.5, 3.0, ((0, 32),)),
        "key_weight": normal_values(streams_of[6], (D, D), D ** -0.5, 0.21875, ((0, 32),)),
        "value_weight": normal_values(streams_of[7], (D, D), D ** -0.5, 0.21875, ((0, 32),)),
        "value_bias": normal_values(streams_of[8], (D,), 0.5, 3.0, ((0, 32),)),
        "out_weight": normal_values(streams_of[9], (D, D), (D // 16) ** -0.5, 0.875, ((0, 32),)),
        "out_bias": normal_values(streams_of[10], (D,), 0.5, 3.0, ((0, 32),)),
        "attn_gain": jnp.clip(1.0 + 0.1 * jax.random.normal(streams_of[11], (D,), jnp.float32), 0.5, 1.5).astype(jnp.bfloat16),
        "attn_shift": normal_values(streams_of[12], (D,), 0.5, 3.0, ((0, 32),)),
        "up_weight": normal_values(streams_of[13], (D, FF), D ** -0.5, 0.21875, ((0, 32),)),
        "up_bias": normal_values(streams_of[14], (FF,), 0.5, 3.0, ((0, 32),)),
        "down_weight": normal_values(streams_of[15], (FF, D), FF ** -0.5, 0.109375, ((0, 32),)),
        "down_bias": normal_values(streams_of[16], (D,), 0.5, 3.0, ((0, 32),)),
        "ffn_gain": jnp.clip(1.0 + 0.1 * jax.random.normal(streams_of[17], (D,), jnp.float32), 0.5, 1.5).astype(jnp.bfloat16),
        "ffn_shift": normal_values(streams_of[18], (D,), 0.5, 3.0, ((0, 32),)),
    }


@jax.custom_vjp
def low(v):
    return lax.optimization_barrier(v.astype(jnp.bfloat16)).astype(jnp.float32)

@jax.custom_vjp
def low_back(v):
    return v

def low_keep(v):
    return (low(v), None)

def low_pass(kept, grad):
    return (grad,)

def back_keep(v):
    return (v, None)

def back_low(kept, grad):
    return (low(grad),)
low.defvjp(low_keep, low_pass)
low_back.defvjp(back_keep, back_low)

def highest(left_side, right_side):
    return jnp.dot(left_side, right_side, precision=lax.Precision.HIGHEST)

def layer_norm(values, norm_gain, norm_shift):
    center = lax.optimization_barrier(jnp.mean(values, axis=-1, keepdims=True))
    centred = values - center
    spread = lax.optimization_barrier(jnp.mean(centred * centred, axis=-1, keepdims=True))
    return centred * lax.rsqrt(spread + 1e-12) * norm_gain + norm_shift

def block_attention(queries, keys, values, random_rows, global_rows):
    blocks = LENGTH // BLOCK
    attn_scale = HD ** (-0.5)
    query_blocks = queries.reshape(blocks, BLOCK, HEADS, HD)
    key_table = keys.reshape(blocks, BLOCK, HEADS, HD).transpose(0, 2, 1, 3).reshape(blocks * HEADS, BLOCK, HD)
    value_table = values.reshape(blocks, BLOCK, HEADS, HD).transpose(0, 2, 1, 3).reshape(blocks * HEADS, BLOCK, HD)
    head_range = jnp.arange(HEADS, dtype=jnp.int32)
    listed = 3 + RAND + GLOB

    def sparse_group(start):
        block_ids = start + jnp.arange(QG, dtype=jnp.int32)
        neighbour = block_ids[:, None] + jnp.arange(-1, 2, dtype=jnp.int32)[None, :]
        inside = (neighbour >= 0) & (neighbour < blocks)
        neighbour = jnp.clip(neighbour, 0, blocks - 1)
        chosen = lax.dynamic_slice_in_dim(random_rows, start, QG, 0)
        every_block = jnp.concatenate([jnp.broadcast_to(neighbour[:, None, :], (QG, HEADS, 3)), chosen, jnp.broadcast_to(global_rows[None, None, :], (QG, HEADS, GLOB))], axis=2)
        flat_rows = every_block * HEADS + head_range[None, :, None]
        listed_keys = key_table[flat_rows].reshape(QG, HEADS, listed * BLOCK, HD)
        listed_values = value_table[flat_rows].reshape(QG, HEADS, listed * BLOCK, HD)
        local_queries = lax.dynamic_slice_in_dim(query_blocks, start, QG, 0)
        scores = low_back(jnp.einsum('gqhd,ghkd->ghqk', local_queries, listed_keys, precision=lax.Precision.HIGHEST) * attn_scale)
        allowed = jnp.concatenate([inside, jnp.ones((QG, RAND + GLOB), jnp.bool_)], axis=1)
        allowed = jnp.repeat(allowed, BLOCK, axis=1)
        scores = jnp.where(allowed[:, None, None, :], scores, -jnp.inf)
        row_top = lax.optimization_barrier(jnp.max(scores, axis=-1, keepdims=True))
        raised = jnp.exp(scores - row_top)
        probs = raised / lax.optimization_barrier(jnp.sum(raised, axis=-1, keepdims=True))
        return jnp.einsum('ghqk,ghkd->gqhd', low(probs), listed_values, precision=lax.Precision.HIGHEST)
    starts = jnp.arange(0, blocks, QG, dtype=jnp.int32)
    sparse = lax.map(jax.checkpoint(sparse_group), starts).reshape(blocks, BLOCK, HEADS, HD)
    all_keys = keys.reshape(LENGTH, HEADS, HD)
    all_values = values.reshape(LENGTH, HEADS, HD)

    def global_group(block_id):
        local_queries = lax.dynamic_slice_in_dim(query_blocks, block_id, 1, 0)[0]
        scores = low_back(jnp.einsum('qhd,khd->hqk', local_queries, all_keys, precision=lax.Precision.HIGHEST) * attn_scale)
        row_top = lax.optimization_barrier(jnp.max(scores, axis=-1, keepdims=True))
        raised = jnp.exp(scores - row_top)
        probs = raised / lax.optimization_barrier(jnp.sum(raised, axis=-1, keepdims=True))
        return jnp.einsum('hqk,khd->qhd', probs, all_values, precision=lax.Precision.HIGHEST)
    full_rows = lax.map(jax.checkpoint(global_group), global_rows)
    merged = sparse.at[global_rows].set(full_rows)
    return merged.reshape(LENGTH, D)

def layer(tokens, weights, random_rows, global_rows):
    query_weight, query_bias, key_weight, value_weight, value_bias, out_weight, out_bias, attn_gain, attn_shift, up_weight, up_bias, down_weight, down_bias, ffn_gain, ffn_shift = weights
    queries = low_back(low(highest(tokens, query_weight) + query_bias))
    keys = low_back(low(highest(tokens, key_weight)))
    values = low_back(low(highest(tokens, value_weight) + value_bias))
    context = low_back(low(block_attention(queries, keys, values, random_rows, global_rows)))
    branch = low_back(highest(context, out_weight) + out_bias)
    first_norm = layer_norm(tokens + branch, attn_gain, attn_shift)
    hidden = low_back(highest(low(first_norm), up_weight) + up_bias)
    act_low = low(jax.nn.gelu(hidden, approximate=False))
    ffn_out = low_back(highest(act_low, down_weight) + down_bias)
    return layer_norm(first_norm + ffn_out, ffn_gain, ffn_shift)

def reference(inputs, cotangent, random_blocks, global_blocks, query_weight, query_bias, key_weight, value_weight, value_bias, out_weight, out_bias, attn_gain, attn_shift, up_weight, up_bias, down_weight, down_bias, ffn_gain, ffn_shift):
    weights = tuple((weight_item.astype(jnp.float32) for weight_item in (query_weight, query_bias, key_weight, value_weight, value_bias, out_weight, out_bias, attn_gain, attn_shift, up_weight, up_bias, down_weight, down_bias, ffn_gain, ffn_shift)))

    def per_sequence(totals, packed):
        tokens, cotangent_rows, random_rows, global_rows = packed

        def forward(token_values, params):
            return layer(token_values, params, random_rows, global_rows)
        result, pullback = jax.vjp(forward, tokens.astype(jnp.float32), weights)
        token_grad, weight_grads = pullback(cotangent_rows.astype(jnp.float32))
        totals = tuple((total_sum + extra_sum for total_sum, extra_sum in zip(totals, weight_grads)))
        return (totals, (result.astype(jnp.bfloat16), token_grad.astype(jnp.bfloat16)))
    zeros = tuple((jnp.zeros_like(weight_item) for weight_item in weights))
    totals, (layer_out, input_grad) = lax.scan(per_sequence, zeros, (inputs, cotangent, random_blocks, global_blocks))
    return (layer_out, input_grad, totals[0], totals[1], totals[2], totals[3], totals[4], totals[5], totals[6], totals[7], totals[8], totals[9], totals[10], totals[11], totals[12], totals[13], totals[14])
```

```python
from functools import partial

import jax
import jax.numpy as jnp
from jax import lax
from jax.experimental import pallas as pl
from jax.experimental.pallas import tpu as pltpu
from jax.sharding import PartitionSpec as P

HEADS = 12
HD = 64
BLOCK = 64
RAND = 3
GLOB = 2


MESH = pl.DeviceIdType.MESH


def places():
    b = lax.axis_index("blk")
    h = lax.axis_index("head")
    core = b % 2
    x = (b // 2) % 2
    y = b // 4
    across_x = b + 2 - 4 * x
    across_y = b + 4 - 8 * y
    partner = b + 1 - 2 * core
    line = (h, h + 1 - 2 * (h % 2), h + 2 - 4 * (h // 2), 3 - h)
    return b, h, core, x, y, across_x, across_y, partner, line


def meet(b, h, others, line):
    barrier = pltpu.get_barrier_semaphore()
    for other in others:
        pl.semaphore_signal(barrier, inc=1, device_id=(other, h), device_id_type=MESH)
    for d in range(1, 4):
        pl.semaphore_signal(barrier, inc=1, device_id=(b, line[d]), device_id_type=MESH)
    pl.semaphore_wait(barrier, len(others) + 3)


def remote(src, dst, send_sem, recv_sem, device):
    return pltpu.make_async_remote_copy(
        src_ref=src,
        dst_ref=dst,
        send_sem=send_sem,
        recv_sem=recv_sem,
        device_id=device,
        device_id_type=MESH,
    )


def gather_kernel(kinds, *refs):
    n = len(kinds)
    ins = refs[:n]
    outs = refs[n : 2 * n]
    own_sem, line_send, line_recv, send, recv = refs[2 * n :]
    b, h, core, x, y, across_x, across_y, partner, line = places()
    corner = across_x + 4 - 8 * y
    meet(b, h, (across_x, across_y, partner), line)

    def piece(i, place):
        return ins[i].at[place] if kinds[i][0] else ins[i]

    def slot(i, shard, place):
        return outs[i].at[shard * 4 + place] if kinds[i][1] else outs[i].at[place]

    def part(ref, cut):
        axis, start, size = cut
        return ref.at[(slice(None),) * axis + (pl.ds(start, size),)]

    started = []

    def go(copy):
        copy.start()
        started.append(copy)

    spread = [i for i in range(n) if kinds[i][1]]
    locals_ = []
    for i in range(n):
        for d in range(1, 4):
            go(
                remote(
                    piece(i, line[d]),
                    slot(i, b, h),
                    line_send.at[i, d],
                    line_recv.at[i, d],
                    (b, line[d]),
                )
            )
        own = pltpu.make_async_copy(piece(i, h), slot(i, b, h), own_sem.at[i])
        own.start()
        locals_.append(own)

    def out_of(i, d):
        return piece(i, h) if d == 0 else slot(i, b, line[d])

    def send_plane(i, d):
        for k, other in enumerate((across_x, across_y, partner)):
            go(
                remote(
                    out_of(i, d),
                    slot(i, b, line[d]),
                    send.at[i, d, k],
                    recv.at[i, d, k],
                    (other, h),
                )
            )

    def arrived(i, d, k, shard, cut=None):
        here = slot(i, shard, line[d])
        if cut is not None:
            here = part(here, cut)
        remote(here, here, send.at[i, d, k], recv.at[i, d, k], (partner, h)).wait_recv()
        return here

    def pass_on(i, d):
        first, second = kinds[i][2]
        here = arrived(i, d, 0, across_x)
        if first is not None:
            go(
                remote(
                    part(here, first),
                    part(here, first),
                    send.at[i, d, 6],
                    recv.at[i, d, 6],
                    (across_y, h),
                )
            )
        go(remote(here, here, send.at[i, d, 3], recv.at[i, d, 3], (partner, h)))
        here = arrived(i, d, 1, across_y)
        if second is not None:
            go(
                remote(
                    part(here, second),
                    part(here, second),
                    send.at[i, d, 7],
                    recv.at[i, d, 7],
                    (across_x, h),
                )
            )
        go(remote(here, here, send.at[i, d, 4], recv.at[i, d, 4], (partner, h)))

    def finish_corner(i, d):
        first, second = kinds[i][2]
        if first is not None:
            arrived(i, d, 6, corner, first)
        if second is not None:
            arrived(i, d, 7, corner, second)
        here = slot(i, corner, line[d])
        go(remote(here, here, send.at[i, d, 5], recv.at[i, d, 5], (partner, h)))

    def line_arrived(i, d):
        here = slot(i, b, line[d])
        remote(
            here, here, line_send.at[i, d], line_recv.at[i, d], (b, line[d])
        ).wait_recv()

    for d in range(4):
        for i in spread:
            if d > 0:
                line_arrived(i, d)
            send_plane(i, d)
        if d > 0:
            for i in spread:
                pass_on(i, d - 1)
        if d > 1:
            for i in spread:
                finish_corner(i, d - 2)
    for i in spread:
        pass_on(i, 3)
    for d in (2, 3):
        for i in spread:
            finish_corner(i, d)
    for i in range(n):
        if i not in spread:
            for d in range(1, 4):
                line_arrived(i, d)
    partner_x = partner + 2 - 4 * x
    partner_y = partner + 4 - 8 * y
    partner_corner = partner_x + 4 - 8 * y
    for i in spread:
        for d in range(4):
            for k, shard in ((2, partner), (3, partner_x), (4, partner_y), (5, partner_corner)):
                arrived(i, d, k, shard)
    for own in locals_:
        own.wait()
    for copy in started:
        copy.wait_send()


def gather_call(arrays, kinds, collective):
    n = len(arrays)
    shapes = []
    for a, (per_place, spread, _) in zip(arrays, kinds):
        chunk = a.shape[1:] if per_place else a.shape
        shapes.append(jax.ShapeDtypeStruct(((32 if spread else 4),) + chunk, a.dtype))
    return pl.pallas_call(
        partial(gather_kernel, kinds),
        out_shape=tuple(shapes),
        in_specs=[pl.BlockSpec(memory_space=pl.ANY)] * n,
        out_specs=tuple([pl.BlockSpec(memory_space=pl.ANY)] * n),
        scratch_shapes=[
            pltpu.SemaphoreType.DMA((n,)),
            pltpu.SemaphoreType.DMA((n, 4)),
            pltpu.SemaphoreType.DMA((n, 4)),
            pltpu.SemaphoreType.DMA((n, 4, 8)),
            pltpu.SemaphoreType.DMA((n, 4, 8)),
        ],
        compiler_params=pltpu.CompilerParams(collective_id=collective, has_side_effects=True),
        name=f"gather{collective}",
    )(*arrays)


def scatter_kernel(kinds, *refs):
    n = len(kinds)
    ins = refs[:n]
    outs = refs[n : 2 * n]
    rest = list(refs[2 * n :])
    bufs = {}
    for i in range(n):
        if kinds[i][1]:
            bufs[i] = rest[:6]
            rest = rest[6:]
            if kinds[i][0]:
                bufs[i] = bufs[i] + [rest[0]]
                rest = rest[1:]
    local_sem, own_sem, line_send, line_recv, send, recv = rest
    b, h, core, x, y, across_x, across_y, partner, line = places()
    meet(b, h, (across_x, across_y, partner), line)
    chip = b // 2
    targets = (3 - chip, chip + 1 - 2 * x, chip + 2 - 4 * y, chip)
    started = []
    spread = [i for i in range(n) if kinds[i][1]]

    def go(copy):
        copy.start()
        started.append(copy)

    def part(ref, cut):
        axis, start, size = cut
        return ref.at[(slice(None),) * (axis + 1) + (pl.ds(start, size),)]

    locals_ = []
    for i in range(n):
        if i in spread:
            continue
        for d in range(1, 4):
            go(
                remote(
                    ins[i].at[line[d]], outs[i].at[h], line_send.at[i, d], line_recv.at[i, d], (b, line[d])
                )
            )
        own = pltpu.make_async_copy(ins[i].at[h], outs[i].at[h], own_sem.at[i])
        own.start()
        locals_.append(own)
    loads = {}
    for t in range(4):
        for i in spread:
            from_partner, total = bufs[i][0], bufs[i][1]
            go(
                remote(
                    ins[i].at[pl.ds((targets[t] * 2 + 1 - core) * 4, 4)],
                    from_partner.at[t],
                    send.at[i, t],
                    recv.at[i, t],
                    (partner, h),
                )
            )
            load = pltpu.make_async_copy(
                ins[i].at[pl.ds((targets[t] * 2 + core) * 4, 4)], total.at[t], local_sem.at[i, t]
            )
            load.start()
            loads[i, t] = load

    def wait_for(ref, i, k):
        remote(ref, ref, send.at[i, k], recv.at[i, k], (partner, h)).wait_recv()

    def both_cores(i, t, extra=(), cut=None):
        from_partner, total = bufs[i][0], bufs[i][1]
        loads[i, t].wait()
        wait_for(from_partner.at[t], i, t)

        def add(place, carry):
            value = total[t, place].astype(jnp.float32) + from_partner[t, place].astype(jnp.float32)
            for ref in extra:
                value = value + ref[place].astype(jnp.float32)
            total[t, place] = value.astype(total.dtype)
            return carry

        lax.fori_loop(0, 4, add, 0)

    def add_corner(i, t, ref, cut):
        total = bufs[i][1]
        axis, start, size = cut
        index = (slice(None),) * axis + (pl.ds(start, size),)

        def add(place, carry):
            at = (t, place) + index
            value = total[at].astype(jnp.float32) + ref[place].astype(jnp.float32)
            total[at] = value.astype(total.dtype)
            return carry

        lax.fori_loop(0, 4, add, 0)

    for i in spread:
        total = bufs[i][1]
        first, second = kinds[i][2]
        both_cores(i, 0)
        if first is not None:
            go(remote(part(total.at[0], first), bufs[i][2], send.at[i, 4], recv.at[i, 4], (across_x, h)))
        if second is not None:
            go(remote(part(total.at[0], second), bufs[i][3], send.at[i, 5], recv.at[i, 5], (across_y, h)))
    for i in spread:
        total = bufs[i][1]
        first, second = kinds[i][2]
        both_cores(i, 1)
        if second is not None:
            wait_for(bufs[i][3], i, 5)
            add_corner(i, 1, bufs[i][3], second)
        go(remote(total.at[1], bufs[i][4], send.at[i, 6], recv.at[i, 6], (across_x, h)))
        both_cores(i, 2)
        if first is not None:
            wait_for(bufs[i][2], i, 4)
            add_corner(i, 2, bufs[i][2], first)
        go(remote(total.at[2], bufs[i][5], send.at[i, 7], recv.at[i, 7], (across_y, h)))
    for i in spread:
        summed = kinds[i][0]
        total = bufs[i][1]
        wait_for(bufs[i][4], i, 6)
        wait_for(bufs[i][5], i, 7)
        both_cores(i, 3, (bufs[i][4], bufs[i][5]))
        for d in range(1, 4):
            landing = bufs[i][6].at[d - 1] if summed else outs[i].at[h]
            go(
                remote(
                    total.at[3, line[d]], landing, line_send.at[i, d], line_recv.at[i, d], (b, line[d])
                )
            )
        if not summed:
            own = pltpu.make_async_copy(total.at[3, h], outs[i].at[h], own_sem.at[i])
            own.start()
            locals_.append(own)
    for i in range(n):
        summed = kinds[i][0]
        for d in range(1, 4):
            landing = bufs[i][6].at[d - 1] if summed else outs[i].at[line[d]]
            remote(
                landing, landing, line_send.at[i, d], line_recv.at[i, d], (b, line[d])
            ).wait_recv()
        if summed:
            value = bufs[i][1][3, h].astype(jnp.float32)
            for d in range(3):
                value = value + bufs[i][6][d].astype(jnp.float32)
            outs[i][...] = value
    for own in locals_:
        own.wait()
    for copy in started:
        copy.wait_send()


def scatter_call(arrays, kinds, collective):
    n = len(arrays)
    shapes = []
    out_specs = []
    scratch = []
    for a, (summed, spread, halves) in zip(arrays, kinds):
        chunk = a.shape[1:]
        if spread:
            scratch += [pltpu.VMEM((4, 4) + chunk, a.dtype), pltpu.VMEM((4, 4) + chunk, a.dtype)]
            for cut in halves:
                size = list(chunk)
                if cut is not None:
                    size[cut[0]] = cut[2]
                else:
                    size = [8, 128]
                scratch.append(pltpu.VMEM((4,) + tuple(size), a.dtype))
            scratch += [pltpu.VMEM((4,) + chunk, a.dtype)] * 2
            if summed:
                scratch.append(pltpu.VMEM((3,) + chunk, a.dtype))
        if summed:
            shapes.append(jax.ShapeDtypeStruct(chunk, jnp.float32))
            out_specs.append(pl.BlockSpec(memory_space=pltpu.VMEM))
        else:
            shapes.append(jax.ShapeDtypeStruct((4,) + chunk, a.dtype))
            out_specs.append(pl.BlockSpec(memory_space=pl.ANY))
    return pl.pallas_call(
        partial(scatter_kernel, kinds),
        out_shape=tuple(shapes),
        in_specs=[pl.BlockSpec(memory_space=pl.ANY)] * n,
        out_specs=tuple(out_specs),
        scratch_shapes=scratch
        + [
            pltpu.SemaphoreType.DMA((n, 4)),
            pltpu.SemaphoreType.DMA((n,)),
            pltpu.SemaphoreType.DMA((n, 4)),
            pltpu.SemaphoreType.DMA((n, 4)),
            pltpu.SemaphoreType.DMA((n, 8)),
            pltpu.SemaphoreType.DMA((n, 8)),
        ],
        compiler_params=pltpu.CompilerParams(
            collective_id=collective, has_side_effects=True, vmem_limit_bytes=60 * 2**20
        ),
        name=f"scatter{collective}",
    )(*arrays)


def lanes_of(shape, low):
    lane = lax.broadcasted_iota(jnp.int32, shape, len(shape) - 1)
    return lane < HD if low else lane >= HD


def dot(left_side, right_side, contract=((1,), (0,))):
    return lax.dot_general(
        left_side, right_side, (contract, ((), ())), preferred_element_type=jnp.float32
    )


ROWS = ((1,), (1,))
COLS = ((0,), (0,))


def halves(array, col):
    return array[:, col : col + HD]


def project_kernel(x_ref, w_ref, bias_ref, q_out, kv_out):
    rows = x_ref.shape[1]
    width = x_ref.shape[2]
    tokens = x_ref[...].reshape(2 * rows, width)
    made = []
    for k in range(3):
        part = dot(tokens, w_ref[:, k * width : (k + 1) * width])
        if k != 1:
            part = part + bias_ref[k // 2 : k // 2 + 1, :]
        made.append(part.astype(jnp.bfloat16))
    q, k, v = made
    groups, per, _, _ = q_out.shape
    for g in range(groups):
        for j in range(per):
            col = (g * per + j) * HD
            q_out[g, j] = jnp.concatenate([halves(q[:rows], col), halves(q[rows:], col)], axis=1)
            kv_out[g, j] = jnp.concatenate([halves(k[:rows], col), halves(v[:rows], col)], axis=1)
            kv_out[g, per + j] = jnp.concatenate([halves(v[rows:], col), halves(k[rows:], col)], axis=1)


def project_call(tokens, weight, bias, groups):
    micro, rows, width = tokens.shape
    per = HEADS // groups
    whole = pl.BlockSpec(memory_space=pltpu.VMEM)
    return pl.pallas_call(
        project_kernel,
        out_shape=(
            jax.ShapeDtypeStruct((groups, per, rows, 2 * HD), jnp.bfloat16),
            jax.ShapeDtypeStruct((groups, 2 * per, rows, 2 * HD), jnp.bfloat16),
        ),
        grid=(1,),
        in_specs=[
            pl.BlockSpec((micro, rows, width), lambda i: (0, 0, 0)),
            pl.BlockSpec((width, 3 * width), lambda i: (0, 0)),
            pl.BlockSpec(bias.shape, lambda i: (0, 0)),
        ],
        out_specs=(
            pl.BlockSpec((groups, per, rows, 2 * HD), lambda i: (0, 0, 0, 0)),
            pl.BlockSpec((groups, 2 * per, rows, 2 * HD), lambda i: (0, 0, 0, 0)),
        ),
        compiler_params=pltpu.CompilerParams(vmem_limit_bytes=56 * 2**20),
        name="project",
    )(tokens, weight, bias)


def listed_rows(table_ref, blocks, per, m, n, j):
    shard = table_ref[2 * blocks * per * RAND + 2 * GLOB]
    total = table_ref[2 * blocks * per * RAND + 2 * GLOB + 1]
    here = shard * blocks + n
    rows = [jnp.maximum(here - 1, 0), here, jnp.minimum(here + 1, total - 1)]
    for r in range(RAND):
        rows.append(table_ref[((m * blocks + n) * per + j) * RAND + r])
    for g in range(GLOB):
        rows.append(table_ref[2 * blocks * per * RAND + m * GLOB + g])
    return rows, here, total


def globals_of(table_ref, blocks, per, m):
    at = 2 * blocks * per * RAND
    return [table_ref[at + m * GLOB + g] for g in range(GLOB)], table_ref[at + 2 * GLOB]


def allowed_mask(here, total, rows, listed):
    lane = lax.broadcasted_iota(jnp.int32, (rows, listed * BLOCK), 1)
    before = jnp.logical_and(lane < BLOCK, here == 0)
    after = jnp.logical_and(
        jnp.logical_and(lane >= 2 * BLOCK, lane < 3 * BLOCK), here == total - 1
    )
    return jnp.logical_not(jnp.logical_or(before, after))


def only(value, low):
    return jnp.where(lanes_of(value.shape, low), value, jnp.zeros_like(value))


def attend_kernel(table_ref, q_ref, kv_ref, out_ref):
    places_, per, in_place, block, _ = q_ref.shape
    blocks = places_ * in_place
    scale = jnp.bfloat16(HD ** (-0.5))

    def query_block(n, carry):
        for j in range(per):
            outs = []
            for m in range(2):
                rows, here, total = listed_rows(table_ref, blocks, per, m, n, j)
                kv = jnp.concatenate(
                    [kv_ref[r // in_place, m * per + j, r % in_place] for r in rows], axis=0
                )
                q = only(q_ref[n // in_place, j, n % in_place], m == 0) * scale
                scores = dot(q, kv, ROWS)
                scores = jnp.where(allowed_mask(here, total, block, len(rows)), scores, -jnp.inf)
                top = jnp.max(scores, axis=1, keepdims=True)
                raised = jnp.exp(scores - top)
                share = 1.0 / jnp.sum(raised, axis=1, keepdims=True)
                outs.append(dot((raised * share).astype(jnp.bfloat16), kv))
            out_ref[n // in_place, j, n % in_place] = jnp.where(
                lanes_of(outs[0].shape, True), outs[1], outs[0]
            ).astype(jnp.bfloat16)
        return carry

    lax.fori_loop(0, blocks, query_block, 0)
    step = 8
    for m in range(2):
        chosen, shard = globals_of(table_ref, blocks, per, m)
        for row in chosen:
            local = row % blocks

            @pl.when(row // blocks == shard)
            def _():
                for j in range(per):
                    q = only(q_ref[local // in_place, j, local % in_place], m == 0) * scale
                    kvs = [
                        kv_ref[pl.ds(s, step), m * per + j].reshape(step * in_place * block, 2 * HD)
                        for s in range(0, kv_ref.shape[0], step)
                    ]
                    scores = [dot(q, kv, ROWS) for kv in kvs]
                    top = scores[0].max(axis=1, keepdims=True)
                    for s in scores[1:]:
                        top = jnp.maximum(top, s.max(axis=1, keepdims=True))
                    total_sum = jnp.zeros((block, 1), jnp.float32)
                    total_out = jnp.zeros((block, 2 * HD), jnp.float32)
                    for s, kv in zip(scores, kvs):
                        raised = jnp.exp(s - top)
                        total_sum = total_sum + jnp.sum(raised, axis=1, keepdims=True)
                        total_out = total_out + dot(raised.astype(jnp.bfloat16), kv)
                    old = out_ref[local // in_place, j, local % in_place]
                    out_ref[local // in_place, j, local % in_place] = jnp.where(
                        lanes_of(old.shape, m == 1), (total_out / total_sum).astype(jnp.bfloat16), old
                    )


def attend_call(table, q, kv):
    spec = pl.BlockSpec(memory_space=pltpu.VMEM)
    return pl.pallas_call(
        attend_kernel,
        out_shape=jax.ShapeDtypeStruct(q.shape, jnp.bfloat16),
        in_specs=[pl.BlockSpec(memory_space=pltpu.SMEM), spec, spec],
        out_specs=spec,
        compiler_params=pltpu.CompilerParams(vmem_limit_bytes=56 * 2**20),
        name="attend",
    )(table, q, kv)


def attend_back_kernel(table_ref, q_ref, kv_ref, d_ref, dq_ref, dkv_ref, total_ref):
    places_, per, in_place, block, _ = q_ref.shape
    blocks = places_ * in_place
    scale = jnp.bfloat16(HD ** (-0.5))

    def clear(i, carry):
        total_ref[i] = jnp.zeros(total_ref.shape[1:], jnp.float32)
        return carry

    lax.fori_loop(0, total_ref.shape[0], clear, 0)

    def pair_of(n, j, m, keep):
        q = only(q_ref[n // in_place, j, n % in_place], m == 0) * scale
        d = only(d_ref[n // in_place, j, n % in_place], m == 1)
        if keep is not None:
            d = d * keep
        return jnp.concatenate([q, d], axis=0)

    def query_block(n, carry):
        for j in range(per):
            outs = []
            for m in range(2):
                rows, here, total = listed_rows(table_ref, blocks, per, m, n, j)
                is_global = jnp.logical_or(here == rows[-1], here == rows[-2])
                keep = jnp.where(is_global, 0.0, 1.0).astype(jnp.bfloat16)
                kv = jnp.concatenate(
                    [kv_ref[r // in_place, m * per + j, r % in_place] for r in rows], axis=0
                )
                pair = pair_of(n, j, m, keep)
                both = dot(pair, kv, ROWS)
                scores = jnp.where(
                    allowed_mask(here, total, block, len(rows)), both[:block], -jnp.inf
                )
                d_probs = both[block:]
                top = jnp.max(scores, axis=1, keepdims=True)
                raised = jnp.exp(scores - top)
                probs = raised * (1.0 / jnp.sum(raised, axis=1, keepdims=True))
                delta = jnp.sum(probs * d_probs, axis=1, keepdims=True)
                d_scores = (probs * (d_probs - delta)).astype(jnp.bfloat16)
                weights = jnp.concatenate([d_scores, probs.astype(jnp.bfloat16)], axis=0)
                d_kv = dot(weights, pair, COLS)
                for at, r in enumerate(rows):
                    total_ref[r // in_place, m * per + j, r % in_place] += d_kv[
                        at * block : (at + 1) * block
                    ]
                outs.append(dot(d_scores, kv) * HD ** (-0.5))
            dq_ref[n // in_place, j, n % in_place] = jnp.where(
                lanes_of(outs[0].shape, True), outs[0], outs[1]
            ).astype(jnp.bfloat16)
        return carry

    lax.fori_loop(0, blocks, query_block, 0)
    step = 8
    for m in range(2):
        chosen, shard = globals_of(table_ref, blocks, per, m)
        for row in chosen:
            local = row % blocks

            @pl.when(row // blocks == shard)
            def _():
                for j in range(per):
                    pair = pair_of(local, j, m, None)
                    spots = range(0, kv_ref.shape[0], step)
                    kvs = [
                        kv_ref[pl.ds(s, step), m * per + j].reshape(step * in_place * block, 2 * HD)
                        for s in spots
                    ]
                    boths = [dot(pair, kv, ROWS) for kv in kvs]
                    top = boths[0][:block].max(axis=1, keepdims=True)
                    for both in boths[1:]:
                        top = jnp.maximum(top, both[:block].max(axis=1, keepdims=True))
                    raised = [jnp.exp(both[:block] - top) for both in boths]
                    total_sum = sum(jnp.sum(r, axis=1, keepdims=True) for r in raised)
                    share = 1.0 / total_sum
                    probs = [r * share for r in raised]
                    delta = sum(
                        jnp.sum(p * both[block:], axis=1, keepdims=True)
                        for p, both in zip(probs, boths)
                    )
                    d_q = jnp.zeros((block, 2 * HD), jnp.float32)
                    for s, kv, p, both in zip(spots, kvs, probs, boths):
                        d_scores = (p * (both[block:] - delta)).astype(jnp.bfloat16)
                        weights = jnp.concatenate([d_scores, p.astype(jnp.bfloat16)], axis=0)
                        d_kv = dot(weights, pair, COLS)
                        total_ref[pl.ds(s, step), m * per + j] += d_kv.reshape(
                            step, in_place, block, 2 * HD
                        )
                        d_q = d_q + dot(d_scores, kv)
                    old = dq_ref[local // in_place, j, local % in_place]
                    dq_ref[local // in_place, j, local % in_place] = jnp.where(
                        lanes_of(old.shape, m == 0), (d_q * HD ** (-0.5)).astype(jnp.bfloat16), old
                    )

    def give(i, carry):
        dkv_ref[i] = total_ref[i].astype(jnp.bfloat16)
        return carry

    lax.fori_loop(0, total_ref.shape[0], give, 0)


def attend_back_call(table, q, kv, d):
    spec = pl.BlockSpec(memory_space=pltpu.VMEM)
    return pl.pallas_call(
        attend_back_kernel,
        out_shape=(
            jax.ShapeDtypeStruct(q.shape, jnp.bfloat16),
            jax.ShapeDtypeStruct(kv.shape, jnp.bfloat16),
        ),
        in_specs=[pl.BlockSpec(memory_space=pltpu.SMEM), spec, spec, spec],
        out_specs=(spec, spec),
        scratch_shapes=[pltpu.VMEM(kv.shape, jnp.float32)],
        compiler_params=pltpu.CompilerParams(vmem_limit_bytes=60 * 2**20),
        name="attend_back",
    )(table, q, kv, d)


def centre(values):
    center = jnp.mean(values, axis=1, keepdims=True)
    centred = values - center
    spread = jnp.mean(centred * centred, axis=1, keepdims=True)
    inverse = lax.rsqrt(spread + 1e-12)
    return centred * inverse, inverse


def centre_back(hat, inverse, grad):
    return inverse * (
        grad
        - jnp.mean(grad, axis=1, keepdims=True)
        - hat * jnp.mean(grad * hat, axis=1, keepdims=True)
    )


def rows_sum(values):
    return jnp.sum(values, axis=0, keepdims=True)


def dense_kernel(
    c_ref, x_ref, cot_ref, wo_ref, up_ref, down_ref, vec_ref, up_bias_ref,
    out_ref, d_mix_ref, d_c_ref, g_out_ref, g_up_ref, g_down_ref, g_vec_ref, g_up_bias_ref,
    ctx, first, hat, low, low_t, act, slope, ffn,
):
    groups, per, rows, _ = c_ref.shape
    width = x_ref.shape[2]
    ff = up_ref.shape[1]
    chunk = 384
    out_bias, attn_gain, attn_shift, down_bias, ffn_gain, ffn_shift = (
        vec_ref[k : k + 1, :] for k in range(6)
    )
    for p in range(HEADS // 2):
        one = c_ref[(2 * p) // per, (2 * p) % per]
        two = c_ref[(2 * p + 1) // per, (2 * p + 1) % per]
        at = pl.ds(p * 2 * HD, 2 * HD)
        ctx[:rows, at] = jnp.concatenate([one[:, HD:], two[:, HD:]], axis=1)
        ctx[rows:, at] = jnp.concatenate([one[:, :HD], two[:, :HD]], axis=1)
    tokens = x_ref[...].reshape(2 * rows, width).astype(jnp.float32)
    hat_first, inverse_first = centre(tokens + dot(ctx[...], wo_ref[...]) + out_bias)
    hat[...] = hat_first
    first[...] = hat_first * attn_gain + attn_shift
    low[...] = first[...].astype(jnp.bfloat16)
    low_t[...] = first[...].T.astype(jnp.bfloat16)
    ffn[...] = first[...] + down_bias

    def forward(i, carry):
        at = pl.ds(pl.multiple_of(i * chunk, chunk), chunk)
        hidden = dot(low[...], up_ref[:, at]) + up_bias_ref[:, at]
        share = 0.5 * (1.0 + lax.erf(hidden * 0.7071067811865476))
        bell = jnp.exp(-0.5 * hidden * hidden) * 0.3989422804014327
        slope[:, at] = share + hidden * bell
        act_low = (hidden * share).astype(jnp.bfloat16)
        act[:, at] = act_low
        ffn[...] += dot(act_low, down_ref[at, :])
        return carry

    lax.fori_loop(0, ff // chunk, forward, 0)
    hat_second, inverse_second = centre(ffn[...])
    out_ref[...] = (
        (hat_second * ffn_gain + ffn_shift).astype(jnp.bfloat16).reshape(2, rows, width)
    )
    cot = cot_ref[...].reshape(2 * rows, width).astype(jnp.float32)
    g_vec_ref[4:5, :] = rows_sum(cot * hat_second)
    g_vec_ref[5:6, :] = rows_sum(cot)
    d_second = centre_back(hat_second, inverse_second, cot * ffn_gain)
    d_ffn = d_second.astype(jnp.bfloat16)
    g_vec_ref[3:4, :] = rows_sum(d_ffn.astype(jnp.float32))
    ffn[...] = d_second

    def backward(i, carry):
        at = pl.ds(pl.multiple_of(i * chunk, chunk), chunk)
        d_act = dot(d_ffn, down_ref[at, :], ROWS)
        d_hidden = (d_act * slope[:, at]).astype(jnp.bfloat16)
        g_up_bias_ref[:, at] = rows_sum(d_hidden.astype(jnp.float32))
        g_down_ref[at, :] = dot(act[:, at], d_ffn, COLS).astype(jnp.bfloat16)
        g_up_ref[:, at] = dot(low_t[...], d_hidden).astype(jnp.bfloat16)
        ffn[...] += dot(d_hidden, up_ref[:, at], ROWS)
        return carry

    lax.fori_loop(0, ff // chunk, backward, 0)
    d_first = ffn[...]
    g_vec_ref[1:2, :] = rows_sum(d_first * hat[...])
    g_vec_ref[2:3, :] = rows_sum(d_first)
    d_mix = centre_back(hat[...], inverse_first, d_first * attn_gain)
    d_mix_ref[...] = d_mix
    d_branch = d_mix.astype(jnp.bfloat16)
    g_vec_ref[0:1, :] = rows_sum(d_branch.astype(jnp.float32))
    g_vec_ref[6:8, :] = jnp.zeros((2, width), jnp.float32)
    g_out_ref[...] = dot(ctx[...], d_branch, COLS).astype(jnp.bfloat16)
    d_ctx = dot(d_branch, wo_ref[...], ROWS).astype(jnp.bfloat16)
    for head in range(HEADS):
        d_c_ref[head // per, head % per] = jnp.concatenate(
            [halves(d_ctx[rows:], head * HD), halves(d_ctx[:rows], head * HD)], axis=1
        )


def dense_call(c, tokens, cot, mixed, up, down, vec, up_bias):
    micro, rows, width = tokens.shape
    ff = up.shape[1]
    both = micro * rows
    spec = pl.BlockSpec(memory_space=pltpu.VMEM)
    f32, bf16 = jnp.float32, jnp.bfloat16

    def full(shape):
        return pl.BlockSpec(shape, lambda i: (0,) * len(shape))

    outs = (
        jax.ShapeDtypeStruct(tokens.shape, bf16),
        jax.ShapeDtypeStruct((both, width), f32),
        jax.ShapeDtypeStruct(c.shape, bf16),
        jax.ShapeDtypeStruct((width, width), bf16),
        jax.ShapeDtypeStruct((width, ff), bf16),
        jax.ShapeDtypeStruct((ff, width), bf16),
        jax.ShapeDtypeStruct((8, width), f32),
        jax.ShapeDtypeStruct((1, ff), f32),
    )
    return pl.pallas_call(
        dense_kernel,
        out_shape=outs,
        grid=(1,),
        in_specs=[
            full(c.shape),
            full(tokens.shape),
            full(cot.shape),
            pl.BlockSpec((width, width), lambda i: (0, 3), pipeline_mode=pl.Buffered(1)),
            pl.BlockSpec((width, ff), lambda i: (0, 0), pipeline_mode=pl.Buffered(1)),
            pl.BlockSpec((ff, width), lambda i: (0, 0), pipeline_mode=pl.Buffered(1)),
            full(vec.shape),
            full(up_bias.shape),
        ],
        out_specs=tuple(
            pl.BlockSpec(o.shape, lambda i, r=len(o.shape): (0,) * r, pipeline_mode=pl.Buffered(1))
            for o in outs
        ),
        scratch_shapes=[
            pltpu.VMEM((both, width), bf16),
            pltpu.VMEM((both, width), f32),
            pltpu.VMEM((both, width), f32),
            pltpu.VMEM((both, width), bf16),
            pltpu.VMEM((width, both), bf16),
            pltpu.VMEM((both, ff), bf16),
            pltpu.VMEM((both, ff), f32),
            pltpu.VMEM((both, width), f32),
        ],
        compiler_params=pltpu.CompilerParams(vmem_limit_bytes=60 * 2**20),
        name="dense",
    )(c, tokens, cot, mixed, up, down, vec, up_bias)


def project_back_kernel(
    q_ref, kv_ref, x_ref, w_ref, d_mix_ref, g_out_ref, d_x_ref, g_ref, g_vec_ref, d_q, d_k, d_v
):
    groups, per, rows, _ = q_ref.shape
    width = x_ref.shape[2]
    for p in range(HEADS // 2):
        at = pl.ds(p * 2 * HD, 2 * HD)

        def of(ref, shift, low):
            sides = []
            for head in (2 * p, 2 * p + 1):
                tile = ref[head // per, shift + head % per]
                sides.append(tile[:, :HD] if low else tile[:, HD:])
            return jnp.concatenate(sides, axis=1)

        d_q[:rows, at] = of(q_ref, 0, True)
        d_q[rows:, at] = of(q_ref, 0, False)
        d_k[:rows, at] = of(kv_ref, 0, True)
        d_v[:rows, at] = of(kv_ref, 0, False)
        d_k[rows:, at] = of(kv_ref, per, False)
        d_v[rows:, at] = of(kv_ref, per, True)
    tokens = x_ref[...].reshape(2 * rows, width)
    d_x = d_mix_ref[...]
    for k, part in enumerate((d_q, d_k, d_v)):
        at = slice(k * width, (k + 1) * width)
        d_x = d_x + dot(part[...], w_ref[:, at], ROWS)
        g_ref[:, at] = dot(tokens, part[...], COLS).astype(jnp.bfloat16)
        if k != 1:
            g_vec_ref[k // 2 : k // 2 + 1, :] = rows_sum(part[...].astype(jnp.float32))
    g_ref[:, 3 * width :] = g_out_ref[...]
    g_vec_ref[2:8, :] = jnp.zeros((6, width), jnp.float32)
    d_x_ref[...] = d_x.astype(jnp.bfloat16).reshape(2, rows, width)


def project_back_call(q, kv, tokens, mixed, d_mix, g_out):
    micro, rows, width = tokens.shape
    f32, bf16 = jnp.float32, jnp.bfloat16

    def full(shape):
        return pl.BlockSpec(shape, lambda i: (0,) * len(shape), pipeline_mode=pl.Buffered(1))

    outs = (
        jax.ShapeDtypeStruct(tokens.shape, bf16),
        jax.ShapeDtypeStruct((width, 4 * width), bf16),
        jax.ShapeDtypeStruct((8, width), f32),
    )
    return pl.pallas_call(
        project_back_kernel,
        out_shape=outs,
        grid=(1,),
        in_specs=[
            full(q.shape),
            full(kv.shape),
            full(tokens.shape),
            full((width, 3 * width)),
            full(d_mix.shape),
            full(g_out.shape),
        ],
        out_specs=tuple(full(o.shape) for o in outs),
        scratch_shapes=[pltpu.VMEM((micro * rows, width), bf16)] * 3,
        compiler_params=pltpu.CompilerParams(vmem_limit_bytes=56 * 2**20),
        name="project_back",
    )(q, kv, tokens, mixed, d_mix, g_out)


def cut(axis, start, size):
    return (axis, start, size)


def near_body(inputs, cotangent, random_blocks, global_blocks, *shards):
    (
        query_weight, query_bias, key_weight, value_weight, value_bias, out_weight, out_bias, attn_gain,
        attn_shift, up_weight, up_bias, down_weight, down_bias, ffn_gain, ffn_shift,
    ) = shards
    groups = lax.axis_size("head")
    shard_count = lax.axis_size("blk")
    devices = groups * shard_count
    shard = lax.axis_index("blk")
    group = lax.axis_index("head")
    micro, rows, width = inputs.shape
    depth = query_weight.shape[0]
    ff = up_weight.shape[1]
    per = HEADS // groups
    in_place = rows // BLOCK
    blocks = groups * in_place
    vectors = jnp.stack(
        [query_bias, value_bias, out_bias, attn_gain, attn_shift, down_bias, ffn_gain, ffn_shift], axis=1
    )
    vectors = jnp.concatenate([vectors, up_bias.reshape(depth, -1)], axis=1)
    vectors = jnp.pad(vectors, ((0, 0), (0, 128 - vectors.shape[1])))
    mixed_shard = jnp.concatenate(
        [query_weight, key_weight, value_weight, out_weight, vectors], axis=1
    )
    half = 2 * width
    (mixed,) = gather_call(
        [mixed_shard], [(False, True, (cut(1, 0, half), cut(1, half, half + 128)))], 1
    )
    mixed = mixed.reshape(width, -1)
    rows_f32 = mixed[:, 4 * width : 4 * width + 16].astype(jnp.float32).T
    bias = rows_f32[:8]
    vec = rows_f32[2:10]
    up_bias_row = mixed[:, 4 * width + 8 : 4 * width + 8 + ff // width].astype(jnp.float32).reshape(1, ff)
    q_parts, kv_parts = project_call(inputs, mixed, bias, groups)
    pairs = (cut(0, 0, per), cut(0, per, per))
    q, kv, up, down = gather_call(
        [q_parts, kv_parts, up_weight, down_weight],
        [
            (True, False, None),
            (True, True, pairs),
            (False, True, (cut(1, 0, ff), None)),
            (False, True, (None, cut(1, 0, width))),
        ],
        2,
    )
    up = up.reshape(width, ff)
    down = down.reshape(ff, width)
    mine = lax.dynamic_slice(
        random_blocks,
        (0, shard * blocks, group * per, 0),
        (micro, blocks, per, RAND),
    )
    table = jnp.concatenate(
        [
            mine.reshape(-1),
            global_blocks.reshape(-1),
            jnp.stack([shard, shard_count * blocks]).astype(jnp.int32),
        ]
    )
    split = (in_place, BLOCK, 2 * HD)
    q = q.reshape((groups, per) + split)
    kv = kv.reshape((devices, 2 * per) + split)
    packed = (groups, per, rows, 2 * HD)
    context = attend_call(table, q, kv).reshape(packed)
    (context,) = gather_call([context], [(True, False, None)], 3)
    layer_out, d_mix, d_context, g_out, g_up, g_down, g_vec, g_up_bias = dense_call(
        context, inputs, cotangent, mixed, up, down, vec, up_bias_row
    )
    (d_context,) = gather_call([d_context], [(True, False, None)], 4)
    d_q, d_kv = attend_back_call(table, q, kv, d_context.reshape(q.shape))
    d_q, d_kv, grad_up, grad_down = scatter_call(
        [
            d_q.reshape(packed),
            d_kv.reshape(devices, 2 * per, rows, 2 * HD),
            g_up.reshape(devices, depth, ff),
            g_down.reshape(devices, -1, width),
        ],
        [
            (False, False, None),
            (False, True, pairs),
            (True, True, (cut(1, 0, ff), None)),
            (True, True, (None, cut(1, 0, width))),
        ],
        5,
    )
    input_grad, g_mixed, g_vec_two = project_back_call(d_q, d_kv, inputs, mixed, d_mix, g_out)
    sums = jnp.concatenate([g_vec_two[:2], g_vec[:6]], axis=0).reshape(8, devices, depth)
    sums = jnp.concatenate(
        [sums.transpose(1, 0, 2), g_up_bias.reshape(devices, ff // width, depth)], axis=1
    )
    sums = jnp.pad(sums, ((0, 0), (0, 16 - sums.shape[1]), (0, 128 - depth)))
    grad_mixed, grad_vec = scatter_call(
        [g_mixed.reshape(devices, depth, 4 * width), sums],
        [
            (True, True, (cut(1, 0, half), cut(1, half, half))),
            (True, True, (cut(1, 0, 128), None)),
        ],
        6,
    )
    grad_query, grad_key, grad_value, grad_out = (
        grad_mixed[:, k * width : (k + 1) * width] for k in range(4)
    )
    vector = [grad_vec[k, :depth] for k in range(8)]
    grad_up_bias = grad_vec[8 : 8 + ff // width, :depth].reshape(-1)
    return (
        layer_out, input_grad, grad_query, vector[0], grad_key, grad_value, vector[1], grad_out,
        vector[2], vector[3], vector[4], grad_up, grad_up_bias, grad_down, vector[5], vector[6], vector[7],
    )


def with_halo(cells, sides, width):
    for axis, dim in sides:
        count = lax.axis_size(axis)
        ends = count - 1
        head = lax.slice_in_dim(cells, 0, width, axis=dim)
        tail = lax.slice_in_dim(cells, cells.shape[dim] - width, cells.shape[dim], axis=dim)
        cells = jnp.concatenate(
            [
                lax.ppermute(tail, axis, [(i, (i + 1) % count) for i in range(ends)]),
                cells,
                lax.ppermute(head, axis, [((i + 1) % count, i) for i in range(ends)]),
            ],
            axis=dim,
        )
    return cells


def combined_all(part, axis, combine):
    gathered = jax.tree.map(lambda a: lax.all_gather(a, axis), part)

    def take(source):
        return jax.tree.map(lambda a: lax.dynamic_index_in_dim(a, source, 0, False), gathered)

    return lax.fori_loop(
        1, lax.axis_size(axis), lambda source, state: combine(state, take(source)), take(0)
    )


def taken(table, rows):
    return lax.map(lambda row: lax.dynamic_index_in_dim(table, row, 0, False), rows)


def layer_norm(values, norm_gain, norm_shift):
    center = jnp.mean(values, axis=-1, keepdims=True)
    centred = values - center
    spread = jnp.mean(centred * centred, axis=-1, keepdims=True)
    return centred * lax.rsqrt(spread + 1e-12) * norm_gain + norm_shift


def gelu_exact(values):
    return jax.nn.gelu(values, approximate=False)


def matmul(left_side, right_side):
    return jnp.dot(left_side, right_side, preferred_element_type=jnp.float32)


def matmul_left(left_side, right_side):
    return lax.dot_general(
        left_side, right_side, (((0,), (0,)), ((), ())), preferred_element_type=jnp.float32
    )


def matmul_right(left_side, right_side):
    return lax.dot_general(
        left_side, right_side, (((1,), (1,)), ((), ())), preferred_element_type=jnp.float32
    )


def column_sum(values):
    return jnp.sum(values.astype(jnp.float32), axis=0)


def combine_parts(earlier, later_part):
    joint_top = jnp.maximum(earlier[0], later_part[0])
    first_factor = jnp.exp(earlier[0] - joint_top)
    second_factor = jnp.exp(later_part[0] - joint_top)
    return (
        joint_top,
        earlier[1] * first_factor + later_part[1] * second_factor,
        earlier[2] * first_factor[..., None] + later_part[2] * second_factor[..., None],
    )


def fetch_weights(
    query_weight,
    query_bias,
    key_weight,
    value_weight,
    value_bias,
    out_weight,
    out_bias,
    attn_gain,
    attn_shift,
    up_weight,
    up_bias,
    down_weight,
    down_bias,
    ffn_gain,
    ffn_shift,
):
    return (
        lax.all_gather(query_weight, ("blk", "head"), axis=0, tiled=True),
        lax.all_gather(query_bias, ("blk", "head"), axis=0, tiled=True),
        lax.all_gather(key_weight, ("blk", "head"), axis=0, tiled=True),
        lax.all_gather(value_weight, ("blk", "head"), axis=0, tiled=True),
        lax.all_gather(value_bias, ("blk", "head"), axis=0, tiled=True),
        lax.all_gather(out_weight, ("blk", "head"), axis=0, tiled=True),
        lax.all_gather(out_bias, ("blk", "head"), axis=0, tiled=True),
        lax.all_gather(attn_gain, ("blk", "head"), axis=0, tiled=True),
        lax.all_gather(attn_shift, ("blk", "head"), axis=0, tiled=True),
        lax.all_gather(up_weight, ("blk", "head"), axis=0, tiled=True),
        lax.all_gather(up_bias, ("blk", "head"), axis=0, tiled=True),
        lax.all_gather(down_weight, ("blk", "head"), axis=0, tiled=True),
        lax.all_gather(down_bias, ("blk", "head"), axis=0, tiled=True),
        lax.all_gather(ffn_gain, ("blk", "head"), axis=0, tiled=True),
        lax.all_gather(ffn_shift, ("blk", "head"), axis=0, tiled=True),
    )


def reduce_grads(totals):
    return (
        lax.psum_scatter(totals[0], ("blk", "head"), scatter_dimension=0, tiled=True),
        lax.psum_scatter(totals[1], ("blk", "head"), scatter_dimension=0, tiled=True),
        lax.psum_scatter(totals[2], ("blk", "head"), scatter_dimension=0, tiled=True),
        lax.psum_scatter(totals[3], ("blk", "head"), scatter_dimension=0, tiled=True),
        lax.psum_scatter(totals[4], ("blk", "head"), scatter_dimension=0, tiled=True),
        lax.psum_scatter(totals[5], ("blk", "head"), scatter_dimension=0, tiled=True),
        lax.psum_scatter(totals[6], ("blk", "head"), scatter_dimension=0, tiled=True),
        lax.psum_scatter(totals[7], ("blk", "head"), scatter_dimension=0, tiled=True),
        lax.psum_scatter(totals[8], ("blk", "head"), scatter_dimension=0, tiled=True),
        lax.psum_scatter(totals[9], ("blk", "head"), scatter_dimension=0, tiled=True),
        lax.psum_scatter(totals[10], ("blk", "head"), scatter_dimension=0, tiled=True),
        lax.psum_scatter(totals[11], ("blk", "head"), scatter_dimension=0, tiled=True),
        lax.psum_scatter(totals[12], ("blk", "head"), scatter_dimension=0, tiled=True),
        lax.psum_scatter(totals[13], ("blk", "head"), scatter_dimension=0, tiled=True),
        lax.psum_scatter(totals[14], ("blk", "head"), scatter_dimension=0, tiled=True),
    )


def sparse_forward(packed):
    group_queries, group_keys, group_values, group_allowed = packed
    attn_scale = HD ** (-0.5)
    scores = (
        jnp.einsum("gqhd,ghkd->ghqk", group_queries, group_keys, preferred_element_type=jnp.float32)
        * attn_scale
    )
    scores = jnp.where(group_allowed[:, None, None, :], scores, -jnp.inf)
    row_top = jnp.max(scores, axis=-1, keepdims=True)
    raised = jnp.exp(scores - row_top)
    row_total = jnp.sum(raised, axis=-1, keepdims=True)
    probs_low = (raised / row_total).astype(jnp.bfloat16)
    output = jnp.einsum(
        "ghqk,ghkd->gqhd", probs_low, group_values, preferred_element_type=jnp.float32
    )
    return (output, (row_top + jnp.log(row_total))[..., 0])


def sparse_backward(nearby, carried, packed):
    group_queries, group_keys, group_values, group_allowed, group_lse, group_grad = packed
    attn_scale = HD ** (-0.5)
    per_group = group_queries.shape[0]
    heads_dev = group_queries.shape[2]
    scores = (
        jnp.einsum("gqhd,ghkd->ghqk", group_queries, group_keys, preferred_element_type=jnp.float32)
        * attn_scale
    )
    scores = jnp.where(group_allowed[:, None, None, :], scores, -jnp.inf)
    probs = jnp.exp(scores - group_lse[..., None])
    d_probs = jnp.einsum(
        "gqhd,ghkd->ghqk", group_grad, group_values, preferred_element_type=jnp.float32
    )
    row_delta = jnp.sum(probs * d_probs, axis=-1, keepdims=True)
    d_scores = (probs * (d_probs - row_delta)).astype(jnp.bfloat16)
    d_queries = (
        jnp.einsum("ghqk,ghkd->gqhd", d_scores, group_keys, preferred_element_type=jnp.float32)
        * attn_scale
    )
    d_keys = (
        jnp.einsum("ghqk,gqhd->ghkd", d_scores, group_queries, preferred_element_type=jnp.float32)
        * attn_scale
    )
    d_values = jnp.einsum(
        "ghqk,gqhd->ghkd",
        probs.astype(jnp.bfloat16),
        group_grad,
        preferred_element_type=jnp.float32,
    )
    d_keys = d_keys.reshape(per_group, heads_dev, -1, BLOCK, HD)
    d_values = d_values.reshape(per_group, heads_dev, -1, BLOCK, HD)
    carried = (
        carried[0] + jnp.sum(d_keys[:, :, nearby:], axis=0),
        carried[1] + jnp.sum(d_values[:, :, nearby:], axis=0),
    )
    return (carried, (d_queries, d_keys[:, :, :nearby], d_values[:, :, :nearby]))


def micro_batch(tokens, cotangent_rows, random_rows, global_rows, weights):
    (
        full_query,
        full_query_bias,
        full_key,
        full_value,
        full_value_bias,
        full_out,
        full_out_bias,
        full_attn_gain,
        full_attn_shift,
        full_up,
        full_up_bias,
        full_down,
        full_down_bias,
        full_ffn_gain,
        full_ffn_shift,
    ) = weights
    attn_scale = HD ** (-0.5)
    shards = lax.axis_size("blk")
    head_groups = lax.axis_size("head")
    shard_index = lax.axis_index("blk")
    group_index = lax.axis_index("head")
    heads_dev = HEADS // head_groups
    group_width = heads_dev * HD
    listed = 3 + RAND + GLOB
    nearby = 3 + RAND
    projected = jnp.stack(
        [
            matmul(tokens, full_query) + full_query_bias,
            matmul(tokens, full_key),
            matmul(tokens, full_value) + full_value_bias,
        ]
    ).astype(jnp.bfloat16)
    by_head = lax.all_to_all(projected, "head", split_axis=2, concat_axis=1, tiled=True)
    row_count = by_head.shape[1]
    block_count = row_count // BLOCK
    blocks_all = block_count * shards
    key_rows = by_head[1]
    value_rows = by_head[2]
    padded = with_halo(by_head[1:3], (("blk", 1),), BLOCK)
    extended = padded.reshape(2, block_count + 2, BLOCK, heads_dev, HD).transpose(0, 1, 3, 2, 4)
    window = jnp.stack([extended[:, offset : offset + block_count] for offset in range(3)], axis=3)
    block_ids = shard_index * block_count + jnp.arange(block_count, dtype=jnp.int32)
    neighbour = block_ids[:, None] + jnp.arange(-1, 2, dtype=jnp.int32)[None, :]
    inside = (neighbour >= 0) & (neighbour < blocks_all)
    head_table = lax.dynamic_slice_in_dim(random_rows, group_index * heads_dev, heads_dev, 1)
    requests = block_count * heads_dev * RAND
    all_requests = head_table.reshape(shards, requests)
    capacity = (requests + shards - 1) // shards + 1
    wanted = lax.dynamic_slice_in_dim(all_requests, shard_index, 1, 0)[0]
    source = wanted // block_count
    place = jnp.arange(requests, dtype=jnp.int32)
    earlier = (place[:, None] > place[None, :]).astype(jnp.int32)
    same_source = (source[:, None] == source[None, :]).astype(jnp.int32)
    slot_index = jnp.sum(earlier * same_source, axis=1)
    mine_mask = (all_requests // block_count == shard_index).astype(jnp.int32)
    send_order = jnp.sum(earlier[None] * mine_mask[:, None, :], axis=2)
    match_mask = mine_mask[:, :, None] * (
        send_order[:, :, None] == jnp.arange(capacity, dtype=jnp.int32)[None, None, :]
    ).astype(jnp.int32)
    head_of = jnp.arange(requests, dtype=jnp.int32) // RAND % heads_dev
    row_of = all_requests % block_count * heads_dev + head_of[None, :]
    send_rows = jnp.sum(match_mask * row_of[:, :, None], axis=1)
    filled = jnp.sum(match_mask, axis=1).astype(jnp.float32)
    block_table = (
        by_head[1:3]
        .reshape(2, block_count, BLOCK, heads_dev, HD)
        .transpose(1, 3, 0, 2, 4)
        .reshape(block_count * heads_dev, 2, BLOCK, HD)
    )
    outgoing = taken(block_table, send_rows.reshape(-1))
    incoming = lax.all_to_all(outgoing, "blk", split_axis=0, concat_axis=0, tiled=True)
    fetched = taken(incoming, source * capacity + slot_index).reshape(
        block_count, heads_dev, RAND, 2, BLOCK, HD
    )
    owner_shard = global_rows // block_count
    present = owner_shard == shard_index
    local_block = global_rows % block_count
    own_rows = jnp.stack(
        [
            lax.dynamic_index_in_dim(
                by_head.reshape(3, block_count, BLOCK, group_width), local_block[g], 1, False
            )
            for g in range(GLOB)
        ],
        axis=1,
    )
    shared = lax.psum(
        jnp.where(present[None, :, None, None], own_rows.astype(jnp.float32), 0.0), "blk"
    ).astype(jnp.bfloat16)
    shared_pairs = shared[1:3].reshape(2, GLOB, BLOCK, heads_dev, HD).transpose(0, 3, 1, 2, 4)

    def listed_blocks(which):
        near_part = window[which]
        random_part = fetched[:, :, :, which]
        global_part = jnp.broadcast_to(
            shared_pairs[which][None], (block_count, heads_dev, GLOB, BLOCK, HD)
        )
        return jnp.concatenate([near_part, random_part, global_part], axis=2).reshape(
            block_count, heads_dev, listed * BLOCK, HD
        )

    per_group = min(8, block_count)
    group_count = block_count // per_group
    query_groups = by_head[0].reshape(group_count, per_group, BLOCK, heads_dev, HD)
    key_groups = listed_blocks(0).reshape(group_count, per_group, heads_dev, listed * BLOCK, HD)
    value_groups = listed_blocks(1).reshape(group_count, per_group, heads_dev, listed * BLOCK, HD)
    allowed = jnp.repeat(
        jnp.concatenate([inside, jnp.ones((block_count, RAND + GLOB), jnp.bool_)], axis=1),
        BLOCK,
        axis=1,
    )
    allow_groups = allowed.reshape(group_count, per_group, listed * BLOCK)
    sparse_out, sparse_lse = lax.map(
        sparse_forward, (query_groups, key_groups, value_groups, allow_groups)
    )
    global_queries = shared[0].reshape(GLOB, BLOCK, heads_dev, HD)
    key_heads = key_rows.reshape(row_count, heads_dev, HD)
    value_wide = value_rows.reshape(row_count, heads_dev, HD).astype(jnp.float32)
    global_scores = (
        jnp.einsum("gqhd,khd->ghqk", global_queries, key_heads, preferred_element_type=jnp.float32)
        * attn_scale
    )
    global_top = jnp.max(global_scores, axis=-1)
    global_raised = jnp.exp(global_scores - global_top[..., None])
    merged = combined_all(
        (
            global_top,
            jnp.sum(global_raised, axis=-1),
            jnp.einsum(
                "ghqk,khd->ghqd", global_raised, value_wide, precision=lax.Precision.HIGHEST
            ),
        ),
        "blk",
        combine_parts,
    )
    global_out = merged[2] / merged[1][..., None]
    global_lse = merged[0] + jnp.log(merged[1])
    global_hits = (block_ids[:, None] == global_rows[None, :]).astype(jnp.float32)
    is_global = jnp.sum(global_hits, axis=1) > 0
    replaced = jnp.einsum("ng,ghqd->nqhd", global_hits, global_out, precision=lax.Precision.HIGHEST)
    context = jnp.where(
        is_global[:, None, None, None],
        replaced,
        sparse_out.reshape(block_count, BLOCK, heads_dev, HD),
    )
    context_rows = context.reshape(row_count, group_width).astype(jnp.bfloat16)
    context_tokens = lax.all_to_all(context_rows, "head", split_axis=0, concat_axis=1, tiled=True)
    branch = matmul(context_tokens, full_out) + full_out_bias
    first_in = tokens.astype(jnp.float32) + branch
    first_norm, first_pull = jax.vjp(
        layer_norm,
        first_in,
        full_attn_gain.astype(jnp.float32),
        full_attn_shift.astype(jnp.float32),
    )
    first_low = first_norm.astype(jnp.bfloat16)
    hidden = matmul(first_low, full_up) + full_up_bias
    act_value, gelu_pull = jax.vjp(gelu_exact, hidden)
    act_low = act_value.astype(jnp.bfloat16)
    ffn_out = matmul(act_low, full_down) + full_down_bias
    result, second_pull = jax.vjp(
        layer_norm,
        first_norm + ffn_out,
        full_ffn_gain.astype(jnp.float32),
        full_ffn_shift.astype(jnp.float32),
    )
    d_second, grad_ffn_gain, grad_ffn_shift = second_pull(cotangent_rows.astype(jnp.float32))
    d_ffn = d_second.astype(jnp.bfloat16)
    grad_down = matmul_left(act_low, d_ffn)
    grad_down_bias = column_sum(d_ffn)
    (d_hidden,) = gelu_pull(matmul_right(d_ffn, full_down))
    d_hidden_low = d_hidden.astype(jnp.bfloat16)
    grad_up = matmul_left(first_low, d_hidden_low)
    grad_up_bias = column_sum(d_hidden_low)
    d_first = d_second + matmul_right(d_hidden_low, full_up)
    d_mix, grad_attn_gain, grad_attn_shift = first_pull(d_first)
    d_branch = d_mix.astype(jnp.bfloat16)
    grad_out = matmul_left(context_tokens, d_branch)
    grad_out_bias = column_sum(d_branch)
    d_context = matmul_right(d_branch, full_out).astype(jnp.bfloat16)
    d_heads = lax.all_to_all(d_context, "head", split_axis=1, concat_axis=0, tiled=True).reshape(
        block_count, BLOCK, heads_dev, HD
    )
    d_sparse = jnp.where(is_global[:, None, None, None], jnp.zeros_like(d_heads), d_heads)
    d_global = lax.psum(
        jnp.where(
            present[:, None, None, None], taken(d_heads, local_block).astype(jnp.float32), 0.0
        ),
        "blk",
    )
    start_carry = (
        jnp.zeros((heads_dev, GLOB, BLOCK, HD), jnp.float32),
        jnp.zeros((heads_dev, GLOB, BLOCK, HD), jnp.float32),
    )
    global_sums, (d_query_parts, near_keys, near_values) = lax.scan(
        partial(sparse_backward, nearby),
        start_carry,
        (
            query_groups,
            key_groups,
            value_groups,
            allow_groups,
            sparse_lse,
            d_sparse.reshape(group_count, per_group, BLOCK, heads_dev, HD),
        ),
    )
    d_query_sparse = d_query_parts.reshape(block_count, BLOCK, heads_dev, HD)
    near_keys = near_keys.reshape(block_count, heads_dev, nearby, BLOCK, HD)
    near_values = near_values.reshape(block_count, heads_dev, nearby, BLOCK, HD)
    near_grads = jnp.stack([near_keys[:, :, :3], near_values[:, :, :3]])
    ext_grads = jnp.zeros((2, block_count + 2, heads_dev, BLOCK, HD), jnp.float32)
    for offset in range(3):
        ext_grads = ext_grads + jnp.pad(
            near_grads[:, :, :, offset], ((0, 0), (offset, 2 - offset), (0, 0), (0, 0), (0, 0))
        )
    rim_pair = jnp.stack([ext_grads[:, 0], ext_grads[:, block_count + 1]], axis=1)
    arrived = with_halo(rim_pair.astype(jnp.bfloat16), (("blk", 1),), 1).astype(rim_pair.dtype)
    inner_grads = ext_grads[:, 1 : block_count + 1]
    inner_grads = inner_grads.at[:, 0].add(arrived[:, 0]).at[:, block_count - 1].add(arrived[:, 3])
    far_grads = jnp.stack([near_keys[:, :, 3:], near_values[:, :, 3:]], axis=3).reshape(
        requests, 2, BLOCK, HD
    )
    outbox = (
        jnp.zeros((shards, capacity, 2, BLOCK, HD), jnp.float32)
        .at[source, slot_index]
        .set(far_grads)
    )
    arrived_slots = (
        lax.all_to_all(
            outbox.astype(jnp.bfloat16), "blk", split_axis=0, concat_axis=0, tiled=True
        ).astype(outbox.dtype)
        * filled[:, :, None, None, None]
    )
    landed = (
        jnp.zeros((block_count * heads_dev, 2, BLOCK, HD), jnp.float32)
        .at[send_rows.reshape(-1)]
        .add(arrived_slots.reshape(shards * capacity, 2, BLOCK, HD))
    )
    landed = landed.reshape(block_count, heads_dev, 2, BLOCK, HD)
    global_probs = jnp.exp(global_scores - global_lse[..., None])
    d_probs_global = jnp.einsum(
        "gqhd,khd->ghqk", d_global, value_wide, precision=lax.Precision.HIGHEST
    )
    delta_global = jnp.einsum(
        "gqhd,ghqd->ghq", d_global, global_out, precision=lax.Precision.HIGHEST
    )
    d_scores_global = (global_probs * (d_probs_global - delta_global[..., None])).astype(
        jnp.bfloat16
    )
    d_global_queries = (
        jnp.einsum("ghqk,khd->gqhd", d_scores_global, key_heads, preferred_element_type=jnp.float32)
        * attn_scale
    )
    d_keys_global = (
        jnp.einsum(
            "ghqk,gqhd->khd", d_scores_global, global_queries, preferred_element_type=jnp.float32
        )
        * attn_scale
    )
    d_values_global = jnp.einsum(
        "ghqk,gqhd->khd", global_probs, d_global, precision=lax.Precision.HIGHEST
    )
    returned = lax.psum(
        jnp.stack(
            [
                d_global_queries,
                global_sums[0].transpose(1, 2, 0, 3),
                global_sums[1].transpose(1, 2, 0, 3),
            ]
        ),
        "blk",
    )
    owned_grads = jnp.einsum(
        "ng,cgqhd->cnqhd", global_hits, returned, precision=lax.Precision.HIGHEST
    )
    d_query_total = d_query_sparse + owned_grads[0]
    d_key_total = (
        (inner_grads[0] + landed[:, :, 0]).transpose(0, 2, 1, 3)
        + d_keys_global.reshape(block_count, BLOCK, heads_dev, HD)
        + owned_grads[1]
    )
    d_value_total = (
        (inner_grads[1] + landed[:, :, 1]).transpose(0, 2, 1, 3)
        + d_values_global.reshape(block_count, BLOCK, heads_dev, HD)
        + owned_grads[2]
    )
    stacked = (
        jnp.stack([d_query_total, d_key_total, d_value_total])
        .reshape(3, row_count, group_width)
        .astype(jnp.bfloat16)
    )
    token_grads = lax.all_to_all(stacked, "head", split_axis=1, concat_axis=2, tiled=True)
    d_tokens = (
        d_mix
        + matmul_right(token_grads[0], full_query)
        + matmul_right(token_grads[1], full_key)
        + matmul_right(token_grads[2], full_value)
    )
    grads = (
        matmul_left(tokens, token_grads[0]),
        column_sum(token_grads[0]),
        matmul_left(tokens, token_grads[1]),
        matmul_left(tokens, token_grads[2]),
        column_sum(token_grads[2]),
        grad_out,
        grad_out_bias,
        grad_attn_gain,
        grad_attn_shift,
        grad_up,
        grad_up_bias,
        grad_down,
        grad_down_bias,
        grad_ffn_gain,
        grad_ffn_shift,
    )
    return (result.astype(jnp.bfloat16), d_tokens.astype(jnp.bfloat16), grads)


def body(
    inputs,
    cotangent,
    random_blocks,
    global_blocks,
    query_weight,
    query_bias,
    key_weight,
    value_weight,
    value_bias,
    out_weight,
    out_bias,
    attn_gain,
    attn_shift,
    up_weight,
    up_bias,
    down_weight,
    down_bias,
    ffn_gain,
    ffn_shift,
):
    weight_shards = (
        query_weight,
        query_bias,
        key_weight,
        value_weight,
        value_bias,
        out_weight,
        out_bias,
        attn_gain,
        attn_shift,
        up_weight,
        up_bias,
        down_weight,
        down_bias,
        ffn_gain,
        ffn_shift,
    )
    results = []
    input_grads = []
    totals = None
    for micro_index in range(inputs.shape[0]):
        weights = fetch_weights(*weight_shards)
        result, token_grad, grads = micro_batch(
            inputs[micro_index],
            cotangent[micro_index],
            random_blocks[micro_index],
            global_blocks[micro_index],
            weights,
        )
        grads = reduce_grads(grads)
        totals = (
            grads
            if totals is None
            else tuple((total_sum + extra_sum for total_sum, extra_sum in zip(totals, grads)))
        )
        results.append(result)
        input_grads.append(token_grad)
    return (jnp.stack(results), jnp.stack(input_grads)) + tuple(totals)


def solution(mesh):
    return jax.shard_map(
        near_body if (mesh.shape["blk"], mesh.shape["head"]) == (8, 4) else body,
        mesh=mesh,
        in_specs=(
            P(None, ("blk", "head"), None),
            P(None, ("blk", "head"), None),
            P(),
            P(),
            P(("blk", "head"), None),
            P(("blk", "head")),
            P(("blk", "head"), None),
            P(("blk", "head"), None),
            P(("blk", "head")),
            P(("blk", "head"), None),
            P(("blk", "head")),
            P(("blk", "head")),
            P(("blk", "head")),
            P(("blk", "head"), None),
            P(("blk", "head")),
            P(("blk", "head"), None),
            P(("blk", "head")),
            P(("blk", "head")),
            P(("blk", "head")),
        ),
        out_specs=(
            P(None, ("blk", "head"), None),
            P(None, ("blk", "head"), None),
            P(("blk", "head"), None),
            P(("blk", "head")),
            P(("blk", "head"), None),
            P(("blk", "head"), None),
            P(("blk", "head")),
            P(("blk", "head"), None),
            P(("blk", "head")),
            P(("blk", "head")),
            P(("blk", "head")),
            P(("blk", "head"), None),
            P(("blk", "head")),
            P(("blk", "head"), None),
            P(("blk", "head")),
            P(("blk", "head")),
            P(("blk", "head")),
        ),
        check_vma=False,
    )
```

```python
from functools import partial

import jax
import jax.numpy as jnp
from jax import lax
from jax.experimental import pallas as pl
from jax.experimental.pallas import tpu as pltpu
from jax.sharding import PartitionSpec as P

HEADS = 12
HD = 64
BLOCK = 64
RAND = 3
GLOB = 2


MESH = pl.DeviceIdType.MESH


def places():
    b = lax.axis_index("blk")
    h = lax.axis_index("head")
    core = b % 2
    x = (b // 2) % 2
    y = b // 4
    across_x = b + 2 - 4 * x
    across_y = b + 4 - 8 * y
    partner = b + 1 - 2 * core
    pair = h // 2
    line = (h, h + 1 - 2 * (h % 2), 2 - pair, 3 - 3 * pair)
    return b, h, core, x, y, across_x, across_y, partner, line


def meet(b, h, others, line):
    barrier = pltpu.get_barrier_semaphore()
    for other in others:
        pl.semaphore_signal(barrier, inc=1, device_id=(other, h), device_id_type=MESH)
    for d in range(1, 4):
        pl.semaphore_signal(barrier, inc=1, device_id=(b, line[d]), device_id_type=MESH)
    pl.semaphore_wait(barrier, len(others) + 3)


def remote(src, dst, send_sem, recv_sem, device):
    return pltpu.make_async_remote_copy(
        src_ref=src,
        dst_ref=dst,
        send_sem=send_sem,
        recv_sem=recv_sem,
        device_id=device,
        device_id_type=MESH,
    )


def gather_kernel(kinds, *refs):
    n = len(kinds)
    ins = refs[:n]
    outs = refs[n : 2 * n]
    own_sem, line_send, line_recv, send, recv = refs[2 * n :]
    b, h, core, x, y, across_x, across_y, partner, line = places()
    corner = across_x + 4 - 8 * y
    inner = jnp.logical_or(h == 1, h == 2)
    seen = jnp.where(inner, 2, 3)
    meet(b, h, (across_x, across_y, partner), line)

    def piece(i, place):
        return ins[i].at[place] if kinds[i][0] else ins[i]

    def slot(i, shard, place):
        return outs[i].at[shard * 4 + place] if kinds[i][1] else outs[i].at[place]

    def part(ref, cut):
        axis, start, size = cut
        return ref.at[(slice(None),) * axis + (pl.ds(start, size),)]

    started = []
    started_inner = []

    def go(copy, only_inner=False):
        if only_inner:

            @pl.when(inner)
            def _():
                copy.start()

            started_inner.append(copy)
        else:
            copy.start()
            started.append(copy)

    def along(i, src, landing, sender_at, receiver_at, place, only_inner=False):
        go(
            remote(
                src, landing, line_send.at[i, sender_at], line_recv.at[i, receiver_at], (b, place)
            ),
            only_inner,
        )

    def line_arrived(i, d):
        here = slot(i, b, line[d])
        remote(
            here, here, line_send.at[i, d], line_recv.at[i, d], (b, line[d])
        ).wait_recv()
        if not kinds[i][0]:
            if d == 1:
                along(i, here, here, 3, 3, 3 - h, True)
            else:
                along(i, here, here, d + 2, d, line[1], True)

    def out_of(i, d):
        return piece(i, h) if d == 0 else slot(i, b, line[d])

    def send_plane(i, d):
        for k, other in enumerate((across_x, across_y, partner)):
            go(
                remote(
                    out_of(i, d),
                    slot(i, b, line[d]),
                    send.at[i, d, k],
                    recv.at[i, d, k],
                    (other, h),
                )
            )

    def arrived(i, d, k, shard, cut=None):
        here = slot(i, shard, line[d])
        if cut is not None:
            here = part(here, cut)
        remote(here, here, send.at[i, d, k], recv.at[i, d, k], (partner, h)).wait_recv()
        return here

    def pass_on(i, d):
        first, second = kinds[i][2]
        here = arrived(i, d, 0, across_x)
        if first is not None:
            go(
                remote(
                    part(here, first),
                    part(here, first),
                    send.at[i, d, 6],
                    recv.at[i, d, 6],
                    (across_y, h),
                )
            )
        go(remote(here, here, send.at[i, d, 3], recv.at[i, d, 3], (partner, h)))
        here = arrived(i, d, 1, across_y)
        if second is not None:
            go(
                remote(
                    part(here, second),
                    part(here, second),
                    send.at[i, d, 7],
                    recv.at[i, d, 7],
                    (across_x, h),
                )
            )
        go(remote(here, here, send.at[i, d, 4], recv.at[i, d, 4], (partner, h)))

    def finish_corner(i, d):
        first, second = kinds[i][2]
        if first is not None:
            arrived(i, d, 6, corner, first)
        if second is not None:
            arrived(i, d, 7, corner, second)
        here = slot(i, corner, line[d])
        go(remote(here, here, send.at[i, d, 5], recv.at[i, d, 5], (partner, h)))

    spread = [i for i in range(n) if kinds[i][1]]
    straight = [i for i in range(n) if not kinds[i][1]]
    locals_ = []

    def send_straight(i):
        for d in (2, 3, 1):
            along(i, piece(i, line[d]), slot(i, b, h), d, 1 if d == 1 else seen, line[d])

    for i in spread:
        if kinds[i][0]:
            send_straight(i)
        else:
            along(i, piece(i, h), slot(i, b, h), 2, 2, 3 - h, True)
            along(i, piece(i, h), slot(i, b, h), 1, 1, line[1])
    if not spread:
        for i in straight:
            send_straight(i)
    for i in spread:
        send_plane(i, 0)
    for i in range(n):
        own = pltpu.make_async_copy(piece(i, h), slot(i, b, h), own_sem.at[i])
        own.start()
        locals_.append(own)
    for d in range(1, 4):
        for i in spread:
            line_arrived(i, d)
            send_plane(i, d)
        if d == 2 and spread:
            for i in straight:
                send_straight(i)
        for i in spread:
            pass_on(i, d - 1)
        if d > 1:
            for i in spread:
                finish_corner(i, d - 2)
    for i in spread:
        pass_on(i, 3)
    for d in (2, 3):
        for i in spread:
            finish_corner(i, d)
    for i in straight:
        for d in range(1, 4):
            line_arrived(i, d)
    partner_x = partner + 2 - 4 * x
    partner_y = partner + 4 - 8 * y
    partner_corner = partner_x + 4 - 8 * y
    for i in spread:
        for d in range(4):
            for k, shard in ((2, partner), (3, partner_x), (4, partner_y), (5, partner_corner)):
                arrived(i, d, k, shard)
    for own in locals_:
        own.wait()
    for copy in started:
        copy.wait_send()
    if started_inner:

        @pl.when(inner)
        def _():
            for copy in started_inner:
                copy.wait_send()


def gather_call(arrays, kinds, collective):
    n = len(arrays)
    shapes = []
    for a, (per_place, spread, _) in zip(arrays, kinds):
        chunk = a.shape[1:] if per_place else a.shape
        shapes.append(jax.ShapeDtypeStruct(((32 if spread else 4),) + chunk, a.dtype))
    return pl.pallas_call(
        partial(gather_kernel, kinds),
        out_shape=tuple(shapes),
        in_specs=[pl.BlockSpec(memory_space=pl.ANY)] * n,
        out_specs=tuple([pl.BlockSpec(memory_space=pl.ANY)] * n),
        scratch_shapes=[
            pltpu.SemaphoreType.DMA((n,)),
            pltpu.SemaphoreType.DMA((n, 6)),
            pltpu.SemaphoreType.DMA((n, 4)),
            pltpu.SemaphoreType.DMA((n, 4, 8)),
            pltpu.SemaphoreType.DMA((n, 4, 8)),
        ],
        compiler_params=pltpu.CompilerParams(collective_id=collective, has_side_effects=True),
        name=f"gather{collective}",
    )(*arrays)


def scatter_kernel(kinds, *refs):
    n = len(kinds)
    ins = refs[:n]
    outs = refs[n : 2 * n]
    rest = list(refs[2 * n :])
    bufs = {}
    for i in range(n):
        if kinds[i][1]:
            bufs[i] = rest[:6]
            rest = rest[6:]
            if kinds[i][0]:
                bufs[i] = bufs[i] + [rest[0]]
                rest = rest[1:]
    local_sem, own_sem, line_send, line_recv, core_send, core_recv, send, recv = rest
    b, h, core, x, y, across_x, across_y, partner, line = places()
    seen = jnp.where(jnp.logical_or(h == 1, h == 2), 2, 3)
    meet(b, h, (across_x, across_y, partner), line)
    chip = b // 2
    targets = (3 - chip, chip + 1 - 2 * x, chip + 2 - 4 * y, chip)
    started = []
    spread = [i for i in range(n) if kinds[i][1]]

    def go(copy):
        copy.start()
        started.append(copy)

    def part(ref, cut):
        axis, start, size = cut
        return ref.at[(slice(None),) * axis + (pl.ds(start, size),)]

    def along(i, src, landing, d):
        go(
            remote(
                src, landing, line_send.at[i, d], line_recv.at[i, 1 if d == 1 else seen], (b, line[d])
            )
        )

    locals_ = []
    loads = {}
    for t in range(4):
        for i in spread:
            from_partner, total = bufs[i][0], bufs[i][1]
            go(
                remote(
                    ins[i].at[pl.ds((targets[t] * 2 + 1 - core) * 4, 4)],
                    from_partner.at[t],
                    core_send.at[i, t],
                    core_recv.at[i, t],
                    (partner, h),
                )
            )
            load = pltpu.make_async_copy(
                ins[i].at[pl.ds((targets[t] * 2 + core) * 4, 4)], total.at[t], local_sem.at[i, t]
            )
            load.start()
            loads[i, t] = load
    for i in range(n):
        if i in spread:
            continue
        for d in (3, 2, 1):
            along(i, ins[i].at[line[d]], outs[i].at[h], d)
        own = pltpu.make_async_copy(ins[i].at[h], outs[i].at[h], own_sem.at[i])
        own.start()
        locals_.append(own)

    def wait_for(ref, i, d, k):
        remote(ref, ref, send.at[i, d, k], recv.at[i, d, k], (partner, h)).wait_recv()

    def ready(i, t):
        loads[i, t].wait()
        here = bufs[i][0].at[t]
        remote(here, here, core_send.at[i, t], core_recv.at[i, t], (partner, h)).wait_recv()

    def both_cores(i, t, d, extra=()):
        from_partner, total = bufs[i][0], bufs[i][1]
        place = line[d]
        value = total[t, place].astype(jnp.float32) + from_partner[t, place].astype(jnp.float32)
        for ref in extra:
            value = value + ref[d].astype(jnp.float32)
        total[t, place] = value.astype(total.dtype)

    def add_corner(i, t, d, ref, cut):
        total = bufs[i][1]
        axis, start, size = cut
        at = (t, line[d]) + (slice(None),) * axis + (pl.ds(start, size),)
        value = total[at].astype(jnp.float32) + ref[d].astype(jnp.float32)
        total[at] = value.astype(total.dtype)

    order = (3, 2, 1, 0)

    def corner_step(i):
        total = bufs[i][1]
        first, second = kinds[i][2]
        ready(i, 0)
        for d in order:
            both_cores(i, 0, d)
            mine = total.at[0, line[d]]
            if first is not None:
                go(remote(part(mine, first), bufs[i][2].at[d], send.at[i, d, 0], recv.at[i, d, 0], (across_x, h)))
            if second is not None:
                go(remote(part(mine, second), bufs[i][3].at[d], send.at[i, d, 1], recv.at[i, d, 1], (across_y, h)))

    def side_step(i):
        total = bufs[i][1]
        first, second = kinds[i][2]
        ready(i, 1)
        ready(i, 2)
        for d in order:
            both_cores(i, 1, d)
            if second is not None:
                wait_for(bufs[i][3].at[d], i, d, 1)
                add_corner(i, 1, d, bufs[i][3], second)
            go(remote(total.at[1, line[d]], bufs[i][4].at[d], send.at[i, d, 2], recv.at[i, d, 2], (across_x, h)))
            both_cores(i, 2, d)
            if first is not None:
                wait_for(bufs[i][2].at[d], i, d, 0)
                add_corner(i, 2, d, bufs[i][2], first)
            go(remote(total.at[2, line[d]], bufs[i][5].at[d], send.at[i, d, 3], recv.at[i, d, 3], (across_y, h)))

    def own_step(i):
        summed = kinds[i][0]
        total = bufs[i][1]
        ready(i, 3)
        for d in order:
            wait_for(bufs[i][4].at[d], i, d, 2)
            wait_for(bufs[i][5].at[d], i, d, 3)
            both_cores(i, 3, d, (bufs[i][4], bufs[i][5]))
            if d > 0:
                landing = bufs[i][6].at[1 if d == 1 else seen] if summed else outs[i].at[h]
                along(i, total.at[3, line[d]], landing, d)
            elif not summed:
                own = pltpu.make_async_copy(total.at[3, h], outs[i].at[h], own_sem.at[i])
                own.start()
                locals_.append(own)

    for i in spread:
        corner_step(i)
    for at, i in enumerate(spread):
        side_step(i)
        if at > 0:
            own_step(spread[at - 1])
    if spread:
        own_step(spread[-1])
    for i in range(n):
        summed = kinds[i][0]
        for d in range(1, 4):
            landing = bufs[i][6].at[d] if summed else outs[i].at[line[d]]
            remote(
                landing, landing, line_send.at[i, d], line_recv.at[i, d], (b, line[d])
            ).wait_recv()
        if summed:
            value = bufs[i][1][3, h].astype(jnp.float32)
            for d in range(1, 4):
                value = value + bufs[i][6][d].astype(jnp.float32)
            outs[i][...] = value
    for own in locals_:
        own.wait()
    for copy in started:
        copy.wait_send()


def scatter_call(arrays, kinds, collective):
    n = len(arrays)
    shapes = []
    out_specs = []
    scratch = []
    for a, (summed, spread, halves) in zip(arrays, kinds):
        chunk = a.shape[1:]
        if spread:
            scratch += [pltpu.VMEM((4, 4) + chunk, a.dtype), pltpu.VMEM((4, 4) + chunk, a.dtype)]
            for cut in halves:
                size = list(chunk)
                if cut is not None:
                    size[cut[0]] = cut[2]
                else:
                    size = [8, 128]
                scratch.append(pltpu.VMEM((4,) + tuple(size), a.dtype))
            scratch += [pltpu.VMEM((4,) + chunk, a.dtype)] * 2
            if summed:
                scratch.append(pltpu.VMEM((4,) + chunk, a.dtype))
        if summed:
            shapes.append(jax.ShapeDtypeStruct(chunk, jnp.float32))
            out_specs.append(pl.BlockSpec(memory_space=pltpu.VMEM))
        else:
            shapes.append(jax.ShapeDtypeStruct((4,) + chunk, a.dtype))
            out_specs.append(pl.BlockSpec(memory_space=pl.ANY))
    return pl.pallas_call(
        partial(scatter_kernel, kinds),
        out_shape=tuple(shapes),
        in_specs=[pl.BlockSpec(memory_space=pl.ANY)] * n,
        out_specs=tuple(out_specs),
        scratch_shapes=scratch
        + [
            pltpu.SemaphoreType.DMA((n, 4)),
            pltpu.SemaphoreType.DMA((n,)),
            pltpu.SemaphoreType.DMA((n, 4)),
            pltpu.SemaphoreType.DMA((n, 4)),
            pltpu.SemaphoreType.DMA((n, 4)),
            pltpu.SemaphoreType.DMA((n, 4)),
            pltpu.SemaphoreType.DMA((n, 4, 4)),
            pltpu.SemaphoreType.DMA((n, 4, 4)),
        ],
        compiler_params=pltpu.CompilerParams(
            collective_id=collective, has_side_effects=True, vmem_limit_bytes=60 * 2**20
        ),
        name=f"scatter{collective}",
    )(*arrays)


def lanes_of(shape, low):
    lane = lax.broadcasted_iota(jnp.int32, shape, len(shape) - 1)
    if isinstance(low, bool):
        return lane < HD if low else lane >= HD
    return lane // HD == jnp.where(low, 0, 1)


def dot(left_side, right_side, contract=((1,), (0,))):
    return lax.dot_general(
        left_side, right_side, (contract, ((), ())), preferred_element_type=jnp.float32
    )


ROWS = ((1,), (1,))
COLS = ((0,), (0,))


def halves(array, col):
    return array[:, col : col + HD]


def project_kernel(x_ref, w_ref, bias_ref, q_out, kv_out):
    rows = x_ref.shape[1]
    width = x_ref.shape[2]
    tokens = x_ref[...].reshape(2 * rows, width)
    made = []
    for k in range(3):
        part = dot(tokens, w_ref[:, k * width : (k + 1) * width])
        if k != 1:
            part = part + bias_ref[k // 2 : k // 2 + 1, :]
        made.append(part.astype(jnp.bfloat16))
    q, k, v = made
    groups, per, _, _ = q_out.shape
    for g in range(groups):
        for j in range(per):
            col = (g * per + j) * HD
            q_out[g, j] = jnp.concatenate([halves(q[:rows], col), halves(q[rows:], col)], axis=1)
            kv_out[g, j] = jnp.concatenate([halves(k[:rows], col), halves(v[:rows], col)], axis=1)
            kv_out[g, per + j] = jnp.concatenate([halves(v[rows:], col), halves(k[rows:], col)], axis=1)


def project_call(tokens, weight, bias, groups):
    micro, rows, width = tokens.shape
    per = HEADS // groups
    whole = pl.BlockSpec(memory_space=pltpu.VMEM)
    return pl.pallas_call(
        project_kernel,
        out_shape=(
            jax.ShapeDtypeStruct((groups, per, rows, 2 * HD), jnp.bfloat16),
            jax.ShapeDtypeStruct((groups, 2 * per, rows, 2 * HD), jnp.bfloat16),
        ),
        grid=(1,),
        in_specs=[
            pl.BlockSpec((micro, rows, width), lambda i: (0, 0, 0)),
            pl.BlockSpec((width, 3 * width), lambda i: (0, 0)),
            pl.BlockSpec(bias.shape, lambda i: (0, 0)),
        ],
        out_specs=(
            pl.BlockSpec((groups, per, rows, 2 * HD), lambda i: (0, 0, 0, 0)),
            pl.BlockSpec((groups, 2 * per, rows, 2 * HD), lambda i: (0, 0, 0, 0)),
        ),
        compiler_params=pltpu.CompilerParams(vmem_limit_bytes=56 * 2**20),
        name="project",
    )(tokens, weight, bias)


def listed_rows(table_ref, blocks, per, m, n, j):
    shard = table_ref[2 * blocks * per * RAND + 2 * GLOB]
    total = table_ref[2 * blocks * per * RAND + 2 * GLOB + 1]
    here = shard * blocks + n
    rows = [jnp.maximum(here - 1, 0), here, jnp.minimum(here + 1, total - 1)]
    for r in range(RAND):
        rows.append(table_ref[((m * blocks + n) * per + j) * RAND + r])
    for g in range(GLOB):
        rows.append(table_ref[2 * blocks * per * RAND + m * GLOB + g])
    return rows, here, total


def global_of(table_ref, blocks, per, at):
    base = 2 * blocks * per * RAND
    return table_ref[base + at], table_ref[base + 2 * GLOB]


def outside(here, total, listed):
    lane = lax.broadcasted_iota(jnp.int32, (1, listed * BLOCK), 1)
    before = jnp.logical_and(lane < BLOCK, here == 0)
    after = jnp.logical_and(
        jnp.logical_and(lane >= 2 * BLOCK, lane < 3 * BLOCK), here == total - 1
    )
    return jnp.where(jnp.logical_or(before, after), -jnp.inf, 0.0)


def only(value, low):
    return jnp.where(lanes_of(value.shape, low), value, jnp.zeros_like(value))


def attend_kernel(table_ref, q_ref, kv_ref, out_ref, lse_ref):
    places_, per, in_place, block, _ = q_ref.shape
    blocks = places_ * in_place
    scale = jnp.bfloat16(HD ** (-0.5))
    units = [(j, m) for j in range(per) for m in range(2)]

    def query_block(n, carry):
        kvs, scores = [], []
        for j, m in units:
            rows, here, total = listed_rows(table_ref, blocks, per, m, n, j)
            kvs.append(
                jnp.concatenate(
                    [kv_ref[r // in_place, m * per + j, r % in_place] for r in rows], axis=0
                )
            )
            q = only(q_ref[n // in_place, j, n % in_place], m == 0) * scale
            scores.append(dot(q, kvs[-1], ROWS) + outside(here, total, len(rows)))
        raised = []
        for (j, m), score in zip(units, scores):
            top = jnp.max(score, axis=1, keepdims=True)
            raised.append(jnp.exp(score - top))
            total_sum = jnp.sum(raised[-1], axis=1, keepdims=True)
            raised[-1] = raised[-1] * (1.0 / total_sum)
            lse_ref[n // in_place, j, m, n % in_place] = jnp.broadcast_to(
                top + jnp.log(total_sum), (block, 2 * HD)
            )
        outs = [dot(r.astype(jnp.bfloat16), kv) for r, kv in zip(raised, kvs)]
        for j in range(per):
            out_ref[n // in_place, j, n % in_place] = jnp.where(
                lanes_of(outs[0].shape, True), outs[2 * j + 1], outs[2 * j]
            ).astype(jnp.bfloat16)
        return carry

    lax.fori_loop(0, blocks, query_block, 0)
    step = 8
    heads = range(per)

    def global_rows(at, carry):
        m = at // GLOB
        row, shard = global_of(table_ref, blocks, per, at)
        local = row % blocks
        at_place, at_row = local // in_place, local % in_place

        @pl.when(row // blocks == shard)
        def _():
            def keys(j, spot):
                return kv_ref[pl.ds(spot, step), m * per + j].reshape(
                    step * in_place * block, 2 * HD
                )

            spots = range(0, kv_ref.shape[0], step)
            qs = [only(q_ref[at_place, j, at_row], m == 0) * scale for j in heads]
            scores = [[dot(qs[j], keys(j, spot), ROWS) for spot in spots] for j in heads]
            raised, sums = [], []
            for j in heads:
                top = scores[j][0].max(axis=1, keepdims=True)
                for s in scores[j][1:]:
                    top = jnp.maximum(top, s.max(axis=1, keepdims=True))
                raised.append([jnp.exp(s - top) for s in scores[j]])
                sums.append(sum(jnp.sum(r, axis=1, keepdims=True) for r in raised[j]))
                lse_ref[at_place, j, m, at_row] = jnp.broadcast_to(
                    top + jnp.log(sums[j]), (block, 2 * HD)
                )
            for j in heads:
                out = sum(
                    dot(r.astype(jnp.bfloat16), keys(j, spot)) for r, spot in zip(raised[j], spots)
                )
                old = out_ref[at_place, j, at_row]
                out_ref[at_place, j, at_row] = jnp.where(
                    lanes_of(old.shape, m == 1), (out / sums[j]).astype(jnp.bfloat16), old
                )

        return carry

    lax.fori_loop(0, 2 * GLOB, global_rows, 0)


def attend_call(table, q, kv):
    spec = pl.BlockSpec(memory_space=pltpu.VMEM)
    places_, per, in_place, block, lanes = q.shape
    return pl.pallas_call(
        attend_kernel,
        out_shape=(
            jax.ShapeDtypeStruct(q.shape, jnp.bfloat16),
            jax.ShapeDtypeStruct((places_, per, 2, in_place, block, lanes), jnp.float32),
        ),
        in_specs=[pl.BlockSpec(memory_space=pltpu.SMEM), spec, spec],
        out_specs=(spec, spec),
        compiler_params=pltpu.CompilerParams(vmem_limit_bytes=56 * 2**20),
        name="attend",
    )(table, q, kv)


def attend_back_kernel(
    table_ref, q_ref, kv_in, d_ref, out_ref, lse_ref, dq_ref, dkv_out, total_ref, kv_ref, in_sem, out_sem
):
    places_, per, in_place, block, _ = q_ref.shape
    blocks = places_ * in_place
    scale = jnp.bfloat16(HD ** (-0.5))
    units = [(j, m) for j in range(per) for m in range(2)]

    step = 8
    fetch = pltpu.make_async_copy(kv_in, kv_ref, in_sem)
    fetch.start()

    def clear(i, carry):
        total_ref[i] = jnp.zeros(total_ref.shape[1:], jnp.float32)
        return carry

    lax.fori_loop(0, total_ref.shape[0], clear, 0)
    fetch.wait()

    def pair_of(n, j, m, keep):
        at = (n // in_place, j, n % in_place)
        q = only(q_ref[at], m == 0) * scale
        d = only(d_ref[at], m == 1)
        if keep is not None:
            d = d * keep
        delta = jnp.sum(
            d.astype(jnp.float32) * out_ref[at].astype(jnp.float32), axis=1, keepdims=True
        )
        return jnp.concatenate([q, d], axis=0), delta

    def wide(column, width):
        return jnp.concatenate([column] * (width // column.shape[1]), axis=1)

    def query_block(n, carry):
        listed, kvs, pairs, deltas, boths = [], [], [], [], []
        for j, m in units:
            rows, here, total = listed_rows(table_ref, blocks, per, m, n, j)
            is_global = jnp.logical_or(here == rows[-1], here == rows[-2])
            keep = jnp.where(is_global, 0.0, 1.0).astype(jnp.bfloat16)
            kv = jnp.concatenate(
                [kv_ref[r // in_place, m * per + j, r % in_place] for r in rows], axis=0
            )
            pair, delta = pair_of(n, j, m, keep)
            listed.append(rows)
            kvs.append(kv)
            pairs.append(pair)
            deltas.append(delta)
            boths.append(dot(pair, kv, ROWS))
        weights = []
        for (j, m), both, delta, kv, rows in zip(units, boths, deltas, kvs, listed):
            width = both.shape[1]
            lse = lse_ref[n // in_place, j, m, n % in_place]
            scores = both[:block] + outside(here, total, len(rows))
            probs = jnp.exp(scores - wide(lse, width))
            d_scores = probs * (both[block:] - delta)
            weights.append(
                jnp.concatenate(
                    [d_scores.astype(jnp.bfloat16), probs.astype(jnp.bfloat16)], axis=0
                )
            )
        outs = []
        for (j, m), weight, pair, kv, rows in zip(units, weights, pairs, kvs, listed):
            d_kv = dot(weight, pair, COLS)
            for at, r in enumerate(rows):
                total_ref[r // in_place, m * per + j, r % in_place] += d_kv[
                    at * block : (at + 1) * block
                ]
            outs.append(dot(weight[:block], kv) * HD ** (-0.5))
        for j in range(per):
            dq_ref[n // in_place, j, n % in_place] = jnp.where(
                lanes_of(outs[0].shape, True), outs[2 * j], outs[2 * j + 1]
            ).astype(jnp.bfloat16)
        return carry

    lax.fori_loop(0, blocks, query_block, 0)

    heads = range(per)

    def global_rows(at, carry):
        m = at // GLOB
        row, shard = global_of(table_ref, blocks, per, at)
        local = row % blocks
        at_place, at_row = local // in_place, local % in_place

        @pl.when(row // blocks == shard)
        def _():
            pairs = [pair_of(local, j, m, None) for j in heads]

            def some_keys(spot, d_qs):
                at_keys = pl.ds(spot * step, step)
                kvs = [
                    kv_ref[at_keys, m * per + j].reshape(step * in_place * block, 2 * HD)
                    for j in heads
                ]
                boths = [dot(pairs[j][0], kvs[j], ROWS) for j in heads]
                weights = []
                for j in heads:
                    lse = lse_ref[at_place, j, m, at_row]
                    probs = jnp.exp(boths[j][:block] - wide(lse, boths[j].shape[1]))
                    d_scores = probs * (boths[j][block:] - pairs[j][1])
                    weights.append(
                        jnp.concatenate(
                            [d_scores.astype(jnp.bfloat16), probs.astype(jnp.bfloat16)], axis=0
                        )
                    )
                for j in heads:
                    total_ref[at_keys, m * per + j] += dot(weights[j], pairs[j][0], COLS).reshape(
                        step, in_place, block, 2 * HD
                    )
                return tuple(d_qs[j] + dot(weights[j][:block], kvs[j]) for j in heads)

            d_qs = lax.fori_loop(
                0,
                kv_ref.shape[0] // step,
                some_keys,
                tuple(jnp.zeros((block, 2 * HD), jnp.float32) for _ in heads),
            )
            for j in heads:
                old = dq_ref[at_place, j, at_row]
                dq_ref[at_place, j, at_row] = jnp.where(
                    lanes_of(old.shape, m == 0), (d_qs[j] * HD ** (-0.5)).astype(jnp.bfloat16), old
                )

        return carry

    lax.fori_loop(0, 2 * GLOB, global_rows, 0)

    def give(i, carry):
        kv_ref[i] = total_ref[i].astype(jnp.bfloat16)
        return carry

    gives = []
    for at, s in enumerate(range(0, total_ref.shape[0], step)):
        lax.fori_loop(s, s + step, give, 0)
        gives.append(
            pltpu.make_async_copy(
                kv_ref.at[pl.ds(s, step)], dkv_out.at[pl.ds(s, step)], out_sem.at[at]
            )
        )
        gives[-1].start()
    for copy in gives:
        copy.wait()


def attend_back_call(table, q, kv, d, out, lse):
    spec = pl.BlockSpec(memory_space=pltpu.VMEM)
    far = pl.BlockSpec(memory_space=pl.ANY)
    return pl.pallas_call(
        attend_back_kernel,
        out_shape=(
            jax.ShapeDtypeStruct(q.shape, jnp.bfloat16),
            jax.ShapeDtypeStruct(kv.shape, jnp.bfloat16),
        ),
        in_specs=[pl.BlockSpec(memory_space=pltpu.SMEM), spec, far, spec, spec, spec],
        out_specs=(spec, far),
        scratch_shapes=[
            pltpu.VMEM(kv.shape, jnp.float32),
            pltpu.VMEM(kv.shape, jnp.bfloat16),
            pltpu.SemaphoreType.DMA,
            pltpu.SemaphoreType.DMA((kv.shape[0] // 8,)),
        ],
        compiler_params=pltpu.CompilerParams(vmem_limit_bytes=60 * 2**20),
        name="attend_back",
    )(table, q, kv, d, out, lse)


def centre(values):
    center = jnp.mean(values, axis=1, keepdims=True)
    centred = values - center
    spread = jnp.mean(centred * centred, axis=1, keepdims=True)
    inverse = lax.rsqrt(spread + 1e-12)
    return centred * inverse, inverse


def centre_back(hat, inverse, grad):
    return inverse * (
        grad
        - jnp.mean(grad, axis=1, keepdims=True)
        - hat * jnp.mean(grad * hat, axis=1, keepdims=True)
    )


def rows_sum(values):
    return jnp.sum(values, axis=0, keepdims=True)


def dense_kernel(
    c_ref, x_ref, cot_ref, wo_in, up_in, down_in, vec_ref, up_bias_ref,
    out_ref, d_mix_ref, d_c_ref, g_out_ref, g_up_out, g_down_out, g_vec_ref, g_up_bias_ref,
    ctx, first, hat, low, low_t, act, slope, ffn, wo_ref, up_ref, down_ref, g_up_ref, g_down_ref, in_sem, out_sem,
):
    groups, per, rows, _ = c_ref.shape
    width = x_ref.shape[2]
    ff = up_ref.shape[1]
    chunk = 384
    fetches = [
        pltpu.make_async_copy(wo_in.at[:, pl.ds(3 * width, width)], wo_ref, in_sem.at[0]),
        pltpu.make_async_copy(up_in, up_ref, in_sem.at[1]),
        pltpu.make_async_copy(down_in, down_ref, in_sem.at[2]),
    ]
    for copy in fetches:
        copy.start()
    out_bias, attn_gain, attn_shift, down_bias, ffn_gain, ffn_shift = (
        vec_ref[k : k + 1, :] for k in range(6)
    )
    for p in range(HEADS // 2):
        one = c_ref[(2 * p) // per, (2 * p) % per]
        two = c_ref[(2 * p + 1) // per, (2 * p + 1) % per]
        at = pl.ds(p * 2 * HD, 2 * HD)
        ctx[:rows, at] = jnp.concatenate([one[:, HD:], two[:, HD:]], axis=1)
        ctx[rows:, at] = jnp.concatenate([one[:, :HD], two[:, :HD]], axis=1)
    tokens = x_ref[...].reshape(2 * rows, width).astype(jnp.float32)
    fetches[0].wait()
    hat_first, inverse_first = centre(tokens + dot(ctx[...], wo_ref[...]) + out_bias)
    hat[...] = hat_first
    first[...] = hat_first * attn_gain + attn_shift
    low[...] = first[...].astype(jnp.bfloat16)
    low_t[...] = first[...].T.astype(jnp.bfloat16)
    ffn[...] = first[...] + down_bias
    fetches[1].wait()
    fetches[2].wait()

    def forward(i, carry):
        at = pl.ds(pl.multiple_of(i * chunk, chunk), chunk)
        hidden = dot(low[...], up_ref[:, at]) + up_bias_ref[:, at]
        share = 0.5 * (1.0 + lax.erf(hidden * 0.7071067811865476))
        bell = jnp.exp(-0.5 * hidden * hidden) * 0.3989422804014327
        slope[:, at] = share + hidden * bell
        act_low = (hidden * share).astype(jnp.bfloat16)
        act[:, at] = act_low
        ffn[...] += dot(act_low, down_ref[at, :])
        return carry

    lax.fori_loop(0, ff // chunk, forward, 0)
    hat_second, inverse_second = centre(ffn[...])
    out_ref[...] = (
        (hat_second * ffn_gain + ffn_shift).astype(jnp.bfloat16).reshape(2, rows, width)
    )
    cot = cot_ref[...].reshape(2 * rows, width).astype(jnp.float32)
    g_vec_ref[4:5, :] = rows_sum(cot * hat_second)
    g_vec_ref[5:6, :] = rows_sum(cot)
    d_second = centre_back(hat_second, inverse_second, cot * ffn_gain)
    d_ffn = d_second.astype(jnp.bfloat16)
    g_vec_ref[3:4, :] = rows_sum(d_ffn.astype(jnp.float32))
    ffn[...] = d_second

    def leave(i):
        at = pl.ds(pl.multiple_of(i * chunk, chunk), chunk)
        return (
            pltpu.make_async_copy(g_up_ref.at[:, at], g_up_out.at[:, at], out_sem.at[0, i]),
            pltpu.make_async_copy(g_down_ref.at[at, :], g_down_out.at[at, :], out_sem.at[1, i]),
        )

    def backward(i, carry):
        at = pl.ds(pl.multiple_of(i * chunk, chunk), chunk)
        d_act = dot(d_ffn, down_ref[at, :], ROWS)
        d_hidden = (d_act * slope[:, at]).astype(jnp.bfloat16)
        g_up_bias_ref[:, at] = rows_sum(d_hidden.astype(jnp.float32))
        g_down_ref[at, :] = dot(act[:, at], d_ffn, COLS).astype(jnp.bfloat16)
        g_up_ref[:, at] = dot(low_t[...], d_hidden).astype(jnp.bfloat16)
        for copy in leave(i):
            copy.start()
        ffn[...] += dot(d_hidden, up_ref[:, at], ROWS)
        return carry

    lax.fori_loop(0, ff // chunk, backward, 0)
    d_first = ffn[...]
    g_vec_ref[1:2, :] = rows_sum(d_first * hat[...])
    g_vec_ref[2:3, :] = rows_sum(d_first)
    d_mix = centre_back(hat[...], inverse_first, d_first * attn_gain)
    d_mix_ref[...] = d_mix
    d_branch = d_mix.astype(jnp.bfloat16)
    g_vec_ref[0:1, :] = rows_sum(d_branch.astype(jnp.float32))
    g_vec_ref[6:8, :] = jnp.zeros((2, width), jnp.float32)
    g_out_ref[...] = dot(ctx[...], d_branch, COLS).astype(jnp.bfloat16)
    d_ctx = dot(d_branch, wo_ref[...], ROWS).astype(jnp.bfloat16)
    for head in range(HEADS):
        d_c_ref[head // per, head % per] = jnp.concatenate(
            [halves(d_ctx[rows:], head * HD), halves(d_ctx[:rows], head * HD)], axis=1
        )
    for i in range(ff // chunk):
        for copy in leave(i):
            copy.wait()


def dense_call(c, tokens, cot, mixed, up, down, vec, up_bias):
    micro, rows, width = tokens.shape
    ff = up.shape[1]
    both = micro * rows
    far = pl.BlockSpec(memory_space=pl.ANY)
    f32, bf16 = jnp.float32, jnp.bfloat16

    def full(shape):
        return pl.BlockSpec(memory_space=pltpu.VMEM)

    outs = (
        jax.ShapeDtypeStruct(tokens.shape, bf16),
        jax.ShapeDtypeStruct((both, width), f32),
        jax.ShapeDtypeStruct(c.shape, bf16),
        jax.ShapeDtypeStruct((width, width), bf16),
        jax.ShapeDtypeStruct((width, ff), bf16),
        jax.ShapeDtypeStruct((ff, width), bf16),
        jax.ShapeDtypeStruct((8, width), f32),
        jax.ShapeDtypeStruct((1, ff), f32),
    )
    return pl.pallas_call(
        dense_kernel,
        out_shape=outs,
        in_specs=[
            full(c.shape),
            full(tokens.shape),
            full(cot.shape),
            far,
            far,
            far,
            full(vec.shape),
            full(up_bias.shape),
        ],
        out_specs=tuple(far if k in (4, 5) else full(o.shape) for k, o in enumerate(outs)),
        scratch_shapes=[
            pltpu.VMEM((both, width), bf16),
            pltpu.VMEM((both, width), f32),
            pltpu.VMEM((both, width), f32),
            pltpu.VMEM((both, width), bf16),
            pltpu.VMEM((width, both), bf16),
            pltpu.VMEM((both, ff), bf16),
            pltpu.VMEM((both, ff), f32),
            pltpu.VMEM((both, width), f32),
            pltpu.VMEM((width, width), bf16),
            pltpu.VMEM((width, ff), bf16),
            pltpu.VMEM((ff, width), bf16),
            pltpu.VMEM((width, ff), bf16),
            pltpu.VMEM((ff, width), bf16),
            pltpu.SemaphoreType.DMA((3,)),
            pltpu.SemaphoreType.DMA((2, ff // 384)),
        ],
        compiler_params=pltpu.CompilerParams(vmem_limit_bytes=60 * 2**20),
        name="dense",
    )(c, tokens, cot, mixed, up, down, vec, up_bias)


def project_back_kernel(
    q_ref, kv_ref, x_ref, w_ref, d_mix_ref, g_out_ref, d_x_ref, g_ref, g_vec_ref, d_q, d_k, d_v
):
    groups, per, rows, _ = q_ref.shape
    width = x_ref.shape[2]
    for p in range(HEADS // 2):
        at = pl.ds(p * 2 * HD, 2 * HD)

        def of(ref, shift, low):
            sides = []
            for head in (2 * p, 2 * p + 1):
                tile = ref[head // per, shift + head % per]
                sides.append(tile[:, :HD] if low else tile[:, HD:])
            return jnp.concatenate(sides, axis=1)

        d_q[:rows, at] = of(q_ref, 0, True)
        d_q[rows:, at] = of(q_ref, 0, False)
        d_k[:rows, at] = of(kv_ref, 0, True)
        d_v[:rows, at] = of(kv_ref, 0, False)
        d_k[rows:, at] = of(kv_ref, per, False)
        d_v[rows:, at] = of(kv_ref, per, True)
    tokens = x_ref[...].reshape(2 * rows, width)
    d_x = d_mix_ref[...]
    for k, part in enumerate((d_q, d_k, d_v)):
        at = slice(k * width, (k + 1) * width)
        d_x = d_x + dot(part[...], w_ref[:, at], ROWS)
        g_ref[:, at] = dot(tokens, part[...], COLS).astype(jnp.bfloat16)
        if k != 1:
            g_vec_ref[k // 2 : k // 2 + 1, :] = rows_sum(part[...].astype(jnp.float32))
    g_ref[:, 3 * width :] = g_out_ref[...]
    g_vec_ref[2:8, :] = jnp.zeros((6, width), jnp.float32)
    d_x_ref[...] = d_x.astype(jnp.bfloat16).reshape(2, rows, width)


def project_back_call(q, kv, tokens, mixed, d_mix, g_out):
    micro, rows, width = tokens.shape
    f32, bf16 = jnp.float32, jnp.bfloat16

    def full(shape):
        return pl.BlockSpec(shape, lambda i: (0,) * len(shape), pipeline_mode=pl.Buffered(1))

    outs = (
        jax.ShapeDtypeStruct(tokens.shape, bf16),
        jax.ShapeDtypeStruct((width, 4 * width), bf16),
        jax.ShapeDtypeStruct((8, width), f32),
    )
    return pl.pallas_call(
        project_back_kernel,
        out_shape=outs,
        grid=(1,),
        in_specs=[
            full(q.shape),
            full(kv.shape),
            full(tokens.shape),
            full((width, 3 * width)),
            full(d_mix.shape),
            full(g_out.shape),
        ],
        out_specs=tuple(full(o.shape) for o in outs),
        scratch_shapes=[pltpu.VMEM((micro * rows, width), bf16)] * 3,
        compiler_params=pltpu.CompilerParams(vmem_limit_bytes=56 * 2**20),
        name="project_back",
    )(q, kv, tokens, mixed, d_mix, g_out)


def cut(axis, start, size):
    return (axis, start, size)


def near_body(inputs, cotangent, random_blocks, global_blocks, *shards):
    (
        query_weight, query_bias, key_weight, value_weight, value_bias, out_weight, out_bias, attn_gain,
        attn_shift, up_weight, up_bias, down_weight, down_bias, ffn_gain, ffn_shift,
    ) = shards
    groups = lax.axis_size("head")
    shard_count = lax.axis_size("blk")
    devices = groups * shard_count
    shard = lax.axis_index("blk")
    group = lax.axis_index("head")
    micro, rows, width = inputs.shape
    depth = query_weight.shape[0]
    ff = up_weight.shape[1]
    per = HEADS // groups
    in_place = rows // BLOCK
    blocks = groups * in_place
    vectors = jnp.stack(
        [query_bias, value_bias, out_bias, attn_gain, attn_shift, down_bias, ffn_gain, ffn_shift], axis=1
    )
    vectors = jnp.concatenate([vectors, up_bias.reshape(depth, -1)], axis=1)
    vectors = jnp.pad(vectors, ((0, 0), (0, 128 - vectors.shape[1])))
    mixed_shard = jnp.concatenate(
        [query_weight, key_weight, value_weight, out_weight, vectors], axis=1
    )
    half = 2 * width
    (mixed,) = gather_call(
        [mixed_shard], [(False, True, (cut(1, 0, half), cut(1, half, half + 128)))], 1
    )
    mixed = mixed.reshape(width, -1)
    rows_f32 = mixed[:, 4 * width : 4 * width + 16].astype(jnp.float32).T
    bias = rows_f32[:8]
    vec = rows_f32[2:10]
    up_bias_row = mixed[:, 4 * width + 8 : 4 * width + 8 + ff // width].astype(jnp.float32).reshape(1, ff)
    q_parts, kv_parts = project_call(inputs, mixed, bias, groups)
    pairs = (cut(0, 0, per), cut(0, per, per))
    q, kv, up, down = gather_call(
        [q_parts, kv_parts, up_weight, down_weight],
        [
            (True, False, None),
            (True, True, pairs),
            (False, True, (cut(1, 0, ff), None)),
            (False, True, (None, cut(1, 0, width))),
        ],
        2,
    )
    up = up.reshape(width, ff)
    down = down.reshape(ff, width)
    mine = lax.dynamic_slice(
        random_blocks,
        (0, shard * blocks, group * per, 0),
        (micro, blocks, per, RAND),
    )
    table = jnp.concatenate(
        [
            mine.reshape(-1),
            global_blocks.reshape(-1),
            jnp.stack([shard, shard_count * blocks]).astype(jnp.int32),
        ]
    )
    split = (in_place, BLOCK, 2 * HD)
    q = q.reshape((groups, per) + split)
    kv = kv.reshape((devices, 2 * per) + split)
    packed = (groups, per, rows, 2 * HD)
    attended, lse = attend_call(table, q, kv)
    (context,) = gather_call([attended.reshape(packed)], [(True, False, None)], 3)
    layer_out, d_mix, d_context, g_out, g_up, g_down, g_vec, g_up_bias = dense_call(
        context, inputs, cotangent, mixed, up, down, vec, up_bias_row
    )
    (d_context,) = gather_call([d_context], [(True, False, None)], 4)
    d_q, d_kv = attend_back_call(table, q, kv, d_context.reshape(q.shape), attended, lse)
    d_q, d_kv, grad_up, grad_down = scatter_call(
        [
            d_q.reshape(packed),
            d_kv.reshape(devices, 2 * per, rows, 2 * HD),
            g_up.reshape(devices, depth, ff),
            g_down.reshape(devices, -1, width),
        ],
        [
            (False, False, None),
            (False, True, pairs),
            (True, True, (cut(1, 0, ff), None)),
            (True, True, (None, cut(1, 0, width))),
        ],
        5,
    )
    input_grad, g_mixed, g_vec_two = project_back_call(d_q, d_kv, inputs, mixed, d_mix, g_out)
    sums = jnp.concatenate([g_vec_two[:2], g_vec[:6]], axis=0).reshape(8, devices, depth)
    sums = jnp.concatenate(
        [sums.transpose(1, 0, 2), g_up_bias.reshape(devices, ff // width, depth)], axis=1
    )
    sums = jnp.pad(sums, ((0, 0), (0, 16 - sums.shape[1]), (0, 128 - depth)))
    grad_mixed, grad_vec = scatter_call(
        [g_mixed.reshape(devices, depth, 4 * width), sums],
        [
            (True, True, (cut(1, 0, half), cut(1, half, half))),
            (True, True, (cut(1, 0, 128), None)),
        ],
        6,
    )
    grad_query, grad_key, grad_value, grad_out = (
        grad_mixed[:, k * width : (k + 1) * width] for k in range(4)
    )
    vector = [grad_vec[k, :depth] for k in range(8)]
    grad_up_bias = grad_vec[8 : 8 + ff // width, :depth].reshape(-1)
    return (
        layer_out, input_grad, grad_query, vector[0], grad_key, grad_value, vector[1], grad_out,
        vector[2], vector[3], vector[4], grad_up, grad_up_bias, grad_down, vector[5], vector[6], vector[7],
    )


def with_halo(cells, sides, width):
    for axis, dim in sides:
        count = lax.axis_size(axis)
        ends = count - 1
        head = lax.slice_in_dim(cells, 0, width, axis=dim)
        tail = lax.slice_in_dim(cells, cells.shape[dim] - width, cells.shape[dim], axis=dim)
        cells = jnp.concatenate(
            [
                lax.ppermute(tail, axis, [(i, (i + 1) % count) for i in range(ends)]),
                cells,
                lax.ppermute(head, axis, [((i + 1) % count, i) for i in range(ends)]),
            ],
            axis=dim,
        )
    return cells


def combined_all(part, axis, combine):
    gathered = jax.tree.map(lambda a: lax.all_gather(a, axis), part)

    def take(source):
        return jax.tree.map(lambda a: lax.dynamic_index_in_dim(a, source, 0, False), gathered)

    return lax.fori_loop(
        1, lax.axis_size(axis), lambda source, state: combine(state, take(source)), take(0)
    )


def taken(table, rows):
    return lax.map(lambda row: lax.dynamic_index_in_dim(table, row, 0, False), rows)


def layer_norm(values, norm_gain, norm_shift):
    center = jnp.mean(values, axis=-1, keepdims=True)
    centred = values - center
    spread = jnp.mean(centred * centred, axis=-1, keepdims=True)
    return centred * lax.rsqrt(spread + 1e-12) * norm_gain + norm_shift


def gelu_exact(values):
    return jax.nn.gelu(values, approximate=False)


def matmul(left_side, right_side):
    return jnp.dot(left_side, right_side, preferred_element_type=jnp.float32)


def matmul_left(left_side, right_side):
    return lax.dot_general(
        left_side, right_side, (((0,), (0,)), ((), ())), preferred_element_type=jnp.float32
    )


def matmul_right(left_side, right_side):
    return lax.dot_general(
        left_side, right_side, (((1,), (1,)), ((), ())), preferred_element_type=jnp.float32
    )


def column_sum(values):
    return jnp.sum(values.astype(jnp.float32), axis=0)


def combine_parts(earlier, later_part):
    joint_top = jnp.maximum(earlier[0], later_part[0])
    first_factor = jnp.exp(earlier[0] - joint_top)
    second_factor = jnp.exp(later_part[0] - joint_top)
    return (
        joint_top,
        earlier[1] * first_factor + later_part[1] * second_factor,
        earlier[2] * first_factor[..., None] + later_part[2] * second_factor[..., None],
    )


def fetch_weights(
    query_weight,
    query_bias,
    key_weight,
    value_weight,
    value_bias,
    out_weight,
    out_bias,
    attn_gain,
    attn_shift,
    up_weight,
    up_bias,
    down_weight,
    down_bias,
    ffn_gain,
    ffn_shift,
):
    return (
        lax.all_gather(query_weight, ("blk", "head"), axis=0, tiled=True),
        lax.all_gather(query_bias, ("blk", "head"), axis=0, tiled=True),
        lax.all_gather(key_weight, ("blk", "head"), axis=0, tiled=True),
        lax.all_gather(value_weight, ("blk", "head"), axis=0, tiled=True),
        lax.all_gather(value_bias, ("blk", "head"), axis=0, tiled=True),
        lax.all_gather(out_weight, ("blk", "head"), axis=0, tiled=True),
        lax.all_gather(out_bias, ("blk", "head"), axis=0, tiled=True),
        lax.all_gather(attn_gain, ("blk", "head"), axis=0, tiled=True),
        lax.all_gather(attn_shift, ("blk", "head"), axis=0, tiled=True),
        lax.all_gather(up_weight, ("blk", "head"), axis=0, tiled=True),
        lax.all_gather(up_bias, ("blk", "head"), axis=0, tiled=True),
        lax.all_gather(down_weight, ("blk", "head"), axis=0, tiled=True),
        lax.all_gather(down_bias, ("blk", "head"), axis=0, tiled=True),
        lax.all_gather(ffn_gain, ("blk", "head"), axis=0, tiled=True),
        lax.all_gather(ffn_shift, ("blk", "head"), axis=0, tiled=True),
    )


def reduce_grads(totals):
    return (
        lax.psum_scatter(totals[0], ("blk", "head"), scatter_dimension=0, tiled=True),
        lax.psum_scatter(totals[1], ("blk", "head"), scatter_dimension=0, tiled=True),
        lax.psum_scatter(totals[2], ("blk", "head"), scatter_dimension=0, tiled=True),
        lax.psum_scatter(totals[3], ("blk", "head"), scatter_dimension=0, tiled=True),
        lax.psum_scatter(totals[4], ("blk", "head"), scatter_dimension=0, tiled=True),
        lax.psum_scatter(totals[5], ("blk", "head"), scatter_dimension=0, tiled=True),
        lax.psum_scatter(totals[6], ("blk", "head"), scatter_dimension=0, tiled=True),
        lax.psum_scatter(totals[7], ("blk", "head"), scatter_dimension=0, tiled=True),
        lax.psum_scatter(totals[8], ("blk", "head"), scatter_dimension=0, tiled=True),
        lax.psum_scatter(totals[9], ("blk", "head"), scatter_dimension=0, tiled=True),
        lax.psum_scatter(totals[10], ("blk", "head"), scatter_dimension=0, tiled=True),
        lax.psum_scatter(totals[11], ("blk", "head"), scatter_dimension=0, tiled=True),
        lax.psum_scatter(totals[12], ("blk", "head"), scatter_dimension=0, tiled=True),
        lax.psum_scatter(totals[13], ("blk", "head"), scatter_dimension=0, tiled=True),
        lax.psum_scatter(totals[14], ("blk", "head"), scatter_dimension=0, tiled=True),
    )


def sparse_forward(packed):
    group_queries, group_keys, group_values, group_allowed = packed
    attn_scale = HD ** (-0.5)
    scores = (
        jnp.einsum("gqhd,ghkd->ghqk", group_queries, group_keys, preferred_element_type=jnp.float32)
        * attn_scale
    )
    scores = jnp.where(group_allowed[:, None, None, :], scores, -jnp.inf)
    row_top = jnp.max(scores, axis=-1, keepdims=True)
    raised = jnp.exp(scores - row_top)
    row_total = jnp.sum(raised, axis=-1, keepdims=True)
    probs_low = (raised / row_total).astype(jnp.bfloat16)
    output = jnp.einsum(
        "ghqk,ghkd->gqhd", probs_low, group_values, preferred_element_type=jnp.float32
    )
    return (output, (row_top + jnp.log(row_total))[..., 0])


def sparse_backward(nearby, carried, packed):
    group_queries, group_keys, group_values, group_allowed, group_lse, group_grad = packed
    attn_scale = HD ** (-0.5)
    per_group = group_queries.shape[0]
    heads_dev = group_queries.shape[2]
    scores = (
        jnp.einsum("gqhd,ghkd->ghqk", group_queries, group_keys, preferred_element_type=jnp.float32)
        * attn_scale
    )
    scores = jnp.where(group_allowed[:, None, None, :], scores, -jnp.inf)
    probs = jnp.exp(scores - group_lse[..., None])
    d_probs = jnp.einsum(
        "gqhd,ghkd->ghqk", group_grad, group_values, preferred_element_type=jnp.float32
    )
    row_delta = jnp.sum(probs * d_probs, axis=-1, keepdims=True)
    d_scores = (probs * (d_probs - row_delta)).astype(jnp.bfloat16)
    d_queries = (
        jnp.einsum("ghqk,ghkd->gqhd", d_scores, group_keys, preferred_element_type=jnp.float32)
        * attn_scale
    )
    d_keys = (
        jnp.einsum("ghqk,gqhd->ghkd", d_scores, group_queries, preferred_element_type=jnp.float32)
        * attn_scale
    )
    d_values = jnp.einsum(
        "ghqk,gqhd->ghkd",
        probs.astype(jnp.bfloat16),
        group_grad,
        preferred_element_type=jnp.float32,
    )
    d_keys = d_keys.reshape(per_group, heads_dev, -1, BLOCK, HD)
    d_values = d_values.reshape(per_group, heads_dev, -1, BLOCK, HD)
    carried = (
        carried[0] + jnp.sum(d_keys[:, :, nearby:], axis=0),
        carried[1] + jnp.sum(d_values[:, :, nearby:], axis=0),
    )
    return (carried, (d_queries, d_keys[:, :, :nearby], d_values[:, :, :nearby]))


def micro_batch(tokens, cotangent_rows, random_rows, global_rows, weights):
    (
        full_query,
        full_query_bias,
        full_key,
        full_value,
        full_value_bias,
        full_out,
        full_out_bias,
        full_attn_gain,
        full_attn_shift,
        full_up,
        full_up_bias,
        full_down,
        full_down_bias,
        full_ffn_gain,
        full_ffn_shift,
    ) = weights
    attn_scale = HD ** (-0.5)
    shards = lax.axis_size("blk")
    head_groups = lax.axis_size("head")
    shard_index = lax.axis_index("blk")
    group_index = lax.axis_index("head")
    heads_dev = HEADS // head_groups
    group_width = heads_dev * HD
    listed = 3 + RAND + GLOB
    nearby = 3 + RAND
    projected = jnp.stack(
        [
            matmul(tokens, full_query) + full_query_bias,
            matmul(tokens, full_key),
            matmul(tokens, full_value) + full_value_bias,
        ]
    ).astype(jnp.bfloat16)
    by_head = lax.all_to_all(projected, "head", split_axis=2, concat_axis=1, tiled=True)
    row_count = by_head.shape[1]
    block_count = row_count // BLOCK
    blocks_all = block_count * shards
    key_rows = by_head[1]
    value_rows = by_head[2]
    padded = with_halo(by_head[1:3], (("blk", 1),), BLOCK)
    extended = padded.reshape(2, block_count + 2, BLOCK, heads_dev, HD).transpose(0, 1, 3, 2, 4)
    window = jnp.stack([extended[:, offset : offset + block_count] for offset in range(3)], axis=3)
    block_ids = shard_index * block_count + jnp.arange(block_count, dtype=jnp.int32)
    neighbour = block_ids[:, None] + jnp.arange(-1, 2, dtype=jnp.int32)[None, :]
    inside = (neighbour >= 0) & (neighbour < blocks_all)
    head_table = lax.dynamic_slice_in_dim(random_rows, group_index * heads_dev, heads_dev, 1)
    requests = block_count * heads_dev * RAND
    all_requests = head_table.reshape(shards, requests)
    capacity = (requests + shards - 1) // shards + 1
    wanted = lax.dynamic_slice_in_dim(all_requests, shard_index, 1, 0)[0]
    source = wanted // block_count
    place = jnp.arange(requests, dtype=jnp.int32)
    earlier = (place[:, None] > place[None, :]).astype(jnp.int32)
    same_source = (source[:, None] == source[None, :]).astype(jnp.int32)
    slot_index = jnp.sum(earlier * same_source, axis=1)
    mine_mask = (all_requests // block_count == shard_index).astype(jnp.int32)
    send_order = jnp.sum(earlier[None] * mine_mask[:, None, :], axis=2)
    match_mask = mine_mask[:, :, None] * (
        send_order[:, :, None] == jnp.arange(capacity, dtype=jnp.int32)[None, None, :]
    ).astype(jnp.int32)
    head_of = jnp.arange(requests, dtype=jnp.int32) // RAND % heads_dev
    row_of = all_requests % block_count * heads_dev + head_of[None, :]
    send_rows = jnp.sum(match_mask * row_of[:, :, None], axis=1)
    filled = jnp.sum(match_mask, axis=1).astype(jnp.float32)
    block_table = (
        by_head[1:3]
        .reshape(2, block_count, BLOCK, heads_dev, HD)
        .transpose(1, 3, 0, 2, 4)
        .reshape(block_count * heads_dev, 2, BLOCK, HD)
    )
    outgoing = taken(block_table, send_rows.reshape(-1))
    incoming = lax.all_to_all(outgoing, "blk", split_axis=0, concat_axis=0, tiled=True)
    fetched = taken(incoming, source * capacity + slot_index).reshape(
        block_count, heads_dev, RAND, 2, BLOCK, HD
    )
    owner_shard = global_rows // block_count
    present = owner_shard == shard_index
    local_block = global_rows % block_count
    own_rows = jnp.stack(
        [
            lax.dynamic_index_in_dim(
                by_head.reshape(3, block_count, BLOCK, group_width), local_block[g], 1, False
            )
            for g in range(GLOB)
        ],
        axis=1,
    )
    shared = lax.psum(
        jnp.where(present[None, :, None, None], own_rows.astype(jnp.float32), 0.0), "blk"
    ).astype(jnp.bfloat16)
    shared_pairs = shared[1:3].reshape(2, GLOB, BLOCK, heads_dev, HD).transpose(0, 3, 1, 2, 4)

    def listed_blocks(which):
        near_part = window[which]
        random_part = fetched[:, :, :, which]
        global_part = jnp.broadcast_to(
            shared_pairs[which][None], (block_count, heads_dev, GLOB, BLOCK, HD)
        )
        return jnp.concatenate([near_part, random_part, global_part], axis=2).reshape(
            block_count, heads_dev, listed * BLOCK, HD
        )

    per_group = min(8, block_count)
    group_count = block_count // per_group
    query_groups = by_head[0].reshape(group_count, per_group, BLOCK, heads_dev, HD)
    key_groups = listed_blocks(0).reshape(group_count, per_group, heads_dev, listed * BLOCK, HD)
    value_groups = listed_blocks(1).reshape(group_count, per_group, heads_dev, listed * BLOCK, HD)
    allowed = jnp.repeat(
        jnp.concatenate([inside, jnp.ones((block_count, RAND + GLOB), jnp.bool_)], axis=1),
        BLOCK,
        axis=1,
    )
    allow_groups = allowed.reshape(group_count, per_group, listed * BLOCK)
    sparse_out, sparse_lse = lax.map(
        sparse_forward, (query_groups, key_groups, value_groups, allow_groups)
    )
    global_queries = shared[0].reshape(GLOB, BLOCK, heads_dev, HD)
    key_heads = key_rows.reshape(row_count, heads_dev, HD)
    value_wide = value_rows.reshape(row_count, heads_dev, HD).astype(jnp.float32)
    global_scores = (
        jnp.einsum("gqhd,khd->ghqk", global_queries, key_heads, preferred_element_type=jnp.float32)
        * attn_scale
    )
    global_top = jnp.max(global_scores, axis=-1)
    global_raised = jnp.exp(global_scores - global_top[..., None])
    merged = combined_all(
        (
            global_top,
            jnp.sum(global_raised, axis=-1),
            jnp.einsum(
                "ghqk,khd->ghqd", global_raised, value_wide, precision=lax.Precision.HIGHEST
            ),
        ),
        "blk",
        combine_parts,
    )
    global_out = merged[2] / merged[1][..., None]
    global_lse = merged[0] + jnp.log(merged[1])
    global_hits = (block_ids[:, None] == global_rows[None, :]).astype(jnp.float32)
    is_global = jnp.sum(global_hits, axis=1) > 0
    replaced = jnp.einsum("ng,ghqd->nqhd", global_hits, global_out, precision=lax.Precision.HIGHEST)
    context = jnp.where(
        is_global[:, None, None, None],
        replaced,
        sparse_out.reshape(block_count, BLOCK, heads_dev, HD),
    )
    context_rows = context.reshape(row_count, group_width).astype(jnp.bfloat16)
    context_tokens = lax.all_to_all(context_rows, "head", split_axis=0, concat_axis=1, tiled=True)
    branch = matmul(context_tokens, full_out) + full_out_bias
    first_in = tokens.astype(jnp.float32) + branch
    first_norm, first_pull = jax.vjp(
        layer_norm,
        first_in,
        full_attn_gain.astype(jnp.float32),
        full_attn_shift.astype(jnp.float32),
    )
    first_low = first_norm.astype(jnp.bfloat16)
    hidden = matmul(first_low, full_up) + full_up_bias
    act_value, gelu_pull = jax.vjp(gelu_exact, hidden)
    act_low = act_value.astype(jnp.bfloat16)
    ffn_out = matmul(act_low, full_down) + full_down_bias
    result, second_pull = jax.vjp(
        layer_norm,
        first_norm + ffn_out,
        full_ffn_gain.astype(jnp.float32),
        full_ffn_shift.astype(jnp.float32),
    )
    d_second, grad_ffn_gain, grad_ffn_shift = second_pull(cotangent_rows.astype(jnp.float32))
    d_ffn = d_second.astype(jnp.bfloat16)
    grad_down = matmul_left(act_low, d_ffn)
    grad_down_bias = column_sum(d_ffn)
    (d_hidden,) = gelu_pull(matmul_right(d_ffn, full_down))
    d_hidden_low = d_hidden.astype(jnp.bfloat16)
    grad_up = matmul_left(first_low, d_hidden_low)
    grad_up_bias = column_sum(d_hidden_low)
    d_first = d_second + matmul_right(d_hidden_low, full_up)
    d_mix, grad_attn_gain, grad_attn_shift = first_pull(d_first)
    d_branch = d_mix.astype(jnp.bfloat16)
    grad_out = matmul_left(context_tokens, d_branch)
    grad_out_bias = column_sum(d_branch)
    d_context = matmul_right(d_branch, full_out).astype(jnp.bfloat16)
    d_heads = lax.all_to_all(d_context, "head", split_axis=1, concat_axis=0, tiled=True).reshape(
        block_count, BLOCK, heads_dev, HD
    )
    d_sparse = jnp.where(is_global[:, None, None, None], jnp.zeros_like(d_heads), d_heads)
    d_global = lax.psum(
        jnp.where(
            present[:, None, None, None], taken(d_heads, local_block).astype(jnp.float32), 0.0
        ),
        "blk",
    )
    start_carry = (
        jnp.zeros((heads_dev, GLOB, BLOCK, HD), jnp.float32),
        jnp.zeros((heads_dev, GLOB, BLOCK, HD), jnp.float32),
    )
    global_sums, (d_query_parts, near_keys, near_values) = lax.scan(
        partial(sparse_backward, nearby),
        start_carry,
        (
            query_groups,
            key_groups,
            value_groups,
            allow_groups,
            sparse_lse,
            d_sparse.reshape(group_count, per_group, BLOCK, heads_dev, HD),
        ),
    )
    d_query_sparse = d_query_parts.reshape(block_count, BLOCK, heads_dev, HD)
    near_keys = near_keys.reshape(block_count, heads_dev, nearby, BLOCK, HD)
    near_values = near_values.reshape(block_count, heads_dev, nearby, BLOCK, HD)
    near_grads = jnp.stack([near_keys[:, :, :3], near_values[:, :, :3]])
    ext_grads = jnp.zeros((2, block_count + 2, heads_dev, BLOCK, HD), jnp.float32)
    for offset in range(3):
        ext_grads = ext_grads + jnp.pad(
            near_grads[:, :, :, offset], ((0, 0), (offset, 2 - offset), (0, 0), (0, 0), (0, 0))
        )
    rim_pair = jnp.stack([ext_grads[:, 0], ext_grads[:, block_count + 1]], axis=1)
    arrived = with_halo(rim_pair.astype(jnp.bfloat16), (("blk", 1),), 1).astype(rim_pair.dtype)
    inner_grads = ext_grads[:, 1 : block_count + 1]
    inner_grads = inner_grads.at[:, 0].add(arrived[:, 0]).at[:, block_count - 1].add(arrived[:, 3])
    far_grads = jnp.stack([near_keys[:, :, 3:], near_values[:, :, 3:]], axis=3).reshape(
        requests, 2, BLOCK, HD
    )
    outbox = (
        jnp.zeros((shards, capacity, 2, BLOCK, HD), jnp.float32)
        .at[source, slot_index]
        .set(far_grads)
    )
    arrived_slots = (
        lax.all_to_all(
            outbox.astype(jnp.bfloat16), "blk", split_axis=0, concat_axis=0, tiled=True
        ).astype(outbox.dtype)
        * filled[:, :, None, None, None]
    )
    landed = (
        jnp.zeros((block_count * heads_dev, 2, BLOCK, HD), jnp.float32)
        .at[send_rows.reshape(-1)]
        .add(arrived_slots.reshape(shards * capacity, 2, BLOCK, HD))
    )
    landed = landed.reshape(block_count, heads_dev, 2, BLOCK, HD)
    global_probs = jnp.exp(global_scores - global_lse[..., None])
    d_probs_global = jnp.einsum(
        "gqhd,khd->ghqk", d_global, value_wide, precision=lax.Precision.HIGHEST
    )
    delta_global = jnp.einsum(
        "gqhd,ghqd->ghq", d_global, global_out, precision=lax.Precision.HIGHEST
    )
    d_scores_global = (global_probs * (d_probs_global - delta_global[..., None])).astype(
        jnp.bfloat16
    )
    d_global_queries = (
        jnp.einsum("ghqk,khd->gqhd", d_scores_global, key_heads, preferred_element_type=jnp.float32)
        * attn_scale
    )
    d_keys_global = (
        jnp.einsum(
            "ghqk,gqhd->khd", d_scores_global, global_queries, preferred_element_type=jnp.float32
        )
        * attn_scale
    )
    d_values_global = jnp.einsum(
        "ghqk,gqhd->khd", global_probs, d_global, precision=lax.Precision.HIGHEST
    )
    returned = lax.psum(
        jnp.stack(
            [
                d_global_queries,
                global_sums[0].transpose(1, 2, 0, 3),
                global_sums[1].transpose(1, 2, 0, 3),
            ]
        ),
        "blk",
    )
    owned_grads = jnp.einsum(
        "ng,cgqhd->cnqhd", global_hits, returned, precision=lax.Precision.HIGHEST
    )
    d_query_total = d_query_sparse + owned_grads[0]
    d_key_total = (
        (inner_grads[0] + landed[:, :, 0]).transpose(0, 2, 1, 3)
        + d_keys_global.reshape(block_count, BLOCK, heads_dev, HD)
        + owned_grads[1]
    )
    d_value_total = (
        (inner_grads[1] + landed[:, :, 1]).transpose(0, 2, 1, 3)
        + d_values_global.reshape(block_count, BLOCK, heads_dev, HD)
        + owned_grads[2]
    )
    stacked = (
        jnp.stack([d_query_total, d_key_total, d_value_total])
        .reshape(3, row_count, group_width)
        .astype(jnp.bfloat16)
    )
    token_grads = lax.all_to_all(stacked, "head", split_axis=1, concat_axis=2, tiled=True)
    d_tokens = (
        d_mix
        + matmul_right(token_grads[0], full_query)
        + matmul_right(token_grads[1], full_key)
        + matmul_right(token_grads[2], full_value)
    )
    grads = (
        matmul_left(tokens, token_grads[0]),
        column_sum(token_grads[0]),
        matmul_left(tokens, token_grads[1]),
        matmul_left(tokens, token_grads[2]),
        column_sum(token_grads[2]),
        grad_out,
        grad_out_bias,
        grad_attn_gain,
        grad_attn_shift,
        grad_up,
        grad_up_bias,
        grad_down,
        grad_down_bias,
        grad_ffn_gain,
        grad_ffn_shift,
    )
    return (result.astype(jnp.bfloat16), d_tokens.astype(jnp.bfloat16), grads)


def body(
    inputs,
    cotangent,
    random_blocks,
    global_blocks,
    query_weight,
    query_bias,
    key_weight,
    value_weight,
    value_bias,
    out_weight,
    out_bias,
    attn_gain,
    attn_shift,
    up_weight,
    up_bias,
    down_weight,
    down_bias,
    ffn_gain,
    ffn_shift,
):
    weight_shards = (
        query_weight,
        query_bias,
        key_weight,
        value_weight,
        value_bias,
        out_weight,
        out_bias,
        attn_gain,
        attn_shift,
        up_weight,
        up_bias,
        down_weight,
        down_bias,
        ffn_gain,
        ffn_shift,
    )
    results = []
    input_grads = []
    totals = None
    for micro_index in range(inputs.shape[0]):
        weights = fetch_weights(*weight_shards)
        result, token_grad, grads = micro_batch(
            inputs[micro_index],
            cotangent[micro_index],
            random_blocks[micro_index],
            global_blocks[micro_index],
            weights,
        )
        grads = reduce_grads(grads)
        totals = (
            grads
            if totals is None
            else tuple((total_sum + extra_sum for total_sum, extra_sum in zip(totals, grads)))
        )
        results.append(result)
        input_grads.append(token_grad)
    return (jnp.stack(results), jnp.stack(input_grads)) + tuple(totals)


def solution(mesh):
    return jax.shard_map(
        near_body if (mesh.shape["blk"], mesh.shape["head"]) == (8, 4) else body,
        mesh=mesh,
        in_specs=(
            P(None, ("blk", "head"), None),
            P(None, ("blk", "head"), None),
            P(),
            P(),
            P(("blk", "head"), None),
            P(("blk", "head")),
            P(("blk", "head"), None),
            P(("blk", "head"), None),
            P(("blk", "head")),
            P(("blk", "head"), None),
            P(("blk", "head")),
            P(("blk", "head")),
            P(("blk", "head")),
            P(("blk", "head"), None),
            P(("blk", "head")),
            P(("blk", "head"), None),
            P(("blk", "head")),
            P(("blk", "head")),
            P(("blk", "head")),
        ),
        out_specs=(
            P(None, ("blk", "head"), None),
            P(None, ("blk", "head"), None),
            P(("blk", "head"), None),
            P(("blk", "head")),
            P(("blk", "head"), None),
            P(("blk", "head"), None),
            P(("blk", "head")),
            P(("blk", "head"), None),
            P(("blk", "head")),
            P(("blk", "head")),
            P(("blk", "head")),
            P(("blk", "head"), None),
            P(("blk", "head")),
            P(("blk", "head"), None),
            P(("blk", "head")),
            P(("blk", "head")),
            P(("blk", "head")),
        ),
        check_vma=False,
    )
```

```python
from functools import partial

import jax
import jax.numpy as jnp
from jax import lax
from jax.experimental import pallas as pl
from jax.experimental.pallas import tpu as pltpu
from jax.sharding import PartitionSpec as P

HEADS = 12
HD = 64
BLOCK = 64
RAND = 3
GLOB = 2


MESH = pl.DeviceIdType.MESH


def places():
    b = lax.axis_index("blk")
    h = lax.axis_index("head")
    core = b % 2
    x = (b // 2) % 2
    y = b // 4
    across_x = b + 2 - 4 * x
    across_y = b + 4 - 8 * y
    partner = b + 1 - 2 * core
    pair = h // 2
    line = (h, h + 1 - 2 * (h % 2), 2 - pair, 3 - 3 * pair)
    return b, h, core, x, y, across_x, across_y, partner, line


def meet(b, h, others, line):
    barrier = pltpu.get_barrier_semaphore()
    for other in others:
        pl.semaphore_signal(barrier, inc=1, device_id=(other, h), device_id_type=MESH)
    for d in range(1, 4):
        pl.semaphore_signal(barrier, inc=1, device_id=(b, line[d]), device_id_type=MESH)
    pl.semaphore_wait(barrier, len(others) + 3)


def remote(src, dst, send_sem, recv_sem, device):
    return pltpu.make_async_remote_copy(
        src_ref=src,
        dst_ref=dst,
        send_sem=send_sem,
        recv_sem=recv_sem,
        device_id=device,
        device_id_type=MESH,
    )


def gather_steps(kinds, ins, outs, sems):
    own_sem, line_send, line_recv, send, recv = sems
    b, h, core, x, y, across_x, across_y, partner, line = places()
    far_corner = across_x + 4 - 8 * y
    partner_x = partner + 2 - 4 * x
    partner_y = partner + 4 - 8 * y
    partner_corner = partner_x + 4 - 8 * y
    inner = jnp.logical_or(h == 1, h == 2)
    seen = jnp.where(inner, 2, 3)
    started = []
    started_inner = []
    locals_ = []

    def enter():
        meet(b, h, (across_x, across_y, partner), line)

    def piece(i, place):
        return ins[i].at[place] if kinds[i][0] else ins[i]

    def slot(i, shard, place):
        return outs[i].at[shard * 4 + place] if kinds[i][1] else outs[i].at[place]

    def part(ref, cut_):
        axis, start, size = cut_
        return ref.at[(slice(None),) * axis + (pl.ds(start, size),)]

    def go(copy, only_inner=False):
        if only_inner:

            @pl.when(inner)
            def _():
                copy.start()

            started_inner.append(copy)
        else:
            copy.start()
            started.append(copy)

    def along(i, src, landing, sender_at, receiver_at, place, only_inner=False):
        go(
            remote(
                src, landing, line_send.at[i, sender_at], line_recv.at[i, receiver_at], (b, place)
            ),
            only_inner,
        )

    def plane(i, d):
        src = piece(i, h) if d == 0 else slot(i, b, line[d])
        for k, other in enumerate((across_x, across_y, partner)):
            go(
                remote(
                    src, slot(i, b, line[d]), send.at[i, d, k], recv.at[i, d, k], (other, h)
                )
            )

    def arrived(i, d, k, shard, cut_=None):
        here = slot(i, shard, line[d])
        if cut_ is not None:
            here = part(here, cut_)
        remote(here, here, send.at[i, d, k], recv.at[i, d, k], (partner, h)).wait_recv()
        return here

    def begin(i):
        if kinds[i][0]:
            for d in (2, 3, 1):
                along(i, piece(i, line[d]), slot(i, b, h), d, 1 if d == 1 else seen, line[d])
        else:
            along(i, piece(i, h), slot(i, b, h), 2, 2, 3 - h, True)
            along(i, piece(i, h), slot(i, b, h), 1, 1, line[1])
        if kinds[i][1]:
            plane(i, 0)
        own = pltpu.make_async_copy(piece(i, h), slot(i, b, h), own_sem.at[i])
        own.start()
        locals_.append(own)

    def along_done(i, d):
        here = slot(i, b, line[d])
        remote(
            here, here, line_send.at[i, d], line_recv.at[i, d], (b, line[d])
        ).wait_recv()
        if not kinds[i][0]:
            if d == 1:
                along(i, here, here, 3, 3, 3 - h, True)
            else:
                along(i, here, here, d + 2, d, line[1], True)
        if kinds[i][1]:
            plane(i, d)

    def pass_on(i, d):
        first, second = kinds[i][2]
        for k, shard, cut_, onward in (
            (0, across_x, first, across_y),
            (1, across_y, second, across_x),
        ):
            here = arrived(i, d, k, shard)
            if cut_ is not None:
                go(
                    remote(
                        part(here, cut_),
                        part(here, cut_),
                        send.at[i, d, 6 + k],
                        recv.at[i, d, 6 + k],
                        (onward, h),
                    )
                )
            go(remote(here, here, send.at[i, d, 3 + k], recv.at[i, d, 3 + k], (partner, h)))

    def corner(i, d):
        for k, cut_ in enumerate(kinds[i][2]):
            if cut_ is not None:
                arrived(i, d, 6 + k, far_corner, cut_)
        here = slot(i, far_corner, line[d])
        go(remote(here, here, send.at[i, d, 5], recv.at[i, d, 5], (partner, h)))

    def finish(i):
        for d in range(4):
            for k, shard in ((2, partner), (3, partner_x), (4, partner_y), (5, partner_corner)):
                arrived(i, d, k, shard)

    def kept():
        for own in locals_:
            own.wait()
        locals_.clear()

    def sent():
        for copy in started:
            copy.wait_send()
        if started_inner:

            @pl.when(inner)
            def _():
                for copy in started_inner:
                    copy.wait_send()

    return enter, begin, along_done, pass_on, corner, finish, kept, sent


def gather_semaphores(n):
    dma = pltpu.SemaphoreType.DMA
    return [dma((n,)), dma((n, 6)), dma((n, 4)), dma((n, 4, 8)), dma((n, 4, 8))]


def swap_kernel(in_ref, out_ref, *sems):
    enter, begin, along_done, _, _, _, kept, sent = gather_steps(
        [(True, False, None)], [in_ref], [out_ref], sems
    )
    enter()
    begin(0)
    for d in range(1, 4):
        along_done(0, d)
    kept()
    sent()


def swap_call(array, collective):
    far = pl.BlockSpec(memory_space=pl.ANY)
    return pl.pallas_call(
        swap_kernel,
        out_shape=jax.ShapeDtypeStruct(array.shape, array.dtype),
        in_specs=[far],
        out_specs=far,
        scratch_shapes=gather_semaphores(1),
        compiler_params=pltpu.CompilerParams(collective_id=collective, has_side_effects=True),
        name=f"swap{collective}",
    )(array)


def spread_of(rows, width):
    shards, n = rows.shape
    total = shards * width
    lane = lax.broadcasted_iota(jnp.int32, (n, total), 0)
    column = lax.broadcasted_iota(jnp.int32, (n, total), 1)
    repeat = jnp.where(column % width == lane, 1.0, 0.0).astype(jnp.bfloat16)
    shard = lax.broadcasted_iota(jnp.int32, (shards, total), 0)
    column = lax.broadcasted_iota(jnp.int32, (shards, total), 1)
    return rows_sum(jnp.where(column // width == shard, dot(rows.astype(jnp.bfloat16), repeat), 0.0))


def front_kernel(kinds, *refs):
    (
        x_ref, wq_in, wk_in, wv_in, wo_in, up_in, down_in, *vectors,
    ) = refs[:16]
    (
        q_out, kv_out, up_out, down_out, w_out, vec_ref, up_bias_ref,
        tile, chunk, mixed, rows_wide, w_ref, q_parts, kv_parts, join_sem, w_sem,
    ) = refs[16:32]
    rows = x_ref.shape[1]
    width = x_ref.shape[2]
    shards, depth, _ = mixed.shape
    groups, per, _, _ = q_parts.shape
    enter, begin, along_done, pass_on, corner, finish, kept, sent = gather_steps(
        kinds,
        [chunk, up_in, down_in, kv_parts, q_parts],
        [mixed, up_out, down_out, kv_out, q_out],
        refs[32:],
    )
    joins = [
        pltpu.make_async_copy(ref, chunk.at[:, pl.ds(k * width, width)], join_sem.at[k])
        for k, ref in enumerate((wq_in, wk_in, wv_in, wo_in))
    ]
    for copy in joins:
        copy.start()
    tile[...] = jnp.zeros(tile.shape, jnp.float32)
    for k, ref in enumerate(vectors):
        tile[k, : ref.shape[0]] = ref[...].astype(jnp.float32)
    chunk[:, 4 * width :] = tile[...].astype(jnp.bfloat16)
    for copy in joins:
        copy.wait()
    enter()
    begin(0)
    begin(1)
    begin(2)
    along_done(0, 1)
    pass_on(0, 0)
    along_done(0, 2)
    along_done(1, 1)
    along_done(2, 1)
    pass_on(0, 1)
    corner(0, 0)
    along_done(0, 3)
    pass_on(1, 0)
    pass_on(2, 0)
    pass_on(0, 2)
    corner(0, 1)
    pass_on(0, 3)
    corner(0, 2)
    along_done(1, 2)
    along_done(2, 2)
    corner(0, 3)
    finish(0)
    kept()
    for s in range(0, 4 * width, width):
        part = mixed[:, :, s : s + width].astype(jnp.float32).reshape(width, width)
        w_ref[:, s : s + width] = part.astype(jnp.bfloat16)
    leave = pltpu.make_async_copy(w_ref, w_out, w_sem)
    leave.start()
    rows_wide[...] = mixed[:, :, 4 * width :].astype(jnp.float32)
    for k in range(8):
        vec_ref[k : k + 1, :] = spread_of(rows_wide[:, k, :], depth)
    up_bias_ref[...] = spread_of(rows_wide[:, 8, :], up_bias_ref.shape[1] // shards)
    tokens = x_ref[...].reshape(2 * rows, width)
    made = []
    for k in range(3):
        part = dot(tokens, w_ref[:, k * width : (k + 1) * width])
        if k != 1:
            part = part + vec_ref[k // 2 : k // 2 + 1, :]
        made.append(part.astype(jnp.bfloat16))
    q, k, v = made
    for g in range(groups):
        for j in range(per):
            col = (g * per + j) * HD
            kv_parts[g, j] = jnp.concatenate([halves(k[:rows], col), halves(v[:rows], col)], axis=1)
            kv_parts[g, per + j] = jnp.concatenate([halves(v[rows:], col), halves(k[rows:], col)], axis=1)
    begin(3)
    for g in range(groups):
        for j in range(per):
            col = (g * per + j) * HD
            q_parts[g, j] = jnp.concatenate([halves(q[:rows], col), halves(q[rows:], col)], axis=1)
    pass_on(1, 1)
    pass_on(2, 1)
    corner(1, 0)
    corner(2, 0)
    along_done(3, 1)
    pass_on(3, 0)
    begin(4)
    along_done(3, 2)
    corner(3, 0)
    pass_on(3, 1)
    along_done(3, 3)
    along_done(1, 3)
    along_done(2, 3)
    corner(3, 1)
    pass_on(3, 2)
    pass_on(1, 2)
    pass_on(2, 2)
    corner(1, 1)
    corner(2, 1)
    corner(3, 2)
    pass_on(3, 3)
    corner(3, 3)
    corner(1, 2)
    corner(2, 2)
    pass_on(1, 3)
    pass_on(2, 3)
    corner(1, 3)
    corner(2, 3)
    for d in range(1, 4):
        along_done(4, d)
    finish(3)
    finish(1)
    finish(2)
    kept()
    leave.wait()
    sent()


def front_call(tokens, matrices, up, down, vectors, collective):
    micro, rows, width = tokens.shape
    depth, ff = up.shape
    groups = lax.axis_size("head")
    devices = groups * lax.axis_size("blk")
    per = HEADS // groups
    f32, bf16 = jnp.float32, jnp.bfloat16
    half = 2 * width
    kinds = [
        (False, True, (cut(1, 0, half), cut(1, half, half + 128))),
        (False, True, (cut(1, 0, ff), None)),
        (False, True, (None, cut(1, 0, width))),
        (True, True, (cut(0, 0, per), cut(0, per, per))),
        (True, False, None),
    ]
    near = pl.BlockSpec(memory_space=pltpu.VMEM)
    far = pl.BlockSpec(memory_space=pl.ANY)
    return pl.pallas_call(
        partial(front_kernel, kinds),
        out_shape=(
            jax.ShapeDtypeStruct((groups, per, rows, 2 * HD), bf16),
            jax.ShapeDtypeStruct((devices, 2 * per, rows, 2 * HD), bf16),
            jax.ShapeDtypeStruct((devices,) + up.shape, bf16),
            jax.ShapeDtypeStruct((devices,) + down.shape, bf16),
            jax.ShapeDtypeStruct((width, 4 * width), bf16),
            jax.ShapeDtypeStruct((8, width), f32),
            jax.ShapeDtypeStruct((1, ff), f32),
        ),
        in_specs=[near] + [far] * 6 + [near] * 9,
        out_specs=(far,) * 5 + (near,) * 2,
        scratch_shapes=[
            pltpu.VMEM((depth, 128), f32),
            pltpu.VMEM((depth, 4 * width + 128), bf16),
            pltpu.VMEM((devices, depth, 4 * width + 128), bf16),
            pltpu.VMEM((devices, depth, 128), f32),
            pltpu.VMEM((width, 4 * width), bf16),
            pltpu.VMEM((groups, per, rows, 2 * HD), bf16),
            pltpu.VMEM((groups, 2 * per, rows, 2 * HD), bf16),
            pltpu.SemaphoreType.DMA((4,)),
            pltpu.SemaphoreType.DMA,
        ]
        + gather_semaphores(5),
        compiler_params=pltpu.CompilerParams(
            collective_id=collective, has_side_effects=True, vmem_limit_bytes=56 * 2**20
        ),
        name="front",
    )(tokens, *matrices, up, down, *vectors)


def scatter_steps(kinds, ins, lands, bufs, sems):
    local_sem, own_sem, line_send, line_recv, core_send, core_recv, send, recv = sems
    b, h, core, x, y, across_x, across_y, partner, line = places()
    seen = jnp.where(jnp.logical_or(h == 1, h == 2), 2, 3)
    chip = b // 2
    targets = (3 - chip, chip + 1 - 2 * x, chip + 2 - 4 * y, chip)
    started = []
    locals_ = []
    loads = {}
    order = (3, 2, 1, 0)

    def go(copy):
        copy.start()
        started.append(copy)

    def part(ref, cut):
        axis, start, size = cut
        return ref.at[(slice(None),) * axis + (pl.ds(start, size),)]

    def along(i, src, landing, d):
        go(
            remote(
                src, landing, line_send.at[i, d], line_recv.at[i, 1 if d == 1 else seen], (b, line[d])
            )
        )

    def keep(src, i):
        own = pltpu.make_async_copy(src, lands[i].at[h], own_sem.at[i])
        own.start()
        locals_.append(own)

    def begin(i):
        if not kinds[i][1]:
            for d in (3, 2, 1):
                along(i, ins[i].at[line[d]], lands[i].at[h], d)
            keep(ins[i].at[h], i)
            return
        from_partner, total = bufs[i][0], bufs[i][1]
        for t in range(4):
            go(
                remote(
                    ins[i].at[pl.ds((targets[t] * 2 + 1 - core) * 4, 4)],
                    from_partner.at[t],
                    core_send.at[i, t],
                    core_recv.at[i, t],
                    (partner, h),
                )
            )
            load = pltpu.make_async_copy(
                ins[i].at[pl.ds((targets[t] * 2 + core) * 4, 4)], total.at[t], local_sem.at[i, t]
            )
            load.start()
            loads[i, t] = load

    def wait_for(ref, i, d, k):
        remote(ref, ref, send.at[i, d, k], recv.at[i, d, k], (partner, h)).wait_recv()

    def ready(i, t):
        loads[i, t].wait()
        here = bufs[i][0].at[t]
        remote(here, here, core_send.at[i, t], core_recv.at[i, t], (partner, h)).wait_recv()

    def both_cores(i, t, d, extra=()):
        from_partner, total = bufs[i][0], bufs[i][1]
        place = line[d]
        value = total[t, place].astype(jnp.float32) + from_partner[t, place].astype(jnp.float32)
        for ref in extra:
            value = value + ref[d].astype(jnp.float32)
        total[t, place] = value.astype(total.dtype)

    def add_corner(i, t, d, ref, cut):
        total = bufs[i][1]
        axis, start, size = cut
        at = (t, line[d]) + (slice(None),) * axis + (pl.ds(start, size),)
        value = total[at].astype(jnp.float32) + ref[d].astype(jnp.float32)
        total[at] = value.astype(total.dtype)

    def corner(i):
        total = bufs[i][1]
        first, second = kinds[i][2]
        ready(i, 0)
        for d in order:
            both_cores(i, 0, d)
            mine = total.at[0, line[d]]
            if first is not None:
                go(remote(part(mine, first), bufs[i][2].at[d], send.at[i, d, 0], recv.at[i, d, 0], (across_x, h)))
            if second is not None:
                go(remote(part(mine, second), bufs[i][3].at[d], send.at[i, d, 1], recv.at[i, d, 1], (across_y, h)))

    def sides(i):
        total = bufs[i][1]
        first, second = kinds[i][2]
        ready(i, 1)
        ready(i, 2)
        for d in order:
            both_cores(i, 1, d)
            if second is not None:
                wait_for(bufs[i][3].at[d], i, d, 1)
                add_corner(i, 1, d, bufs[i][3], second)
            go(remote(total.at[1, line[d]], bufs[i][4].at[d], send.at[i, d, 2], recv.at[i, d, 2], (across_x, h)))
            both_cores(i, 2, d)
            if first is not None:
                wait_for(bufs[i][2].at[d], i, d, 0)
                add_corner(i, 2, d, bufs[i][2], first)
            go(remote(total.at[2, line[d]], bufs[i][5].at[d], send.at[i, d, 3], recv.at[i, d, 3], (across_y, h)))

    def own(i):
        summed = kinds[i][0]
        total = bufs[i][1]
        ready(i, 3)
        for d in order:
            wait_for(bufs[i][4].at[d], i, d, 2)
            wait_for(bufs[i][5].at[d], i, d, 3)
            both_cores(i, 3, d, (bufs[i][4], bufs[i][5]))
            if d > 0:
                landing = bufs[i][6].at[1 if d == 1 else seen] if summed else lands[i].at[h]
                along(i, total.at[3, line[d]], landing, d)
            elif not summed:
                keep(total.at[3, h], i)

    def finish(i):
        summed = kinds[i][0]
        for d in range(1, 4):
            landing = bufs[i][6].at[d] if summed else lands[i].at[line[d]]
            remote(
                landing, landing, line_send.at[i, d], line_recv.at[i, d], (b, line[d])
            ).wait_recv()
        if not summed:
            return None
        value = bufs[i][1][3, h].astype(jnp.float32)
        for d in range(1, 4):
            value = value + bufs[i][6][d].astype(jnp.float32)
        return value

    def kept():
        for copy in locals_:
            copy.wait()
        locals_.clear()

    def sent():
        for copy in started:
            copy.wait_send()

    def enter():
        meet(b, h, (across_x, across_y, partner), line)

    return enter, begin, corner, sides, own, finish, kept, sent


def scatter_scratch(chunk, dtype, kind):
    summed, spread, cuts = kind
    if not spread:
        return []
    scratch = [pltpu.VMEM((4, 4) + chunk, dtype), pltpu.VMEM((4, 4) + chunk, dtype)]
    for cut_ in cuts:
        size = list(chunk)
        if cut_ is not None:
            size[cut_[0]] = cut_[2]
        else:
            size = [8, 128]
        scratch.append(pltpu.VMEM((4,) + tuple(size), dtype))
    scratch += [pltpu.VMEM((4,) + chunk, dtype)] * 2
    if summed:
        scratch.append(pltpu.VMEM((4,) + chunk, dtype))
    return scratch


def scatter_semaphores(n):
    dma = pltpu.SemaphoreType.DMA
    return [dma((n, 4)), dma((n,))] + [dma((n, 4))] * 4 + [dma((n, 4, 4))] * 2


def back_kernel(kinds, counts, *refs):
    (
        dq_in, dkv_in, up_in, down_in, x_ref, mixed_in, d_mix_ref, g_out_ref, g_vec_ref, g_up_bias_ref,
        d_x_ref, g_mixed_ref, g_up_ref, g_down_ref, g_small_ref,
        dq_land, dkv_land, terms, small, w_ref, d_q, d_k, d_v, w_sem,
    ), rest = refs[:24], list(refs[24:])
    bufs = []
    for count in counts:
        bufs.append(rest[:count])
        rest = rest[count:]
    groups, per, rows, _ = dq_land.shape
    width = x_ref.shape[2]
    depth = terms.shape[1]
    shards = terms.shape[0]
    ins = (dq_in, dkv_in, up_in, down_in, terms, small)
    enter, begin, corner, sides, own, finish, kept, sent = scatter_steps(
        kinds, ins, (dq_land, dkv_land, None, None, None, None), bufs, rest
    )
    load = pltpu.make_async_copy(mixed_in.at[:, pl.ds(0, 3 * width)], w_ref, w_sem)
    load.start()
    enter()
    for i in (1, 0, 2, 3):
        begin(i)
    small[...] = jnp.zeros(small.shape, jnp.float32)
    out_terms = g_out_ref[...].astype(jnp.float32).reshape(shards, depth, width)
    terms[:, :, 3 * width :] = out_terms.astype(jnp.bfloat16)
    corner(1)
    sides(1)
    corner(2)
    corner(3)
    own(1)
    sides(2)
    sides(3)
    finish(0)
    finish(1)
    kept()
    for p in range(HEADS // 2):
        at = pl.ds(p * 2 * HD, 2 * HD)

        def of(ref, shift, low):
            both = []
            for head in (2 * p, 2 * p + 1):
                tile = ref[head // per, shift + head % per]
                both.append(tile[:, :HD] if low else tile[:, HD:])
            return jnp.concatenate(both, axis=1)

        d_q[:rows, at] = of(dq_land, 0, True)
        d_q[rows:, at] = of(dq_land, 0, False)
        d_k[:rows, at] = of(dkv_land, 0, True)
        d_v[:rows, at] = of(dkv_land, 0, False)
        d_k[rows:, at] = of(dkv_land, per, False)
        d_v[rows:, at] = of(dkv_land, per, True)
    load.wait()
    tokens = x_ref[...].reshape(2 * rows, width)
    sums = []
    for k, half_ref in enumerate((d_q, d_k, d_v)):
        at = slice(k * width, (k + 1) * width)
        term = dot(tokens, half_ref[...], COLS).reshape(shards, depth, width)
        terms[:, :, at] = term.astype(jnp.bfloat16)
        if k != 1:
            sums.append(rows_sum(half_ref[...].astype(jnp.float32)))
    vectors = jnp.concatenate(sums + [g_vec_ref[:6, :]], axis=0)
    up_bias = g_up_bias_ref[...]
    up_depth = up_bias.shape[1] // shards
    for s in range(shards):
        small[s, :8, :depth] = vectors[:, s * depth : (s + 1) * depth]
        small[s, 8:9, :up_depth] = up_bias[:, s * up_depth : (s + 1) * up_depth]
    begin(4)
    begin(5)
    own(2)
    corner(4)
    corner(5)
    own(3)
    d_x = d_mix_ref[...]
    for k, half_ref in enumerate((d_q, d_k, d_v)):
        d_x = d_x + dot(half_ref[...], w_ref[:, k * width : (k + 1) * width], ROWS)
    d_x_ref[...] = d_x.astype(jnp.bfloat16).reshape(2, rows, width)
    sides(4)
    sides(5)
    g_up_ref[...] = finish(2)
    own(4)
    own(5)
    g_down_ref[...] = finish(3)
    g_mixed_ref[...] = finish(4)
    g_small_ref[...] = finish(5)
    sent()


def back_call(d_q, d_kv, g_up, g_down, tokens, mixed, d_mix, g_out, g_vec, g_up_bias, collective):
    micro, rows, width = tokens.shape
    devices, depth, ff = g_up.shape
    groups, per = d_q.shape[:2]
    f32, bf16 = jnp.float32, jnp.bfloat16
    half = 2 * width
    kinds = [
        (False, False, None),
        (False, True, (cut(0, 0, per), cut(0, per, per))),
        (True, True, (cut(1, 0, ff), None)),
        (True, True, (None, cut(1, 0, width))),
        (True, True, (cut(1, 0, half), cut(1, half, half))),
        (True, True, (cut(1, 0, 128), None)),
    ]
    chunks = [
        (d_q.shape[1:], bf16),
        (d_kv.shape[1:], bf16),
        (g_up.shape[1:], bf16),
        (g_down.shape[1:], bf16),
        ((depth, 4 * width), bf16),
        ((16, 128), f32),
    ]
    scratch = [scatter_scratch(chunk, dtype, kind) for (chunk, dtype), kind in zip(chunks, kinds)]
    near = pl.BlockSpec(memory_space=pltpu.VMEM)
    far = pl.BlockSpec(memory_space=pl.ANY)
    outs = [jax.ShapeDtypeStruct(tokens.shape, bf16)]
    outs += [
        jax.ShapeDtypeStruct((depth, 4 * width), f32),
        jax.ShapeDtypeStruct((depth, ff), f32),
        jax.ShapeDtypeStruct(g_down.shape[1:], f32),
        jax.ShapeDtypeStruct((16, 128), f32),
    ]
    return pl.pallas_call(
        partial(back_kernel, kinds, [len(s) for s in scratch]),
        out_shape=tuple(outs),
        in_specs=[far] * 4 + [near, far] + [near] * 4,
        out_specs=(near,) * 5,
        scratch_shapes=[
            pltpu.VMEM(d_q.shape, bf16),
            pltpu.VMEM((groups,) + d_kv.shape[1:], bf16),
            pltpu.VMEM((devices, depth, 4 * width), bf16),
            pltpu.VMEM((devices, 16, 128), f32),
            pltpu.VMEM((width, 3 * width), bf16),
        ]
        + [pltpu.VMEM((micro * rows, width), bf16)] * 3
        + [pltpu.SemaphoreType.DMA]
        + [one for some in scratch for one in some]
        + scatter_semaphores(6),
        compiler_params=pltpu.CompilerParams(
            collective_id=collective, has_side_effects=True, vmem_limit_bytes=61 * 2**20
        ),
        name="back",
    )(d_q, d_kv, g_up, g_down, tokens, mixed, d_mix, g_out, g_vec, g_up_bias)


def leave_kernel(d_x_in, mixed_in, up_in, down_in, small_in, d_x_ref, *refs):
    d_x_ref[...] = d_x_in[...]
    width = d_x_in.shape[2]
    for k in range(4):
        refs[k][...] = mixed_in[:, k * width : (k + 1) * width]
    refs[4][...] = up_in[...]
    refs[5][...] = down_in[...]
    for k, ref in enumerate(refs[6:]):
        ref[...] = small_in[k, : ref.shape[0]]


def leave_call(d_x, mixed, up, down, small):
    depth, wide_ = mixed.shape
    f32 = jnp.float32
    outs = [jax.ShapeDtypeStruct(d_x.shape, d_x.dtype)]
    outs += [jax.ShapeDtypeStruct((depth, wide_ // 4), f32)] * 4
    outs += [jax.ShapeDtypeStruct(up.shape, f32), jax.ShapeDtypeStruct(down.shape, f32)]
    outs += [jax.ShapeDtypeStruct((depth,), f32)] * 8
    outs += [jax.ShapeDtypeStruct((down.shape[0],), f32)]
    near = pl.BlockSpec(memory_space=pltpu.VMEM)
    return pl.pallas_call(
        leave_kernel,
        out_shape=tuple(outs),
        in_specs=[near] * 5,
        out_specs=(near,) * len(outs),
        name="leave",
    )(d_x, mixed, up, down, small)


def cut(axis, start, size):
    return (axis, start, size)


def lanes_of(shape, low):
    lane = lax.broadcasted_iota(jnp.int32, shape, len(shape) - 1)
    if isinstance(low, bool):
        return lane < HD if low else lane >= HD
    return lane // HD == jnp.where(low, 0, 1)


def dot(left_side, right_side, contract=((1,), (0,))):
    return lax.dot_general(
        left_side, right_side, (contract, ((), ())), preferred_element_type=jnp.float32
    )


ROWS = ((1,), (1,))
COLS = ((0,), (0,))


def halves(array, col):
    return array[:, col : col + HD]


def listed_rows(table_ref, blocks, per, m, n, j):
    shard = table_ref[2 * blocks * per * RAND + 2 * GLOB]
    total = table_ref[2 * blocks * per * RAND + 2 * GLOB + 1]
    here = shard * blocks + n
    rows = [jnp.maximum(here - 1, 0), here, jnp.minimum(here + 1, total - 1)]
    for r in range(RAND):
        rows.append(table_ref[((m * blocks + n) * per + j) * RAND + r])
    for g in range(GLOB):
        rows.append(table_ref[2 * blocks * per * RAND + m * GLOB + g])
    return rows, here, total


def global_of(table_ref, blocks, per, at):
    base = 2 * blocks * per * RAND
    return table_ref[base + at], table_ref[base + 2 * GLOB]


def outside(here, total, listed):
    lane = lax.broadcasted_iota(jnp.int32, (1, listed * BLOCK), 1)
    before = jnp.logical_and(lane < BLOCK, here == 0)
    after = jnp.logical_and(
        jnp.logical_and(lane >= 2 * BLOCK, lane < 3 * BLOCK), here == total - 1
    )
    return jnp.where(jnp.logical_or(before, after), -jnp.inf, 0.0)


def only(value, low):
    return jnp.where(lanes_of(value.shape, low), value, jnp.zeros_like(value))


def attend_kernel(table_ref, q_ref, kv_ref, out_ref, lse_ref):
    places_, per, in_place, block, _ = q_ref.shape
    blocks = places_ * in_place
    scale = jnp.bfloat16(HD ** (-0.5))
    units = [(j, m) for j in range(per) for m in range(2)]

    def query_block(n, carry):
        kvs, scores = [], []
        for j, m in units:
            rows, here, total = listed_rows(table_ref, blocks, per, m, n, j)
            kvs.append(
                jnp.concatenate(
                    [kv_ref[r // in_place, m * per + j, r % in_place] for r in rows], axis=0
                )
            )
            q = only(q_ref[n // in_place, j, n % in_place], m == 0) * scale
            scores.append(dot(q, kvs[-1], ROWS) + outside(here, total, len(rows)))
        raised = []
        for (j, m), score in zip(units, scores):
            top = jnp.max(score, axis=1, keepdims=True)
            raised.append(jnp.exp(score - top))
            total_sum = jnp.sum(raised[-1], axis=1, keepdims=True)
            raised[-1] = raised[-1] * (1.0 / total_sum)
            lse_ref[n // in_place, j, m, n % in_place] = jnp.broadcast_to(
                top + jnp.log(total_sum), (block, 2 * HD)
            )
        outs = [dot(r.astype(jnp.bfloat16), kv) for r, kv in zip(raised, kvs)]
        for j in range(per):
            out_ref[n // in_place, j, n % in_place] = jnp.where(
                lanes_of(outs[0].shape, True), outs[2 * j + 1], outs[2 * j]
            ).astype(jnp.bfloat16)
        return carry

    lax.fori_loop(0, blocks, query_block, 0)
    step = 8
    heads = range(per)

    def global_rows(at, carry):
        m = at // GLOB
        row, shard = global_of(table_ref, blocks, per, at)
        local = row % blocks
        at_place, at_row = local // in_place, local % in_place

        @pl.when(row // blocks == shard)
        def _():
            def keys(j, spot):
                return kv_ref[pl.ds(spot, step), m * per + j].reshape(
                    step * in_place * block, 2 * HD
                )

            spots = range(0, kv_ref.shape[0], step)
            qs = [only(q_ref[at_place, j, at_row], m == 0) * scale for j in heads]
            scores = [[dot(qs[j], keys(j, spot), ROWS) for spot in spots] for j in heads]
            raised, sums = [], []
            for j in heads:
                top = scores[j][0].max(axis=1, keepdims=True)
                for s in scores[j][1:]:
                    top = jnp.maximum(top, s.max(axis=1, keepdims=True))
                raised.append([jnp.exp(s - top) for s in scores[j]])
                sums.append(sum(jnp.sum(r, axis=1, keepdims=True) for r in raised[j]))
                lse_ref[at_place, j, m, at_row] = jnp.broadcast_to(
                    top + jnp.log(sums[j]), (block, 2 * HD)
                )
            for j in heads:
                out = sum(
                    dot(r.astype(jnp.bfloat16), keys(j, spot)) for r, spot in zip(raised[j], spots)
                )
                old = out_ref[at_place, j, at_row]
                out_ref[at_place, j, at_row] = jnp.where(
                    lanes_of(old.shape, m == 1), (out / sums[j]).astype(jnp.bfloat16), old
                )

        return carry

    lax.fori_loop(0, 2 * GLOB, global_rows, 0)


def attend_call(table, q, kv):
    spec = pl.BlockSpec(memory_space=pltpu.VMEM)
    places_, per, in_place, block, lanes = q.shape
    return pl.pallas_call(
        attend_kernel,
        out_shape=(
            jax.ShapeDtypeStruct(q.shape, jnp.bfloat16),
            jax.ShapeDtypeStruct((places_, per, 2, in_place, block, lanes), jnp.float32),
        ),
        in_specs=[pl.BlockSpec(memory_space=pltpu.SMEM), spec, spec],
        out_specs=(spec, spec),
        compiler_params=pltpu.CompilerParams(vmem_limit_bytes=56 * 2**20),
        name="attend",
    )(table, q, kv)


def attend_back_kernel(
    table_ref, q_ref, kv_in, d_ref, out_ref, lse_ref, dq_ref, dkv_out, total_ref, kv_ref, in_sem, out_sem
):
    places_, per, in_place, block, _ = q_ref.shape
    blocks = places_ * in_place
    scale = jnp.bfloat16(HD ** (-0.5))
    units = [(j, m) for j in range(per) for m in range(2)]

    step = 8
    fetch = pltpu.make_async_copy(kv_in, kv_ref, in_sem)
    fetch.start()

    def clear(i, carry):
        total_ref[i] = jnp.zeros(total_ref.shape[1:], jnp.float32)
        return carry

    lax.fori_loop(0, total_ref.shape[0], clear, 0)
    fetch.wait()

    def pair_of(n, j, m, keep):
        at = (n // in_place, j, n % in_place)
        q = only(q_ref[at], m == 0) * scale
        d = only(d_ref[at], m == 1)
        if keep is not None:
            d = d * keep
        delta = jnp.sum(
            d.astype(jnp.float32) * out_ref[at].astype(jnp.float32), axis=1, keepdims=True
        )
        return jnp.concatenate([q, d], axis=0), delta

    def wide(column, width):
        return jnp.concatenate([column] * (width // column.shape[1]), axis=1)

    def query_block(n, carry):
        listed, kvs, pairs, deltas, boths = [], [], [], [], []
        for j, m in units:
            rows, here, total = listed_rows(table_ref, blocks, per, m, n, j)
            is_global = jnp.logical_or(here == rows[-1], here == rows[-2])
            keep = jnp.where(is_global, 0.0, 1.0).astype(jnp.bfloat16)
            kv = jnp.concatenate(
                [kv_ref[r // in_place, m * per + j, r % in_place] for r in rows], axis=0
            )
            pair, delta = pair_of(n, j, m, keep)
            listed.append(rows)
            kvs.append(kv)
            pairs.append(pair)
            deltas.append(delta)
            boths.append(dot(pair, kv, ROWS))
        weights = []
        for (j, m), both, delta, kv, rows in zip(units, boths, deltas, kvs, listed):
            width = both.shape[1]
            lse = lse_ref[n // in_place, j, m, n % in_place]
            scores = both[:block] + outside(here, total, len(rows))
            probs = jnp.exp(scores - wide(lse, width))
            d_scores = probs * (both[block:] - delta)
            weights.append(
                jnp.concatenate(
                    [d_scores.astype(jnp.bfloat16), probs.astype(jnp.bfloat16)], axis=0
                )
            )
        outs = []
        for (j, m), weight, pair, kv, rows in zip(units, weights, pairs, kvs, listed):
            d_kv = dot(weight, pair, COLS)
            for at, r in enumerate(rows):
                total_ref[r // in_place, m * per + j, r % in_place] += d_kv[
                    at * block : (at + 1) * block
                ]
            outs.append(dot(weight[:block], kv) * HD ** (-0.5))
        for j in range(per):
            dq_ref[n // in_place, j, n % in_place] = jnp.where(
                lanes_of(outs[0].shape, True), outs[2 * j], outs[2 * j + 1]
            ).astype(jnp.bfloat16)
        return carry

    lax.fori_loop(0, blocks, query_block, 0)

    heads = range(per)

    def global_rows(at, carry):
        m = at // GLOB
        row, shard = global_of(table_ref, blocks, per, at)
        local = row % blocks
        at_place, at_row = local // in_place, local % in_place

        @pl.when(row // blocks == shard)
        def _():
            pairs = [pair_of(local, j, m, None) for j in heads]

            def some_keys(spot, d_qs):
                at_keys = pl.ds(spot * step, step)
                kvs = [
                    kv_ref[at_keys, m * per + j].reshape(step * in_place * block, 2 * HD)
                    for j in heads
                ]
                boths = [dot(pairs[j][0], kvs[j], ROWS) for j in heads]
                weights = []
                for j in heads:
                    lse = lse_ref[at_place, j, m, at_row]
                    probs = jnp.exp(boths[j][:block] - wide(lse, boths[j].shape[1]))
                    d_scores = probs * (boths[j][block:] - pairs[j][1])
                    weights.append(
                        jnp.concatenate(
                            [d_scores.astype(jnp.bfloat16), probs.astype(jnp.bfloat16)], axis=0
                        )
                    )
                for j in heads:
                    total_ref[at_keys, m * per + j] += dot(weights[j], pairs[j][0], COLS).reshape(
                        step, in_place, block, 2 * HD
                    )
                return tuple(d_qs[j] + dot(weights[j][:block], kvs[j]) for j in heads)

            d_qs = lax.fori_loop(
                0,
                kv_ref.shape[0] // step,
                some_keys,
                tuple(jnp.zeros((block, 2 * HD), jnp.float32) for _ in heads),
            )
            for j in heads:
                old = dq_ref[at_place, j, at_row]
                dq_ref[at_place, j, at_row] = jnp.where(
                    lanes_of(old.shape, m == 0), (d_qs[j] * HD ** (-0.5)).astype(jnp.bfloat16), old
                )

        return carry

    lax.fori_loop(0, 2 * GLOB, global_rows, 0)

    def give(i, carry):
        kv_ref[i] = total_ref[i].astype(jnp.bfloat16)
        return carry

    gives = []
    for at, s in enumerate(range(0, total_ref.shape[0], step)):
        lax.fori_loop(s, s + step, give, 0)
        gives.append(
            pltpu.make_async_copy(
                kv_ref.at[pl.ds(s, step)], dkv_out.at[pl.ds(s, step)], out_sem.at[at]
            )
        )
        gives[-1].start()
    for copy in gives:
        copy.wait()


def attend_back_call(table, q, kv, d, out, lse):
    spec = pl.BlockSpec(memory_space=pltpu.VMEM)
    far = pl.BlockSpec(memory_space=pl.ANY)
    return pl.pallas_call(
        attend_back_kernel,
        out_shape=(
            jax.ShapeDtypeStruct(q.shape, jnp.bfloat16),
            jax.ShapeDtypeStruct(kv.shape, jnp.bfloat16),
        ),
        in_specs=[pl.BlockSpec(memory_space=pltpu.SMEM), spec, far, spec, spec, spec],
        out_specs=(spec, far),
        scratch_shapes=[
            pltpu.VMEM(kv.shape, jnp.float32),
            pltpu.VMEM(kv.shape, jnp.bfloat16),
            pltpu.SemaphoreType.DMA,
            pltpu.SemaphoreType.DMA((kv.shape[0] // 8,)),
        ],
        compiler_params=pltpu.CompilerParams(vmem_limit_bytes=60 * 2**20),
        name="attend_back",
    )(table, q, kv, d, out, lse)


def centre(values):
    center = jnp.mean(values, axis=1, keepdims=True)
    centred = values - center
    spread = jnp.mean(centred * centred, axis=1, keepdims=True)
    inverse = lax.rsqrt(spread + 1e-12)
    return centred * inverse, inverse


def centre_back(hat, inverse, grad):
    return inverse * (
        grad
        - jnp.mean(grad, axis=1, keepdims=True)
        - hat * jnp.mean(grad * hat, axis=1, keepdims=True)
    )


def rows_sum(values):
    return jnp.sum(values, axis=0, keepdims=True)


def dense_kernel(
    c_ref, x_ref, cot_ref, wo_in, up_in, down_in, vec_ref, up_bias_ref,
    out_ref, d_mix_ref, d_c_ref, g_out_ref, g_up_out, g_down_out, g_vec_ref, g_up_bias_ref,
    ctx, first, hat, low, low_t, act, slope, ffn, wo_ref, up_ref, down_ref, g_up_ref, g_down_ref, in_sem, out_sem,
):
    groups, per, rows, _ = c_ref.shape
    width = x_ref.shape[2]
    ff = up_ref.shape[1]
    chunk = 384
    fetches = [
        pltpu.make_async_copy(wo_in.at[:, pl.ds(3 * width, width)], wo_ref, in_sem.at[0]),
        pltpu.make_async_copy(up_in, up_ref, in_sem.at[1]),
        pltpu.make_async_copy(down_in, down_ref, in_sem.at[2]),
    ]
    for copy in fetches:
        copy.start()
    out_bias, attn_gain, attn_shift, down_bias, ffn_gain, ffn_shift = (
        vec_ref[k : k + 1, :] for k in range(2, 8)
    )
    for p in range(HEADS // 2):
        one = c_ref[(2 * p) // per, (2 * p) % per]
        two = c_ref[(2 * p + 1) // per, (2 * p + 1) % per]
        at = pl.ds(p * 2 * HD, 2 * HD)
        ctx[:rows, at] = jnp.concatenate([one[:, HD:], two[:, HD:]], axis=1)
        ctx[rows:, at] = jnp.concatenate([one[:, :HD], two[:, :HD]], axis=1)
    tokens = x_ref[...].reshape(2 * rows, width).astype(jnp.float32)
    fetches[0].wait()
    hat_first, inverse_first = centre(tokens + dot(ctx[...], wo_ref[...]) + out_bias)
    hat[...] = hat_first
    first[...] = hat_first * attn_gain + attn_shift
    low[...] = first[...].astype(jnp.bfloat16)
    low_t[...] = first[...].T.astype(jnp.bfloat16)
    ffn[...] = first[...] + down_bias
    fetches[1].wait()
    fetches[2].wait()

    def forward(i, carry):
        at = pl.ds(pl.multiple_of(i * chunk, chunk), chunk)
        hidden = dot(low[...], up_ref[:, at]) + up_bias_ref[:, at]
        share = 0.5 * (1.0 + lax.erf(hidden * 0.7071067811865476))
        bell = jnp.exp(-0.5 * hidden * hidden) * 0.3989422804014327
        slope[:, at] = share + hidden * bell
        act_low = (hidden * share).astype(jnp.bfloat16)
        act[:, at] = act_low
        ffn[...] += dot(act_low, down_ref[at, :])
        return carry

    lax.fori_loop(0, ff // chunk, forward, 0)
    hat_second, inverse_second = centre(ffn[...])
    out_ref[...] = (
        (hat_second * ffn_gain + ffn_shift).astype(jnp.bfloat16).reshape(2, rows, width)
    )
    cot = cot_ref[...].reshape(2 * rows, width).astype(jnp.float32)
    g_vec_ref[4:5, :] = rows_sum(cot * hat_second)
    g_vec_ref[5:6, :] = rows_sum(cot)
    d_second = centre_back(hat_second, inverse_second, cot * ffn_gain)
    d_ffn = d_second.astype(jnp.bfloat16)
    g_vec_ref[3:4, :] = rows_sum(d_ffn.astype(jnp.float32))
    ffn[...] = d_second

    def leave(i):
        at = pl.ds(pl.multiple_of(i * chunk, chunk), chunk)
        return (
            pltpu.make_async_copy(g_up_ref.at[:, at], g_up_out.at[:, at], out_sem.at[0, i]),
            pltpu.make_async_copy(g_down_ref.at[at, :], g_down_out.at[at, :], out_sem.at[1, i]),
        )

    def backward(i, carry):
        at = pl.ds(pl.multiple_of(i * chunk, chunk), chunk)
        d_act = dot(d_ffn, down_ref[at, :], ROWS)
        d_hidden = (d_act * slope[:, at]).astype(jnp.bfloat16)
        g_up_bias_ref[:, at] = rows_sum(d_hidden.astype(jnp.float32))
        g_down_ref[at, :] = dot(act[:, at], d_ffn, COLS).astype(jnp.bfloat16)
        g_up_ref[:, at] = dot(low_t[...], d_hidden).astype(jnp.bfloat16)
        for copy in leave(i):
            copy.start()
        ffn[...] += dot(d_hidden, up_ref[:, at], ROWS)
        return carry

    lax.fori_loop(0, ff // chunk, backward, 0)
    d_first = ffn[...]
    g_vec_ref[1:2, :] = rows_sum(d_first * hat[...])
    g_vec_ref[2:3, :] = rows_sum(d_first)
    d_mix = centre_back(hat[...], inverse_first, d_first * attn_gain)
    d_mix_ref[...] = d_mix
    d_branch = d_mix.astype(jnp.bfloat16)
    g_vec_ref[0:1, :] = rows_sum(d_branch.astype(jnp.float32))
    g_vec_ref[6:8, :] = jnp.zeros((2, width), jnp.float32)
    g_out_ref[...] = dot(ctx[...], d_branch, COLS).astype(jnp.bfloat16)
    d_ctx = dot(d_branch, wo_ref[...], ROWS).astype(jnp.bfloat16)
    for head in range(HEADS):
        d_c_ref[head // per, head % per] = jnp.concatenate(
            [halves(d_ctx[rows:], head * HD), halves(d_ctx[:rows], head * HD)], axis=1
        )
    for i in range(ff // chunk):
        for copy in leave(i):
            copy.wait()


def dense_call(c, tokens, cot, mixed, up, down, vec, up_bias):
    micro, rows, width = tokens.shape
    ff = up.shape[1]
    both = micro * rows
    far = pl.BlockSpec(memory_space=pl.ANY)
    f32, bf16 = jnp.float32, jnp.bfloat16

    def full(shape):
        return pl.BlockSpec(memory_space=pltpu.VMEM)

    outs = (
        jax.ShapeDtypeStruct(tokens.shape, bf16),
        jax.ShapeDtypeStruct((both, width), f32),
        jax.ShapeDtypeStruct(c.shape, bf16),
        jax.ShapeDtypeStruct((width, width), bf16),
        jax.ShapeDtypeStruct((width, ff), bf16),
        jax.ShapeDtypeStruct((ff, width), bf16),
        jax.ShapeDtypeStruct((8, width), f32),
        jax.ShapeDtypeStruct((1, ff), f32),
    )
    return pl.pallas_call(
        dense_kernel,
        out_shape=outs,
        in_specs=[
            full(c.shape),
            full(tokens.shape),
            full(cot.shape),
            far,
            far,
            far,
            full(vec.shape),
            full(up_bias.shape),
        ],
        out_specs=tuple(far if k in (4, 5) else full(o.shape) for k, o in enumerate(outs)),
        scratch_shapes=[
            pltpu.VMEM((both, width), bf16),
            pltpu.VMEM((both, width), f32),
            pltpu.VMEM((both, width), f32),
            pltpu.VMEM((both, width), bf16),
            pltpu.VMEM((width, both), bf16),
            pltpu.VMEM((both, ff), bf16),
            pltpu.VMEM((both, ff), f32),
            pltpu.VMEM((both, width), f32),
            pltpu.VMEM((width, width), bf16),
            pltpu.VMEM((width, ff), bf16),
            pltpu.VMEM((ff, width), bf16),
            pltpu.VMEM((width, ff), bf16),
            pltpu.VMEM((ff, width), bf16),
            pltpu.SemaphoreType.DMA((3,)),
            pltpu.SemaphoreType.DMA((2, ff // 384)),
        ],
        compiler_params=pltpu.CompilerParams(vmem_limit_bytes=60 * 2**20),
        name="dense",
    )(c, tokens, cot, mixed, up, down, vec, up_bias)


def near_body(inputs, cotangent, random_blocks, global_blocks, *shards):
    (
        query_weight, query_bias, key_weight, value_weight, value_bias, out_weight, out_bias, attn_gain,
        attn_shift, up_weight, up_bias, down_weight, down_bias, ffn_gain, ffn_shift,
    ) = shards
    groups = lax.axis_size("head")
    shard_count = lax.axis_size("blk")
    devices = groups * shard_count
    shard = lax.axis_index("blk")
    group = lax.axis_index("head")
    micro, rows, width = inputs.shape
    depth = query_weight.shape[0]
    ff = up_weight.shape[1]
    per = HEADS // groups
    in_place = rows // BLOCK
    blocks = groups * in_place
    q, kv, up, down, mixed, vec, up_bias_row = front_call(
        inputs,
        (query_weight, key_weight, value_weight, out_weight),
        up_weight,
        down_weight,
        (
            query_bias, value_bias, out_bias, attn_gain, attn_shift, down_bias, ffn_gain, ffn_shift, up_bias,
        ),
        1,
    )
    up = up.reshape(width, ff)
    down = down.reshape(ff, width)
    mine = lax.dynamic_slice(
        random_blocks,
        (0, shard * blocks, group * per, 0),
        (micro, blocks, per, RAND),
    )
    table = jnp.concatenate(
        [
            mine.reshape(-1),
            global_blocks.reshape(-1),
            jnp.stack([shard, shard_count * blocks]).astype(jnp.int32),
        ]
    )
    split = (in_place, BLOCK, 2 * HD)
    q = q.reshape((groups, per) + split)
    kv = kv.reshape((devices, 2 * per) + split)
    packed = (groups, per, rows, 2 * HD)
    attended, lse = attend_call(table, q, kv)
    context = swap_call(attended.reshape(packed), 3)
    layer_out, d_mix, d_context, g_out, g_up, g_down, g_vec, g_up_bias = dense_call(
        context, inputs, cotangent, mixed, up, down, vec, up_bias_row
    )
    d_context = swap_call(d_context, 4)
    d_q, d_kv = attend_back_call(table, q, kv, d_context.reshape(q.shape), attended, lse)
    results = back_call(
        d_q.reshape(packed),
        d_kv.reshape(devices, 2 * per, rows, 2 * HD),
        g_up.reshape(devices, depth, ff),
        g_down.reshape(devices, -1, width),
        inputs,
        mixed,
        d_mix,
        g_out,
        g_vec,
        g_up_bias,
        5,
    )
    (
        input_grad, grad_query, grad_key, grad_value, grad_out, grad_up, grad_down, *vector, grad_up_bias,
    ) = leave_call(*results)
    return (
        layer_out, input_grad, grad_query, vector[0], grad_key, grad_value, vector[1], grad_out,
        vector[2], vector[3], vector[4], grad_up, grad_up_bias, grad_down, vector[5], vector[6], vector[7],
    )


def with_halo(cells, sides, width):
    for axis, dim in sides:
        count = lax.axis_size(axis)
        ends = count - 1
        head = lax.slice_in_dim(cells, 0, width, axis=dim)
        tail = lax.slice_in_dim(cells, cells.shape[dim] - width, cells.shape[dim], axis=dim)
        cells = jnp.concatenate(
            [
                lax.ppermute(tail, axis, [(i, (i + 1) % count) for i in range(ends)]),
                cells,
                lax.ppermute(head, axis, [((i + 1) % count, i) for i in range(ends)]),
            ],
            axis=dim,
        )
    return cells


def combined_all(part, axis, combine):
    gathered = jax.tree.map(lambda a: lax.all_gather(a, axis), part)

    def take(source):
        return jax.tree.map(lambda a: lax.dynamic_index_in_dim(a, source, 0, False), gathered)

    return lax.fori_loop(
        1, lax.axis_size(axis), lambda source, state: combine(state, take(source)), take(0)
    )


def taken(table, rows):
    return lax.map(lambda row: lax.dynamic_index_in_dim(table, row, 0, False), rows)


def layer_norm(values, norm_gain, norm_shift):
    center = jnp.mean(values, axis=-1, keepdims=True)
    centred = values - center
    spread = jnp.mean(centred * centred, axis=-1, keepdims=True)
    return centred * lax.rsqrt(spread + 1e-12) * norm_gain + norm_shift


def gelu_exact(values):
    return jax.nn.gelu(values, approximate=False)


def matmul(left_side, right_side):
    return jnp.dot(left_side, right_side, preferred_element_type=jnp.float32)


def matmul_left(left_side, right_side):
    return lax.dot_general(
        left_side, right_side, (((0,), (0,)), ((), ())), preferred_element_type=jnp.float32
    )


def matmul_right(left_side, right_side):
    return lax.dot_general(
        left_side, right_side, (((1,), (1,)), ((), ())), preferred_element_type=jnp.float32
    )


def column_sum(values):
    return jnp.sum(values.astype(jnp.float32), axis=0)


def combine_parts(earlier, later_part):
    joint_top = jnp.maximum(earlier[0], later_part[0])
    first_factor = jnp.exp(earlier[0] - joint_top)
    second_factor = jnp.exp(later_part[0] - joint_top)
    return (
        joint_top,
        earlier[1] * first_factor + later_part[1] * second_factor,
        earlier[2] * first_factor[..., None] + later_part[2] * second_factor[..., None],
    )


def fetch_weights(
    query_weight,
    query_bias,
    key_weight,
    value_weight,
    value_bias,
    out_weight,
    out_bias,
    attn_gain,
    attn_shift,
    up_weight,
    up_bias,
    down_weight,
    down_bias,
    ffn_gain,
    ffn_shift,
):
    return (
        lax.all_gather(query_weight, ("blk", "head"), axis=0, tiled=True),
        lax.all_gather(query_bias, ("blk", "head"), axis=0, tiled=True),
        lax.all_gather(key_weight, ("blk", "head"), axis=0, tiled=True),
        lax.all_gather(value_weight, ("blk", "head"), axis=0, tiled=True),
        lax.all_gather(value_bias, ("blk", "head"), axis=0, tiled=True),
        lax.all_gather(out_weight, ("blk", "head"), axis=0, tiled=True),
        lax.all_gather(out_bias, ("blk", "head"), axis=0, tiled=True),
        lax.all_gather(attn_gain, ("blk", "head"), axis=0, tiled=True),
        lax.all_gather(attn_shift, ("blk", "head"), axis=0, tiled=True),
        lax.all_gather(up_weight, ("blk", "head"), axis=0, tiled=True),
        lax.all_gather(up_bias, ("blk", "head"), axis=0, tiled=True),
        lax.all_gather(down_weight, ("blk", "head"), axis=0, tiled=True),
        lax.all_gather(down_bias, ("blk", "head"), axis=0, tiled=True),
        lax.all_gather(ffn_gain, ("blk", "head"), axis=0, tiled=True),
        lax.all_gather(ffn_shift, ("blk", "head"), axis=0, tiled=True),
    )


def reduce_grads(totals):
    return (
        lax.psum_scatter(totals[0], ("blk", "head"), scatter_dimension=0, tiled=True),
        lax.psum_scatter(totals[1], ("blk", "head"), scatter_dimension=0, tiled=True),
        lax.psum_scatter(totals[2], ("blk", "head"), scatter_dimension=0, tiled=True),
        lax.psum_scatter(totals[3], ("blk", "head"), scatter_dimension=0, tiled=True),
        lax.psum_scatter(totals[4], ("blk", "head"), scatter_dimension=0, tiled=True),
        lax.psum_scatter(totals[5], ("blk", "head"), scatter_dimension=0, tiled=True),
        lax.psum_scatter(totals[6], ("blk", "head"), scatter_dimension=0, tiled=True),
        lax.psum_scatter(totals[7], ("blk", "head"), scatter_dimension=0, tiled=True),
        lax.psum_scatter(totals[8], ("blk", "head"), scatter_dimension=0, tiled=True),
        lax.psum_scatter(totals[9], ("blk", "head"), scatter_dimension=0, tiled=True),
        lax.psum_scatter(totals[10], ("blk", "head"), scatter_dimension=0, tiled=True),
        lax.psum_scatter(totals[11], ("blk", "head"), scatter_dimension=0, tiled=True),
        lax.psum_scatter(totals[12], ("blk", "head"), scatter_dimension=0, tiled=True),
        lax.psum_scatter(totals[13], ("blk", "head"), scatter_dimension=0, tiled=True),
        lax.psum_scatter(totals[14], ("blk", "head"), scatter_dimension=0, tiled=True),
    )


def sparse_forward(packed):
    group_queries, group_keys, group_values, group_allowed = packed
    attn_scale = HD ** (-0.5)
    scores = (
        jnp.einsum("gqhd,ghkd->ghqk", group_queries, group_keys, preferred_element_type=jnp.float32)
        * attn_scale
    )
    scores = jnp.where(group_allowed[:, None, None, :], scores, -jnp.inf)
    row_top = jnp.max(scores, axis=-1, keepdims=True)
    raised = jnp.exp(scores - row_top)
    row_total = jnp.sum(raised, axis=-1, keepdims=True)
    probs_low = (raised / row_total).astype(jnp.bfloat16)
    output = jnp.einsum(
        "ghqk,ghkd->gqhd", probs_low, group_values, preferred_element_type=jnp.float32
    )
    return (output, (row_top + jnp.log(row_total))[..., 0])


def sparse_backward(nearby, carried, packed):
    group_queries, group_keys, group_values, group_allowed, group_lse, group_grad = packed
    attn_scale = HD ** (-0.5)
    per_group = group_queries.shape[0]
    heads_dev = group_queries.shape[2]
    scores = (
        jnp.einsum("gqhd,ghkd->ghqk", group_queries, group_keys, preferred_element_type=jnp.float32)
        * attn_scale
    )
    scores = jnp.where(group_allowed[:, None, None, :], scores, -jnp.inf)
    probs = jnp.exp(scores - group_lse[..., None])
    d_probs = jnp.einsum(
        "gqhd,ghkd->ghqk", group_grad, group_values, preferred_element_type=jnp.float32
    )
    row_delta = jnp.sum(probs * d_probs, axis=-1, keepdims=True)
    d_scores = (probs * (d_probs - row_delta)).astype(jnp.bfloat16)
    d_queries = (
        jnp.einsum("ghqk,ghkd->gqhd", d_scores, group_keys, preferred_element_type=jnp.float32)
        * attn_scale
    )
    d_keys = (
        jnp.einsum("ghqk,gqhd->ghkd", d_scores, group_queries, preferred_element_type=jnp.float32)
        * attn_scale
    )
    d_values = jnp.einsum(
        "ghqk,gqhd->ghkd",
        probs.astype(jnp.bfloat16),
        group_grad,
        preferred_element_type=jnp.float32,
    )
    d_keys = d_keys.reshape(per_group, heads_dev, -1, BLOCK, HD)
    d_values = d_values.reshape(per_group, heads_dev, -1, BLOCK, HD)
    carried = (
        carried[0] + jnp.sum(d_keys[:, :, nearby:], axis=0),
        carried[1] + jnp.sum(d_values[:, :, nearby:], axis=0),
    )
    return (carried, (d_queries, d_keys[:, :, :nearby], d_values[:, :, :nearby]))


def micro_batch(tokens, cotangent_rows, random_rows, global_rows, weights):
    (
        full_query,
        full_query_bias,
        full_key,
        full_value,
        full_value_bias,
        full_out,
        full_out_bias,
        full_attn_gain,
        full_attn_shift,
        full_up,
        full_up_bias,
        full_down,
        full_down_bias,
        full_ffn_gain,
        full_ffn_shift,
    ) = weights
    attn_scale = HD ** (-0.5)
    shards = lax.axis_size("blk")
    head_groups = lax.axis_size("head")
    shard_index = lax.axis_index("blk")
    group_index = lax.axis_index("head")
    heads_dev = HEADS // head_groups
    group_width = heads_dev * HD
    listed = 3 + RAND + GLOB
    nearby = 3 + RAND
    projected = jnp.stack(
        [
            matmul(tokens, full_query) + full_query_bias,
            matmul(tokens, full_key),
            matmul(tokens, full_value) + full_value_bias,
        ]
    ).astype(jnp.bfloat16)
    by_head = lax.all_to_all(projected, "head", split_axis=2, concat_axis=1, tiled=True)
    row_count = by_head.shape[1]
    block_count = row_count // BLOCK
    blocks_all = block_count * shards
    key_rows = by_head[1]
    value_rows = by_head[2]
    padded = with_halo(by_head[1:3], (("blk", 1),), BLOCK)
    extended = padded.reshape(2, block_count + 2, BLOCK, heads_dev, HD).transpose(0, 1, 3, 2, 4)
    window = jnp.stack([extended[:, offset : offset + block_count] for offset in range(3)], axis=3)
    block_ids = shard_index * block_count + jnp.arange(block_count, dtype=jnp.int32)
    neighbour = block_ids[:, None] + jnp.arange(-1, 2, dtype=jnp.int32)[None, :]
    inside = (neighbour >= 0) & (neighbour < blocks_all)
    head_table = lax.dynamic_slice_in_dim(random_rows, group_index * heads_dev, heads_dev, 1)
    requests = block_count * heads_dev * RAND
    all_requests = head_table.reshape(shards, requests)
    capacity = (requests + shards - 1) // shards + 1
    wanted = lax.dynamic_slice_in_dim(all_requests, shard_index, 1, 0)[0]
    source = wanted // block_count
    place = jnp.arange(requests, dtype=jnp.int32)
    earlier = (place[:, None] > place[None, :]).astype(jnp.int32)
    same_source = (source[:, None] == source[None, :]).astype(jnp.int32)
    slot_index = jnp.sum(earlier * same_source, axis=1)
    mine_mask = (all_requests // block_count == shard_index).astype(jnp.int32)
    send_order = jnp.sum(earlier[None] * mine_mask[:, None, :], axis=2)
    match_mask = mine_mask[:, :, None] * (
        send_order[:, :, None] == jnp.arange(capacity, dtype=jnp.int32)[None, None, :]
    ).astype(jnp.int32)
    head_of = jnp.arange(requests, dtype=jnp.int32) // RAND % heads_dev
    row_of = all_requests % block_count * heads_dev + head_of[None, :]
    send_rows = jnp.sum(match_mask * row_of[:, :, None], axis=1)
    filled = jnp.sum(match_mask, axis=1).astype(jnp.float32)
    block_table = (
        by_head[1:3]
        .reshape(2, block_count, BLOCK, heads_dev, HD)
        .transpose(1, 3, 0, 2, 4)
        .reshape(block_count * heads_dev, 2, BLOCK, HD)
    )
    outgoing = taken(block_table, send_rows.reshape(-1))
    incoming = lax.all_to_all(outgoing, "blk", split_axis=0, concat_axis=0, tiled=True)
    fetched = taken(incoming, source * capacity + slot_index).reshape(
        block_count, heads_dev, RAND, 2, BLOCK, HD
    )
    owner_shard = global_rows // block_count
    present = owner_shard == shard_index
    local_block = global_rows % block_count
    own_rows = jnp.stack(
        [
            lax.dynamic_index_in_dim(
                by_head.reshape(3, block_count, BLOCK, group_width), local_block[g], 1, False
            )
            for g in range(GLOB)
        ],
        axis=1,
    )
    shared = lax.psum(
        jnp.where(present[None, :, None, None], own_rows.astype(jnp.float32), 0.0), "blk"
    ).astype(jnp.bfloat16)
    shared_pairs = shared[1:3].reshape(2, GLOB, BLOCK, heads_dev, HD).transpose(0, 3, 1, 2, 4)

    def listed_blocks(which):
        near_part = window[which]
        random_part = fetched[:, :, :, which]
        global_part = jnp.broadcast_to(
            shared_pairs[which][None], (block_count, heads_dev, GLOB, BLOCK, HD)
        )
        return jnp.concatenate([near_part, random_part, global_part], axis=2).reshape(
            block_count, heads_dev, listed * BLOCK, HD
        )

    per_group = min(8, block_count)
    group_count = block_count // per_group
    query_groups = by_head[0].reshape(group_count, per_group, BLOCK, heads_dev, HD)
    key_groups = listed_blocks(0).reshape(group_count, per_group, heads_dev, listed * BLOCK, HD)
    value_groups = listed_blocks(1).reshape(group_count, per_group, heads_dev, listed * BLOCK, HD)
    allowed = jnp.repeat(
        jnp.concatenate([inside, jnp.ones((block_count, RAND + GLOB), jnp.bool_)], axis=1),
        BLOCK,
        axis=1,
    )
    allow_groups = allowed.reshape(group_count, per_group, listed * BLOCK)
    sparse_out, sparse_lse = lax.map(
        sparse_forward, (query_groups, key_groups, value_groups, allow_groups)
    )
    global_queries = shared[0].reshape(GLOB, BLOCK, heads_dev, HD)
    key_heads = key_rows.reshape(row_count, heads_dev, HD)
    value_wide = value_rows.reshape(row_count, heads_dev, HD).astype(jnp.float32)
    global_scores = (
        jnp.einsum("gqhd,khd->ghqk", global_queries, key_heads, preferred_element_type=jnp.float32)
        * attn_scale
    )
    global_top = jnp.max(global_scores, axis=-1)
    global_raised = jnp.exp(global_scores - global_top[..., None])
    merged = combined_all(
        (
            global_top,
            jnp.sum(global_raised, axis=-1),
            jnp.einsum(
                "ghqk,khd->ghqd", global_raised, value_wide, precision=lax.Precision.HIGHEST
            ),
        ),
        "blk",
        combine_parts,
    )
    global_out = merged[2] / merged[1][..., None]
    global_lse = merged[0] + jnp.log(merged[1])
    global_hits = (block_ids[:, None] == global_rows[None, :]).astype(jnp.float32)
    is_global = jnp.sum(global_hits, axis=1) > 0
    replaced = jnp.einsum("ng,ghqd->nqhd", global_hits, global_out, precision=lax.Precision.HIGHEST)
    context = jnp.where(
        is_global[:, None, None, None],
        replaced,
        sparse_out.reshape(block_count, BLOCK, heads_dev, HD),
    )
    context_rows = context.reshape(row_count, group_width).astype(jnp.bfloat16)
    context_tokens = lax.all_to_all(context_rows, "head", split_axis=0, concat_axis=1, tiled=True)
    branch = matmul(context_tokens, full_out) + full_out_bias
    first_in = tokens.astype(jnp.float32) + branch
    first_norm, first_pull = jax.vjp(
        layer_norm,
        first_in,
        full_attn_gain.astype(jnp.float32),
        full_attn_shift.astype(jnp.float32),
    )
    first_low = first_norm.astype(jnp.bfloat16)
    hidden = matmul(first_low, full_up) + full_up_bias
    act_value, gelu_pull = jax.vjp(gelu_exact, hidden)
    act_low = act_value.astype(jnp.bfloat16)
    ffn_out = matmul(act_low, full_down) + full_down_bias
    result, second_pull = jax.vjp(
        layer_norm,
        first_norm + ffn_out,
        full_ffn_gain.astype(jnp.float32),
        full_ffn_shift.astype(jnp.float32),
    )
    d_second, grad_ffn_gain, grad_ffn_shift = second_pull(cotangent_rows.astype(jnp.float32))
    d_ffn = d_second.astype(jnp.bfloat16)
    grad_down = matmul_left(act_low, d_ffn)
    grad_down_bias = column_sum(d_ffn)
    (d_hidden,) = gelu_pull(matmul_right(d_ffn, full_down))
    d_hidden_low = d_hidden.astype(jnp.bfloat16)
    grad_up = matmul_left(first_low, d_hidden_low)
    grad_up_bias = column_sum(d_hidden_low)
    d_first = d_second + matmul_right(d_hidden_low, full_up)
    d_mix, grad_attn_gain, grad_attn_shift = first_pull(d_first)
    d_branch = d_mix.astype(jnp.bfloat16)
    grad_out = matmul_left(context_tokens, d_branch)
    grad_out_bias = column_sum(d_branch)
    d_context = matmul_right(d_branch, full_out).astype(jnp.bfloat16)
    d_heads = lax.all_to_all(d_context, "head", split_axis=1, concat_axis=0, tiled=True).reshape(
        block_count, BLOCK, heads_dev, HD
    )
    d_sparse = jnp.where(is_global[:, None, None, None], jnp.zeros_like(d_heads), d_heads)
    d_global = lax.psum(
        jnp.where(
            present[:, None, None, None], taken(d_heads, local_block).astype(jnp.float32), 0.0
        ),
        "blk",
    )
    start_carry = (
        jnp.zeros((heads_dev, GLOB, BLOCK, HD), jnp.float32),
        jnp.zeros((heads_dev, GLOB, BLOCK, HD), jnp.float32),
    )
    global_sums, (d_query_parts, near_keys, near_values) = lax.scan(
        partial(sparse_backward, nearby),
        start_carry,
        (
            query_groups,
            key_groups,
            value_groups,
            allow_groups,
            sparse_lse,
            d_sparse.reshape(group_count, per_group, BLOCK, heads_dev, HD),
        ),
    )
    d_query_sparse = d_query_parts.reshape(block_count, BLOCK, heads_dev, HD)
    near_keys = near_keys.reshape(block_count, heads_dev, nearby, BLOCK, HD)
    near_values = near_values.reshape(block_count, heads_dev, nearby, BLOCK, HD)
    near_grads = jnp.stack([near_keys[:, :, :3], near_values[:, :, :3]])
    ext_grads = jnp.zeros((2, block_count + 2, heads_dev, BLOCK, HD), jnp.float32)
    for offset in range(3):
        ext_grads = ext_grads + jnp.pad(
            near_grads[:, :, :, offset], ((0, 0), (offset, 2 - offset), (0, 0), (0, 0), (0, 0))
        )
    rim_pair = jnp.stack([ext_grads[:, 0], ext_grads[:, block_count + 1]], axis=1)
    arrived = with_halo(rim_pair.astype(jnp.bfloat16), (("blk", 1),), 1).astype(rim_pair.dtype)
    inner_grads = ext_grads[:, 1 : block_count + 1]
    inner_grads = inner_grads.at[:, 0].add(arrived[:, 0]).at[:, block_count - 1].add(arrived[:, 3])
    far_grads = jnp.stack([near_keys[:, :, 3:], near_values[:, :, 3:]], axis=3).reshape(
        requests, 2, BLOCK, HD
    )
    outbox = (
        jnp.zeros((shards, capacity, 2, BLOCK, HD), jnp.float32)
        .at[source, slot_index]
        .set(far_grads)
    )
    arrived_slots = (
        lax.all_to_all(
            outbox.astype(jnp.bfloat16), "blk", split_axis=0, concat_axis=0, tiled=True
        ).astype(outbox.dtype)
        * filled[:, :, None, None, None]
    )
    landed = (
        jnp.zeros((block_count * heads_dev, 2, BLOCK, HD), jnp.float32)
        .at[send_rows.reshape(-1)]
        .add(arrived_slots.reshape(shards * capacity, 2, BLOCK, HD))
    )
    landed = landed.reshape(block_count, heads_dev, 2, BLOCK, HD)
    global_probs = jnp.exp(global_scores - global_lse[..., None])
    d_probs_global = jnp.einsum(
        "gqhd,khd->ghqk", d_global, value_wide, precision=lax.Precision.HIGHEST
    )
    delta_global = jnp.einsum(
        "gqhd,ghqd->ghq", d_global, global_out, precision=lax.Precision.HIGHEST
    )
    d_scores_global = (global_probs * (d_probs_global - delta_global[..., None])).astype(
        jnp.bfloat16
    )
    d_global_queries = (
        jnp.einsum("ghqk,khd->gqhd", d_scores_global, key_heads, preferred_element_type=jnp.float32)
        * attn_scale
    )
    d_keys_global = (
        jnp.einsum(
            "ghqk,gqhd->khd", d_scores_global, global_queries, preferred_element_type=jnp.float32
        )
        * attn_scale
    )
    d_values_global = jnp.einsum(
        "ghqk,gqhd->khd", global_probs, d_global, precision=lax.Precision.HIGHEST
    )
    returned = lax.psum(
        jnp.stack(
            [
                d_global_queries,
                global_sums[0].transpose(1, 2, 0, 3),
                global_sums[1].transpose(1, 2, 0, 3),
            ]
        ),
        "blk",
    )
    owned_grads = jnp.einsum(
        "ng,cgqhd->cnqhd", global_hits, returned, precision=lax.Precision.HIGHEST
    )
    d_query_total = d_query_sparse + owned_grads[0]
    d_key_total = (
        (inner_grads[0] + landed[:, :, 0]).transpose(0, 2, 1, 3)
        + d_keys_global.reshape(block_count, BLOCK, heads_dev, HD)
        + owned_grads[1]
    )
    d_value_total = (
        (inner_grads[1] + landed[:, :, 1]).transpose(0, 2, 1, 3)
        + d_values_global.reshape(block_count, BLOCK, heads_dev, HD)
        + owned_grads[2]
    )
    stacked = (
        jnp.stack([d_query_total, d_key_total, d_value_total])
        .reshape(3, row_count, group_width)
        .astype(jnp.bfloat16)
    )
    token_grads = lax.all_to_all(stacked, "head", split_axis=1, concat_axis=2, tiled=True)
    d_tokens = (
        d_mix
        + matmul_right(token_grads[0], full_query)
        + matmul_right(token_grads[1], full_key)
        + matmul_right(token_grads[2], full_value)
    )
    grads = (
        matmul_left(tokens, token_grads[0]),
        column_sum(token_grads[0]),
        matmul_left(tokens, token_grads[1]),
        matmul_left(tokens, token_grads[2]),
        column_sum(token_grads[2]),
        grad_out,
        grad_out_bias,
        grad_attn_gain,
        grad_attn_shift,
        grad_up,
        grad_up_bias,
        grad_down,
        grad_down_bias,
        grad_ffn_gain,
        grad_ffn_shift,
    )
    return (result.astype(jnp.bfloat16), d_tokens.astype(jnp.bfloat16), grads)


def body(
    inputs,
    cotangent,
    random_blocks,
    global_blocks,
    query_weight,
    query_bias,
    key_weight,
    value_weight,
    value_bias,
    out_weight,
    out_bias,
    attn_gain,
    attn_shift,
    up_weight,
    up_bias,
    down_weight,
    down_bias,
    ffn_gain,
    ffn_shift,
):
    weight_shards = (
        query_weight,
        query_bias,
        key_weight,
        value_weight,
        value_bias,
        out_weight,
        out_bias,
        attn_gain,
        attn_shift,
        up_weight,
        up_bias,
        down_weight,
        down_bias,
        ffn_gain,
        ffn_shift,
    )
    results = []
    input_grads = []
    totals = None
    for micro_index in range(inputs.shape[0]):
        weights = fetch_weights(*weight_shards)
        result, token_grad, grads = micro_batch(
            inputs[micro_index],
            cotangent[micro_index],
            random_blocks[micro_index],
            global_blocks[micro_index],
            weights,
        )
        grads = reduce_grads(grads)
        totals = (
            grads
            if totals is None
            else tuple((total_sum + extra_sum for total_sum, extra_sum in zip(totals, grads)))
        )
        results.append(result)
        input_grads.append(token_grad)
    return (jnp.stack(results), jnp.stack(input_grads)) + tuple(totals)


def solution(mesh):
    return jax.shard_map(
        near_body if (mesh.shape["blk"], mesh.shape["head"]) == (8, 4) else body,
        mesh=mesh,
        in_specs=(
            P(None, ("blk", "head"), None),
            P(None, ("blk", "head"), None),
            P(),
            P(),
            P(("blk", "head"), None),
            P(("blk", "head")),
            P(("blk", "head"), None),
            P(("blk", "head"), None),
            P(("blk", "head")),
            P(("blk", "head"), None),
            P(("blk", "head")),
            P(("blk", "head")),
            P(("blk", "head")),
            P(("blk", "head"), None),
            P(("blk", "head")),
            P(("blk", "head"), None),
            P(("blk", "head")),
            P(("blk", "head")),
            P(("blk", "head")),
        ),
        out_specs=(
            P(None, ("blk", "head"), None),
            P(None, ("blk", "head"), None),
            P(("blk", "head"), None),
            P(("blk", "head")),
            P(("blk", "head"), None),
            P(("blk", "head"), None),
            P(("blk", "head")),
            P(("blk", "head"), None),
            P(("blk", "head")),
            P(("blk", "head")),
            P(("blk", "head")),
            P(("blk", "head"), None),
            P(("blk", "head")),
            P(("blk", "head"), None),
            P(("blk", "head")),
            P(("blk", "head")),
            P(("blk", "head")),
        ),
        check_vma=False,
    )
```

```python
from functools import partial

import jax
import jax.numpy as jnp
from jax import lax
from jax.experimental import pallas as pl
from jax.experimental.pallas import tpu as pltpu
from jax.sharding import PartitionSpec as P

HEADS = 12
HD = 64
BLOCK = 64
RAND = 3
GLOB = 2


MESH = pl.DeviceIdType.MESH


def places():
    b = lax.axis_index("blk")
    h = lax.axis_index("head")
    core = b % 2
    x = (b // 2) % 2
    y = b // 4
    across_x = b + 2 - 4 * x
    across_y = b + 4 - 8 * y
    partner = b + 1 - 2 * core
    pair = h // 2
    line = (h, h + 1 - 2 * (h % 2), 2 - pair, 3 - 3 * pair)
    return b, h, core, x, y, across_x, across_y, partner, line


def meet(b, h):
    barrier = pltpu.get_barrier_semaphore()
    count = lax.axis_size("blk") * lax.axis_size("head")

    def tell(k, carry):
        other = (b * 4 + h + k) % count
        pl.semaphore_signal(barrier, inc=1, device_id=(other // 4, other % 4), device_id_type=MESH)
        return carry

    lax.fori_loop(1, count, tell, 0)
    pl.semaphore_wait(barrier, count - 1)


def pair_place(pair):
    at, along = pair % 6, pair // 6
    place = at + at // 3 + jnp.where(at > 3, 1, 0)
    x = place // 2 % 2
    return place + along % 2 * (2 - 4 * x), along


def place_pair(b, h):
    x = b // 2 % 2
    place = b + h % 2 * (2 - 4 * x)
    busy = jnp.logical_and(place != 3, place != 5)
    at = place - jnp.where(place > 3, 1, 0) - jnp.where(place > 5, 1, 0)
    return busy, jnp.minimum(h * 6 + at, 23)


def exchange(to_pairs, src, dst, sems, rows=slice(None)):
    send, recv, own = sems
    b = lax.axis_index("blk")
    h = lax.axis_index("head")
    me = b * 4 + h
    devices = lax.axis_size("blk") * lax.axis_size("head")
    pairs = 24
    busy, mine = place_pair(b, h)

    def other(at):
        if to_pairs:
            return pair_place(at)
        return at // 4, at % 4

    def copy(at):
        slot = me if to_pairs else mine
        return remote(
            src.at[at, rows], dst.at[slot, rows], send.at[at], recv.at[slot], other(at)
        )

    def away(at):
        place, along = other(at)
        return jnp.logical_not(jnp.logical_and(place == b, along == h))

    count = pairs if to_pairs else devices
    first = me * count // devices
    kept = pltpu.make_async_copy(
        src.at[mine if to_pairs else me, rows], dst.at[me if to_pairs else mine, rows], own
    )

    def begin():
        def one(k, carry):
            at = (first + k) % count

            @pl.when(away(at))
            def _():
                copy(at).start()

            return carry

        def everything():
            lax.fori_loop(0, count, one, 0)

        if to_pairs:
            everything()
            pl.when(busy)(kept.start)
        else:

            @pl.when(busy)
            def _():
                everything()
                kept.start()

    def arrive():
        def one(at, carry):
            here = dst.at[at, rows]
            landed = remote(here, here, send.at[0], recv.at[at], (b, h))
            if to_pairs:
                pl.when(at != me)(landed.wait_recv)
            else:
                place, along = pair_place(at)
                own_pair = jnp.logical_and(place == b, along == h)
                pl.when(jnp.logical_not(own_pair))(landed.wait_recv)
            return carry

        def everything():
            lax.fori_loop(0, devices if to_pairs else pairs, one, 0)

        if to_pairs:

            @pl.when(busy)
            def _():
                everything()
                kept.wait()
        else:
            everything()
            pl.when(busy)(kept.wait)

    def sent():
        def one(at, carry):
            pl.when(away(at))(copy(at).wait_send)
            return carry

        def everything():
            lax.fori_loop(0, count, one, 0)

        if to_pairs:
            everything()
        else:
            pl.when(busy)(everything)

    return begin, arrive, sent


def exchange_semaphores():
    dma = pltpu.SemaphoreType.DMA
    return [dma((32,)), dma((32,)), dma]


def remote(src, dst, send_sem, recv_sem, device):
    return pltpu.make_async_remote_copy(
        src_ref=src,
        dst_ref=dst,
        send_sem=send_sem,
        recv_sem=recv_sem,
        device_id=device,
        device_id_type=MESH,
    )


def gather_steps(kinds, ins, outs, sems):
    own_sem, line_send, line_recv, send, recv = sems
    b, h, core, x, y, across_x, across_y, partner, line = places()
    far_corner = across_x + 4 - 8 * y
    partner_x = partner + 2 - 4 * x
    partner_y = partner + 4 - 8 * y
    partner_corner = partner_x + 4 - 8 * y
    inner = jnp.logical_or(h == 1, h == 2)
    seen = jnp.where(inner, 2, 3)
    started = []
    started_inner = []
    locals_ = []

    def enter():
        meet(b, h)

    def piece(i, place):
        return ins[i].at[place] if kinds[i][0] else ins[i]

    def slot(i, shard, place):
        return outs[i].at[shard * 4 + place] if kinds[i][1] else outs[i].at[place]

    def part(ref, cut_):
        axis, start, size = cut_
        return ref.at[(slice(None),) * axis + (pl.ds(start, size),)]

    def go(copy, only_inner=False):
        if only_inner:

            @pl.when(inner)
            def _():
                copy.start()

            started_inner.append(copy)
        else:
            copy.start()
            started.append(copy)

    def along(i, src, landing, sender_at, receiver_at, place, only_inner=False):
        go(
            remote(
                src, landing, line_send.at[i, sender_at], line_recv.at[i, receiver_at], (b, place)
            ),
            only_inner,
        )

    def plane(i, d):
        src = piece(i, h) if d == 0 else slot(i, b, line[d])
        for k, other in enumerate((across_x, across_y, partner)):
            go(
                remote(
                    src, slot(i, b, line[d]), send.at[i, d, k], recv.at[i, d, k], (other, h)
                )
            )

    def arrived(i, d, k, shard, cut_=None):
        here = slot(i, shard, line[d])
        if cut_ is not None:
            here = part(here, cut_)
        remote(here, here, send.at[i, d, k], recv.at[i, d, k], (partner, h)).wait_recv()
        return here

    def begin(i):
        if kinds[i][0]:
            for d in (2, 3, 1):
                along(i, piece(i, line[d]), slot(i, b, h), d, 1 if d == 1 else seen, line[d])
        else:
            along(i, piece(i, h), slot(i, b, h), 2, 2, 3 - h, True)
            along(i, piece(i, h), slot(i, b, h), 1, 1, line[1])
        if kinds[i][1]:
            plane(i, 0)
        own = pltpu.make_async_copy(piece(i, h), slot(i, b, h), own_sem.at[i])
        own.start()
        locals_.append(own)

    def along_done(i, d):
        here = slot(i, b, line[d])
        remote(
            here, here, line_send.at[i, d], line_recv.at[i, d], (b, line[d])
        ).wait_recv()
        if not kinds[i][0]:
            if d == 1:
                along(i, here, here, 3, 3, 3 - h, True)
            else:
                along(i, here, here, d + 2, d, line[1], True)
        if kinds[i][1]:
            plane(i, d)

    def pass_on(i, d):
        first, second = kinds[i][2]
        for k, shard, cut_, onward in (
            (0, across_x, first, across_y),
            (1, across_y, second, across_x),
        ):
            here = arrived(i, d, k, shard)
            if cut_ is not None:
                go(
                    remote(
                        part(here, cut_),
                        part(here, cut_),
                        send.at[i, d, 6 + k],
                        recv.at[i, d, 6 + k],
                        (onward, h),
                    )
                )
            go(remote(here, here, send.at[i, d, 3 + k], recv.at[i, d, 3 + k], (partner, h)))

    def corner(i, d):
        for k, cut_ in enumerate(kinds[i][2]):
            if cut_ is not None:
                arrived(i, d, 6 + k, far_corner, cut_)
        here = slot(i, far_corner, line[d])
        go(remote(here, here, send.at[i, d, 5], recv.at[i, d, 5], (partner, h)))

    def finish(i):
        for d in range(4):
            for k, shard in ((2, partner), (3, partner_x), (4, partner_y), (5, partner_corner)):
                arrived(i, d, k, shard)

    def kept():
        for own in locals_:
            own.wait()
        locals_.clear()

    def sent():
        for copy in started:
            copy.wait_send()
        if started_inner:

            @pl.when(inner)
            def _():
                for copy in started_inner:
                    copy.wait_send()

    return enter, begin, along_done, pass_on, corner, finish, kept, sent


def gather_semaphores(n):
    dma = pltpu.SemaphoreType.DMA
    return [dma((n,)), dma((n, 6)), dma((n, 4)), dma((n, 4, 8)), dma((n, 4, 8))]


def exchange_kernel(to_pairs, in_ref, out_ref, *sems):
    begin, arrive, sent = exchange(to_pairs, in_ref, out_ref, sems)
    meet(lax.axis_index("blk"), lax.axis_index("head"))
    begin()
    arrive()
    sent()


def exchange_call(to_pairs, array, collective):
    far = pl.BlockSpec(memory_space=pl.ANY)
    return pl.pallas_call(
        partial(exchange_kernel, to_pairs),
        out_shape=jax.ShapeDtypeStruct((32 if to_pairs else 24,) + array.shape[1:], array.dtype),
        in_specs=[far],
        out_specs=far,
        scratch_shapes=exchange_semaphores(),
        compiler_params=pltpu.CompilerParams(collective_id=collective, has_side_effects=True),
        name=f"exchange{collective}",
    )(array)


def spread_of(rows, width):
    shards, n = rows.shape
    total = shards * width
    lane = lax.broadcasted_iota(jnp.int32, (n, total), 0)
    column = lax.broadcasted_iota(jnp.int32, (n, total), 1)
    repeat = jnp.where(column % width == lane, 1.0, 0.0).astype(jnp.bfloat16)
    shard = lax.broadcasted_iota(jnp.int32, (shards, total), 0)
    column = lax.broadcasted_iota(jnp.int32, (shards, total), 1)
    return rows_sum(jnp.where(column // width == shard, dot(rows.astype(jnp.bfloat16), repeat), 0.0))


def front_kernel(kinds, *refs):
    (
        x_ref, wq_in, wk_in, wv_in, wo_in, up_in, down_in, *vectors,
    ) = refs[:16]
    (
        land_out, up_out, down_out, w_out, vec_ref, up_bias_ref,
        tile, chunk, mixed, rows_wide, w_ref, parts, join_sem, w_sem,
    ) = refs[16:30]
    rows = x_ref.shape[1]
    width = x_ref.shape[2]
    shards, depth, _ = mixed.shape
    enter, begin, along_done, pass_on, corner, finish, kept, sent = gather_steps(
        kinds,
        [chunk, up_in, down_in],
        [mixed, up_out, down_out],
        refs[33:],
    )
    begin_pairs, arrive_pairs, sent_pairs = exchange(True, parts, land_out, refs[30:33])
    joins = [
        pltpu.make_async_copy(ref, chunk.at[:, pl.ds(k * width, width)], join_sem.at[k])
        for k, ref in enumerate((wq_in, wk_in, wv_in, wo_in))
    ]
    for copy in joins:
        copy.start()
    tile[...] = jnp.zeros(tile.shape, jnp.float32)
    for k, ref in enumerate(vectors):
        tile[k, : ref.shape[0]] = ref[...].astype(jnp.float32)
    chunk[:, 4 * width :] = tile[...].astype(jnp.bfloat16)
    for copy in joins:
        copy.wait()
    enter()
    begin(0)
    begin(1)
    begin(2)
    along_done(0, 1)
    pass_on(0, 0)
    along_done(0, 2)
    along_done(1, 1)
    along_done(2, 1)
    pass_on(0, 1)
    corner(0, 0)
    along_done(0, 3)
    pass_on(1, 0)
    pass_on(2, 0)
    pass_on(0, 2)
    corner(0, 1)
    pass_on(0, 3)
    corner(0, 2)
    along_done(1, 2)
    along_done(2, 2)
    corner(0, 3)
    finish(0)
    kept()
    for s in range(0, 4 * width, width):
        part = mixed[:, :, s : s + width].astype(jnp.float32).reshape(width, width)
        w_ref[:, s : s + width] = part.astype(jnp.bfloat16)
    leave = pltpu.make_async_copy(w_ref, w_out, w_sem)
    leave.start()
    rows_wide[...] = mixed[:, :, 4 * width :].astype(jnp.float32)
    for k in range(8):
        vec_ref[k : k + 1, :] = spread_of(rows_wide[:, k, :], depth)
    up_bias_ref[...] = spread_of(rows_wide[:, 8, :], up_bias_ref.shape[1] // shards)
    tokens = x_ref[...].reshape(2 * rows, width)
    made = []
    for k in range(3):
        part = dot(tokens, w_ref[:, k * width : (k + 1) * width])
        if k != 1:
            part = part + vec_ref[k // 2 : k // 2 + 1, :]
        made.append(part.astype(jnp.bfloat16))
    q, k, v = made
    for pair in range(parts.shape[0]):
        col, at = pair // 2 * HD, pair % 2 * rows
        mid = at + rows // 2
        parts[pair, :rows] = jnp.concatenate(
            [halves(k[at : at + rows], col), halves(v[at : at + rows], col)], axis=1
        )
        parts[pair, rows:] = jnp.concatenate(
            [halves(q[at:mid], col), halves(q[mid : at + rows], col)], axis=1
        )
    begin_pairs()
    for i in (1, 2):
        pass_on(i, 1)
        corner(i, 0)
    for i in (1, 2):
        along_done(i, 3)
    for i in (1, 2):
        pass_on(i, 2)
        corner(i, 1)
    for i in (1, 2):
        pass_on(i, 3)
        corner(i, 2)
    for i in (1, 2):
        corner(i, 3)
    arrive_pairs()
    finish(1)
    finish(2)
    kept()
    leave.wait()
    sent()
    sent_pairs()


def front_call(tokens, matrices, up, down, vectors, collective):
    micro, rows, width = tokens.shape
    depth, ff = up.shape
    groups = lax.axis_size("head")
    devices = groups * lax.axis_size("blk")
    f32, bf16 = jnp.float32, jnp.bfloat16
    half = 2 * width
    kinds = [
        (False, True, (cut(1, 0, half), cut(1, half, half + 128))),
        (False, True, (cut(1, 0, ff), None)),
        (False, True, (None, cut(1, 0, width))),
    ]
    near = pl.BlockSpec(memory_space=pltpu.VMEM)
    far = pl.BlockSpec(memory_space=pl.ANY)
    return pl.pallas_call(
        partial(front_kernel, kinds),
        out_shape=(
            jax.ShapeDtypeStruct((devices, rows + rows // 2, 2 * HD), bf16),
            jax.ShapeDtypeStruct((devices,) + up.shape, bf16),
            jax.ShapeDtypeStruct((devices,) + down.shape, bf16),
            jax.ShapeDtypeStruct((width, 4 * width), bf16),
            jax.ShapeDtypeStruct((8, width), f32),
            jax.ShapeDtypeStruct((1, ff), f32),
        ),
        in_specs=[near] + [far] * 6 + [near] * 9,
        out_specs=(far,) * 4 + (near,) * 2,
        scratch_shapes=[
            pltpu.VMEM((depth, 128), f32),
            pltpu.VMEM((depth, 4 * width + 128), bf16),
            pltpu.VMEM((devices, depth, 4 * width + 128), bf16),
            pltpu.VMEM((devices, depth, 128), f32),
            pltpu.VMEM((width, 4 * width), bf16),
            pltpu.VMEM((HEADS * micro, rows + rows // 2, 2 * HD), bf16),
            pltpu.SemaphoreType.DMA((4,)),
            pltpu.SemaphoreType.DMA,
        ]
        + exchange_semaphores()
        + gather_semaphores(3),
        compiler_params=pltpu.CompilerParams(
            collective_id=collective, has_side_effects=True, vmem_limit_bytes=56 * 2**20
        ),
        name="front",
    )(tokens, *matrices, up, down, *vectors)


def scatter_steps(cuts, ins, bufs, sems):
    local_sem, line_send, line_recv, core_send, core_recv, send, recv = sems
    b, h, core, x, y, across_x, across_y, partner, line = places()
    seen = jnp.where(jnp.logical_or(h == 1, h == 2), 2, 3)
    chip = b // 2
    targets = (3 - chip, chip + 1 - 2 * x, chip + 2 - 4 * y, chip)
    started = []
    loads = {}
    order = (3, 2, 1, 0)

    def go(copy):
        copy.start()
        started.append(copy)

    def part(ref, cut):
        axis, start, size = cut
        return ref.at[(slice(None),) * axis + (pl.ds(start, size),)]

    def along(i, src, landing, d):
        go(
            remote(
                src, landing, line_send.at[i, d], line_recv.at[i, 1 if d == 1 else seen], (b, line[d])
            )
        )

    def begin(i, some=(0, 1, 2, 3)):
        from_partner, total = bufs[i][0], bufs[i][1]
        for t in some:
            go(
                remote(
                    ins[i].at[pl.ds((targets[t] * 2 + 1 - core) * 4, 4)],
                    from_partner.at[t],
                    core_send.at[i, t],
                    core_recv.at[i, t],
                    (partner, h),
                )
            )
            load = pltpu.make_async_copy(
                ins[i].at[pl.ds((targets[t] * 2 + core) * 4, 4)], total.at[t], local_sem.at[i, t]
            )
            load.start()
            loads[i, t] = load

    def wait_for(ref, i, d, k):
        remote(ref, ref, send.at[i, d, k], recv.at[i, d, k], (partner, h)).wait_recv()

    def ready(i, t):
        loads[i, t].wait()
        here = bufs[i][0].at[t]
        remote(here, here, core_send.at[i, t], core_recv.at[i, t], (partner, h)).wait_recv()

    def both_cores(i, t, d, extra=()):
        from_partner, total = bufs[i][0], bufs[i][1]
        place = line[d]
        value = total[t, place].astype(jnp.float32) + from_partner[t, place].astype(jnp.float32)
        for ref in extra:
            value = value + ref[d].astype(jnp.float32)
        total[t, place] = value.astype(total.dtype)

    def add_corner(i, t, d, ref, cut):
        total = bufs[i][1]
        axis, start, size = cut
        at = (t, line[d]) + (slice(None),) * axis + (pl.ds(start, size),)
        value = total[at].astype(jnp.float32) + ref[d].astype(jnp.float32)
        total[at] = value.astype(total.dtype)

    def corner(i):
        total = bufs[i][1]
        first, second = cuts[i]
        ready(i, 0)
        for d in order:
            both_cores(i, 0, d)
            mine = total.at[0, line[d]]
            if first is not None:
                go(remote(part(mine, first), bufs[i][2].at[d], send.at[i, d, 0], recv.at[i, d, 0], (across_x, h)))
            if second is not None:
                go(remote(part(mine, second), bufs[i][3].at[d], send.at[i, d, 1], recv.at[i, d, 1], (across_y, h)))

    def sides(i):
        total = bufs[i][1]
        first, second = cuts[i]
        ready(i, 1)
        ready(i, 2)
        for d in order:
            both_cores(i, 1, d)
            if second is not None:
                wait_for(bufs[i][3].at[d], i, d, 1)
                add_corner(i, 1, d, bufs[i][3], second)
            go(remote(total.at[1, line[d]], bufs[i][4].at[d], send.at[i, d, 2], recv.at[i, d, 2], (across_x, h)))
            both_cores(i, 2, d)
            if first is not None:
                wait_for(bufs[i][2].at[d], i, d, 0)
                add_corner(i, 2, d, bufs[i][2], first)
            go(remote(total.at[2, line[d]], bufs[i][5].at[d], send.at[i, d, 3], recv.at[i, d, 3], (across_y, h)))

    def own(i):
        total = bufs[i][1]
        ready(i, 3)
        for d in order:
            wait_for(bufs[i][4].at[d], i, d, 2)
            wait_for(bufs[i][5].at[d], i, d, 3)
            both_cores(i, 3, d, (bufs[i][4], bufs[i][5]))
            if d > 0:
                along(i, total.at[3, line[d]], bufs[i][6].at[1 if d == 1 else seen], d)

    def finish(i):
        value = bufs[i][1][3, h].astype(jnp.float32)
        for d in range(1, 4):
            landing = bufs[i][6].at[d]
            remote(
                landing, landing, line_send.at[i, d], line_recv.at[i, d], (b, line[d])
            ).wait_recv()
            value = value + bufs[i][6][d].astype(jnp.float32)
        return value

    def sent():
        for copy in started:
            copy.wait_send()

    def enter():
        meet(b, h)

    return enter, begin, corner, sides, own, finish, sent


def scatter_scratch(chunk, dtype, cuts):
    shapes = [(4, 4) + chunk, (4, 4) + chunk]
    for cut_ in cuts:
        size = [16, 128]
        if cut_ is not None:
            size = list(chunk)
            size[cut_[0]] = cut_[2]
        shapes.append((4,) + tuple(size))
    shapes += [(4,) + chunk] * 3
    return [pltpu.VMEM(shape, dtype) for shape in shapes]


def scatter_semaphores(n):
    dma = pltpu.SemaphoreType.DMA
    return [dma((n, 4))] * 5 + [dma((n, 4, 4))] * 2


UP, DOWN, OUT, QUERY, KEY, VALUE, SMALL = range(7)


def back_kernel(cuts, *refs):
    (
        parts_in, up_in, down_in, x_ref, mixed_in, d_mix_ref, g_out_ref, g_vec_ref, g_up_bias_ref,
        d_x_ref, g_outw_ref, g_query_ref, g_key_ref, g_value_ref, g_up_ref, g_down_ref, g_small_ref,
        land, terms, small, w_ref, d_q, d_k, d_v, w_sem,
    ), rest = refs[:25], list(refs[25:])
    q_sems, kv_sems, rest = rest[:3], rest[3:6], rest[6:]
    bufs = [rest[7 * i : 7 * i + 7] for i in range(len(cuts))]
    rows = x_ref.shape[1]
    width = x_ref.shape[2]
    _, shards, depth, _ = terms.shape
    ins = (up_in, down_in, terms.at[0], terms.at[1], terms.at[2], terms.at[3], small)
    enter, begin, corner, sides, own, finish, sent = scatter_steps(
        cuts, ins, bufs, rest[7 * len(cuts) :]
    )
    begin_q, arrive_q, sent_q = exchange(False, parts_in, land, q_sems, pl.ds(rows, rows // 2))
    begin_kv, arrive_kv, sent_kv = exchange(False, parts_in, land, kv_sems, pl.ds(0, rows))
    load = pltpu.make_async_copy(mixed_in.at[:, pl.ds(0, 3 * width)], w_ref, w_sem)
    load.start()
    def keep_term(at, value):
        terms[at] = value.reshape(shards, depth, width).astype(jnp.bfloat16)

    enter()
    begin_q()
    begin_kv()
    keep_term(0, g_out_ref[...].astype(jnp.float32))
    small[...] = jnp.zeros(small.shape, jnp.float32)
    arrive_q()
    begin(UP, (0,))
    begin(DOWN, (0,))
    corner(UP)
    corner(DOWN)
    begin(UP, (1, 2, 3,))
    begin(DOWN, (1, 2, 3,))
    arrive_kv()
    spans = []
    for m in range(2):
        top, mid = m * rows, m * rows + rows // 2
        spans.append((m, slice(top, top + rows), slice(top, mid), slice(mid, top + rows)))
    tokens = x_ref[...].reshape(2 * rows, width)
    for p in range(HEADS // 2):
        at = pl.ds(p * 2 * HD, 2 * HD)
        for m, _, early, late in spans:
            one, two = land[4 * p + m, rows:], land[4 * p + 2 + m, rows:]
            d_q[early, at] = jnp.concatenate([one[:, :HD], two[:, :HD]], axis=1)
            d_q[late, at] = jnp.concatenate([one[:, HD:], two[:, HD:]], axis=1)
    for p in range(HEADS // 2):
        at = pl.ds(p * 2 * HD, 2 * HD)
        for m, both, _, _ in spans:
            one, two = land[4 * p + m, :rows], land[4 * p + 2 + m, :rows]
            d_k[both, at] = jnp.concatenate([one[:, :HD], two[:, :HD]], axis=1)
            d_v[both, at] = jnp.concatenate([one[:, HD:], two[:, HD:]], axis=1)
    keep_term(1, dot(tokens, d_q[...], COLS))
    keep_term(2, dot(tokens, d_k[...], COLS))
    keep_term(3, dot(tokens, d_v[...], COLS))
    vectors = jnp.concatenate(
        [
            rows_sum(d_q[...].astype(jnp.float32)),
            rows_sum(d_v[...].astype(jnp.float32)),
            g_vec_ref[:6, :],
        ],
        axis=0,
    )
    up_bias = g_up_bias_ref[...]
    up_depth = up_bias.shape[1] // shards
    for s in range(shards):
        small[s, :8, :depth] = vectors[:, s * depth : (s + 1) * depth]
        small[s, 8:9, :up_depth] = up_bias[:, s * up_depth : (s + 1) * up_depth]
    begin(OUT)
    begin(QUERY)
    begin(KEY)
    begin(VALUE)
    begin(SMALL)
    corner(OUT)
    corner(QUERY)
    corner(KEY)
    corner(VALUE)
    corner(SMALL)
    sides(UP)
    sides(DOWN)
    sides(OUT)
    sides(QUERY)
    sides(KEY)
    sides(VALUE)
    sides(SMALL)
    own(UP)
    load.wait()
    d_x = d_mix_ref[...]
    for k, half_ref in enumerate((d_q, d_k, d_v)):
        d_x = d_x + dot(half_ref[...], w_ref[:, k * width : (k + 1) * width], ROWS)
    d_x_ref[...] = d_x.astype(jnp.bfloat16).reshape(2, rows, width)
    own(DOWN)
    g_up_ref[...] = finish(UP)
    own(OUT)
    own(QUERY)
    own(KEY)
    own(VALUE)
    own(SMALL)
    g_down_ref[...] = finish(DOWN)
    g_outw_ref[...] = finish(OUT)
    g_query_ref[...] = finish(QUERY)
    g_key_ref[...] = finish(KEY)
    g_value_ref[...] = finish(VALUE)
    g_small_ref[...] = finish(SMALL)
    sent_q()
    sent()
    sent_kv()


def back_call(parts, g_up, g_down, tokens, mixed, d_mix, g_out, g_vec, g_up_bias, collective):
    micro, rows, width = tokens.shape
    devices, depth, ff = g_up.shape
    f32, bf16 = jnp.float32, jnp.bfloat16
    one_way, other_way = (cut(1, 0, width), None), (None, cut(1, 0, width))
    cuts = [(cut(1, 0, ff), None), other_way, one_way, other_way, one_way, other_way, (cut(1, 0, 128), None)]
    square = (depth, width)
    chunks = [(g_up.shape[1:], bf16), (g_down.shape[1:], bf16)] + [(square, bf16)] * 4
    chunks += [((16, 128), f32)]
    scratch = [
        one for (chunk, dtype), c in zip(chunks, cuts) for one in scatter_scratch(chunk, dtype, c)
    ]
    near = pl.BlockSpec(memory_space=pltpu.VMEM)
    far = pl.BlockSpec(memory_space=pl.ANY)
    outs = [jax.ShapeDtypeStruct(tokens.shape, bf16)]
    outs += [jax.ShapeDtypeStruct(square, f32)] * 4
    outs += [
        jax.ShapeDtypeStruct((depth, ff), f32),
        jax.ShapeDtypeStruct(g_down.shape[1:], f32),
        jax.ShapeDtypeStruct((16, 128), f32),
    ]
    return pl.pallas_call(
        partial(back_kernel, cuts),
        out_shape=tuple(outs),
        in_specs=[far] * 3 + [near, far] + [near] * 4,
        out_specs=(near,) * len(outs),
        scratch_shapes=[
            pltpu.VMEM((HEADS * micro,) + parts.shape[1:], bf16),
            pltpu.VMEM((4, devices) + square, bf16),
            pltpu.VMEM((devices, 16, 128), f32),
            pltpu.VMEM((width, 3 * width), bf16),
        ]
        + [pltpu.VMEM((micro * rows, width), bf16)] * 3
        + [pltpu.SemaphoreType.DMA]
        + exchange_semaphores() * 2
        + scratch
        + scatter_semaphores(len(cuts)),
        compiler_params=pltpu.CompilerParams(
            collective_id=collective, has_side_effects=True, vmem_limit_bytes=61 * 2**20
        ),
        name="back",
    )(parts, g_up, g_down, tokens, mixed, d_mix, g_out, g_vec, g_up_bias)


def leave_kernel(*refs):
    *wholes, small_in = refs[:8]
    outs = refs[8:]
    for from_ref, to_ref in zip(wholes, outs):
        to_ref[...] = from_ref[...]
    for k, ref in enumerate(outs[7:]):
        ref[...] = small_in[k, : ref.shape[0]]


def leave_call(*arrays):
    *wholes, _ = arrays
    depth, width = wholes[1].shape
    f32 = jnp.float32
    outs = [jax.ShapeDtypeStruct(a.shape, a.dtype) for a in wholes]
    outs += [jax.ShapeDtypeStruct((depth,), f32)] * 8
    outs += [jax.ShapeDtypeStruct((wholes[6].shape[0],), f32)]
    near = pl.BlockSpec(memory_space=pltpu.VMEM)
    return pl.pallas_call(
        leave_kernel,
        out_shape=tuple(outs),
        in_specs=[near] * 8,
        out_specs=(near,) * len(outs),
        name="leave",
    )(*arrays)


def cut(axis, start, size):
    return (axis, start, size)


def lanes_of(shape, low):
    lane = lax.broadcasted_iota(jnp.int32, shape, len(shape) - 1)
    if isinstance(low, bool):
        return lane < HD if low else lane >= HD
    return lane // HD == jnp.where(low, 0, 1)


def dot(left_side, right_side, contract=((1,), (0,))):
    return lax.dot_general(
        left_side, right_side, (contract, ((), ())), preferred_element_type=jnp.float32
    )


ROWS = ((1,), (1,))
COLS = ((0,), (0,))


def halves(array, col):
    return array[:, col : col + HD]


def listed_rows(table_ref, blocks, n):
    rows = [jnp.maximum(n - 1, 0), n, jnp.minimum(n + 1, blocks - 1)]
    rows += [table_ref[n * RAND + r] for r in range(RAND)]
    return rows + [table_ref[blocks * RAND + g] for g in range(GLOB)]


def outside(here, total, listed):
    lane = lax.broadcasted_iota(jnp.int32, (1, listed * BLOCK), 1)
    before = jnp.logical_and(lane < BLOCK, here == 0)
    after = jnp.logical_and(
        jnp.logical_and(lane >= 2 * BLOCK, lane < 3 * BLOCK), here == total - 1
    )
    return jnp.where(jnp.logical_or(before, after), -jnp.inf, 0.0)


def only(value, low):
    return jnp.where(lanes_of(value.shape, low), value, jnp.zeros_like(value))


def turned(value):
    return jnp.concatenate([value[:, HD:], value[:, :HD]], axis=1)


def to_side(value, odd, low):
    if isinstance(odd, bool):
        return only(turned(value) if odd == low else value, low)
    return only(jnp.where((odd == 1) == low, turned(value), value), low)


def key_rows(ref, spot, step):
    return ref[pl.ds(spot, step), :2].reshape(step * 2 * BLOCK, 2 * HD)


GROUP = 8
STEP = 8


def attend_kernel(table_ref, land_ref, out_ref, lse_ref):
    devices = land_ref.shape[0]
    blocks = 2 * devices
    scale = jnp.bfloat16(HD ** (-0.5))

    def query_blocks(group, carry):
        kvs, scores = [], []
        for u in range(GROUP):
            n = group * GROUP + u
            rows = listed_rows(table_ref, blocks, n)
            kvs.append(jnp.concatenate([land_ref[r // 2, r % 2] for r in rows], axis=0))
            q = to_side(land_ref[group * (GROUP // 2) + u // 2, 2], u % 2 == 1, True) * scale
            scores.append(dot(q, kvs[-1], ROWS) + outside(n, blocks, len(rows)))
        raised = []
        for u, score in enumerate(scores):
            top = jnp.max(score, axis=1, keepdims=True)
            probs = jnp.exp(score - top)
            total_sum = jnp.sum(probs, axis=1, keepdims=True)
            raised.append((probs * (1.0 / total_sum)).astype(jnp.bfloat16))
            lse_ref[group * GROUP + u] = jnp.broadcast_to(
                top + jnp.log(total_sum), lse_ref.shape[1:]
            )
        outs = [dot(r, kv) for r, kv in zip(raised, kvs)]
        for u in range(0, GROUP, 2):
            out_ref[group * (GROUP // 2) + u // 2] = jnp.where(
                lanes_of(outs[u].shape, True), turned(outs[u]), outs[u + 1]
            ).astype(jnp.bfloat16)
        return carry

    def everything():
        lax.fori_loop(0, blocks // GROUP, query_blocks, 0)
        spots = range(0, devices, STEP)
        chosen = [table_ref[blocks * RAND + g] for g in range(GLOB)]
        q = jnp.concatenate(
            [to_side(land_ref[row // 2, 2], row % 2, True) for row in chosen], axis=0
        )
        scores = [dot(q * scale, key_rows(land_ref, spot, STEP), ROWS) for spot in spots]
        top = scores[0].max(axis=1, keepdims=True)
        for score in scores[1:]:
            top = jnp.maximum(top, score.max(axis=1, keepdims=True))
        raised = [jnp.exp(score - top) for score in scores]
        total_sum = sum(jnp.sum(r, axis=1, keepdims=True) for r in raised)
        out = sum(
            dot(r.astype(jnp.bfloat16), key_rows(land_ref, spot, STEP))
            for r, spot in zip(raised, spots)
        )
        out = out / total_sum
        lse = jnp.broadcast_to(top + jnp.log(total_sum), out.shape)
        for g, row in enumerate(chosen):
            at = slice(g * BLOCK, (g + 1) * BLOCK)
            lse_ref[row] = lse[at]
            new = jnp.where(row % 2 == 0, turned(out[at]), out[at]).astype(jnp.bfloat16)
            old = out_ref[row // 2]
            out_ref[row // 2] = jnp.where(lanes_of(old.shape, row % 2 == 0), new, old)

    pl.when(table_ref[blocks * RAND + GLOB] == 1)(everything)


def attend_call(table, land):
    spec = pl.BlockSpec(memory_space=pltpu.VMEM)
    devices, _, block, lanes = land.shape
    return pl.pallas_call(
        attend_kernel,
        out_shape=(
            jax.ShapeDtypeStruct((devices, block, lanes), jnp.bfloat16),
            jax.ShapeDtypeStruct((2 * devices, block, lanes), jnp.float32),
        ),
        in_specs=[pl.BlockSpec(memory_space=pltpu.SMEM), spec],
        out_specs=(spec, spec),
        compiler_params=pltpu.CompilerParams(vmem_limit_bytes=56 * 2**20),
        name="attend",
    )(table, land)


def attend_back_kernel(table_ref, land_ref, d_ref, out_ref, lse_ref, parts_ref, total_ref):
    devices = land_ref.shape[0]
    blocks = 2 * devices
    scale = jnp.bfloat16(HD ** (-0.5))

    def wide(column, width):
        return jnp.concatenate([column] * (width // column.shape[1]), axis=1)

    def pair_of(place, odd, keep):
        q = to_side(land_ref[place, 2], odd, True) * scale
        d = to_side(d_ref[place], odd, False)
        if keep is not None:
            d = d * keep
        out = to_side(out_ref[place], odd, False)
        delta = jnp.sum(d.astype(jnp.float32) * out.astype(jnp.float32), axis=1, keepdims=True)
        return q, d, delta

    def query_blocks(group, carry):
        listed, kvs, pairs, deltas, boths = [], [], [], [], []
        for u in range(GROUP):
            n = group * GROUP + u
            rows = listed_rows(table_ref, blocks, n)
            is_global = jnp.logical_or(n == rows[-1], n == rows[-2])
            keep = jnp.where(is_global, 0.0, 1.0).astype(jnp.bfloat16)
            kv = jnp.concatenate([land_ref[r // 2, r % 2] for r in rows], axis=0)
            q, d, delta = pair_of(group * (GROUP // 2) + u // 2, u % 2 == 1, keep)
            listed.append(rows)
            kvs.append(kv)
            pairs.append(jnp.concatenate([q, d], axis=0))
            deltas.append(delta)
            boths.append(dot(pairs[-1], kv, ROWS))
        weights = []
        for u, both in enumerate(boths):
            n = group * GROUP + u
            width = both.shape[1]
            scores = both[:BLOCK] + outside(n, blocks, width // BLOCK)
            probs = jnp.exp(scores - wide(lse_ref[n], width))
            d_scores = probs * (both[BLOCK:] - deltas[u])
            weights.append(
                jnp.concatenate(
                    [d_scores.astype(jnp.bfloat16), probs.astype(jnp.bfloat16)], axis=0
                )
            )
        outs = []
        for u, weight in enumerate(weights):
            d_kv = dot(weight, pairs[u], COLS)
            for at, r in enumerate(listed[u]):
                total_ref[r // 2, r % 2] += d_kv[at * BLOCK : (at + 1) * BLOCK]
            outs.append(dot(weight[:BLOCK], kvs[u]) * HD ** (-0.5))
        for u in range(0, GROUP, 2):
            parts_ref[group * (GROUP // 2) + u // 2, 2] = jnp.where(
                lanes_of(outs[u].shape, True), outs[u], turned(outs[u + 1])
            ).astype(jnp.bfloat16)
        return carry

    def everything():
        def clear(i, carry):
            total_ref[i] = jnp.zeros(total_ref.shape[1:], jnp.float32)
            return carry

        lax.fori_loop(0, devices, clear, 0)
        lax.fori_loop(0, blocks // GROUP, query_blocks, 0)
        chosen = [table_ref[blocks * RAND + g] for g in range(GLOB)]
        found = [pair_of(row // 2, row % 2, None) for row in chosen]
        both_rows = GLOB * BLOCK
        pairs = jnp.concatenate([f[0] for f in found] + [f[1] for f in found], axis=0)
        delta = jnp.concatenate([f[2] for f in found], axis=0)
        lse = jnp.concatenate([lse_ref[row] for row in chosen], axis=0)

        def some_keys(spot, d_q):
            kv = key_rows(land_ref, spot * STEP, STEP)
            both = dot(pairs, kv, ROWS)
            probs = jnp.exp(both[:both_rows] - wide(lse, both.shape[1]))
            d_scores = probs * (both[both_rows:] - delta)
            weight = jnp.concatenate(
                [d_scores.astype(jnp.bfloat16), probs.astype(jnp.bfloat16)], axis=0
            )
            total_ref[pl.ds(spot * STEP, STEP)] += dot(weight, pairs, COLS).reshape(
                STEP, 2, BLOCK, 2 * HD
            )
            return d_q + dot(weight[:both_rows], kv)

        d_q = lax.fori_loop(
            0, devices // STEP, some_keys, jnp.zeros((both_rows, 2 * HD), jnp.float32)
        )
        d_q = d_q * HD ** (-0.5)
        for g, row in enumerate(chosen):
            part = d_q[g * BLOCK : (g + 1) * BLOCK]
            new = jnp.where(row % 2 == 0, part, turned(part)).astype(jnp.bfloat16)
            old = parts_ref[row // 2, 2]
            parts_ref[row // 2, 2] = jnp.where(lanes_of(old.shape, row % 2 == 0), new, old)

        def give(i, carry):
            parts_ref[i, :2] = total_ref[i].astype(jnp.bfloat16)
            return carry

        lax.fori_loop(0, devices, give, 0)

    pl.when(table_ref[blocks * RAND + GLOB] == 1)(everything)


def attend_back_call(table, land, d, out, lse):
    spec = pl.BlockSpec(memory_space=pltpu.VMEM)
    devices, _, block, lanes = land.shape
    return pl.pallas_call(
        attend_back_kernel,
        out_shape=jax.ShapeDtypeStruct(land.shape, jnp.bfloat16),
        in_specs=[pl.BlockSpec(memory_space=pltpu.SMEM)] + [spec] * 4,
        out_specs=spec,
        scratch_shapes=[pltpu.VMEM((devices, 2, block, lanes), jnp.float32)],
        compiler_params=pltpu.CompilerParams(vmem_limit_bytes=60 * 2**20),
        name="attend_back",
    )(table, land, d, out, lse)


def centre(values):
    center = jnp.mean(values, axis=1, keepdims=True)
    centred = values - center
    spread = jnp.mean(centred * centred, axis=1, keepdims=True)
    inverse = lax.rsqrt(spread + 1e-12)
    return centred * inverse, inverse


def centre_back(hat, inverse, grad):
    return inverse * (
        grad
        - jnp.mean(grad, axis=1, keepdims=True)
        - hat * jnp.mean(grad * hat, axis=1, keepdims=True)
    )


def rows_sum(values):
    return jnp.sum(values, axis=0, keepdims=True)


WEIGHT_CHUNK = 1024


def dense_kernel(
    c_ref, x_ref, cot_ref, wo_in, up_in, down_in, vec_ref, up_bias_ref,
    out_ref, d_mix_ref, d_c_ref, g_out_ref, g_up_out, g_down_out, g_vec_ref, g_up_bias_ref,
    ctx, first, hat, low, low_t, act, slope, ffn, wo_ref, up_ref, down_ref, g_up_ref, g_down_ref, in_sem, out_sem,
):
    rows = x_ref.shape[1]
    width = x_ref.shape[2]
    ff = up_ref.shape[1]
    chunk = WEIGHT_CHUNK
    fetches = [
        pltpu.make_async_copy(wo_in.at[:, pl.ds(3 * width, width)], wo_ref, in_sem.at[0]),
    ]
    for i in range(ff // chunk):
        at = pl.ds(i * chunk, chunk)
        fetches.append(pltpu.make_async_copy(up_in.at[:, at], up_ref.at[:, at], in_sem.at[2 * i + 1]))
        fetches.append(pltpu.make_async_copy(down_in.at[at], down_ref.at[at], in_sem.at[2 * i + 2]))
    for copy in fetches:
        copy.start()
    out_bias, attn_gain, attn_shift, down_bias, ffn_gain, ffn_shift = (
        vec_ref[k : k + 1, :] for k in range(2, 8)
    )
    for p in range(HEADS // 2):
        at = pl.ds(p * 2 * HD, 2 * HD)
        for m in range(2):
            one, two = c_ref[4 * p + m], c_ref[4 * p + 2 + m]
            top, mid = m * rows, m * rows + rows // 2
            ctx[top:mid, at] = jnp.concatenate([one[:, :HD], two[:, :HD]], axis=1)
            ctx[mid : top + rows, at] = jnp.concatenate([one[:, HD:], two[:, HD:]], axis=1)
    tokens = x_ref[...].reshape(2 * rows, width).astype(jnp.float32)
    fetches[0].wait()
    hat_first, inverse_first = centre(tokens + dot(ctx[...], wo_ref[...]) + out_bias)
    hat[...] = hat_first
    first[...] = hat_first * attn_gain + attn_shift
    low[...] = first[...].astype(jnp.bfloat16)
    low_t[...] = first[...].T.astype(jnp.bfloat16)
    ffn[...] = first[...] + down_bias

    def forward(i):
        at = pl.ds(i * chunk, chunk)
        fetches[2 * i + 1].wait()
        fetches[2 * i + 2].wait()
        hidden = dot(low[...], up_ref[:, at]) + up_bias_ref[:, at]
        share = 0.5 * (1.0 + lax.erf(hidden * 0.7071067811865476))
        bell = jnp.exp(-0.5 * hidden * hidden) * 0.3989422804014327
        slope[:, at] = share + hidden * bell
        act_low = (hidden * share).astype(jnp.bfloat16)
        act[:, at] = act_low
        ffn[...] += dot(act_low, down_ref[at, :])

    for i in range(ff // chunk):
        forward(i)
    hat_second, inverse_second = centre(ffn[...])
    out_ref[...] = (
        (hat_second * ffn_gain + ffn_shift).astype(jnp.bfloat16).reshape(2, rows, width)
    )
    cot = cot_ref[...].reshape(2 * rows, width).astype(jnp.float32)
    g_vec_ref[4:5, :] = rows_sum(cot * hat_second)
    g_vec_ref[5:6, :] = rows_sum(cot)
    d_second = centre_back(hat_second, inverse_second, cot * ffn_gain)
    d_ffn = d_second.astype(jnp.bfloat16)
    g_vec_ref[3:4, :] = rows_sum(d_ffn.astype(jnp.float32))
    ffn[...] = d_second

    def leave(i):
        at = pl.ds(pl.multiple_of(i * chunk, chunk), chunk)
        return (
            pltpu.make_async_copy(g_up_ref.at[:, at], g_up_out.at[:, at], out_sem.at[0, i]),
            pltpu.make_async_copy(g_down_ref.at[at, :], g_down_out.at[at, :], out_sem.at[1, i]),
        )

    def backward(i, carry):
        at = pl.ds(pl.multiple_of(i * chunk, chunk), chunk)
        d_act = dot(d_ffn, down_ref[at, :], ROWS)
        d_hidden = (d_act * slope[:, at]).astype(jnp.bfloat16)
        g_up_bias_ref[:, at] = rows_sum(d_hidden.astype(jnp.float32))
        g_down_ref[at, :] = dot(act[:, at], d_ffn, COLS).astype(jnp.bfloat16)
        g_up_ref[:, at] = dot(low_t[...], d_hidden).astype(jnp.bfloat16)
        for copy in leave(i):
            copy.start()
        ffn[...] += dot(d_hidden, up_ref[:, at], ROWS)
        return carry

    lax.fori_loop(0, ff // chunk, backward, 0)
    d_first = ffn[...]
    g_vec_ref[1:2, :] = rows_sum(d_first * hat[...])
    g_vec_ref[2:3, :] = rows_sum(d_first)
    d_mix = centre_back(hat[...], inverse_first, d_first * attn_gain)
    d_mix_ref[...] = d_mix
    d_branch = d_mix.astype(jnp.bfloat16)
    g_vec_ref[0:1, :] = rows_sum(d_branch.astype(jnp.float32))
    g_vec_ref[6:8, :] = jnp.zeros((2, width), jnp.float32)
    g_out_ref[...] = dot(ctx[...], d_branch, COLS).astype(jnp.bfloat16)
    d_ctx = dot(d_branch, wo_ref[...], ROWS).astype(jnp.bfloat16)
    for pair in range(d_c_ref.shape[0]):
        col, top = pair // 2 * HD, pair % 2 * rows
        mid = top + rows // 2
        d_c_ref[pair] = jnp.concatenate(
            [halves(d_ctx[top:mid], col), halves(d_ctx[mid : top + rows], col)], axis=1
        )
    for i in range(ff // chunk):
        for copy in leave(i):
            copy.wait()


def dense_call(c, tokens, cot, mixed, up, down, vec, up_bias):
    micro, rows, width = tokens.shape
    ff = up.shape[1]
    both = micro * rows
    far = pl.BlockSpec(memory_space=pl.ANY)
    f32, bf16 = jnp.float32, jnp.bfloat16

    def full(shape):
        return pl.BlockSpec(memory_space=pltpu.VMEM)

    outs = (
        jax.ShapeDtypeStruct(tokens.shape, bf16),
        jax.ShapeDtypeStruct((both, width), f32),
        jax.ShapeDtypeStruct(c.shape, bf16),
        jax.ShapeDtypeStruct((width, width), bf16),
        jax.ShapeDtypeStruct((width, ff), bf16),
        jax.ShapeDtypeStruct((ff, width), bf16),
        jax.ShapeDtypeStruct((8, width), f32),
        jax.ShapeDtypeStruct((1, ff), f32),
    )
    return pl.pallas_call(
        dense_kernel,
        out_shape=outs,
        in_specs=[
            full(c.shape),
            full(tokens.shape),
            full(cot.shape),
            far,
            far,
            far,
            full(vec.shape),
            full(up_bias.shape),
        ],
        out_specs=tuple(far if k in (4, 5) else full(o.shape) for k, o in enumerate(outs)),
        scratch_shapes=[
            pltpu.VMEM((both, width), bf16),
            pltpu.VMEM((both, width), f32),
            pltpu.VMEM((both, width), f32),
            pltpu.VMEM((both, width), bf16),
            pltpu.VMEM((width, both), bf16),
            pltpu.VMEM((both, ff), bf16),
            pltpu.VMEM((both, ff), f32),
            pltpu.VMEM((both, width), f32),
            pltpu.VMEM((width, width), bf16),
            pltpu.VMEM((width, ff), bf16),
            pltpu.VMEM((ff, width), bf16),
            pltpu.VMEM((width, ff), bf16),
            pltpu.VMEM((ff, width), bf16),
            pltpu.SemaphoreType.DMA((1 + 2 * (ff // WEIGHT_CHUNK),)),
            pltpu.SemaphoreType.DMA((2, ff // WEIGHT_CHUNK)),
        ],
        compiler_params=pltpu.CompilerParams(vmem_limit_bytes=60 * 2**20),
        name="dense",
    )(c, tokens, cot, mixed, up, down, vec, up_bias)


def near_body(inputs, cotangent, random_blocks, global_blocks, *shards):
    (
        query_weight, query_bias, key_weight, value_weight, value_bias, out_weight, out_bias, attn_gain,
        attn_shift, up_weight, up_bias, down_weight, down_bias, ffn_gain, ffn_shift,
    ) = shards
    devices = lax.axis_size("head") * lax.axis_size("blk")
    micro, rows, width = inputs.shape
    depth = query_weight.shape[0]
    ff = up_weight.shape[1]
    land, up, down, mixed, vec, up_bias_row = front_call(
        inputs,
        (query_weight, key_weight, value_weight, out_weight),
        up_weight,
        down_weight,
        (
            query_bias, value_bias, out_bias, attn_gain, attn_shift, down_bias, ffn_gain, ffn_shift, up_bias,
        ),
        1,
    )
    up = up.reshape(width, ff)
    down = down.reshape(ff, width)
    busy, pair = place_pair(lax.axis_index("blk"), lax.axis_index("head"))
    head, at = pair // micro, pair % micro
    table = jnp.concatenate(
        [
            lax.dynamic_slice(
                random_blocks, (at, 0, head, 0), (1, random_blocks.shape[1], 1, RAND)
            ).reshape(-1),
            lax.dynamic_slice(global_blocks, (at, 0), (1, GLOB)).reshape(-1),
            busy.astype(jnp.int32)[None],
        ]
    )
    land = land.reshape(devices, 3, rows // 2, 2 * HD)
    attended, lse = attend_call(table, land)
    context = exchange_call(False, attended, 3)
    layer_out, d_mix, d_context, g_out, g_up, g_down, g_vec, g_up_bias = dense_call(
        context, inputs, cotangent, mixed, up, down, vec, up_bias_row
    )
    d_context = exchange_call(True, d_context, 4)
    parts = attend_back_call(table, land, d_context, attended, lse)
    results = back_call(
        parts.reshape(devices, 3 * rows // 2, 2 * HD),
        g_up.reshape(devices, depth, ff),
        g_down.reshape(devices, -1, width),
        inputs,
        mixed,
        d_mix,
        g_out,
        g_vec,
        g_up_bias,
        5,
    )
    (
        input_grad, grad_out, grad_query, grad_key, grad_value, grad_up, grad_down, *vector, grad_up_bias,
    ) = leave_call(*results)
    return (
        layer_out, input_grad, grad_query, vector[0], grad_key, grad_value, vector[1], grad_out,
        vector[2], vector[3], vector[4], grad_up, grad_up_bias, grad_down, vector[5], vector[6], vector[7],
    )


def with_halo(cells, sides, width):
    for axis, dim in sides:
        count = lax.axis_size(axis)
        ends = count - 1
        head = lax.slice_in_dim(cells, 0, width, axis=dim)
        tail = lax.slice_in_dim(cells, cells.shape[dim] - width, cells.shape[dim], axis=dim)
        cells = jnp.concatenate(
            [
                lax.ppermute(tail, axis, [(i, (i + 1) % count) for i in range(ends)]),
                cells,
                lax.ppermute(head, axis, [((i + 1) % count, i) for i in range(ends)]),
            ],
            axis=dim,
        )
    return cells


def combined_all(part, axis, combine):
    gathered = jax.tree.map(lambda a: lax.all_gather(a, axis), part)

    def take(source):
        return jax.tree.map(lambda a: lax.dynamic_index_in_dim(a, source, 0, False), gathered)

    return lax.fori_loop(
        1, lax.axis_size(axis), lambda source, state: combine(state, take(source)), take(0)
    )


def taken(table, rows):
    return lax.map(lambda row: lax.dynamic_index_in_dim(table, row, 0, False), rows)


def layer_norm(values, norm_gain, norm_shift):
    center = jnp.mean(values, axis=-1, keepdims=True)
    centred = values - center
    spread = jnp.mean(centred * centred, axis=-1, keepdims=True)
    return centred * lax.rsqrt(spread + 1e-12) * norm_gain + norm_shift


def gelu_exact(values):
    return jax.nn.gelu(values, approximate=False)


def matmul(left_side, right_side):
    return jnp.dot(left_side, right_side, preferred_element_type=jnp.float32)


def matmul_left(left_side, right_side):
    return lax.dot_general(
        left_side, right_side, (((0,), (0,)), ((), ())), preferred_element_type=jnp.float32
    )


def matmul_right(left_side, right_side):
    return lax.dot_general(
        left_side, right_side, (((1,), (1,)), ((), ())), preferred_element_type=jnp.float32
    )


def column_sum(values):
    return jnp.sum(values.astype(jnp.float32), axis=0)


def combine_parts(earlier, later_part):
    joint_top = jnp.maximum(earlier[0], later_part[0])
    first_factor = jnp.exp(earlier[0] - joint_top)
    second_factor = jnp.exp(later_part[0] - joint_top)
    return (
        joint_top,
        earlier[1] * first_factor + later_part[1] * second_factor,
        earlier[2] * first_factor[..., None] + later_part[2] * second_factor[..., None],
    )


def fetch_weights(
    query_weight,
    query_bias,
    key_weight,
    value_weight,
    value_bias,
    out_weight,
    out_bias,
    attn_gain,
    attn_shift,
    up_weight,
    up_bias,
    down_weight,
    down_bias,
    ffn_gain,
    ffn_shift,
):
    return (
        lax.all_gather(query_weight, ("blk", "head"), axis=0, tiled=True),
        lax.all_gather(query_bias, ("blk", "head"), axis=0, tiled=True),
        lax.all_gather(key_weight, ("blk", "head"), axis=0, tiled=True),
        lax.all_gather(value_weight, ("blk", "head"), axis=0, tiled=True),
        lax.all_gather(value_bias, ("blk", "head"), axis=0, tiled=True),
        lax.all_gather(out_weight, ("blk", "head"), axis=0, tiled=True),
        lax.all_gather(out_bias, ("blk", "head"), axis=0, tiled=True),
        lax.all_gather(attn_gain, ("blk", "head"), axis=0, tiled=True),
        lax.all_gather(attn_shift, ("blk", "head"), axis=0, tiled=True),
        lax.all_gather(up_weight, ("blk", "head"), axis=0, tiled=True),
        lax.all_gather(up_bias, ("blk", "head"), axis=0, tiled=True),
        lax.all_gather(down_weight, ("blk", "head"), axis=0, tiled=True),
        lax.all_gather(down_bias, ("blk", "head"), axis=0, tiled=True),
        lax.all_gather(ffn_gain, ("blk", "head"), axis=0, tiled=True),
        lax.all_gather(ffn_shift, ("blk", "head"), axis=0, tiled=True),
    )


def reduce_grads(totals):
    return (
        lax.psum_scatter(totals[0], ("blk", "head"), scatter_dimension=0, tiled=True),
        lax.psum_scatter(totals[1], ("blk", "head"), scatter_dimension=0, tiled=True),
        lax.psum_scatter(totals[2], ("blk", "head"), scatter_dimension=0, tiled=True),
        lax.psum_scatter(totals[3], ("blk", "head"), scatter_dimension=0, tiled=True),
        lax.psum_scatter(totals[4], ("blk", "head"), scatter_dimension=0, tiled=True),
        lax.psum_scatter(totals[5], ("blk", "head"), scatter_dimension=0, tiled=True),
        lax.psum_scatter(totals[6], ("blk", "head"), scatter_dimension=0, tiled=True),
        lax.psum_scatter(totals[7], ("blk", "head"), scatter_dimension=0, tiled=True),
        lax.psum_scatter(totals[8], ("blk", "head"), scatter_dimension=0, tiled=True),
        lax.psum_scatter(totals[9], ("blk", "head"), scatter_dimension=0, tiled=True),
        lax.psum_scatter(totals[10], ("blk", "head"), scatter_dimension=0, tiled=True),
        lax.psum_scatter(totals[11], ("blk", "head"), scatter_dimension=0, tiled=True),
        lax.psum_scatter(totals[12], ("blk", "head"), scatter_dimension=0, tiled=True),
        lax.psum_scatter(totals[13], ("blk", "head"), scatter_dimension=0, tiled=True),
        lax.psum_scatter(totals[14], ("blk", "head"), scatter_dimension=0, tiled=True),
    )


def sparse_forward(packed):
    group_queries, group_keys, group_values, group_allowed = packed
    attn_scale = HD ** (-0.5)
    scores = (
        jnp.einsum("gqhd,ghkd->ghqk", group_queries, group_keys, preferred_element_type=jnp.float32)
        * attn_scale
    )
    scores = jnp.where(group_allowed[:, None, None, :], scores, -jnp.inf)
    row_top = jnp.max(scores, axis=-1, keepdims=True)
    raised = jnp.exp(scores - row_top)
    row_total = jnp.sum(raised, axis=-1, keepdims=True)
    probs_low = (raised / row_total).astype(jnp.bfloat16)
    output = jnp.einsum(
        "ghqk,ghkd->gqhd", probs_low, group_values, preferred_element_type=jnp.float32
    )
    return (output, (row_top + jnp.log(row_total))[..., 0])


def sparse_backward(nearby, carried, packed):
    group_queries, group_keys, group_values, group_allowed, group_lse, group_grad = packed
    attn_scale = HD ** (-0.5)
    per_group = group_queries.shape[0]
    heads_dev = group_queries.shape[2]
    scores = (
        jnp.einsum("gqhd,ghkd->ghqk", group_queries, group_keys, preferred_element_type=jnp.float32)
        * attn_scale
    )
    scores = jnp.where(group_allowed[:, None, None, :], scores, -jnp.inf)
    probs = jnp.exp(scores - group_lse[..., None])
    d_probs = jnp.einsum(
        "gqhd,ghkd->ghqk", group_grad, group_values, preferred_element_type=jnp.float32
    )
    row_delta = jnp.sum(probs * d_probs, axis=-1, keepdims=True)
    d_scores = (probs * (d_probs - row_delta)).astype(jnp.bfloat16)
    d_queries = (
        jnp.einsum("ghqk,ghkd->gqhd", d_scores, group_keys, preferred_element_type=jnp.float32)
        * attn_scale
    )
    d_keys = (
        jnp.einsum("ghqk,gqhd->ghkd", d_scores, group_queries, preferred_element_type=jnp.float32)
        * attn_scale
    )
    d_values = jnp.einsum(
        "ghqk,gqhd->ghkd",
        probs.astype(jnp.bfloat16),
        group_grad,
        preferred_element_type=jnp.float32,
    )
    d_keys = d_keys.reshape(per_group, heads_dev, -1, BLOCK, HD)
    d_values = d_values.reshape(per_group, heads_dev, -1, BLOCK, HD)
    carried = (
        carried[0] + jnp.sum(d_keys[:, :, nearby:], axis=0),
        carried[1] + jnp.sum(d_values[:, :, nearby:], axis=0),
    )
    return (carried, (d_queries, d_keys[:, :, :nearby], d_values[:, :, :nearby]))


def micro_batch(tokens, cotangent_rows, random_rows, global_rows, weights):
    (
        full_query,
        full_query_bias,
        full_key,
        full_value,
        full_value_bias,
        full_out,
        full_out_bias,
        full_attn_gain,
        full_attn_shift,
        full_up,
        full_up_bias,
        full_down,
        full_down_bias,
        full_ffn_gain,
        full_ffn_shift,
    ) = weights
    attn_scale = HD ** (-0.5)
    shards = lax.axis_size("blk")
    head_groups = lax.axis_size("head")
    shard_index = lax.axis_index("blk")
    group_index = lax.axis_index("head")
    heads_dev = HEADS // head_groups
    group_width = heads_dev * HD
    listed = 3 + RAND + GLOB
    nearby = 3 + RAND
    projected = jnp.stack(
        [
            matmul(tokens, full_query) + full_query_bias,
            matmul(tokens, full_key),
            matmul(tokens, full_value) + full_value_bias,
        ]
    ).astype(jnp.bfloat16)
    by_head = lax.all_to_all(projected, "head", split_axis=2, concat_axis=1, tiled=True)
    row_count = by_head.shape[1]
    block_count = row_count // BLOCK
    blocks_all = block_count * shards
    key_rows = by_head[1]
    value_rows = by_head[2]
    padded = with_halo(by_head[1:3], (("blk", 1),), BLOCK)
    extended = padded.reshape(2, block_count + 2, BLOCK, heads_dev, HD).transpose(0, 1, 3, 2, 4)
    window = jnp.stack([extended[:, offset : offset + block_count] for offset in range(3)], axis=3)
    block_ids = shard_index * block_count + jnp.arange(block_count, dtype=jnp.int32)
    neighbour = block_ids[:, None] + jnp.arange(-1, 2, dtype=jnp.int32)[None, :]
    inside = (neighbour >= 0) & (neighbour < blocks_all)
    head_table = lax.dynamic_slice_in_dim(random_rows, group_index * heads_dev, heads_dev, 1)
    requests = block_count * heads_dev * RAND
    all_requests = head_table.reshape(shards, requests)
    capacity = (requests + shards - 1) // shards + 1
    wanted = lax.dynamic_slice_in_dim(all_requests, shard_index, 1, 0)[0]
    source = wanted // block_count
    place = jnp.arange(requests, dtype=jnp.int32)
    earlier = (place[:, None] > place[None, :]).astype(jnp.int32)
    same_source = (source[:, None] == source[None, :]).astype(jnp.int32)
    slot_index = jnp.sum(earlier * same_source, axis=1)
    mine_mask = (all_requests // block_count == shard_index).astype(jnp.int32)
    send_order = jnp.sum(earlier[None] * mine_mask[:, None, :], axis=2)
    match_mask = mine_mask[:, :, None] * (
        send_order[:, :, None] == jnp.arange(capacity, dtype=jnp.int32)[None, None, :]
    ).astype(jnp.int32)
    head_of = jnp.arange(requests, dtype=jnp.int32) // RAND % heads_dev
    row_of = all_requests % block_count * heads_dev + head_of[None, :]
    send_rows = jnp.sum(match_mask * row_of[:, :, None], axis=1)
    filled = jnp.sum(match_mask, axis=1).astype(jnp.float32)
    block_table = (
        by_head[1:3]
        .reshape(2, block_count, BLOCK, heads_dev, HD)
        .transpose(1, 3, 0, 2, 4)
        .reshape(block_count * heads_dev, 2, BLOCK, HD)
    )
    outgoing = taken(block_table, send_rows.reshape(-1))
    incoming = lax.all_to_all(outgoing, "blk", split_axis=0, concat_axis=0, tiled=True)
    fetched = taken(incoming, source * capacity + slot_index).reshape(
        block_count, heads_dev, RAND, 2, BLOCK, HD
    )
    owner_shard = global_rows // block_count
    present = owner_shard == shard_index
    local_block = global_rows % block_count
    own_rows = jnp.stack(
        [
            lax.dynamic_index_in_dim(
                by_head.reshape(3, block_count, BLOCK, group_width), local_block[g], 1, False
            )
            for g in range(GLOB)
        ],
        axis=1,
    )
    shared = lax.psum(
        jnp.where(present[None, :, None, None], own_rows.astype(jnp.float32), 0.0), "blk"
    ).astype(jnp.bfloat16)
    shared_pairs = shared[1:3].reshape(2, GLOB, BLOCK, heads_dev, HD).transpose(0, 3, 1, 2, 4)

    def listed_blocks(which):
        near_part = window[which]
        random_part = fetched[:, :, :, which]
        global_part = jnp.broadcast_to(
            shared_pairs[which][None], (block_count, heads_dev, GLOB, BLOCK, HD)
        )
        return jnp.concatenate([near_part, random_part, global_part], axis=2).reshape(
            block_count, heads_dev, listed * BLOCK, HD
        )

    per_group = min(8, block_count)
    group_count = block_count // per_group
    query_groups = by_head[0].reshape(group_count, per_group, BLOCK, heads_dev, HD)
    key_groups = listed_blocks(0).reshape(group_count, per_group, heads_dev, listed * BLOCK, HD)
    value_groups = listed_blocks(1).reshape(group_count, per_group, heads_dev, listed * BLOCK, HD)
    allowed = jnp.repeat(
        jnp.concatenate([inside, jnp.ones((block_count, RAND + GLOB), jnp.bool_)], axis=1),
        BLOCK,
        axis=1,
    )
    allow_groups = allowed.reshape(group_count, per_group, listed * BLOCK)
    sparse_out, sparse_lse = lax.map(
        sparse_forward, (query_groups, key_groups, value_groups, allow_groups)
    )
    global_queries = shared[0].reshape(GLOB, BLOCK, heads_dev, HD)
    key_heads = key_rows.reshape(row_count, heads_dev, HD)
    value_wide = value_rows.reshape(row_count, heads_dev, HD).astype(jnp.float32)
    global_scores = (
        jnp.einsum("gqhd,khd->ghqk", global_queries, key_heads, preferred_element_type=jnp.float32)
        * attn_scale
    )
    global_top = jnp.max(global_scores, axis=-1)
    global_raised = jnp.exp(global_scores - global_top[..., None])
    merged = combined_all(
        (
            global_top,
            jnp.sum(global_raised, axis=-1),
            jnp.einsum(
                "ghqk,khd->ghqd", global_raised, value_wide, precision=lax.Precision.HIGHEST
            ),
        ),
        "blk",
        combine_parts,
    )
    global_out = merged[2] / merged[1][..., None]
    global_lse = merged[0] + jnp.log(merged[1])
    global_hits = (block_ids[:, None] == global_rows[None, :]).astype(jnp.float32)
    is_global = jnp.sum(global_hits, axis=1) > 0
    replaced = jnp.einsum("ng,ghqd->nqhd", global_hits, global_out, precision=lax.Precision.HIGHEST)
    context = jnp.where(
        is_global[:, None, None, None],
        replaced,
        sparse_out.reshape(block_count, BLOCK, heads_dev, HD),
    )
    context_rows = context.reshape(row_count, group_width).astype(jnp.bfloat16)
    context_tokens = lax.all_to_all(context_rows, "head", split_axis=0, concat_axis=1, tiled=True)
    branch = matmul(context_tokens, full_out) + full_out_bias
    first_in = tokens.astype(jnp.float32) + branch
    first_norm, first_pull = jax.vjp(
        layer_norm,
        first_in,
        full_attn_gain.astype(jnp.float32),
        full_attn_shift.astype(jnp.float32),
    )
    first_low = first_norm.astype(jnp.bfloat16)
    hidden = matmul(first_low, full_up) + full_up_bias
    act_value, gelu_pull = jax.vjp(gelu_exact, hidden)
    act_low = act_value.astype(jnp.bfloat16)
    ffn_out = matmul(act_low, full_down) + full_down_bias
    result, second_pull = jax.vjp(
        layer_norm,
        first_norm + ffn_out,
        full_ffn_gain.astype(jnp.float32),
        full_ffn_shift.astype(jnp.float32),
    )
    d_second, grad_ffn_gain, grad_ffn_shift = second_pull(cotangent_rows.astype(jnp.float32))
    d_ffn = d_second.astype(jnp.bfloat16)
    grad_down = matmul_left(act_low, d_ffn)
    grad_down_bias = column_sum(d_ffn)
    (d_hidden,) = gelu_pull(matmul_right(d_ffn, full_down))
    d_hidden_low = d_hidden.astype(jnp.bfloat16)
    grad_up = matmul_left(first_low, d_hidden_low)
    grad_up_bias = column_sum(d_hidden_low)
    d_first = d_second + matmul_right(d_hidden_low, full_up)
    d_mix, grad_attn_gain, grad_attn_shift = first_pull(d_first)
    d_branch = d_mix.astype(jnp.bfloat16)
    grad_out = matmul_left(context_tokens, d_branch)
    grad_out_bias = column_sum(d_branch)
    d_context = matmul_right(d_branch, full_out).astype(jnp.bfloat16)
    d_heads = lax.all_to_all(d_context, "head", split_axis=1, concat_axis=0, tiled=True).reshape(
        block_count, BLOCK, heads_dev, HD
    )
    d_sparse = jnp.where(is_global[:, None, None, None], jnp.zeros_like(d_heads), d_heads)
    d_global = lax.psum(
        jnp.where(
            present[:, None, None, None], taken(d_heads, local_block).astype(jnp.float32), 0.0
        ),
        "blk",
    )
    start_carry = (
        jnp.zeros((heads_dev, GLOB, BLOCK, HD), jnp.float32),
        jnp.zeros((heads_dev, GLOB, BLOCK, HD), jnp.float32),
    )
    global_sums, (d_query_parts, near_keys, near_values) = lax.scan(
        partial(sparse_backward, nearby),
        start_carry,
        (
            query_groups,
            key_groups,
            value_groups,
            allow_groups,
            sparse_lse,
            d_sparse.reshape(group_count, per_group, BLOCK, heads_dev, HD),
        ),
    )
    d_query_sparse = d_query_parts.reshape(block_count, BLOCK, heads_dev, HD)
    near_keys = near_keys.reshape(block_count, heads_dev, nearby, BLOCK, HD)
    near_values = near_values.reshape(block_count, heads_dev, nearby, BLOCK, HD)
    near_grads = jnp.stack([near_keys[:, :, :3], near_values[:, :, :3]])
    ext_grads = jnp.zeros((2, block_count + 2, heads_dev, BLOCK, HD), jnp.float32)
    for offset in range(3):
        ext_grads = ext_grads + jnp.pad(
            near_grads[:, :, :, offset], ((0, 0), (offset, 2 - offset), (0, 0), (0, 0), (0, 0))
        )
    rim_pair = jnp.stack([ext_grads[:, 0], ext_grads[:, block_count + 1]], axis=1)
    arrived = with_halo(rim_pair.astype(jnp.bfloat16), (("blk", 1),), 1).astype(rim_pair.dtype)
    inner_grads = ext_grads[:, 1 : block_count + 1]
    inner_grads = inner_grads.at[:, 0].add(arrived[:, 0]).at[:, block_count - 1].add(arrived[:, 3])
    far_grads = jnp.stack([near_keys[:, :, 3:], near_values[:, :, 3:]], axis=3).reshape(
        requests, 2, BLOCK, HD
    )
    outbox = (
        jnp.zeros((shards, capacity, 2, BLOCK, HD), jnp.float32)
        .at[source, slot_index]
        .set(far_grads)
    )
    arrived_slots = (
        lax.all_to_all(
            outbox.astype(jnp.bfloat16), "blk", split_axis=0, concat_axis=0, tiled=True
        ).astype(outbox.dtype)
        * filled[:, :, None, None, None]
    )
    landed = (
        jnp.zeros((block_count * heads_dev, 2, BLOCK, HD), jnp.float32)
        .at[send_rows.reshape(-1)]
        .add(arrived_slots.reshape(shards * capacity, 2, BLOCK, HD))
    )
    landed = landed.reshape(block_count, heads_dev, 2, BLOCK, HD)
    global_probs = jnp.exp(global_scores - global_lse[..., None])
    d_probs_global = jnp.einsum(
        "gqhd,khd->ghqk", d_global, value_wide, precision=lax.Precision.HIGHEST
    )
    delta_global = jnp.einsum(
        "gqhd,ghqd->ghq", d_global, global_out, precision=lax.Precision.HIGHEST
    )
    d_scores_global = (global_probs * (d_probs_global - delta_global[..., None])).astype(
        jnp.bfloat16
    )
    d_global_queries = (
        jnp.einsum("ghqk,khd->gqhd", d_scores_global, key_heads, preferred_element_type=jnp.float32)
        * attn_scale
    )
    d_keys_global = (
        jnp.einsum(
            "ghqk,gqhd->khd", d_scores_global, global_queries, preferred_element_type=jnp.float32
        )
        * attn_scale
    )
    d_values_global = jnp.einsum(
        "ghqk,gqhd->khd", global_probs, d_global, precision=lax.Precision.HIGHEST
    )
    returned = lax.psum(
        jnp.stack(
            [
                d_global_queries,
                global_sums[0].transpose(1, 2, 0, 3),
                global_sums[1].transpose(1, 2, 0, 3),
            ]
        ),
        "blk",
    )
    owned_grads = jnp.einsum(
        "ng,cgqhd->cnqhd", global_hits, returned, precision=lax.Precision.HIGHEST
    )
    d_query_total = d_query_sparse + owned_grads[0]
    d_key_total = (
        (inner_grads[0] + landed[:, :, 0]).transpose(0, 2, 1, 3)
        + d_keys_global.reshape(block_count, BLOCK, heads_dev, HD)
        + owned_grads[1]
    )
    d_value_total = (
        (inner_grads[1] + landed[:, :, 1]).transpose(0, 2, 1, 3)
        + d_values_global.reshape(block_count, BLOCK, heads_dev, HD)
        + owned_grads[2]
    )
    stacked = (
        jnp.stack([d_query_total, d_key_total, d_value_total])
        .reshape(3, row_count, group_width)
        .astype(jnp.bfloat16)
    )
    token_grads = lax.all_to_all(stacked, "head", split_axis=1, concat_axis=2, tiled=True)
    d_tokens = (
        d_mix
        + matmul_right(token_grads[0], full_query)
        + matmul_right(token_grads[1], full_key)
        + matmul_right(token_grads[2], full_value)
    )
    grads = (
        matmul_left(tokens, token_grads[0]),
        column_sum(token_grads[0]),
        matmul_left(tokens, token_grads[1]),
        matmul_left(tokens, token_grads[2]),
        column_sum(token_grads[2]),
        grad_out,
        grad_out_bias,
        grad_attn_gain,
        grad_attn_shift,
        grad_up,
        grad_up_bias,
        grad_down,
        grad_down_bias,
        grad_ffn_gain,
        grad_ffn_shift,
    )
    return (result.astype(jnp.bfloat16), d_tokens.astype(jnp.bfloat16), grads)


def body(
    inputs,
    cotangent,
    random_blocks,
    global_blocks,
    query_weight,
    query_bias,
    key_weight,
    value_weight,
    value_bias,
    out_weight,
    out_bias,
    attn_gain,
    attn_shift,
    up_weight,
    up_bias,
    down_weight,
    down_bias,
    ffn_gain,
    ffn_shift,
):
    weight_shards = (
        query_weight,
        query_bias,
        key_weight,
        value_weight,
        value_bias,
        out_weight,
        out_bias,
        attn_gain,
        attn_shift,
        up_weight,
        up_bias,
        down_weight,
        down_bias,
        ffn_gain,
        ffn_shift,
    )
    results = []
    input_grads = []
    totals = None
    for micro_index in range(inputs.shape[0]):
        weights = fetch_weights(*weight_shards)
        result, token_grad, grads = micro_batch(
            inputs[micro_index],
            cotangent[micro_index],
            random_blocks[micro_index],
            global_blocks[micro_index],
            weights,
        )
        grads = reduce_grads(grads)
        totals = (
            grads
            if totals is None
            else tuple((total_sum + extra_sum for total_sum, extra_sum in zip(totals, grads)))
        )
        results.append(result)
        input_grads.append(token_grad)
    return (jnp.stack(results), jnp.stack(input_grads)) + tuple(totals)


def solution(mesh):
    return jax.shard_map(
        near_body if (mesh.shape["blk"], mesh.shape["head"]) == (8, 4) else body,
        mesh=mesh,
        in_specs=(
            P(None, ("blk", "head"), None),
            P(None, ("blk", "head"), None),
            P(),
            P(),
            P(("blk", "head"), None),
            P(("blk", "head")),
            P(("blk", "head"), None),
            P(("blk", "head"), None),
            P(("blk", "head")),
            P(("blk", "head"), None),
            P(("blk", "head")),
            P(("blk", "head")),
            P(("blk", "head")),
            P(("blk", "head"), None),
            P(("blk", "head")),
            P(("blk", "head"), None),
            P(("blk", "head")),
            P(("blk", "head")),
            P(("blk", "head")),
        ),
        out_specs=(
            P(None, ("blk", "head"), None),
            P(None, ("blk", "head"), None),
            P(("blk", "head"), None),
            P(("blk", "head")),
            P(("blk", "head"), None),
            P(("blk", "head"), None),
            P(("blk", "head")),
            P(("blk", "head"), None),
            P(("blk", "head")),
            P(("blk", "head")),
            P(("blk", "head")),
            P(("blk", "head"), None),
            P(("blk", "head")),
            P(("blk", "head"), None),
            P(("blk", "head")),
            P(("blk", "head")),
            P(("blk", "head")),
        ),
        check_vma=False,
    )
```

```python
from functools import partial

import jax
import jax.numpy as jnp
from jax import lax
from jax.experimental import pallas as pl
from jax.experimental.pallas import tpu as pltpu
from jax.sharding import PartitionSpec as P

HEADS = 12
HD = 64
BLOCK = 64
RAND = 3
GLOB = 2


MESH = pl.DeviceIdType.MESH


def places():
    b = lax.axis_index("blk")
    h = lax.axis_index("head")
    core = b % 2
    x = (b // 2) % 2
    y = b // 4
    across_x = b + 2 - 4 * x
    across_y = b + 4 - 8 * y
    partner = b + 1 - 2 * core
    pair = h // 2
    line = (h, h + 1 - 2 * (h % 2), 2 - pair, 3 - 3 * pair)
    return b, h, core, x, y, across_x, across_y, partner, line


def meet(b, h):
    barrier = pltpu.get_barrier_semaphore()
    count = lax.axis_size("blk") * lax.axis_size("head")

    def tell(k, carry):
        other = (b * 4 + h + k) % count
        pl.semaphore_signal(barrier, inc=1, device_id=(other // 4, other % 4), device_id_type=MESH)
        return carry

    lax.fori_loop(1, count, tell, 0)
    pl.semaphore_wait(barrier, count - 1)


def pair_place(pair):
    at, along = pair % 6, pair // 6
    place = at + at // 3 + jnp.where(at > 3, 1, 0)
    x = place // 2 % 2
    return place + along % 2 * (2 - 4 * x), along


def place_pair(b, h):
    x = b // 2 % 2
    place = b + h % 2 * (2 - 4 * x)
    busy = jnp.logical_and(place != 3, place != 5)
    at = place - jnp.where(place > 3, 1, 0) - jnp.where(place > 5, 1, 0)
    return busy, jnp.minimum(h * 6 + at, 23)


def exchange(to_pairs, src, dst, sems, rows=slice(None)):
    send, recv, own = sems
    b = lax.axis_index("blk")
    h = lax.axis_index("head")
    me = b * 4 + h
    devices = lax.axis_size("blk") * lax.axis_size("head")
    pairs = 24
    busy, mine = place_pair(b, h)

    def other(at):
        if to_pairs:
            return pair_place(at)
        return at // 4, at % 4

    def copy(at):
        slot = me if to_pairs else mine
        return remote(
            src.at[at, rows], dst.at[slot, rows], send.at[at], recv.at[slot], other(at)
        )

    def away(at):
        place, along = other(at)
        return jnp.logical_not(jnp.logical_and(place == b, along == h))

    count = pairs if to_pairs else devices
    first = me * count // devices
    kept = pltpu.make_async_copy(
        src.at[mine if to_pairs else me, rows], dst.at[me if to_pairs else mine, rows], own
    )

    def begin():
        def one(k, carry):
            at = (first + k) % count

            @pl.when(away(at))
            def _():
                copy(at).start()

            return carry

        def everything():
            lax.fori_loop(0, count, one, 0)

        if to_pairs:
            everything()
            pl.when(busy)(kept.start)
        else:

            @pl.when(busy)
            def _():
                everything()
                kept.start()

    def arrive():
        def one(at, carry):
            here = dst.at[at, rows]
            landed = remote(here, here, send.at[0], recv.at[at], (b, h))
            if to_pairs:
                pl.when(at != me)(landed.wait_recv)
            else:
                place, along = pair_place(at)
                own_pair = jnp.logical_and(place == b, along == h)
                pl.when(jnp.logical_not(own_pair))(landed.wait_recv)
            return carry

        def everything():
            lax.fori_loop(0, devices if to_pairs else pairs, one, 0)

        if to_pairs:

            @pl.when(busy)
            def _():
                everything()
                kept.wait()
        else:
            everything()
            pl.when(busy)(kept.wait)

    def sent():
        def one(at, carry):
            pl.when(away(at))(copy(at).wait_send)
            return carry

        def everything():
            lax.fori_loop(0, count, one, 0)

        if to_pairs:
            everything()
        else:
            pl.when(busy)(everything)

    return begin, arrive, sent


def exchange_semaphores():
    dma = pltpu.SemaphoreType.DMA
    return [dma((32,)), dma((32,)), dma]


def remote(src, dst, send_sem, recv_sem, device):
    return pltpu.make_async_remote_copy(
        src_ref=src,
        dst_ref=dst,
        send_sem=send_sem,
        recv_sem=recv_sem,
        device_id=device,
        device_id_type=MESH,
    )


def gather_steps(kinds, ins, outs, sems):
    own_sem, line_send, line_recv, send, recv = sems
    b, h, core, x, y, across_x, across_y, partner, line = places()
    far_corner = across_x + 4 - 8 * y
    partner_x = partner + 2 - 4 * x
    partner_y = partner + 4 - 8 * y
    partner_corner = partner_x + 4 - 8 * y
    inner = jnp.logical_or(h == 1, h == 2)
    seen = jnp.where(inner, 2, 3)
    started = []
    started_inner = []
    locals_ = []

    def enter():
        meet(b, h)

    def piece(i, place):
        return ins[i].at[place] if kinds[i][0] else ins[i]

    def slot(i, shard, place):
        return outs[i].at[shard * 4 + place] if kinds[i][1] else outs[i].at[place]

    def part(ref, cut_):
        axis, start, size = cut_
        return ref.at[(slice(None),) * axis + (pl.ds(start, size),)]

    def go(copy, only_inner=False):
        if only_inner:

            @pl.when(inner)
            def _():
                copy.start()

            started_inner.append(copy)
        else:
            copy.start()
            started.append(copy)

    def along(i, src, landing, sender_at, receiver_at, place, only_inner=False):
        go(
            remote(
                src, landing, line_send.at[i, sender_at], line_recv.at[i, receiver_at], (b, place)
            ),
            only_inner,
        )

    def plane(i, d):
        src = piece(i, h) if d == 0 else slot(i, b, line[d])
        for k, other in enumerate((across_x, across_y, partner)):
            go(
                remote(
                    src, slot(i, b, line[d]), send.at[i, d, k], recv.at[i, d, k], (other, h)
                )
            )

    def arrived(i, d, k, shard, cut_=None):
        here = slot(i, shard, line[d])
        if cut_ is not None:
            here = part(here, cut_)
        remote(here, here, send.at[i, d, k], recv.at[i, d, k], (partner, h)).wait_recv()
        return here

    def begin(i):
        if kinds[i][0]:
            for d in (2, 3, 1):
                along(i, piece(i, line[d]), slot(i, b, h), d, 1 if d == 1 else seen, line[d])
        else:
            along(i, piece(i, h), slot(i, b, h), 2, 2, 3 - h, True)
            along(i, piece(i, h), slot(i, b, h), 1, 1, line[1])
        if kinds[i][1]:
            plane(i, 0)
        own = pltpu.make_async_copy(piece(i, h), slot(i, b, h), own_sem.at[i])
        own.start()
        locals_.append(own)

    def along_done(i, d):
        here = slot(i, b, line[d])
        remote(
            here, here, line_send.at[i, d], line_recv.at[i, d], (b, line[d])
        ).wait_recv()
        if not kinds[i][0]:
            if d == 1:
                along(i, here, here, 3, 3, 3 - h, True)
            else:
                along(i, here, here, d + 2, d, line[1], True)
        if kinds[i][1]:
            plane(i, d)

    def pass_on(i, d):
        first, second = kinds[i][2]
        for k, shard, cut_, onward in (
            (0, across_x, first, across_y),
            (1, across_y, second, across_x),
        ):
            here = arrived(i, d, k, shard)
            if cut_ is not None:
                go(
                    remote(
                        part(here, cut_),
                        part(here, cut_),
                        send.at[i, d, 6 + k],
                        recv.at[i, d, 6 + k],
                        (onward, h),
                    )
                )
            go(remote(here, here, send.at[i, d, 3 + k], recv.at[i, d, 3 + k], (partner, h)))

    def corner(i, d):
        for k, cut_ in enumerate(kinds[i][2]):
            if cut_ is not None:
                arrived(i, d, 6 + k, far_corner, cut_)
        here = slot(i, far_corner, line[d])
        go(remote(here, here, send.at[i, d, 5], recv.at[i, d, 5], (partner, h)))

    def finish(i):
        for d in range(4):
            for k, shard in ((2, partner), (3, partner_x), (4, partner_y), (5, partner_corner)):
                arrived(i, d, k, shard)

    def kept():
        for own in locals_:
            own.wait()
        locals_.clear()

    def sent():
        for copy in started:
            copy.wait_send()
        if started_inner:

            @pl.when(inner)
            def _():
                for copy in started_inner:
                    copy.wait_send()

    return enter, begin, along_done, pass_on, corner, finish, kept, sent


def gather_semaphores(n):
    dma = pltpu.SemaphoreType.DMA
    return [dma((n,)), dma((n, 6)), dma((n, 4)), dma((n, 4, 8)), dma((n, 4, 8))]


def spread_of(rows, width):
    shards, n = rows.shape
    total = shards * width
    lane = lax.broadcasted_iota(jnp.int32, (n, total), 0)
    column = lax.broadcasted_iota(jnp.int32, (n, total), 1)
    repeat = jnp.where(column % width == lane, 1.0, 0.0).astype(jnp.bfloat16)
    shard = lax.broadcasted_iota(jnp.int32, (shards, total), 0)
    column = lax.broadcasted_iota(jnp.int32, (shards, total), 1)
    return rows_sum(jnp.where(column // width == shard, dot(rows.astype(jnp.bfloat16), repeat), 0.0))


def front_kernel(kinds, *refs):
    (
        x_ref, wq_in, wk_in, wv_in, wo_in, up_in, down_in, *vectors,
    ) = refs[:16]
    (
        land_out, up_out, down_out, w_out, vec_ref, up_bias_ref,
        tile, chunk, mixed, rows_wide, w_ref, parts, join_sem, w_sem,
    ) = refs[16:30]
    rows = x_ref.shape[1]
    width = x_ref.shape[2]
    shards, depth, _ = mixed.shape
    enter, begin, along_done, pass_on, corner, finish, kept, sent = gather_steps(
        kinds,
        [chunk, up_in, down_in],
        [mixed, up_out, down_out],
        refs[33:],
    )
    begin_pairs, arrive_pairs, sent_pairs = exchange(True, parts, land_out, refs[30:33])
    joins = [
        pltpu.make_async_copy(ref, chunk.at[:, pl.ds(k * width, width)], join_sem.at[k])
        for k, ref in enumerate((wq_in, wk_in, wv_in, wo_in))
    ]
    for copy in joins:
        copy.start()
    tile[...] = jnp.zeros(tile.shape, jnp.float32)
    for k, ref in enumerate(vectors):
        tile[k, : ref.shape[0]] = ref[...].astype(jnp.float32)
    chunk[:, 4 * width :] = tile[...].astype(jnp.bfloat16)
    for copy in joins:
        copy.wait()
    enter()
    begin(0)
    begin(1)
    begin(2)
    along_done(0, 1)
    pass_on(0, 0)
    along_done(0, 2)
    along_done(1, 1)
    along_done(2, 1)
    pass_on(0, 1)
    corner(0, 0)
    along_done(0, 3)
    pass_on(1, 0)
    pass_on(2, 0)
    pass_on(0, 2)
    corner(0, 1)
    pass_on(0, 3)
    corner(0, 2)
    along_done(1, 2)
    along_done(2, 2)
    corner(0, 3)
    finish(0)
    kept()
    for s in range(0, 4 * width, width):
        part = mixed[:, :, s : s + width].astype(jnp.float32).reshape(width, width)
        w_ref[:, s : s + width] = part.astype(jnp.bfloat16)
    leave = pltpu.make_async_copy(w_ref, w_out, w_sem)
    leave.start()
    rows_wide[...] = mixed[:, :, 4 * width :].astype(jnp.float32)
    for k in range(8):
        vec_ref[k : k + 1, :] = spread_of(rows_wide[:, k, :], depth)
    up_bias_ref[...] = spread_of(rows_wide[:, 8, :], up_bias_ref.shape[1] // shards)
    tokens = x_ref[...].reshape(2 * rows, width)
    made = []
    for k in range(3):
        part = dot(tokens, w_ref[:, k * width : (k + 1) * width])
        if k != 1:
            part = part + vec_ref[k // 2 : k // 2 + 1, :]
        made.append(part.astype(jnp.bfloat16))
    q, k, v = made
    for pair in range(parts.shape[0]):
        col, at = pair // 2 * HD, pair % 2 * rows
        mid = at + rows // 2
        parts[pair, :rows] = jnp.concatenate(
            [halves(k[at : at + rows], col), halves(v[at : at + rows], col)], axis=1
        )
        parts[pair, rows:] = jnp.concatenate(
            [halves(q[at:mid], col), halves(q[mid : at + rows], col)], axis=1
        )
    begin_pairs()
    for i in (1, 2):
        pass_on(i, 1)
        corner(i, 0)
    for i in (1, 2):
        along_done(i, 3)
    for i in (1, 2):
        pass_on(i, 2)
        corner(i, 1)
    for i in (1, 2):
        pass_on(i, 3)
        corner(i, 2)
    for i in (1, 2):
        corner(i, 3)
    arrive_pairs()
    finish(1)
    finish(2)
    kept()
    leave.wait()
    sent()
    sent_pairs()


def front_call(tokens, matrices, up, down, vectors, collective):
    micro, rows, width = tokens.shape
    depth, ff = up.shape
    groups = lax.axis_size("head")
    devices = groups * lax.axis_size("blk")
    f32, bf16 = jnp.float32, jnp.bfloat16
    half = 2 * width
    kinds = [
        (False, True, (cut(1, 0, half), cut(1, half, half + 128))),
        (False, True, (cut(1, 0, ff), None)),
        (False, True, (None, cut(1, 0, width))),
    ]
    near = pl.BlockSpec(memory_space=pltpu.VMEM)
    far = pl.BlockSpec(memory_space=pl.ANY)
    return pl.pallas_call(
        partial(front_kernel, kinds),
        out_shape=(
            jax.ShapeDtypeStruct((devices, rows + rows // 2, 2 * HD), bf16),
            jax.ShapeDtypeStruct((devices,) + up.shape, bf16),
            jax.ShapeDtypeStruct((devices,) + down.shape, bf16),
            jax.ShapeDtypeStruct((width, 4 * width), bf16),
            jax.ShapeDtypeStruct((8, width), f32),
            jax.ShapeDtypeStruct((1, ff), f32),
        ),
        in_specs=[near] + [far] * 6 + [near] * 9,
        out_specs=(far,) * 4 + (near,) * 2,
        scratch_shapes=[
            pltpu.VMEM((depth, 128), f32),
            pltpu.VMEM((depth, 4 * width + 128), bf16),
            pltpu.VMEM((devices, depth, 4 * width + 128), bf16),
            pltpu.VMEM((devices, depth, 128), f32),
            pltpu.VMEM((width, 4 * width), bf16),
            pltpu.VMEM((HEADS * micro, rows + rows // 2, 2 * HD), bf16),
            pltpu.SemaphoreType.DMA((4,)),
            pltpu.SemaphoreType.DMA,
        ]
        + exchange_semaphores()
        + gather_semaphores(3),
        compiler_params=pltpu.CompilerParams(
            collective_id=collective, has_side_effects=True, vmem_limit_bytes=56 * 2**20
        ),
        name="front",
    )(tokens, *matrices, up, down, *vectors)


def scatter_steps(cuts, ins, bufs, sems):
    local_sem, line_send, line_recv, core_send, core_recv, send, recv = sems
    b, h, core, x, y, across_x, across_y, partner, line = places()
    seen = jnp.where(jnp.logical_or(h == 1, h == 2), 2, 3)
    chip = b // 2
    targets = (3 - chip, chip + 1 - 2 * x, chip + 2 - 4 * y, chip)
    started = []
    loads = {}
    order = (3, 2, 1, 0)

    def go(copy):
        copy.start()
        started.append(copy)

    def part(ref, cut):
        axis, start, size = cut
        return ref.at[(slice(None),) * axis + (pl.ds(start, size),)]

    def along(i, src, landing, d):
        go(
            remote(
                src, landing, line_send.at[i, d], line_recv.at[i, 1 if d == 1 else seen], (b, line[d])
            )
        )

    def begin(i, some=(0, 1, 2, 3)):
        from_partner, total = bufs[i][0], bufs[i][1]
        for t in some:
            go(
                remote(
                    ins[i].at[pl.ds((targets[t] * 2 + 1 - core) * 4, 4)],
                    from_partner.at[t],
                    core_send.at[i, t],
                    core_recv.at[i, t],
                    (partner, h),
                )
            )
            load = pltpu.make_async_copy(
                ins[i].at[pl.ds((targets[t] * 2 + core) * 4, 4)], total.at[t], local_sem.at[i, t]
            )
            load.start()
            loads[i, t] = load

    def wait_for(ref, i, d, k):
        remote(ref, ref, send.at[i, d, k], recv.at[i, d, k], (partner, h)).wait_recv()

    def ready(i, t):
        loads[i, t].wait()
        here = bufs[i][0].at[t]
        remote(here, here, core_send.at[i, t], core_recv.at[i, t], (partner, h)).wait_recv()

    def both_cores(i, t, d, extra=()):
        from_partner, total = bufs[i][0], bufs[i][1]
        place = line[d]
        value = total[t, place].astype(jnp.float32) + from_partner[t, place].astype(jnp.float32)
        for ref in extra:
            value = value + ref[d].astype(jnp.float32)
        total[t, place] = value.astype(total.dtype)

    def add_corner(i, t, d, ref, cut):
        total = bufs[i][1]
        axis, start, size = cut
        at = (t, line[d]) + (slice(None),) * axis + (pl.ds(start, size),)
        value = total[at].astype(jnp.float32) + ref[d].astype(jnp.float32)
        total[at] = value.astype(total.dtype)

    def corner(i):
        total = bufs[i][1]
        first, second = cuts[i]
        ready(i, 0)
        for d in order:
            both_cores(i, 0, d)
            mine = total.at[0, line[d]]
            if first is not None:
                go(remote(part(mine, first), bufs[i][2].at[d], send.at[i, d, 0], recv.at[i, d, 0], (across_x, h)))
            if second is not None:
                go(remote(part(mine, second), bufs[i][3].at[d], send.at[i, d, 1], recv.at[i, d, 1], (across_y, h)))

    def sides(i):
        total = bufs[i][1]
        first, second = cuts[i]
        ready(i, 1)
        ready(i, 2)
        for d in order:
            both_cores(i, 1, d)
            if second is not None:
                wait_for(bufs[i][3].at[d], i, d, 1)
                add_corner(i, 1, d, bufs[i][3], second)
            go(remote(total.at[1, line[d]], bufs[i][4].at[d], send.at[i, d, 2], recv.at[i, d, 2], (across_x, h)))
            both_cores(i, 2, d)
            if first is not None:
                wait_for(bufs[i][2].at[d], i, d, 0)
                add_corner(i, 2, d, bufs[i][2], first)
            go(remote(total.at[2, line[d]], bufs[i][5].at[d], send.at[i, d, 3], recv.at[i, d, 3], (across_y, h)))

    def own(i):
        total = bufs[i][1]
        ready(i, 3)
        for d in order:
            wait_for(bufs[i][4].at[d], i, d, 2)
            wait_for(bufs[i][5].at[d], i, d, 3)
            both_cores(i, 3, d, (bufs[i][4], bufs[i][5]))
            if d > 0:
                along(i, total.at[3, line[d]], bufs[i][6].at[1 if d == 1 else seen], d)

    def finish(i):
        value = bufs[i][1][3, h].astype(jnp.float32)
        for d in range(1, 4):
            landing = bufs[i][6].at[d]
            remote(
                landing, landing, line_send.at[i, d], line_recv.at[i, d], (b, line[d])
            ).wait_recv()
            value = value + bufs[i][6][d].astype(jnp.float32)
        return value

    def sent():
        for copy in started:
            copy.wait_send()

    def enter():
        meet(b, h)

    return enter, begin, corner, sides, own, finish, sent


def scatter_scratch(chunk, dtype, cuts):
    shapes = [(4, 4) + chunk, (4, 4) + chunk]
    for cut_ in cuts:
        size = [16, 128]
        if cut_ is not None:
            size = list(chunk)
            size[cut_[0]] = cut_[2]
        shapes.append((4,) + tuple(size))
    shapes += [(4,) + chunk] * 3
    return [pltpu.VMEM(shape, dtype) for shape in shapes]


def scatter_semaphores(n):
    dma = pltpu.SemaphoreType.DMA
    return [dma((n, 4))] * 5 + [dma((n, 4, 4))] * 2


UP, DOWN, OUT, QUERY, KEY, VALUE, SMALL = range(7)


def back_kernel(cuts, *refs):
    (
        parts_in, up_in, down_in, x_ref, mixed_in, d_mix_ref, g_out_ref, g_vec_ref, g_up_bias_ref,
        d_x_ref, g_outw_ref, g_query_ref, g_key_ref, g_value_ref, g_up_ref, g_down_ref, g_small_ref,
        land, terms, small, w_ref, d_q, d_k, d_v, w_sem,
    ), rest = refs[:25], list(refs[25:])
    q_sems, kv_sems, rest = rest[:3], rest[3:6], rest[6:]
    bufs = [rest[7 * i : 7 * i + 7] for i in range(len(cuts))]
    rows = x_ref.shape[1]
    width = x_ref.shape[2]
    _, shards, depth, _ = terms.shape
    ins = (up_in, down_in, terms.at[0], terms.at[1], terms.at[2], terms.at[3], small)
    enter, begin, corner, sides, own, finish, sent = scatter_steps(
        cuts, ins, bufs, rest[7 * len(cuts) :]
    )
    begin_q, arrive_q, sent_q = exchange(False, parts_in, land, q_sems, pl.ds(rows, rows // 2))
    begin_kv, arrive_kv, sent_kv = exchange(False, parts_in, land, kv_sems, pl.ds(0, rows))
    load = pltpu.make_async_copy(mixed_in.at[:, pl.ds(0, 3 * width)], w_ref, w_sem)
    load.start()
    def keep_term(at, value):
        terms[at] = value.reshape(shards, depth, width).astype(jnp.bfloat16)

    enter()
    begin_q()
    begin_kv()
    keep_term(0, g_out_ref[...].astype(jnp.float32))
    small[...] = jnp.zeros(small.shape, jnp.float32)
    arrive_q()
    begin(UP, (0,))
    begin(DOWN, (0,))
    corner(UP)
    corner(DOWN)
    begin(UP, (1, 2, 3,))
    begin(DOWN, (1, 2, 3,))
    arrive_kv()
    spans = []
    for m in range(2):
        top, mid = m * rows, m * rows + rows // 2
        spans.append((m, slice(top, top + rows), slice(top, mid), slice(mid, top + rows)))
    tokens = x_ref[...].reshape(2 * rows, width)
    for p in range(HEADS // 2):
        at = pl.ds(p * 2 * HD, 2 * HD)
        for m, _, early, late in spans:
            one, two = land[4 * p + m, rows:], land[4 * p + 2 + m, rows:]
            d_q[early, at] = jnp.concatenate([one[:, :HD], two[:, :HD]], axis=1)
            d_q[late, at] = jnp.concatenate([one[:, HD:], two[:, HD:]], axis=1)
    for p in range(HEADS // 2):
        at = pl.ds(p * 2 * HD, 2 * HD)
        for m, both, _, _ in spans:
            one, two = land[4 * p + m, :rows], land[4 * p + 2 + m, :rows]
            d_k[both, at] = jnp.concatenate([one[:, :HD], two[:, :HD]], axis=1)
            d_v[both, at] = jnp.concatenate([one[:, HD:], two[:, HD:]], axis=1)
    keep_term(1, dot(tokens, d_q[...], COLS))
    keep_term(2, dot(tokens, d_k[...], COLS))
    keep_term(3, dot(tokens, d_v[...], COLS))
    vectors = jnp.concatenate(
        [
            rows_sum(d_q[...].astype(jnp.float32)),
            rows_sum(d_v[...].astype(jnp.float32)),
            g_vec_ref[:6, :],
        ],
        axis=0,
    )
    up_bias = g_up_bias_ref[...]
    up_depth = up_bias.shape[1] // shards
    for s in range(shards):
        small[s, :8, :depth] = vectors[:, s * depth : (s + 1) * depth]
        small[s, 8:9, :up_depth] = up_bias[:, s * up_depth : (s + 1) * up_depth]
    begin(OUT)
    begin(QUERY)
    begin(KEY)
    begin(VALUE)
    begin(SMALL)
    corner(OUT)
    corner(QUERY)
    corner(KEY)
    corner(VALUE)
    corner(SMALL)
    sides(UP)
    sides(DOWN)
    sides(OUT)
    sides(QUERY)
    sides(KEY)
    sides(VALUE)
    sides(SMALL)
    own(UP)
    load.wait()
    d_x = d_mix_ref[...]
    for k, half_ref in enumerate((d_q, d_k, d_v)):
        d_x = d_x + dot(half_ref[...], w_ref[:, k * width : (k + 1) * width], ROWS)
    d_x_ref[...] = d_x.astype(jnp.bfloat16).reshape(2, rows, width)
    own(DOWN)
    g_up_ref[...] = finish(UP)
    own(OUT)
    own(QUERY)
    own(KEY)
    own(VALUE)
    own(SMALL)
    g_down_ref[...] = finish(DOWN)
    g_outw_ref[...] = finish(OUT)
    g_query_ref[...] = finish(QUERY)
    g_key_ref[...] = finish(KEY)
    g_value_ref[...] = finish(VALUE)
    g_small_ref[...] = finish(SMALL)
    sent_q()
    sent()
    sent_kv()


def back_call(parts, g_up, g_down, tokens, mixed, d_mix, g_out, g_vec, g_up_bias, collective):
    micro, rows, width = tokens.shape
    devices, depth, ff = g_up.shape
    f32, bf16 = jnp.float32, jnp.bfloat16
    one_way, other_way = (cut(1, 0, width), None), (None, cut(1, 0, width))
    cuts = [(cut(1, 0, ff), None), other_way, one_way, other_way, one_way, other_way, (cut(1, 0, 128), None)]
    square = (depth, width)
    chunks = [(g_up.shape[1:], bf16), (g_down.shape[1:], bf16)] + [(square, bf16)] * 4
    chunks += [((16, 128), f32)]
    scratch = [
        one for (chunk, dtype), c in zip(chunks, cuts) for one in scatter_scratch(chunk, dtype, c)
    ]
    near = pl.BlockSpec(memory_space=pltpu.VMEM)
    far = pl.BlockSpec(memory_space=pl.ANY)
    outs = [jax.ShapeDtypeStruct(tokens.shape, bf16)]
    outs += [jax.ShapeDtypeStruct(square, f32)] * 4
    outs += [
        jax.ShapeDtypeStruct((depth, ff), f32),
        jax.ShapeDtypeStruct(g_down.shape[1:], f32),
        jax.ShapeDtypeStruct((16, 128), f32),
    ]
    return pl.pallas_call(
        partial(back_kernel, cuts),
        out_shape=tuple(outs),
        in_specs=[far] * 3 + [near, far] + [near] * 4,
        out_specs=(near,) * len(outs),
        scratch_shapes=[
            pltpu.VMEM((HEADS * micro,) + parts.shape[1:], bf16),
            pltpu.VMEM((4, devices) + square, bf16),
            pltpu.VMEM((devices, 16, 128), f32),
            pltpu.VMEM((width, 3 * width), bf16),
        ]
        + [pltpu.VMEM((micro * rows, width), bf16)] * 3
        + [pltpu.SemaphoreType.DMA]
        + exchange_semaphores() * 2
        + scratch
        + scatter_semaphores(len(cuts)),
        compiler_params=pltpu.CompilerParams(
            collective_id=collective, has_side_effects=True, vmem_limit_bytes=61 * 2**20
        ),
        name="back",
    )(parts, g_up, g_down, tokens, mixed, d_mix, g_out, g_vec, g_up_bias)


def leave_kernel(*refs):
    *wholes, small_in = refs[:8]
    outs = refs[8:]
    for from_ref, to_ref in zip(wholes, outs):
        to_ref[...] = from_ref[...]
    for k, ref in enumerate(outs[7:]):
        ref[...] = small_in[k, : ref.shape[0]]


def leave_call(*arrays):
    *wholes, _ = arrays
    depth, width = wholes[1].shape
    f32 = jnp.float32
    outs = [jax.ShapeDtypeStruct(a.shape, a.dtype) for a in wholes]
    outs += [jax.ShapeDtypeStruct((depth,), f32)] * 8
    outs += [jax.ShapeDtypeStruct((wholes[6].shape[0],), f32)]
    near = pl.BlockSpec(memory_space=pltpu.VMEM)
    return pl.pallas_call(
        leave_kernel,
        out_shape=tuple(outs),
        in_specs=[near] * 8,
        out_specs=(near,) * len(outs),
        name="leave",
    )(*arrays)


def cut(axis, start, size):
    return (axis, start, size)


def lanes_of(shape, low):
    lane = lax.broadcasted_iota(jnp.int32, shape, len(shape) - 1)
    if isinstance(low, bool):
        return lane < HD if low else lane >= HD
    return lane // HD == jnp.where(low, 0, 1)


def dot(left_side, right_side, contract=((1,), (0,))):
    return lax.dot_general(
        left_side, right_side, (contract, ((), ())), preferred_element_type=jnp.float32
    )


ROWS = ((1,), (1,))
COLS = ((0,), (0,))


def halves(array, col):
    return array[:, col : col + HD]


def listed_rows(table_ref, blocks, n):
    rows = [jnp.maximum(n - 1, 0), n, jnp.minimum(n + 1, blocks - 1)]
    rows += [table_ref[n * RAND + r] for r in range(RAND)]
    return rows + [table_ref[blocks * RAND + g] for g in range(GLOB)]


def outside(here, total, listed):
    lane = lax.broadcasted_iota(jnp.int32, (1, listed * BLOCK), 1)
    before = jnp.logical_and(lane < BLOCK, here == 0)
    after = jnp.logical_and(
        jnp.logical_and(lane >= 2 * BLOCK, lane < 3 * BLOCK), here == total - 1
    )
    return jnp.where(jnp.logical_or(before, after), -jnp.inf, 0.0)


def only(value, low):
    return jnp.where(lanes_of(value.shape, low), value, jnp.zeros_like(value))


def turned(value):
    return jnp.concatenate([value[:, HD:], value[:, :HD]], axis=1)


def to_side(value, odd, low):
    if isinstance(odd, bool):
        return only(turned(value) if odd == low else value, low)
    return only(jnp.where((odd == 1) == low, turned(value), value), low)


def key_rows(ref, spot, step):
    return ref[pl.ds(spot, step), :2].reshape(step * 2 * BLOCK, 2 * HD)


GROUP = 8
STEP = 8


def attend_kernel(table_ref, land_ref, out_ref, lse_ref):
    devices = land_ref.shape[0]
    blocks = 2 * devices
    scale = jnp.bfloat16(HD ** (-0.5))

    def query_blocks(group, carry):
        kvs, scores = [], []
        for u in range(GROUP):
            n = group * GROUP + u
            rows = listed_rows(table_ref, blocks, n)
            kvs.append(jnp.concatenate([land_ref[r // 2, r % 2] for r in rows], axis=0))
            q = to_side(land_ref[group * (GROUP // 2) + u // 2, 2], u % 2 == 1, True) * scale
            scores.append(dot(q, kvs[-1], ROWS) + outside(n, blocks, len(rows)))
        raised = []
        for u, score in enumerate(scores):
            top = jnp.max(score, axis=1, keepdims=True)
            probs = jnp.exp(score - top)
            total_sum = jnp.sum(probs, axis=1, keepdims=True)
            raised.append((probs * (1.0 / total_sum)).astype(jnp.bfloat16))
            lse_ref[group * GROUP + u] = jnp.broadcast_to(
                top + jnp.log(total_sum), lse_ref.shape[1:]
            )
        outs = [dot(r, kv) for r, kv in zip(raised, kvs)]
        for u in range(0, GROUP, 2):
            out_ref[group * (GROUP // 2) + u // 2] = jnp.where(
                lanes_of(outs[u].shape, True), turned(outs[u]), outs[u + 1]
            ).astype(jnp.bfloat16)
        return carry

    def everything():
        lax.fori_loop(0, blocks // GROUP, query_blocks, 0)
        spots = range(0, devices, STEP)
        chosen = [table_ref[blocks * RAND + g] for g in range(GLOB)]
        q = jnp.concatenate(
            [to_side(land_ref[row // 2, 2], row % 2, True) for row in chosen], axis=0
        )
        scores = [dot(q * scale, key_rows(land_ref, spot, STEP), ROWS) for spot in spots]
        top = scores[0].max(axis=1, keepdims=True)
        for score in scores[1:]:
            top = jnp.maximum(top, score.max(axis=1, keepdims=True))
        raised = [jnp.exp(score - top) for score in scores]
        total_sum = sum(jnp.sum(r, axis=1, keepdims=True) for r in raised)
        out = sum(
            dot(r.astype(jnp.bfloat16), key_rows(land_ref, spot, STEP))
            for r, spot in zip(raised, spots)
        )
        out = out / total_sum
        lse = jnp.broadcast_to(top + jnp.log(total_sum), out.shape)
        for g, row in enumerate(chosen):
            at = slice(g * BLOCK, (g + 1) * BLOCK)
            lse_ref[row] = lse[at]
            new = jnp.where(row % 2 == 0, turned(out[at]), out[at]).astype(jnp.bfloat16)
            old = out_ref[row // 2]
            out_ref[row // 2] = jnp.where(lanes_of(old.shape, row % 2 == 0), new, old)

    pl.when(table_ref[blocks * RAND + GLOB] == 1)(everything)


def attend_call(table, land):
    spec = pl.BlockSpec(memory_space=pltpu.VMEM)
    devices, _, block, lanes = land.shape
    return pl.pallas_call(
        attend_kernel,
        out_shape=(
            jax.ShapeDtypeStruct((devices, block, lanes), jnp.bfloat16),
            jax.ShapeDtypeStruct((2 * devices, block, lanes), jnp.float32),
        ),
        in_specs=[pl.BlockSpec(memory_space=pltpu.SMEM), spec],
        out_specs=(spec, spec),
        compiler_params=pltpu.CompilerParams(vmem_limit_bytes=56 * 2**20),
        name="attend",
    )(table, land)


def attend_back_kernel(table_ref, land_ref, d_ref, out_ref, lse_ref, parts_ref, total_ref):
    devices = land_ref.shape[0]
    blocks = 2 * devices
    scale = jnp.bfloat16(HD ** (-0.5))

    def wide(column, width):
        return jnp.concatenate([column] * (width // column.shape[1]), axis=1)

    def pair_of(place, odd, keep):
        q = to_side(land_ref[place, 2], odd, True) * scale
        d = to_side(d_ref[place], odd, False)
        if keep is not None:
            d = d * keep
        out = to_side(out_ref[place], odd, False)
        delta = jnp.sum(d.astype(jnp.float32) * out.astype(jnp.float32), axis=1, keepdims=True)
        return q, d, delta

    def query_blocks(group, carry):
        listed, kvs, pairs, deltas, boths = [], [], [], [], []
        for u in range(GROUP):
            n = group * GROUP + u
            rows = listed_rows(table_ref, blocks, n)
            is_global = jnp.logical_or(n == rows[-1], n == rows[-2])
            keep = jnp.where(is_global, 0.0, 1.0).astype(jnp.bfloat16)
            kv = jnp.concatenate([land_ref[r // 2, r % 2] for r in rows], axis=0)
            q, d, delta = pair_of(group * (GROUP // 2) + u // 2, u % 2 == 1, keep)
            listed.append(rows)
            kvs.append(kv)
            pairs.append(jnp.concatenate([q, d], axis=0))
            deltas.append(delta)
            boths.append(dot(pairs[-1], kv, ROWS))
        weights = []
        for u, both in enumerate(boths):
            n = group * GROUP + u
            width = both.shape[1]
            scores = both[:BLOCK] + outside(n, blocks, width // BLOCK)
            probs = jnp.exp(scores - wide(lse_ref[n], width))
            d_scores = probs * (both[BLOCK:] - deltas[u])
            weights.append(
                jnp.concatenate(
                    [d_scores.astype(jnp.bfloat16), probs.astype(jnp.bfloat16)], axis=0
                )
            )
        outs = []
        for u, weight in enumerate(weights):
            d_kv = dot(weight, pairs[u], COLS)
            for at, r in enumerate(listed[u]):
                total_ref[r // 2, r % 2] += d_kv[at * BLOCK : (at + 1) * BLOCK]
            outs.append(dot(weight[:BLOCK], kvs[u]) * HD ** (-0.5))
        for u in range(0, GROUP, 2):
            parts_ref[group * (GROUP // 2) + u // 2, 2] = jnp.where(
                lanes_of(outs[u].shape, True), outs[u], turned(outs[u + 1])
            ).astype(jnp.bfloat16)
        return carry

    def everything():
        def clear(i, carry):
            total_ref[i] = jnp.zeros(total_ref.shape[1:], jnp.float32)
            return carry

        lax.fori_loop(0, devices, clear, 0)
        lax.fori_loop(0, blocks // GROUP, query_blocks, 0)
        chosen = [table_ref[blocks * RAND + g] for g in range(GLOB)]
        found = [pair_of(row // 2, row % 2, None) for row in chosen]
        both_rows = GLOB * BLOCK
        pairs = jnp.concatenate([f[0] for f in found] + [f[1] for f in found], axis=0)
        delta = jnp.concatenate([f[2] for f in found], axis=0)
        lse = jnp.concatenate([lse_ref[row] for row in chosen], axis=0)

        def some_keys(spot, d_q):
            kv = key_rows(land_ref, spot * STEP, STEP)
            both = dot(pairs, kv, ROWS)
            probs = jnp.exp(both[:both_rows] - wide(lse, both.shape[1]))
            d_scores = probs * (both[both_rows:] - delta)
            weight = jnp.concatenate(
                [d_scores.astype(jnp.bfloat16), probs.astype(jnp.bfloat16)], axis=0
            )
            total_ref[pl.ds(spot * STEP, STEP)] += dot(weight, pairs, COLS).reshape(
                STEP, 2, BLOCK, 2 * HD
            )
            return d_q + dot(weight[:both_rows], kv)

        d_q = lax.fori_loop(
            0, devices // STEP, some_keys, jnp.zeros((both_rows, 2 * HD), jnp.float32)
        )
        d_q = d_q * HD ** (-0.5)
        for g, row in enumerate(chosen):
            part = d_q[g * BLOCK : (g + 1) * BLOCK]
            new = jnp.where(row % 2 == 0, part, turned(part)).astype(jnp.bfloat16)
            old = parts_ref[row // 2, 2]
            parts_ref[row // 2, 2] = jnp.where(lanes_of(old.shape, row % 2 == 0), new, old)

        def give(i, carry):
            parts_ref[i, :2] = total_ref[i].astype(jnp.bfloat16)
            return carry

        lax.fori_loop(0, devices, give, 0)

    pl.when(table_ref[blocks * RAND + GLOB] == 1)(everything)


def attend_back_call(table, land, d, out, lse):
    spec = pl.BlockSpec(memory_space=pltpu.VMEM)
    devices, _, block, lanes = land.shape
    return pl.pallas_call(
        attend_back_kernel,
        out_shape=jax.ShapeDtypeStruct(land.shape, jnp.bfloat16),
        in_specs=[pl.BlockSpec(memory_space=pltpu.SMEM)] + [spec] * 4,
        out_specs=spec,
        scratch_shapes=[pltpu.VMEM((devices, 2, block, lanes), jnp.float32)],
        compiler_params=pltpu.CompilerParams(vmem_limit_bytes=60 * 2**20),
        name="attend_back",
    )(table, land, d, out, lse)


def centre(values):
    center = jnp.mean(values, axis=1, keepdims=True)
    centred = values - center
    spread = jnp.mean(centred * centred, axis=1, keepdims=True)
    inverse = lax.rsqrt(spread + 1e-12)
    return centred * inverse, inverse


def centre_back(hat, inverse, grad):
    return inverse * (
        grad
        - jnp.mean(grad, axis=1, keepdims=True)
        - hat * jnp.mean(grad * hat, axis=1, keepdims=True)
    )


def rows_sum(values):
    return jnp.sum(values, axis=0, keepdims=True)


WEIGHT_CHUNK = 1024


def dense_kernel(
    c_in, x_ref, cot_ref, wo_in, up_in, down_in, vec_ref, up_bias_ref,
    out_ref, d_mix_ref, d_land, g_out_ref, g_up_out, g_down_out, g_vec_ref, g_up_bias_ref,
    ctx, first, hat, low, low_t, act, slope, ffn, wo_ref, up_ref, down_ref, g_up_ref, g_down_ref, in_sem, out_sem,
    c_ref, d_c_ref, *pair_sems,
):
    rows = x_ref.shape[1]
    width = x_ref.shape[2]
    ff = up_ref.shape[1]
    chunk = WEIGHT_CHUNK
    fetches = [
        pltpu.make_async_copy(wo_in.at[:, pl.ds(3 * width, width)], wo_ref, in_sem.at[0]),
    ]
    for i in range(ff // chunk):
        at = pl.ds(i * chunk, chunk)
        fetches.append(pltpu.make_async_copy(up_in.at[:, at], up_ref.at[:, at], in_sem.at[2 * i + 1]))
        fetches.append(pltpu.make_async_copy(down_in.at[at], down_ref.at[at], in_sem.at[2 * i + 2]))
    for copy in fetches:
        copy.start()
    begin_c, arrive_c, sent_c = exchange(False, c_in, c_ref, pair_sems[:3])
    begin_d, arrive_d, sent_d = exchange(True, d_c_ref, d_land, pair_sems[3:])
    meet(lax.axis_index("blk"), lax.axis_index("head"))
    begin_c()
    arrive_c()
    out_bias, attn_gain, attn_shift, down_bias, ffn_gain, ffn_shift = (
        vec_ref[k : k + 1, :] for k in range(2, 8)
    )
    for p in range(HEADS // 2):
        at = pl.ds(p * 2 * HD, 2 * HD)
        for m in range(2):
            one, two = c_ref[4 * p + m], c_ref[4 * p + 2 + m]
            top, mid = m * rows, m * rows + rows // 2
            ctx[top:mid, at] = jnp.concatenate([one[:, :HD], two[:, :HD]], axis=1)
            ctx[mid : top + rows, at] = jnp.concatenate([one[:, HD:], two[:, HD:]], axis=1)
    tokens = x_ref[...].reshape(2 * rows, width).astype(jnp.float32)
    fetches[0].wait()
    hat_first, inverse_first = centre(tokens + dot(ctx[...], wo_ref[...]) + out_bias)
    hat[...] = hat_first
    first[...] = hat_first * attn_gain + attn_shift
    low[...] = first[...].astype(jnp.bfloat16)
    low_t[...] = first[...].T.astype(jnp.bfloat16)
    ffn[...] = first[...] + down_bias

    def forward(i):
        at = pl.ds(i * chunk, chunk)
        fetches[2 * i + 1].wait()
        fetches[2 * i + 2].wait()
        hidden = dot(low[...], up_ref[:, at]) + up_bias_ref[:, at]
        share = 0.5 * (1.0 + lax.erf(hidden * 0.7071067811865476))
        bell = jnp.exp(-0.5 * hidden * hidden) * 0.3989422804014327
        slope[:, at] = share + hidden * bell
        act_low = (hidden * share).astype(jnp.bfloat16)
        act[:, at] = act_low
        ffn[...] += dot(act_low, down_ref[at, :])

    for i in range(ff // chunk):
        forward(i)
    hat_second, inverse_second = centre(ffn[...])
    out_ref[...] = (
        (hat_second * ffn_gain + ffn_shift).astype(jnp.bfloat16).reshape(2, rows, width)
    )
    cot = cot_ref[...].reshape(2 * rows, width).astype(jnp.float32)
    g_vec_ref[4:5, :] = rows_sum(cot * hat_second)
    g_vec_ref[5:6, :] = rows_sum(cot)
    d_second = centre_back(hat_second, inverse_second, cot * ffn_gain)
    d_ffn = d_second.astype(jnp.bfloat16)
    g_vec_ref[3:4, :] = rows_sum(d_ffn.astype(jnp.float32))
    ffn[...] = d_second

    def leave(i):
        at = pl.ds(pl.multiple_of(i * chunk, chunk), chunk)
        return (
            pltpu.make_async_copy(g_up_ref.at[:, at], g_up_out.at[:, at], out_sem.at[0, i]),
            pltpu.make_async_copy(g_down_ref.at[at, :], g_down_out.at[at, :], out_sem.at[1, i]),
        )

    def backward(i, carry):
        at = pl.ds(pl.multiple_of(i * chunk, chunk), chunk)
        d_act = dot(d_ffn, down_ref[at, :], ROWS)
        d_hidden = (d_act * slope[:, at]).astype(jnp.bfloat16)
        g_up_bias_ref[:, at] = rows_sum(d_hidden.astype(jnp.float32))
        g_down_ref[at, :] = dot(act[:, at], d_ffn, COLS).astype(jnp.bfloat16)
        g_up_ref[:, at] = dot(low_t[...], d_hidden).astype(jnp.bfloat16)
        for copy in leave(i):
            copy.start()
        ffn[...] += dot(d_hidden, up_ref[:, at], ROWS)
        return carry

    lax.fori_loop(0, ff // chunk, backward, 0)
    d_first = ffn[...]
    g_vec_ref[1:2, :] = rows_sum(d_first * hat[...])
    g_vec_ref[2:3, :] = rows_sum(d_first)
    d_mix = centre_back(hat[...], inverse_first, d_first * attn_gain)
    d_mix_ref[...] = d_mix
    d_branch = d_mix.astype(jnp.bfloat16)
    g_vec_ref[0:1, :] = rows_sum(d_branch.astype(jnp.float32))
    g_vec_ref[6:8, :] = jnp.zeros((2, width), jnp.float32)
    g_out_ref[...] = dot(ctx[...], d_branch, COLS).astype(jnp.bfloat16)
    d_ctx = dot(d_branch, wo_ref[...], ROWS).astype(jnp.bfloat16)
    for pair in range(d_c_ref.shape[0]):
        col, top = pair // 2 * HD, pair % 2 * rows
        mid = top + rows // 2
        d_c_ref[pair] = jnp.concatenate(
            [halves(d_ctx[top:mid], col), halves(d_ctx[mid : top + rows], col)], axis=1
        )
    begin_d()
    for i in range(ff // chunk):
        for copy in leave(i):
            copy.wait()
    arrive_d()
    sent_c()
    sent_d()


def dense_call(c, tokens, cot, mixed, up, down, vec, up_bias, collective):
    micro, rows, width = tokens.shape
    ff = up.shape[1]
    both = micro * rows
    far = pl.BlockSpec(memory_space=pl.ANY)
    f32, bf16 = jnp.float32, jnp.bfloat16

    def full(shape):
        return pl.BlockSpec(memory_space=pltpu.VMEM)

    outs = (
        jax.ShapeDtypeStruct(tokens.shape, bf16),
        jax.ShapeDtypeStruct((both, width), f32),
        jax.ShapeDtypeStruct(c.shape, bf16),
        jax.ShapeDtypeStruct((width, width), bf16),
        jax.ShapeDtypeStruct((width, ff), bf16),
        jax.ShapeDtypeStruct((ff, width), bf16),
        jax.ShapeDtypeStruct((8, width), f32),
        jax.ShapeDtypeStruct((1, ff), f32),
    )
    return pl.pallas_call(
        dense_kernel,
        out_shape=outs,
        in_specs=[
            far,
            full(tokens.shape),
            full(cot.shape),
            far,
            far,
            far,
            full(vec.shape),
            full(up_bias.shape),
        ],
        out_specs=tuple(far if k in (2, 4, 5) else full(o.shape) for k, o in enumerate(outs)),
        scratch_shapes=[
            pltpu.VMEM((both, width), bf16),
            pltpu.VMEM((both, width), f32),
            pltpu.VMEM((both, width), f32),
            pltpu.VMEM((both, width), bf16),
            pltpu.VMEM((width, both), bf16),
            pltpu.VMEM((both, ff), bf16),
            pltpu.VMEM((both, ff), f32),
            pltpu.VMEM((both, width), f32),
            pltpu.VMEM((width, width), bf16),
            pltpu.VMEM((width, ff), bf16),
            pltpu.VMEM((ff, width), bf16),
            pltpu.VMEM((width, ff), bf16),
            pltpu.VMEM((ff, width), bf16),
            pltpu.SemaphoreType.DMA((1 + 2 * (ff // WEIGHT_CHUNK),)),
            pltpu.SemaphoreType.DMA((2, ff // WEIGHT_CHUNK)),
            pltpu.VMEM((HEADS * micro,) + c.shape[1:], bf16),
            pltpu.VMEM((HEADS * micro,) + c.shape[1:], bf16),
        ]
        + exchange_semaphores() * 2,
        compiler_params=pltpu.CompilerParams(
            collective_id=collective, has_side_effects=True, vmem_limit_bytes=60 * 2**20
        ),
        name="dense",
    )(c, tokens, cot, mixed, up, down, vec, up_bias)


def near_body(inputs, cotangent, random_blocks, global_blocks, *shards):
    (
        query_weight, query_bias, key_weight, value_weight, value_bias, out_weight, out_bias, attn_gain,
        attn_shift, up_weight, up_bias, down_weight, down_bias, ffn_gain, ffn_shift,
    ) = shards
    devices = lax.axis_size("head") * lax.axis_size("blk")
    micro, rows, width = inputs.shape
    depth = query_weight.shape[0]
    ff = up_weight.shape[1]
    land, up, down, mixed, vec, up_bias_row = front_call(
        inputs,
        (query_weight, key_weight, value_weight, out_weight),
        up_weight,
        down_weight,
        (
            query_bias, value_bias, out_bias, attn_gain, attn_shift, down_bias, ffn_gain, ffn_shift, up_bias,
        ),
        1,
    )
    up = up.reshape(width, ff)
    down = down.reshape(ff, width)
    busy, pair = place_pair(lax.axis_index("blk"), lax.axis_index("head"))
    head, at = pair // micro, pair % micro
    table = jnp.concatenate(
        [
            lax.dynamic_slice(
                random_blocks, (at, 0, head, 0), (1, random_blocks.shape[1], 1, RAND)
            ).reshape(-1),
            lax.dynamic_slice(global_blocks, (at, 0), (1, GLOB)).reshape(-1),
            busy.astype(jnp.int32)[None],
        ]
    )
    land = land.reshape(devices, 3, rows // 2, 2 * HD)
    attended, lse = attend_call(table, land)
    layer_out, d_mix, d_context, g_out, g_up, g_down, g_vec, g_up_bias = dense_call(
        attended, inputs, cotangent, mixed, up, down, vec, up_bias_row, 3
    )
    parts = attend_back_call(table, land, d_context, attended, lse)
    results = back_call(
        parts.reshape(devices, 3 * rows // 2, 2 * HD),
        g_up.reshape(devices, depth, ff),
        g_down.reshape(devices, -1, width),
        inputs,
        mixed,
        d_mix,
        g_out,
        g_vec,
        g_up_bias,
        5,
    )
    (
        input_grad, grad_out, grad_query, grad_key, grad_value, grad_up, grad_down, *vector, grad_up_bias,
    ) = leave_call(*results)
    return (
        layer_out, input_grad, grad_query, vector[0], grad_key, grad_value, vector[1], grad_out,
        vector[2], vector[3], vector[4], grad_up, grad_up_bias, grad_down, vector[5], vector[6], vector[7],
    )


def with_halo(cells, sides, width):
    for axis, dim in sides:
        count = lax.axis_size(axis)
        ends = count - 1
        head = lax.slice_in_dim(cells, 0, width, axis=dim)
        tail = lax.slice_in_dim(cells, cells.shape[dim] - width, cells.shape[dim], axis=dim)
        cells = jnp.concatenate(
            [
                lax.ppermute(tail, axis, [(i, (i + 1) % count) for i in range(ends)]),
                cells,
                lax.ppermute(head, axis, [((i + 1) % count, i) for i in range(ends)]),
            ],
            axis=dim,
        )
    return cells


def combined_all(part, axis, combine):
    gathered = jax.tree.map(lambda a: lax.all_gather(a, axis), part)

    def take(source):
        return jax.tree.map(lambda a: lax.dynamic_index_in_dim(a, source, 0, False), gathered)

    return lax.fori_loop(
        1, lax.axis_size(axis), lambda source, state: combine(state, take(source)), take(0)
    )


def taken(table, rows):
    return lax.map(lambda row: lax.dynamic_index_in_dim(table, row, 0, False), rows)


def layer_norm(values, norm_gain, norm_shift):
    center = jnp.mean(values, axis=-1, keepdims=True)
    centred = values - center
    spread = jnp.mean(centred * centred, axis=-1, keepdims=True)
    return centred * lax.rsqrt(spread + 1e-12) * norm_gain + norm_shift


def gelu_exact(values):
    return jax.nn.gelu(values, approximate=False)


def matmul(left_side, right_side):
    return jnp.dot(left_side, right_side, preferred_element_type=jnp.float32)


def matmul_left(left_side, right_side):
    return lax.dot_general(
        left_side, right_side, (((0,), (0,)), ((), ())), preferred_element_type=jnp.float32
    )


def matmul_right(left_side, right_side):
    return lax.dot_general(
        left_side, right_side, (((1,), (1,)), ((), ())), preferred_element_type=jnp.float32
    )


def column_sum(values):
    return jnp.sum(values.astype(jnp.float32), axis=0)


def combine_parts(earlier, later_part):
    joint_top = jnp.maximum(earlier[0], later_part[0])
    first_factor = jnp.exp(earlier[0] - joint_top)
    second_factor = jnp.exp(later_part[0] - joint_top)
    return (
        joint_top,
        earlier[1] * first_factor + later_part[1] * second_factor,
        earlier[2] * first_factor[..., None] + later_part[2] * second_factor[..., None],
    )


def fetch_weights(
    query_weight,
    query_bias,
    key_weight,
    value_weight,
    value_bias,
    out_weight,
    out_bias,
    attn_gain,
    attn_shift,
    up_weight,
    up_bias,
    down_weight,
    down_bias,
    ffn_gain,
    ffn_shift,
):
    return (
        lax.all_gather(query_weight, ("blk", "head"), axis=0, tiled=True),
        lax.all_gather(query_bias, ("blk", "head"), axis=0, tiled=True),
        lax.all_gather(key_weight, ("blk", "head"), axis=0, tiled=True),
        lax.all_gather(value_weight, ("blk", "head"), axis=0, tiled=True),
        lax.all_gather(value_bias, ("blk", "head"), axis=0, tiled=True),
        lax.all_gather(out_weight, ("blk", "head"), axis=0, tiled=True),
        lax.all_gather(out_bias, ("blk", "head"), axis=0, tiled=True),
        lax.all_gather(attn_gain, ("blk", "head"), axis=0, tiled=True),
        lax.all_gather(attn_shift, ("blk", "head"), axis=0, tiled=True),
        lax.all_gather(up_weight, ("blk", "head"), axis=0, tiled=True),
        lax.all_gather(up_bias, ("blk", "head"), axis=0, tiled=True),
        lax.all_gather(down_weight, ("blk", "head"), axis=0, tiled=True),
        lax.all_gather(down_bias, ("blk", "head"), axis=0, tiled=True),
        lax.all_gather(ffn_gain, ("blk", "head"), axis=0, tiled=True),
        lax.all_gather(ffn_shift, ("blk", "head"), axis=0, tiled=True),
    )


def reduce_grads(totals):
    return (
        lax.psum_scatter(totals[0], ("blk", "head"), scatter_dimension=0, tiled=True),
        lax.psum_scatter(totals[1], ("blk", "head"), scatter_dimension=0, tiled=True),
        lax.psum_scatter(totals[2], ("blk", "head"), scatter_dimension=0, tiled=True),
        lax.psum_scatter(totals[3], ("blk", "head"), scatter_dimension=0, tiled=True),
        lax.psum_scatter(totals[4], ("blk", "head"), scatter_dimension=0, tiled=True),
        lax.psum_scatter(totals[5], ("blk", "head"), scatter_dimension=0, tiled=True),
        lax.psum_scatter(totals[6], ("blk", "head"), scatter_dimension=0, tiled=True),
        lax.psum_scatter(totals[7], ("blk", "head"), scatter_dimension=0, tiled=True),
        lax.psum_scatter(totals[8], ("blk", "head"), scatter_dimension=0, tiled=True),
        lax.psum_scatter(totals[9], ("blk", "head"), scatter_dimension=0, tiled=True),
        lax.psum_scatter(totals[10], ("blk", "head"), scatter_dimension=0, tiled=True),
        lax.psum_scatter(totals[11], ("blk", "head"), scatter_dimension=0, tiled=True),
        lax.psum_scatter(totals[12], ("blk", "head"), scatter_dimension=0, tiled=True),
        lax.psum_scatter(totals[13], ("blk", "head"), scatter_dimension=0, tiled=True),
        lax.psum_scatter(totals[14], ("blk", "head"), scatter_dimension=0, tiled=True),
    )


def sparse_forward(packed):
    group_queries, group_keys, group_values, group_allowed = packed
    attn_scale = HD ** (-0.5)
    scores = (
        jnp.einsum("gqhd,ghkd->ghqk", group_queries, group_keys, preferred_element_type=jnp.float32)
        * attn_scale
    )
    scores = jnp.where(group_allowed[:, None, None, :], scores, -jnp.inf)
    row_top = jnp.max(scores, axis=-1, keepdims=True)
    raised = jnp.exp(scores - row_top)
    row_total = jnp.sum(raised, axis=-1, keepdims=True)
    probs_low = (raised / row_total).astype(jnp.bfloat16)
    output = jnp.einsum(
        "ghqk,ghkd->gqhd", probs_low, group_values, preferred_element_type=jnp.float32
    )
    return (output, (row_top + jnp.log(row_total))[..., 0])


def sparse_backward(nearby, carried, packed):
    group_queries, group_keys, group_values, group_allowed, group_lse, group_grad = packed
    attn_scale = HD ** (-0.5)
    per_group = group_queries.shape[0]
    heads_dev = group_queries.shape[2]
    scores = (
        jnp.einsum("gqhd,ghkd->ghqk", group_queries, group_keys, preferred_element_type=jnp.float32)
        * attn_scale
    )
    scores = jnp.where(group_allowed[:, None, None, :], scores, -jnp.inf)
    probs = jnp.exp(scores - group_lse[..., None])
    d_probs = jnp.einsum(
        "gqhd,ghkd->ghqk", group_grad, group_values, preferred_element_type=jnp.float32
    )
    row_delta = jnp.sum(probs * d_probs, axis=-1, keepdims=True)
    d_scores = (probs * (d_probs - row_delta)).astype(jnp.bfloat16)
    d_queries = (
        jnp.einsum("ghqk,ghkd->gqhd", d_scores, group_keys, preferred_element_type=jnp.float32)
        * attn_scale
    )
    d_keys = (
        jnp.einsum("ghqk,gqhd->ghkd", d_scores, group_queries, preferred_element_type=jnp.float32)
        * attn_scale
    )
    d_values = jnp.einsum(
        "ghqk,gqhd->ghkd",
        probs.astype(jnp.bfloat16),
        group_grad,
        preferred_element_type=jnp.float32,
    )
    d_keys = d_keys.reshape(per_group, heads_dev, -1, BLOCK, HD)
    d_values = d_values.reshape(per_group, heads_dev, -1, BLOCK, HD)
    carried = (
        carried[0] + jnp.sum(d_keys[:, :, nearby:], axis=0),
        carried[1] + jnp.sum(d_values[:, :, nearby:], axis=0),
    )
    return (carried, (d_queries, d_keys[:, :, :nearby], d_values[:, :, :nearby]))


def micro_batch(tokens, cotangent_rows, random_rows, global_rows, weights):
    (
        full_query,
        full_query_bias,
        full_key,
        full_value,
        full_value_bias,
        full_out,
        full_out_bias,
        full_attn_gain,
        full_attn_shift,
        full_up,
        full_up_bias,
        full_down,
        full_down_bias,
        full_ffn_gain,
        full_ffn_shift,
    ) = weights
    attn_scale = HD ** (-0.5)
    shards = lax.axis_size("blk")
    head_groups = lax.axis_size("head")
    shard_index = lax.axis_index("blk")
    group_index = lax.axis_index("head")
    heads_dev = HEADS // head_groups
    group_width = heads_dev * HD
    listed = 3 + RAND + GLOB
    nearby = 3 + RAND
    projected = jnp.stack(
        [
            matmul(tokens, full_query) + full_query_bias,
            matmul(tokens, full_key),
            matmul(tokens, full_value) + full_value_bias,
        ]
    ).astype(jnp.bfloat16)
    by_head = lax.all_to_all(projected, "head", split_axis=2, concat_axis=1, tiled=True)
    row_count = by_head.shape[1]
    block_count = row_count // BLOCK
    blocks_all = block_count * shards
    key_rows = by_head[1]
    value_rows = by_head[2]
    padded = with_halo(by_head[1:3], (("blk", 1),), BLOCK)
    extended = padded.reshape(2, block_count + 2, BLOCK, heads_dev, HD).transpose(0, 1, 3, 2, 4)
    window = jnp.stack([extended[:, offset : offset + block_count] for offset in range(3)], axis=3)
    block_ids = shard_index * block_count + jnp.arange(block_count, dtype=jnp.int32)
    neighbour = block_ids[:, None] + jnp.arange(-1, 2, dtype=jnp.int32)[None, :]
    inside = (neighbour >= 0) & (neighbour < blocks_all)
    head_table = lax.dynamic_slice_in_dim(random_rows, group_index * heads_dev, heads_dev, 1)
    requests = block_count * heads_dev * RAND
    all_requests = head_table.reshape(shards, requests)
    capacity = (requests + shards - 1) // shards + 1
    wanted = lax.dynamic_slice_in_dim(all_requests, shard_index, 1, 0)[0]
    source = wanted // block_count
    place = jnp.arange(requests, dtype=jnp.int32)
    earlier = (place[:, None] > place[None, :]).astype(jnp.int32)
    same_source = (source[:, None] == source[None, :]).astype(jnp.int32)
    slot_index = jnp.sum(earlier * same_source, axis=1)
    mine_mask = (all_requests // block_count == shard_index).astype(jnp.int32)
    send_order = jnp.sum(earlier[None] * mine_mask[:, None, :], axis=2)
    match_mask = mine_mask[:, :, None] * (
        send_order[:, :, None] == jnp.arange(capacity, dtype=jnp.int32)[None, None, :]
    ).astype(jnp.int32)
    head_of = jnp.arange(requests, dtype=jnp.int32) // RAND % heads_dev
    row_of = all_requests % block_count * heads_dev + head_of[None, :]
    send_rows = jnp.sum(match_mask * row_of[:, :, None], axis=1)
    filled = jnp.sum(match_mask, axis=1).astype(jnp.float32)
    block_table = (
        by_head[1:3]
        .reshape(2, block_count, BLOCK, heads_dev, HD)
        .transpose(1, 3, 0, 2, 4)
        .reshape(block_count * heads_dev, 2, BLOCK, HD)
    )
    outgoing = taken(block_table, send_rows.reshape(-1))
    incoming = lax.all_to_all(outgoing, "blk", split_axis=0, concat_axis=0, tiled=True)
    fetched = taken(incoming, source * capacity + slot_index).reshape(
        block_count, heads_dev, RAND, 2, BLOCK, HD
    )
    owner_shard = global_rows // block_count
    present = owner_shard == shard_index
    local_block = global_rows % block_count
    own_rows = jnp.stack(
        [
            lax.dynamic_index_in_dim(
                by_head.reshape(3, block_count, BLOCK, group_width), local_block[g], 1, False
            )
            for g in range(GLOB)
        ],
        axis=1,
    )
    shared = lax.psum(
        jnp.where(present[None, :, None, None], own_rows.astype(jnp.float32), 0.0), "blk"
    ).astype(jnp.bfloat16)
    shared_pairs = shared[1:3].reshape(2, GLOB, BLOCK, heads_dev, HD).transpose(0, 3, 1, 2, 4)

    def listed_blocks(which):
        near_part = window[which]
        random_part = fetched[:, :, :, which]
        global_part = jnp.broadcast_to(
            shared_pairs[which][None], (block_count, heads_dev, GLOB, BLOCK, HD)
        )
        return jnp.concatenate([near_part, random_part, global_part], axis=2).reshape(
            block_count, heads_dev, listed * BLOCK, HD
        )

    per_group = min(8, block_count)
    group_count = block_count // per_group
    query_groups = by_head[0].reshape(group_count, per_group, BLOCK, heads_dev, HD)
    key_groups = listed_blocks(0).reshape(group_count, per_group, heads_dev, listed * BLOCK, HD)
    value_groups = listed_blocks(1).reshape(group_count, per_group, heads_dev, listed * BLOCK, HD)
    allowed = jnp.repeat(
        jnp.concatenate([inside, jnp.ones((block_count, RAND + GLOB), jnp.bool_)], axis=1),
        BLOCK,
        axis=1,
    )
    allow_groups = allowed.reshape(group_count, per_group, listed * BLOCK)
    sparse_out, sparse_lse = lax.map(
        sparse_forward, (query_groups, key_groups, value_groups, allow_groups)
    )
    global_queries = shared[0].reshape(GLOB, BLOCK, heads_dev, HD)
    key_heads = key_rows.reshape(row_count, heads_dev, HD)
    value_wide = value_rows.reshape(row_count, heads_dev, HD).astype(jnp.float32)
    global_scores = (
        jnp.einsum("gqhd,khd->ghqk", global_queries, key_heads, preferred_element_type=jnp.float32)
        * attn_scale
    )
    global_top = jnp.max(global_scores, axis=-1)
    global_raised = jnp.exp(global_scores - global_top[..., None])
    merged = combined_all(
        (
            global_top,
            jnp.sum(global_raised, axis=-1),
            jnp.einsum(
                "ghqk,khd->ghqd", global_raised, value_wide, precision=lax.Precision.HIGHEST
            ),
        ),
        "blk",
        combine_parts,
    )
    global_out = merged[2] / merged[1][..., None]
    global_lse = merged[0] + jnp.log(merged[1])
    global_hits = (block_ids[:, None] == global_rows[None, :]).astype(jnp.float32)
    is_global = jnp.sum(global_hits, axis=1) > 0
    replaced = jnp.einsum("ng,ghqd->nqhd", global_hits, global_out, precision=lax.Precision.HIGHEST)
    context = jnp.where(
        is_global[:, None, None, None],
        replaced,
        sparse_out.reshape(block_count, BLOCK, heads_dev, HD),
    )
    context_rows = context.reshape(row_count, group_width).astype(jnp.bfloat16)
    context_tokens = lax.all_to_all(context_rows, "head", split_axis=0, concat_axis=1, tiled=True)
    branch = matmul(context_tokens, full_out) + full_out_bias
    first_in = tokens.astype(jnp.float32) + branch
    first_norm, first_pull = jax.vjp(
        layer_norm,
        first_in,
        full_attn_gain.astype(jnp.float32),
        full_attn_shift.astype(jnp.float32),
    )
    first_low = first_norm.astype(jnp.bfloat16)
    hidden = matmul(first_low, full_up) + full_up_bias
    act_value, gelu_pull = jax.vjp(gelu_exact, hidden)
    act_low = act_value.astype(jnp.bfloat16)
    ffn_out = matmul(act_low, full_down) + full_down_bias
    result, second_pull = jax.vjp(
        layer_norm,
        first_norm + ffn_out,
        full_ffn_gain.astype(jnp.float32),
        full_ffn_shift.astype(jnp.float32),
    )
    d_second, grad_ffn_gain, grad_ffn_shift = second_pull(cotangent_rows.astype(jnp.float32))
    d_ffn = d_second.astype(jnp.bfloat16)
    grad_down = matmul_left(act_low, d_ffn)
    grad_down_bias = column_sum(d_ffn)
    (d_hidden,) = gelu_pull(matmul_right(d_ffn, full_down))
    d_hidden_low = d_hidden.astype(jnp.bfloat16)
    grad_up = matmul_left(first_low, d_hidden_low)
    grad_up_bias = column_sum(d_hidden_low)
    d_first = d_second + matmul_right(d_hidden_low, full_up)
    d_mix, grad_attn_gain, grad_attn_shift = first_pull(d_first)
    d_branch = d_mix.astype(jnp.bfloat16)
    grad_out = matmul_left(context_tokens, d_branch)
    grad_out_bias = column_sum(d_branch)
    d_context = matmul_right(d_branch, full_out).astype(jnp.bfloat16)
    d_heads = lax.all_to_all(d_context, "head", split_axis=1, concat_axis=0, tiled=True).reshape(
        block_count, BLOCK, heads_dev, HD
    )
    d_sparse = jnp.where(is_global[:, None, None, None], jnp.zeros_like(d_heads), d_heads)
    d_global = lax.psum(
        jnp.where(
            present[:, None, None, None], taken(d_heads, local_block).astype(jnp.float32), 0.0
        ),
        "blk",
    )
    start_carry = (
        jnp.zeros((heads_dev, GLOB, BLOCK, HD), jnp.float32),
        jnp.zeros((heads_dev, GLOB, BLOCK, HD), jnp.float32),
    )
    global_sums, (d_query_parts, near_keys, near_values) = lax.scan(
        partial(sparse_backward, nearby),
        start_carry,
        (
            query_groups,
            key_groups,
            value_groups,
            allow_groups,
            sparse_lse,
            d_sparse.reshape(group_count, per_group, BLOCK, heads_dev, HD),
        ),
    )
    d_query_sparse = d_query_parts.reshape(block_count, BLOCK, heads_dev, HD)
    near_keys = near_keys.reshape(block_count, heads_dev, nearby, BLOCK, HD)
    near_values = near_values.reshape(block_count, heads_dev, nearby, BLOCK, HD)
    near_grads = jnp.stack([near_keys[:, :, :3], near_values[:, :, :3]])
    ext_grads = jnp.zeros((2, block_count + 2, heads_dev, BLOCK, HD), jnp.float32)
    for offset in range(3):
        ext_grads = ext_grads + jnp.pad(
            near_grads[:, :, :, offset], ((0, 0), (offset, 2 - offset), (0, 0), (0, 0), (0, 0))
        )
    rim_pair = jnp.stack([ext_grads[:, 0], ext_grads[:, block_count + 1]], axis=1)
    arrived = with_halo(rim_pair.astype(jnp.bfloat16), (("blk", 1),), 1).astype(rim_pair.dtype)
    inner_grads = ext_grads[:, 1 : block_count + 1]
    inner_grads = inner_grads.at[:, 0].add(arrived[:, 0]).at[:, block_count - 1].add(arrived[:, 3])
    far_grads = jnp.stack([near_keys[:, :, 3:], near_values[:, :, 3:]], axis=3).reshape(
        requests, 2, BLOCK, HD
    )
    outbox = (
        jnp.zeros((shards, capacity, 2, BLOCK, HD), jnp.float32)
        .at[source, slot_index]
        .set(far_grads)
    )
    arrived_slots = (
        lax.all_to_all(
            outbox.astype(jnp.bfloat16), "blk", split_axis=0, concat_axis=0, tiled=True
        ).astype(outbox.dtype)
        * filled[:, :, None, None, None]
    )
    landed = (
        jnp.zeros((block_count * heads_dev, 2, BLOCK, HD), jnp.float32)
        .at[send_rows.reshape(-1)]
        .add(arrived_slots.reshape(shards * capacity, 2, BLOCK, HD))
    )
    landed = landed.reshape(block_count, heads_dev, 2, BLOCK, HD)
    global_probs = jnp.exp(global_scores - global_lse[..., None])
    d_probs_global = jnp.einsum(
        "gqhd,khd->ghqk", d_global, value_wide, precision=lax.Precision.HIGHEST
    )
    delta_global = jnp.einsum(
        "gqhd,ghqd->ghq", d_global, global_out, precision=lax.Precision.HIGHEST
    )
    d_scores_global = (global_probs * (d_probs_global - delta_global[..., None])).astype(
        jnp.bfloat16
    )
    d_global_queries = (
        jnp.einsum("ghqk,khd->gqhd", d_scores_global, key_heads, preferred_element_type=jnp.float32)
        * attn_scale
    )
    d_keys_global = (
        jnp.einsum(
            "ghqk,gqhd->khd", d_scores_global, global_queries, preferred_element_type=jnp.float32
        )
        * attn_scale
    )
    d_values_global = jnp.einsum(
        "ghqk,gqhd->khd", global_probs, d_global, precision=lax.Precision.HIGHEST
    )
    returned = lax.psum(
        jnp.stack(
            [
                d_global_queries,
                global_sums[0].transpose(1, 2, 0, 3),
                global_sums[1].transpose(1, 2, 0, 3),
            ]
        ),
        "blk",
    )
    owned_grads = jnp.einsum(
        "ng,cgqhd->cnqhd", global_hits, returned, precision=lax.Precision.HIGHEST
    )
    d_query_total = d_query_sparse + owned_grads[0]
    d_key_total = (
        (inner_grads[0] + landed[:, :, 0]).transpose(0, 2, 1, 3)
        + d_keys_global.reshape(block_count, BLOCK, heads_dev, HD)
        + owned_grads[1]
    )
    d_value_total = (
        (inner_grads[1] + landed[:, :, 1]).transpose(0, 2, 1, 3)
        + d_values_global.reshape(block_count, BLOCK, heads_dev, HD)
        + owned_grads[2]
    )
    stacked = (
        jnp.stack([d_query_total, d_key_total, d_value_total])
        .reshape(3, row_count, group_width)
        .astype(jnp.bfloat16)
    )
    token_grads = lax.all_to_all(stacked, "head", split_axis=1, concat_axis=2, tiled=True)
    d_tokens = (
        d_mix
        + matmul_right(token_grads[0], full_query)
        + matmul_right(token_grads[1], full_key)
        + matmul_right(token_grads[2], full_value)
    )
    grads = (
        matmul_left(tokens, token_grads[0]),
        column_sum(token_grads[0]),
        matmul_left(tokens, token_grads[1]),
        matmul_left(tokens, token_grads[2]),
        column_sum(token_grads[2]),
        grad_out,
        grad_out_bias,
        grad_attn_gain,
        grad_attn_shift,
        grad_up,
        grad_up_bias,
        grad_down,
        grad_down_bias,
        grad_ffn_gain,
        grad_ffn_shift,
    )
    return (result.astype(jnp.bfloat16), d_tokens.astype(jnp.bfloat16), grads)


def body(
    inputs,
    cotangent,
    random_blocks,
    global_blocks,
    query_weight,
    query_bias,
    key_weight,
    value_weight,
    value_bias,
    out_weight,
    out_bias,
    attn_gain,
    attn_shift,
    up_weight,
    up_bias,
    down_weight,
    down_bias,
    ffn_gain,
    ffn_shift,
):
    weight_shards = (
        query_weight,
        query_bias,
        key_weight,
        value_weight,
        value_bias,
        out_weight,
        out_bias,
        attn_gain,
        attn_shift,
        up_weight,
        up_bias,
        down_weight,
        down_bias,
        ffn_gain,
        ffn_shift,
    )
    results = []
    input_grads = []
    totals = None
    for micro_index in range(inputs.shape[0]):
        weights = fetch_weights(*weight_shards)
        result, token_grad, grads = micro_batch(
            inputs[micro_index],
            cotangent[micro_index],
            random_blocks[micro_index],
            global_blocks[micro_index],
            weights,
        )
        grads = reduce_grads(grads)
        totals = (
            grads
            if totals is None
            else tuple((total_sum + extra_sum for total_sum, extra_sum in zip(totals, grads)))
        )
        results.append(result)
        input_grads.append(token_grad)
    return (jnp.stack(results), jnp.stack(input_grads)) + tuple(totals)


def solution(mesh):
    return jax.shard_map(
        near_body if (mesh.shape["blk"], mesh.shape["head"]) == (8, 4) else body,
        mesh=mesh,
        in_specs=(
            P(None, ("blk", "head"), None),
            P(None, ("blk", "head"), None),
            P(),
            P(),
            P(("blk", "head"), None),
            P(("blk", "head")),
            P(("blk", "head"), None),
            P(("blk", "head"), None),
            P(("blk", "head")),
            P(("blk", "head"), None),
            P(("blk", "head")),
            P(("blk", "head")),
            P(("blk", "head")),
            P(("blk", "head"), None),
            P(("blk", "head")),
            P(("blk", "head"), None),
            P(("blk", "head")),
            P(("blk", "head")),
            P(("blk", "head")),
        ),
        out_specs=(
            P(None, ("blk", "head"), None),
            P(None, ("blk", "head"), None),
            P(("blk", "head"), None),
            P(("blk", "head")),
            P(("blk", "head"), None),
            P(("blk", "head"), None),
            P(("blk", "head")),
            P(("blk", "head"), None),
            P(("blk", "head")),
            P(("blk", "head")),
            P(("blk", "head")),
            P(("blk", "head"), None),
            P(("blk", "head")),
            P(("blk", "head"), None),
            P(("blk", "head")),
            P(("blk", "head")),
            P(("blk", "head")),
        ),
        check_vma=False,
    )
```

```python
from functools import partial

import jax
import jax.numpy as jnp
from jax import lax
from jax.experimental import pallas as pl
from jax.experimental.pallas import tpu as pltpu
from jax.sharding import PartitionSpec as P

HEADS = 12
HD = 64
BLOCK = 64
RAND = 3
GLOB = 2


MESH = pl.DeviceIdType.MESH


def places():
    b = lax.axis_index("blk")
    h = lax.axis_index("head")
    core = b % 2
    x = (b // 2) % 2
    y = b // 4
    across_x = b + 2 - 4 * x
    across_y = b + 4 - 8 * y
    partner = b + 1 - 2 * core
    pair = h // 2
    line = (h, h + 1 - 2 * (h % 2), 2 - pair, 3 - 3 * pair)
    return b, h, core, x, y, across_x, across_y, partner, line


def meet(b, h):
    barrier = pltpu.get_barrier_semaphore()
    count = lax.axis_size("blk") * lax.axis_size("head")

    def tell(k, carry):
        other = (b * 4 + h + k) % count
        pl.semaphore_signal(barrier, inc=1, device_id=(other // 4, other % 4), device_id_type=MESH)
        return carry

    lax.fori_loop(1, count, tell, 0)
    pl.semaphore_wait(barrier, count - 1)


def pair_place(pair):
    at, along = pair % 6, pair // 6
    place = at + at // 3 + jnp.where(at > 3, 1, 0)
    x = place // 2 % 2
    return place + along % 2 * (2 - 4 * x), along


def place_pair(b, h):
    x = b // 2 % 2
    place = b + h % 2 * (2 - 4 * x)
    busy = jnp.logical_and(place != 3, place != 5)
    at = place - jnp.where(place > 3, 1, 0) - jnp.where(place > 5, 1, 0)
    return busy, jnp.minimum(h * 6 + at, 23)


def exchange(to_pairs, src, dst, sems, rows=slice(None)):
    send, recv, own = sems
    b = lax.axis_index("blk")
    h = lax.axis_index("head")
    me = b * 4 + h
    devices = lax.axis_size("blk") * lax.axis_size("head")
    pairs = 24
    busy, mine = place_pair(b, h)

    def other(at):
        if to_pairs:
            return pair_place(at)
        return at // 4, at % 4

    def copy(at):
        slot = me if to_pairs else mine
        return remote(
            src.at[at, rows], dst.at[slot, rows], send.at[at], recv.at[slot], other(at)
        )

    def away(at):
        place, along = other(at)
        return jnp.logical_not(jnp.logical_and(place == b, along == h))

    count = pairs if to_pairs else devices
    first = me * count // devices
    kept = pltpu.make_async_copy(
        src.at[mine if to_pairs else me, rows], dst.at[me if to_pairs else mine, rows], own
    )

    def begin():
        def one(k, carry):
            at = (first + k) % count

            @pl.when(away(at))
            def _():
                copy(at).start()

            return carry

        def everything():
            lax.fori_loop(0, count, one, 0)

        if to_pairs:
            everything()
            pl.when(busy)(kept.start)
        else:

            @pl.when(busy)
            def _():
                everything()
                kept.start()

    def arrive():
        def one(at, carry):
            here = dst.at[at, rows]
            landed = remote(here, here, send.at[0], recv.at[at], (b, h))
            if to_pairs:
                pl.when(at != me)(landed.wait_recv)
            else:
                place, along = pair_place(at)
                own_pair = jnp.logical_and(place == b, along == h)
                pl.when(jnp.logical_not(own_pair))(landed.wait_recv)
            return carry

        def everything():
            lax.fori_loop(0, devices if to_pairs else pairs, one, 0)

        if to_pairs:

            @pl.when(busy)
            def _():
                everything()
                kept.wait()
        else:
            everything()
            pl.when(busy)(kept.wait)

    def sent():
        def one(at, carry):
            pl.when(away(at))(copy(at).wait_send)
            return carry

        def everything():
            lax.fori_loop(0, count, one, 0)

        if to_pairs:
            everything()
        else:
            pl.when(busy)(everything)

    return begin, arrive, sent


def exchange_semaphores():
    dma = pltpu.SemaphoreType.DMA
    return [dma((32,)), dma((32,)), dma]


def remote(src, dst, send_sem, recv_sem, device):
    return pltpu.make_async_remote_copy(
        src_ref=src,
        dst_ref=dst,
        send_sem=send_sem,
        recv_sem=recv_sem,
        device_id=device,
        device_id_type=MESH,
    )


def gather_steps(kinds, ins, outs, sems):
    own_sem, line_send, line_recv, send, recv = sems
    b, h, core, x, y, across_x, across_y, partner, line = places()
    far_corner = across_x + 4 - 8 * y
    partner_x = partner + 2 - 4 * x
    partner_y = partner + 4 - 8 * y
    partner_corner = partner_x + 4 - 8 * y
    inner = jnp.logical_or(h == 1, h == 2)
    seen = jnp.where(inner, 2, 3)
    started = []
    started_inner = []
    locals_ = []

    def enter():
        meet(b, h)

    def piece(i, place):
        return ins[i].at[place] if kinds[i][0] else ins[i]

    def slot(i, shard, place):
        return outs[i].at[shard * 4 + place] if kinds[i][1] else outs[i].at[place]

    def part(ref, cut_):
        axis, start, size = cut_
        return ref.at[(slice(None),) * axis + (pl.ds(start, size),)]

    def go(copy, only_inner=False):
        if only_inner:

            @pl.when(inner)
            def _():
                copy.start()

            started_inner.append(copy)
        else:
            copy.start()
            started.append(copy)

    def along(i, src, landing, sender_at, receiver_at, place, only_inner=False):
        go(
            remote(
                src, landing, line_send.at[i, sender_at], line_recv.at[i, receiver_at], (b, place)
            ),
            only_inner,
        )

    def plane(i, d):
        src = piece(i, h) if d == 0 else slot(i, b, line[d])
        for k, other in enumerate((across_x, across_y, partner)):
            go(
                remote(
                    src, slot(i, b, line[d]), send.at[i, d, k], recv.at[i, d, k], (other, h)
                )
            )

    def arrived(i, d, k, shard, cut_=None):
        here = slot(i, shard, line[d])
        if cut_ is not None:
            here = part(here, cut_)
        remote(here, here, send.at[i, d, k], recv.at[i, d, k], (partner, h)).wait_recv()
        return here

    def begin(i):
        if kinds[i][0]:
            for d in (2, 3, 1):
                along(i, piece(i, line[d]), slot(i, b, h), d, 1 if d == 1 else seen, line[d])
        else:
            along(i, piece(i, h), slot(i, b, h), 2, 2, 3 - h, True)
            along(i, piece(i, h), slot(i, b, h), 1, 1, line[1])
        if kinds[i][1]:
            plane(i, 0)
        own = pltpu.make_async_copy(piece(i, h), slot(i, b, h), own_sem.at[i])
        own.start()
        locals_.append(own)

    def along_done(i, d):
        here = slot(i, b, line[d])
        remote(
            here, here, line_send.at[i, d], line_recv.at[i, d], (b, line[d])
        ).wait_recv()
        if not kinds[i][0]:
            if d == 1:
                along(i, here, here, 3, 3, 3 - h, True)
            else:
                along(i, here, here, d + 2, d, line[1], True)
        if kinds[i][1]:
            plane(i, d)

    def pass_on(i, d):
        first, second = kinds[i][2]
        for k, shard, cut_, onward in (
            (0, across_x, first, across_y),
            (1, across_y, second, across_x),
        ):
            here = arrived(i, d, k, shard)
            if cut_ is not None:
                go(
                    remote(
                        part(here, cut_),
                        part(here, cut_),
                        send.at[i, d, 6 + k],
                        recv.at[i, d, 6 + k],
                        (onward, h),
                    )
                )
            go(remote(here, here, send.at[i, d, 3 + k], recv.at[i, d, 3 + k], (partner, h)))

    def corner(i, d):
        for k, cut_ in enumerate(kinds[i][2]):
            if cut_ is not None:
                arrived(i, d, 6 + k, far_corner, cut_)
        here = slot(i, far_corner, line[d])
        go(remote(here, here, send.at[i, d, 5], recv.at[i, d, 5], (partner, h)))

    def finish(i):
        for d in range(4):
            for k, shard in ((2, partner), (3, partner_x), (4, partner_y), (5, partner_corner)):
                arrived(i, d, k, shard)

    def kept():
        for own in locals_:
            own.wait()
        locals_.clear()

    def sent():
        for copy in started:
            copy.wait_send()
        if started_inner:

            @pl.when(inner)
            def _():
                for copy in started_inner:
                    copy.wait_send()

    return enter, begin, along_done, pass_on, corner, finish, kept, sent


def gather_semaphores(n):
    dma = pltpu.SemaphoreType.DMA
    return [dma((n,)), dma((n, 6)), dma((n, 4)), dma((n, 4, 8)), dma((n, 4, 8))]


def spread_of(rows, width):
    shards, n = rows.shape
    total = shards * width
    lane = lax.broadcasted_iota(jnp.int32, (n, total), 0)
    column = lax.broadcasted_iota(jnp.int32, (n, total), 1)
    repeat = jnp.where(column % width == lane, 1.0, 0.0).astype(jnp.bfloat16)
    shard = lax.broadcasted_iota(jnp.int32, (shards, total), 0)
    column = lax.broadcasted_iota(jnp.int32, (shards, total), 1)
    return rows_sum(jnp.where(column // width == shard, dot(rows.astype(jnp.bfloat16), repeat), 0.0))


def front_kernel(kinds, *refs):
    (
        x_ref, wq_in, wk_in, wv_in, wo_in, up_in, down_in, *vectors,
    ) = refs[:16]
    (
        land_out, up_out, down_out, w_out, vec_ref, up_bias_ref,
        tile, chunk, mixed, rows_wide, w_ref, parts, join_sem, w_sem,
    ) = refs[16:30]
    rows = x_ref.shape[1]
    width = x_ref.shape[2]
    shards, depth, _ = mixed.shape
    enter, begin, along_done, pass_on, corner, finish, kept, sent = gather_steps(
        kinds,
        [chunk, up_in, down_in],
        [mixed, up_out, down_out],
        refs[33:],
    )
    begin_pairs, arrive_pairs, sent_pairs = exchange(True, parts, land_out, refs[30:33])
    joins = [
        pltpu.make_async_copy(ref, chunk.at[:, pl.ds(k * width, width)], join_sem.at[k])
        for k, ref in enumerate((wq_in, wk_in, wv_in, wo_in))
    ]
    for copy in joins:
        copy.start()
    tile[...] = jnp.zeros(tile.shape, jnp.float32)
    for k, ref in enumerate(vectors):
        tile[k, : ref.shape[0]] = ref[...].astype(jnp.float32)
    chunk[:, 4 * width :] = tile[...].astype(jnp.bfloat16)
    for copy in joins:
        copy.wait()
    enter()
    begin(0)
    begin(1)
    begin(2)
    along_done(0, 1)
    pass_on(0, 0)
    along_done(0, 2)
    along_done(1, 1)
    along_done(2, 1)
    pass_on(0, 1)
    corner(0, 0)
    along_done(0, 3)
    pass_on(1, 0)
    pass_on(2, 0)
    pass_on(0, 2)
    corner(0, 1)
    pass_on(0, 3)
    corner(0, 2)
    along_done(1, 2)
    along_done(2, 2)
    corner(0, 3)
    finish(0)
    kept()
    for s in range(0, 4 * width, width):
        part = mixed[:, :, s : s + width].astype(jnp.float32).reshape(width, width)
        w_ref[:, s : s + width] = part.astype(jnp.bfloat16)
    leave = pltpu.make_async_copy(w_ref, w_out, w_sem)
    leave.start()
    rows_wide[...] = mixed[:, :, 4 * width :].astype(jnp.float32)
    for k in range(8):
        vec_ref[k : k + 1, :] = spread_of(rows_wide[:, k, :], depth)
    up_bias_ref[...] = spread_of(rows_wide[:, 8, :], up_bias_ref.shape[1] // shards)
    tokens = x_ref[...].reshape(2 * rows, width)
    made = []
    for k in range(3):
        part = dot(tokens, w_ref[:, k * width : (k + 1) * width])
        if k != 1:
            part = part + vec_ref[k // 2 : k // 2 + 1, :]
        made.append(part.astype(jnp.bfloat16))
    q, k, v = made
    for pair in range(parts.shape[0]):
        col, at = pair // 2 * HD, pair % 2 * rows
        mid = at + rows // 2
        parts[pair, :rows] = jnp.concatenate(
            [halves(k[at : at + rows], col), halves(v[at : at + rows], col)], axis=1
        )
        parts[pair, rows:] = jnp.concatenate(
            [halves(q[at:mid], col), halves(q[mid : at + rows], col)], axis=1
        )
    begin_pairs()
    for i in (1, 2):
        pass_on(i, 1)
        corner(i, 0)
    for i in (1, 2):
        along_done(i, 3)
    for i in (1, 2):
        pass_on(i, 2)
        corner(i, 1)
    for i in (1, 2):
        pass_on(i, 3)
        corner(i, 2)
    for i in (1, 2):
        corner(i, 3)
    arrive_pairs()
    finish(1)
    finish(2)
    kept()
    leave.wait()
    sent()
    sent_pairs()


def front_call(tokens, matrices, up, down, vectors, collective):
    micro, rows, width = tokens.shape
    depth, ff = up.shape
    groups = lax.axis_size("head")
    devices = groups * lax.axis_size("blk")
    f32, bf16 = jnp.float32, jnp.bfloat16
    half = 2 * width
    kinds = [
        (False, True, (cut(1, 0, half), cut(1, half, half + 128))),
        (False, True, (cut(1, 0, ff), None)),
        (False, True, (None, cut(1, 0, width))),
    ]
    near = pl.BlockSpec(memory_space=pltpu.VMEM)
    far = pl.BlockSpec(memory_space=pl.ANY)
    return pl.pallas_call(
        partial(front_kernel, kinds),
        out_shape=(
            jax.ShapeDtypeStruct((devices, rows + rows // 2, 2 * HD), bf16),
            jax.ShapeDtypeStruct((devices,) + up.shape, bf16),
            jax.ShapeDtypeStruct((devices,) + down.shape, bf16),
            jax.ShapeDtypeStruct((width, 4 * width), bf16),
            jax.ShapeDtypeStruct((8, width), f32),
            jax.ShapeDtypeStruct((1, ff), f32),
        ),
        in_specs=[near] + [far] * 6 + [near] * 9,
        out_specs=(far,) * 4 + (near,) * 2,
        scratch_shapes=[
            pltpu.VMEM((depth, 128), f32),
            pltpu.VMEM((depth, 4 * width + 128), bf16),
            pltpu.VMEM((devices, depth, 4 * width + 128), bf16),
            pltpu.VMEM((devices, depth, 128), f32),
            pltpu.VMEM((width, 4 * width), bf16),
            pltpu.VMEM((HEADS * micro, rows + rows // 2, 2 * HD), bf16),
            pltpu.SemaphoreType.DMA((4,)),
            pltpu.SemaphoreType.DMA,
        ]
        + exchange_semaphores()
        + gather_semaphores(3),
        compiler_params=pltpu.CompilerParams(
            collective_id=collective, has_side_effects=True, vmem_limit_bytes=56 * 2**20
        ),
        name="front",
    )(tokens, *matrices, up, down, *vectors)


def scatter_steps(cuts, ins, bufs, sems, made=()):
    local_sem, line_send, line_recv, core_send, core_recv, send, recv = sems
    b, h, core, x, y, across_x, across_y, partner, line = places()
    seen = jnp.where(jnp.logical_or(h == 1, h == 2), 2, 3)
    chip = b // 2
    targets = (3 - chip, chip + 1 - 2 * x, chip + 2 - 4 * y, chip)
    started = []
    loads = {}
    order = (3, 2, 1, 0)

    def go(copy):
        copy.start()
        started.append(copy)

    def part(ref, cut):
        axis, start, size = cut
        return ref.at[(slice(None),) * axis + (pl.ds(start, size),)]

    def along(i, src, landing, d):
        go(
            remote(
                src, landing, line_send.at[i, d], line_recv.at[i, 1 if d == 1 else seen], (b, line[d])
            )
        )

    def fetch(i, at, src, dst):
        loads[i, at] = pltpu.make_async_copy(src, dst, local_sem.at[i, at])
        loads[i, at].start()

    def begin(i, some=(0, 1, 2, 3)):
        if i in made:
            fetch(i, 0, ins[i][0], bufs[i][1].at[pl.ds(1, 3)])
            fetch(i, 1, ins[i][1], bufs[i][2])
            fetch(i, 2, ins[i][2], bufs[i][3])
            return
        from_partner, total = bufs[i][0], bufs[i][1]
        for t in some:
            go(
                remote(
                    ins[i].at[pl.ds((targets[t] * 2 + 1 - core) * 4, 4)],
                    from_partner.at[t],
                    core_send.at[i, t],
                    core_recv.at[i, t],
                    (partner, h),
                )
            )
            fetch(i, t, ins[i].at[pl.ds((targets[t] * 2 + core) * 4, 4)], total.at[t])

    def wait_for(ref, i, d, k):
        remote(ref, ref, send.at[i, d, k], recv.at[i, d, k], (partner, h)).wait_recv()

    def ready(i, t):
        loads[i, t].wait()
        here = bufs[i][0].at[t]
        remote(here, here, core_send.at[i, t], core_recv.at[i, t], (partner, h)).wait_recv()

    def both_cores(i, t, d, extra=()):
        from_partner, total = bufs[i][0], bufs[i][1]
        place = line[d]
        value = total[t, place].astype(jnp.float32)
        if i not in made:
            value = value + from_partner[t, place].astype(jnp.float32)
        elif not extra:
            return
        for ref in extra:
            value = value + ref[d].astype(jnp.float32)
        total[t, place] = value.astype(total.dtype)

    def add_corner(i, t, d, ref, cut):
        total = bufs[i][1]
        axis, start, size = cut
        at = (t, line[d]) + (slice(None),) * axis + (pl.ds(start, size),)
        value = total[at].astype(jnp.float32) + ref[d].astype(jnp.float32)
        total[at] = value.astype(total.dtype)

    def corner(i):
        total = bufs[i][1]
        first, second = cuts[i]
        ready(i, 0)
        for d in order:
            both_cores(i, 0, d)
            mine = total.at[0, line[d]]
            if first is not None:
                go(remote(part(mine, first), bufs[i][2].at[d], send.at[i, d, 0], recv.at[i, d, 0], (across_x, h)))
            if second is not None:
                go(remote(part(mine, second), bufs[i][3].at[d], send.at[i, d, 1], recv.at[i, d, 1], (across_y, h)))

    def corner_arrived(i, d, at):
        if cuts[i][at] is not None and i not in made:
            wait_for(bufs[i][2 + at].at[d], i, d, at)

    def leave(i, left, sems_):
        copies = []
        for t in (1, 2, 3):
            ready(i, t)
            for d in order:
                both_cores(i, t, d)
            copies.append(pltpu.make_async_copy(bufs[i][1].at[t], left.at[t - 1], sems_.at[i, t]))
            copies[-1].start()
        for d in order:
            for at in range(2):
                corner_arrived(i, d, at)
        return copies

    def sides(i):
        total = bufs[i][1]
        first, second = cuts[i]
        if i in made:
            for at in range(3):
                loads[i, at].wait()
        else:
            ready(i, 1)
            ready(i, 2)
        for d in order:
            both_cores(i, 1, d)
            if second is not None:
                corner_arrived(i, d, 1)
                add_corner(i, 1, d, bufs[i][3], second)
            go(remote(total.at[1, line[d]], bufs[i][4].at[d], send.at[i, d, 2], recv.at[i, d, 2], (across_x, h)))
            both_cores(i, 2, d)
            if first is not None:
                corner_arrived(i, d, 0)
                add_corner(i, 2, d, bufs[i][2], first)
            go(remote(total.at[2, line[d]], bufs[i][5].at[d], send.at[i, d, 3], recv.at[i, d, 3], (across_y, h)))

    def own(i):
        total = bufs[i][1]
        if i not in made:
            ready(i, 3)
        for d in order:
            wait_for(bufs[i][4].at[d], i, d, 2)
            wait_for(bufs[i][5].at[d], i, d, 3)
            both_cores(i, 3, d, (bufs[i][4], bufs[i][5]))
            if d > 0:
                along(i, total.at[3, line[d]], bufs[i][6].at[1 if d == 1 else seen], d)

    def finish(i):
        value = bufs[i][1][3, h].astype(jnp.float32)
        for d in range(1, 4):
            landing = bufs[i][6].at[d]
            remote(
                landing, landing, line_send.at[i, d], line_recv.at[i, d], (b, line[d])
            ).wait_recv()
            value = value + bufs[i][6][d].astype(jnp.float32)
        return value

    def sent():
        for copy in started:
            copy.wait_send()

    def enter():
        meet(b, h)

    return enter, begin, corner, leave, sides, own, finish, sent


def weight_cuts(ff, width):
    return tuple((cut(1, 0, n // 2), cut(1, n // 2, n // 2)) for n in (ff, width))


def scatter_scratch(chunk, dtype, cuts, made=False):
    shapes = [(16, 128) if made else (4, 4) + chunk, (4, 4) + chunk]
    for cut_ in cuts:
        size = [16, 128]
        if cut_ is not None:
            size = list(chunk)
            size[cut_[0]] = cut_[2]
        shapes.append((4,) + tuple(size))
    shapes += [(4,) + chunk] * 3
    return [pltpu.VMEM(shape, dtype) for shape in shapes]


def scatter_semaphores(n):
    dma = pltpu.SemaphoreType.DMA
    return [dma((n, 4))] * 5 + [dma((n, 4, 4))] * 2


UP, DOWN, OUT, QUERY, KEY, VALUE, SMALL = range(7)


def back_kernel(cuts, *refs):
    (
        parts_in, up_left, up_first, up_second, down_left, down_first, down_second, x_ref, mixed_in, d_mix_ref, g_out_ref, g_vec_ref, g_up_bias_ref,
        d_x_ref, g_outw_ref, g_query_ref, g_key_ref, g_value_ref, g_up_ref, g_down_ref, g_small_ref,
        land, terms, small, w_ref, d_q, d_k, d_v, w_sem,
    ), rest = refs[:29], list(refs[29:])
    q_sems, kv_sems, rest = rest[:3], rest[3:6], rest[6:]
    bufs = [rest[7 * i : 7 * i + 7] for i in range(len(cuts))]
    rows = x_ref.shape[1]
    width = x_ref.shape[2]
    _, shards, depth, _ = terms.shape
    ins = ((up_left, up_first, up_second), (down_left, down_first, down_second), terms.at[0], terms.at[1], terms.at[2], terms.at[3], small)
    enter, begin, corner, _, sides, own, finish, sent = scatter_steps(
        cuts, ins, bufs, rest[7 * len(cuts) :], (UP, DOWN)
    )
    begin_q, arrive_q, sent_q = exchange(False, parts_in, land, q_sems, pl.ds(rows, rows // 2))
    begin_kv, arrive_kv, sent_kv = exchange(False, parts_in, land, kv_sems, pl.ds(0, rows))
    load = pltpu.make_async_copy(mixed_in.at[:, pl.ds(0, 3 * width)], w_ref, w_sem)
    load.start()
    def keep_term(at, value):
        terms[at] = value.reshape(shards, depth, width).astype(jnp.bfloat16)

    def keep_term(at, value):
        terms[at] = value.reshape(shards, depth, width).astype(jnp.bfloat16)

    begin(UP)
    begin(DOWN)
    enter()
    begin_q()
    begin_kv()
    keep_term(0, g_out_ref[...].astype(jnp.float32))
    small[...] = jnp.zeros(small.shape, jnp.float32)
    begin(OUT)
    sides(UP)
    sides(DOWN)
    corner(OUT)
    own(UP)
    arrive_q()
    arrive_kv()
    spans = []
    for m in range(2):
        top, mid = m * rows, m * rows + rows // 2
        spans.append((m, slice(top, top + rows), slice(top, mid), slice(mid, top + rows)))
    tokens = x_ref[...].reshape(2 * rows, width)
    for p in range(HEADS // 2):
        at = pl.ds(p * 2 * HD, 2 * HD)
        for m, _, early, late in spans:
            one, two = land[4 * p + m, rows:], land[4 * p + 2 + m, rows:]
            d_q[early, at] = jnp.concatenate([one[:, :HD], two[:, :HD]], axis=1)
            d_q[late, at] = jnp.concatenate([one[:, HD:], two[:, HD:]], axis=1)
    for p in range(HEADS // 2):
        at = pl.ds(p * 2 * HD, 2 * HD)
        for m, both, _, _ in spans:
            one, two = land[4 * p + m, :rows], land[4 * p + 2 + m, :rows]
            d_k[both, at] = jnp.concatenate([one[:, :HD], two[:, :HD]], axis=1)
            d_v[both, at] = jnp.concatenate([one[:, HD:], two[:, HD:]], axis=1)
    keep_term(1, dot(tokens, d_q[...], COLS))
    keep_term(2, dot(tokens, d_k[...], COLS))
    keep_term(3, dot(tokens, d_v[...], COLS))
    vectors = jnp.concatenate(
        [
            rows_sum(d_q[...].astype(jnp.float32)),
            rows_sum(d_v[...].astype(jnp.float32)),
            g_vec_ref[:6, :],
        ],
        axis=0,
    )
    up_bias = g_up_bias_ref[...]
    up_depth = up_bias.shape[1] // shards
    for s in range(shards):
        small[s, :8, :depth] = vectors[:, s * depth : (s + 1) * depth]
        small[s, 8:9, :up_depth] = up_bias[:, s * up_depth : (s + 1) * up_depth]
    begin(QUERY)
    begin(KEY)
    begin(VALUE)
    begin(SMALL)
    corner(QUERY)
    corner(KEY)
    corner(VALUE)
    corner(SMALL)
    own(DOWN)
    sides(OUT)
    sides(QUERY)
    sides(KEY)
    sides(VALUE)
    sides(SMALL)
    load.wait()
    d_x = d_mix_ref[...]
    for k, half_ref in enumerate((d_q, d_k, d_v)):
        d_x = d_x + dot(half_ref[...], w_ref[:, k * width : (k + 1) * width], ROWS)
    d_x_ref[...] = d_x.astype(jnp.bfloat16).reshape(2, rows, width)
    g_up_ref[...] = finish(UP)
    g_down_ref[...] = finish(DOWN)
    own(OUT)
    own(QUERY)
    own(KEY)
    own(VALUE)
    own(SMALL)
    g_outw_ref[...] = finish(OUT)
    g_query_ref[...] = finish(QUERY)
    g_key_ref[...] = finish(KEY)
    g_value_ref[...] = finish(VALUE)
    g_small_ref[...] = finish(SMALL)
    sent_q()
    sent()
    sent_kv()


def back_call(parts, lefts, tokens, mixed, d_mix, g_out, g_vec, g_up_bias, collective):
    micro, rows, width = tokens.shape
    devices = parts.shape[0]
    depth, ff = lefts[0].shape[2:]
    f32, bf16 = jnp.float32, jnp.bfloat16
    one_way, other_way = (cut(1, 0, width), None), (None, cut(1, 0, width))
    cuts = [*weight_cuts(ff, width), one_way, other_way, one_way, other_way, (cut(1, 0, 128), None)]
    square = (depth, width)
    chunks = [(lefts[0].shape[2:], bf16), (lefts[3].shape[2:], bf16)] + [(square, bf16)] * 4
    chunks += [((16, 128), f32)]
    scratch = [
        one
        for i, ((chunk, dtype), c) in enumerate(zip(chunks, cuts))
        for one in scatter_scratch(chunk, dtype, c, i < 2)
    ]
    near = pl.BlockSpec(memory_space=pltpu.VMEM)
    far = pl.BlockSpec(memory_space=pl.ANY)
    outs = [jax.ShapeDtypeStruct(tokens.shape, bf16)]
    outs += [jax.ShapeDtypeStruct(square, f32)] * 4
    outs += [
        jax.ShapeDtypeStruct((depth, ff), f32),
        jax.ShapeDtypeStruct(lefts[3].shape[2:], f32),
        jax.ShapeDtypeStruct((16, 128), f32),
    ]
    return pl.pallas_call(
        partial(back_kernel, cuts),
        out_shape=tuple(outs),
        in_specs=[far] * 7 + [near, far] + [near] * 4,
        out_specs=(near,) * len(outs),
        scratch_shapes=[
            pltpu.VMEM((HEADS * micro,) + parts.shape[1:], bf16),
            pltpu.VMEM((4, devices) + square, bf16),
            pltpu.VMEM((devices, 16, 128), f32),
            pltpu.VMEM((width, 3 * width), bf16),
        ]
        + [pltpu.VMEM((micro * rows, width), bf16)] * 3
        + [pltpu.SemaphoreType.DMA]
        + exchange_semaphores() * 2
        + scratch
        + scatter_semaphores(len(cuts)),
        compiler_params=pltpu.CompilerParams(
            collective_id=collective, has_side_effects=True, vmem_limit_bytes=61 * 2**20
        ),
        name="back",
    )(parts, *lefts, tokens, mixed, d_mix, g_out, g_vec, g_up_bias)


def leave_kernel(*refs):
    *wholes, small_in = refs[:8]
    outs = refs[8:]
    for from_ref, to_ref in zip(wholes, outs):
        to_ref[...] = from_ref[...]
    for k, ref in enumerate(outs[7:]):
        ref[...] = small_in[k, : ref.shape[0]]


def leave_call(*arrays):
    *wholes, _ = arrays
    depth, width = wholes[1].shape
    f32 = jnp.float32
    outs = [jax.ShapeDtypeStruct(a.shape, a.dtype) for a in wholes]
    outs += [jax.ShapeDtypeStruct((depth,), f32)] * 8
    outs += [jax.ShapeDtypeStruct((wholes[6].shape[0],), f32)]
    near = pl.BlockSpec(memory_space=pltpu.VMEM)
    return pl.pallas_call(
        leave_kernel,
        out_shape=tuple(outs),
        in_specs=[near] * 8,
        out_specs=(near,) * len(outs),
        name="leave",
    )(*arrays)


def cut(axis, start, size):
    return (axis, start, size)


def lanes_of(shape, low):
    lane = lax.broadcasted_iota(jnp.int32, shape, len(shape) - 1)
    if isinstance(low, bool):
        return lane < HD if low else lane >= HD
    return lane // HD == jnp.where(low, 0, 1)


def dot(left_side, right_side, contract=((1,), (0,))):
    return lax.dot_general(
        left_side, right_side, (contract, ((), ())), preferred_element_type=jnp.float32
    )


ROWS = ((1,), (1,))
COLS = ((0,), (0,))


def halves(array, col):
    return array[:, col : col + HD]


def listed_rows(table_ref, blocks, n):
    rows = [jnp.maximum(n - 1, 0), n, jnp.minimum(n + 1, blocks - 1)]
    rows += [table_ref[n * RAND + r] for r in range(RAND)]
    return rows + [table_ref[blocks * RAND + g] for g in range(GLOB)]


def outside(here, total, listed):
    lane = lax.broadcasted_iota(jnp.int32, (1, listed * BLOCK), 1)
    before = jnp.logical_and(lane < BLOCK, here == 0)
    after = jnp.logical_and(
        jnp.logical_and(lane >= 2 * BLOCK, lane < 3 * BLOCK), here == total - 1
    )
    return jnp.where(jnp.logical_or(before, after), -jnp.inf, 0.0)


def only(value, low):
    return jnp.where(lanes_of(value.shape, low), value, jnp.zeros_like(value))


def turned(value):
    return jnp.concatenate([value[:, HD:], value[:, :HD]], axis=1)


def to_side(value, odd, low):
    if isinstance(odd, bool):
        return only(turned(value) if odd == low else value, low)
    return only(jnp.where((odd == 1) == low, turned(value), value), low)


def key_rows(ref, spot, step):
    return ref[pl.ds(spot, step), :2].reshape(step * 2 * BLOCK, 2 * HD)


GROUP = 16
STEP = 8


def attend_kernel(table_ref, land_ref, out_ref, lse_ref):
    devices = land_ref.shape[0]
    blocks = 2 * devices
    scale = jnp.bfloat16(HD ** (-0.5))

    def query_blocks(group, carry):
        kvs, scores = [], []
        for u in range(GROUP):
            n = group * GROUP + u
            rows = listed_rows(table_ref, blocks, n)
            kvs.append(jnp.concatenate([land_ref[r // 2, r % 2] for r in rows], axis=0))
            q = to_side(land_ref[group * (GROUP // 2) + u // 2, 2], u % 2 == 1, True) * scale
            scores.append(dot(q, kvs[-1], ROWS) + outside(n, blocks, len(rows)))
        raised = []
        for u, score in enumerate(scores):
            top = jnp.max(score, axis=1, keepdims=True)
            probs = jnp.exp(score - top)
            total_sum = jnp.sum(probs, axis=1, keepdims=True)
            raised.append((probs * (1.0 / total_sum)).astype(jnp.bfloat16))
            lse_ref[group * GROUP + u] = jnp.broadcast_to(
                top + jnp.log(total_sum), lse_ref.shape[1:]
            )
        outs = [dot(r, kv) for r, kv in zip(raised, kvs)]
        for u in range(0, GROUP, 2):
            out_ref[group * (GROUP // 2) + u // 2] = jnp.where(
                lanes_of(outs[u].shape, True), turned(outs[u]), outs[u + 1]
            ).astype(jnp.bfloat16)
        return carry

    def everything():
        lax.fori_loop(0, blocks // GROUP, query_blocks, 0)
        spots = range(0, devices, STEP)
        chosen = [table_ref[blocks * RAND + g] for g in range(GLOB)]
        q = jnp.concatenate(
            [to_side(land_ref[row // 2, 2], row % 2, True) for row in chosen], axis=0
        )
        scores = [dot(q * scale, key_rows(land_ref, spot, STEP), ROWS) for spot in spots]
        top = scores[0].max(axis=1, keepdims=True)
        for score in scores[1:]:
            top = jnp.maximum(top, score.max(axis=1, keepdims=True))
        raised = [jnp.exp(score - top) for score in scores]
        total_sum = sum(jnp.sum(r, axis=1, keepdims=True) for r in raised)
        out = sum(
            dot(r.astype(jnp.bfloat16), key_rows(land_ref, spot, STEP))
            for r, spot in zip(raised, spots)
        )
        out = out / total_sum
        lse = jnp.broadcast_to(top + jnp.log(total_sum), out.shape)
        for g, row in enumerate(chosen):
            at = slice(g * BLOCK, (g + 1) * BLOCK)
            lse_ref[row] = lse[at]
            new = jnp.where(row % 2 == 0, turned(out[at]), out[at]).astype(jnp.bfloat16)
            old = out_ref[row // 2]
            out_ref[row // 2] = jnp.where(lanes_of(old.shape, row % 2 == 0), new, old)

    pl.when(table_ref[blocks * RAND + GLOB] == 1)(everything)


def attend_call(table, land):
    spec = pl.BlockSpec(memory_space=pltpu.VMEM)
    devices, _, block, lanes = land.shape
    return pl.pallas_call(
        attend_kernel,
        out_shape=(
            jax.ShapeDtypeStruct((devices, block, lanes), jnp.bfloat16),
            jax.ShapeDtypeStruct((2 * devices, block, lanes), jnp.float32),
        ),
        in_specs=[pl.BlockSpec(memory_space=pltpu.SMEM), spec],
        out_specs=(spec, spec),
        compiler_params=pltpu.CompilerParams(vmem_limit_bytes=56 * 2**20),
        name="attend",
    )(table, land)


def attend_back_kernel(table_ref, land_ref, d_ref, out_ref, lse_ref, parts_ref, total_ref):
    devices = land_ref.shape[0]
    blocks = 2 * devices
    scale = jnp.bfloat16(HD ** (-0.5))

    def wide(column, width):
        return jnp.concatenate([column] * (width // column.shape[1]), axis=1)

    def pair_of(place, odd, keep):
        q = to_side(land_ref[place, 2], odd, True) * scale
        d = to_side(d_ref[place], odd, False)
        if keep is not None:
            d = d * keep
        out = to_side(out_ref[place], odd, False)
        delta = jnp.sum(d.astype(jnp.float32) * out.astype(jnp.float32), axis=1, keepdims=True)
        return q, d, delta

    def query_blocks(group, carry):
        listed, kvs, pairs, deltas, boths = [], [], [], [], []
        for u in range(GROUP):
            n = group * GROUP + u
            rows = listed_rows(table_ref, blocks, n)
            is_global = jnp.logical_or(n == rows[-1], n == rows[-2])
            keep = jnp.where(is_global, 0.0, 1.0).astype(jnp.bfloat16)
            kv = jnp.concatenate([land_ref[r // 2, r % 2] for r in rows], axis=0)
            q, d, delta = pair_of(group * (GROUP // 2) + u // 2, u % 2 == 1, keep)
            listed.append(rows)
            kvs.append(kv)
            pairs.append(jnp.concatenate([q, d], axis=0))
            deltas.append(delta)
            boths.append(dot(pairs[-1], kv, ROWS))
        weights = []
        for u, both in enumerate(boths):
            n = group * GROUP + u
            width = both.shape[1]
            scores = both[:BLOCK] + outside(n, blocks, width // BLOCK)
            probs = jnp.exp(scores - wide(lse_ref[n], width))
            d_scores = probs * (both[BLOCK:] - deltas[u])
            weights.append(
                jnp.concatenate(
                    [d_scores.astype(jnp.bfloat16), probs.astype(jnp.bfloat16)], axis=0
                )
            )
        outs = []
        for u, weight in enumerate(weights):
            d_kv = dot(weight, pairs[u], COLS)
            for at, r in enumerate(listed[u]):
                total_ref[r // 2, r % 2] += d_kv[at * BLOCK : (at + 1) * BLOCK]
            outs.append(dot(weight[:BLOCK], kvs[u]) * HD ** (-0.5))
        for u in range(0, GROUP, 2):
            parts_ref[group * (GROUP // 2) + u // 2, 2] = jnp.where(
                lanes_of(outs[u].shape, True), outs[u], turned(outs[u + 1])
            ).astype(jnp.bfloat16)
        return carry

    def everything():
        def clear(i, carry):
            total_ref[i] = jnp.zeros(total_ref.shape[1:], jnp.float32)
            return carry

        lax.fori_loop(0, devices, clear, 0)
        lax.fori_loop(0, blocks // GROUP, query_blocks, 0)
        chosen = [table_ref[blocks * RAND + g] for g in range(GLOB)]
        found = [pair_of(row // 2, row % 2, None) for row in chosen]
        both_rows = GLOB * BLOCK
        pairs = jnp.concatenate([f[0] for f in found] + [f[1] for f in found], axis=0)
        delta = jnp.concatenate([f[2] for f in found], axis=0)
        lse = jnp.concatenate([lse_ref[row] for row in chosen], axis=0)

        def some_keys(spot, d_q):
            kv = key_rows(land_ref, spot * STEP, STEP)
            both = dot(pairs, kv, ROWS)
            probs = jnp.exp(both[:both_rows] - wide(lse, both.shape[1]))
            d_scores = probs * (both[both_rows:] - delta)
            weight = jnp.concatenate(
                [d_scores.astype(jnp.bfloat16), probs.astype(jnp.bfloat16)], axis=0
            )
            total_ref[pl.ds(spot * STEP, STEP)] += dot(weight, pairs, COLS).reshape(
                STEP, 2, BLOCK, 2 * HD
            )
            return d_q + dot(weight[:both_rows], kv)

        d_q = lax.fori_loop(
            0, devices // STEP, some_keys, jnp.zeros((both_rows, 2 * HD), jnp.float32)
        )
        d_q = d_q * HD ** (-0.5)
        for g, row in enumerate(chosen):
            part = d_q[g * BLOCK : (g + 1) * BLOCK]
            new = jnp.where(row % 2 == 0, part, turned(part)).astype(jnp.bfloat16)
            old = parts_ref[row // 2, 2]
            parts_ref[row // 2, 2] = jnp.where(lanes_of(old.shape, row % 2 == 0), new, old)

        def give(i, carry):
            parts_ref[i, :2] = total_ref[i].astype(jnp.bfloat16)
            return carry

        lax.fori_loop(0, devices, give, 0)

    pl.when(table_ref[blocks * RAND + GLOB] == 1)(everything)


def attend_back_call(table, land, d, out, lse):
    spec = pl.BlockSpec(memory_space=pltpu.VMEM)
    devices, _, block, lanes = land.shape
    return pl.pallas_call(
        attend_back_kernel,
        out_shape=jax.ShapeDtypeStruct(land.shape, jnp.bfloat16),
        in_specs=[pl.BlockSpec(memory_space=pltpu.SMEM)] + [spec] * 4,
        out_specs=spec,
        scratch_shapes=[pltpu.VMEM((devices, 2, block, lanes), jnp.float32)],
        compiler_params=pltpu.CompilerParams(vmem_limit_bytes=60 * 2**20),
        name="attend_back",
    )(table, land, d, out, lse)


def centre(values):
    center = jnp.mean(values, axis=1, keepdims=True)
    centred = values - center
    spread = jnp.mean(centred * centred, axis=1, keepdims=True)
    inverse = lax.rsqrt(spread + 1e-12)
    return centred * inverse, inverse


def centre_back(hat, inverse, grad):
    return inverse * (
        grad
        - jnp.mean(grad, axis=1, keepdims=True)
        - hat * jnp.mean(grad * hat, axis=1, keepdims=True)
    )


def rows_sum(values):
    return jnp.sum(values, axis=0, keepdims=True)


WEIGHT_CHUNK = 1024


def dense_kernel(
    c_in, x_ref, cot_ref, wo_in, up_in, down_in, vec_ref, up_bias_ref,
    out_ref, d_mix_ref, d_land, g_out_ref, up_left, up_first, up_second, down_left, down_first, down_second, g_vec_ref, g_up_bias_ref,
    ctx, first, hat, low, low_t, act, slope, ffn, wo_ref, up_ref, down_ref, g_up_ref, g_down_ref, in_sem, out_sem,
    c_ref, d_c_ref, up_other, up_total, down_other, down_total, *sems,
):
    rows = x_ref.shape[1]
    width = x_ref.shape[2]
    ff = up_ref.shape[1]
    chunk = WEIGHT_CHUNK
    fetches = [
        pltpu.make_async_copy(wo_in.at[:, pl.ds(3 * width, width)], wo_ref, in_sem.at[0]),
    ]
    for i in range(ff // chunk):
        at = pl.ds(i * chunk, chunk)
        fetches.append(pltpu.make_async_copy(up_in.at[:, at], up_ref.at[:, at], in_sem.at[2 * i + 1]))
        fetches.append(pltpu.make_async_copy(down_in.at[at], down_ref.at[at], in_sem.at[2 * i + 2]))
    for copy in fetches:
        copy.start()
    begin_c, arrive_c, sent_c = exchange(False, c_in, c_ref, sems[:3])
    begin_d, arrive_d, sent_d = exchange(True, d_c_ref, d_land, sems[3:6])
    enter, begin, corner, leave, _, _, _, sent = scatter_steps(
        weight_cuts(ff, width),
        (g_up_ref, g_down_ref),
        ((up_other, up_total, up_first, up_second), (down_other, down_total, down_first, down_second)),
        sems[6:],
    )
    enter()
    begin_c()
    arrive_c()
    out_bias, attn_gain, attn_shift, down_bias, ffn_gain, ffn_shift = (
        vec_ref[k : k + 1, :] for k in range(2, 8)
    )
    for p in range(HEADS // 2):
        at = pl.ds(p * 2 * HD, 2 * HD)
        for m in range(2):
            one, two = c_ref[4 * p + m], c_ref[4 * p + 2 + m]
            top, mid = m * rows, m * rows + rows // 2
            ctx[top:mid, at] = jnp.concatenate([one[:, :HD], two[:, :HD]], axis=1)
            ctx[mid : top + rows, at] = jnp.concatenate([one[:, HD:], two[:, HD:]], axis=1)
    tokens = x_ref[...].reshape(2 * rows, width).astype(jnp.float32)
    fetches[0].wait()
    hat_first, inverse_first = centre(tokens + dot(ctx[...], wo_ref[...]) + out_bias)
    hat[...] = hat_first
    first[...] = hat_first * attn_gain + attn_shift
    low[...] = first[...].astype(jnp.bfloat16)
    low_t[...] = first[...].T.astype(jnp.bfloat16)
    ffn[...] = first[...] + down_bias

    def forward(i):
        at = pl.ds(i * chunk, chunk)
        fetches[2 * i + 1].wait()
        fetches[2 * i + 2].wait()
        hidden = dot(low[...], up_ref[:, at]) + up_bias_ref[:, at]
        share = 0.5 * (1.0 + lax.erf(hidden * 0.7071067811865476))
        bell = jnp.exp(-0.5 * hidden * hidden) * 0.3989422804014327
        slope[:, at] = share + hidden * bell
        act_low = (hidden * share).astype(jnp.bfloat16)
        act[:, at] = act_low
        ffn[...] += dot(act_low, down_ref[at, :])

    for i in range(ff // chunk):
        forward(i)
    hat_second, inverse_second = centre(ffn[...])
    out_ref[...] = (
        (hat_second * ffn_gain + ffn_shift).astype(jnp.bfloat16).reshape(2, rows, width)
    )
    cot = cot_ref[...].reshape(2 * rows, width).astype(jnp.float32)
    g_vec_ref[4:5, :] = rows_sum(cot * hat_second)
    g_vec_ref[5:6, :] = rows_sum(cot)
    d_second = centre_back(hat_second, inverse_second, cot * ffn_gain)
    d_ffn = d_second.astype(jnp.bfloat16)
    g_vec_ref[3:4, :] = rows_sum(d_ffn.astype(jnp.float32))
    ffn[...] = d_second

    shards, depth, _ = g_up_ref.shape
    down_depth = g_down_ref.shape[1]
    half = ff // 2
    for i in range(2):
        at = pl.ds(i * half, half)
        g_down_ref[pl.ds(i * (shards // 2), shards // 2)] = (
            dot(act[:, at], d_ffn, COLS)
            .reshape(shards // 2, down_depth, width)
            .astype(jnp.bfloat16)
        )
    begin(1, (0,))
    for i in range(2):
        at = pl.ds(i * half, half)
        d_act = dot(d_ffn, down_ref[at, :], ROWS)
        d_hidden = (d_act * slope[:, at]).astype(jnp.bfloat16)
        g_up_bias_ref[:, at] = rows_sum(d_hidden.astype(jnp.float32))
        g_up_ref[:, :, at] = (
            dot(low_t[...], d_hidden).reshape(shards, depth, half).astype(jnp.bfloat16)
        )
        ffn[...] += dot(d_hidden, up_ref[:, at], ROWS)
        if i == 0:
            corner(1)
            begin(1, (1, 2, 3))
    begin(0, (0,))
    d_first = ffn[...]
    g_vec_ref[1:2, :] = rows_sum(d_first * hat[...])
    g_vec_ref[2:3, :] = rows_sum(d_first)
    d_mix = centre_back(hat[...], inverse_first, d_first * attn_gain)
    d_mix_ref[...] = d_mix
    d_branch = d_mix.astype(jnp.bfloat16)
    g_vec_ref[0:1, :] = rows_sum(d_branch.astype(jnp.float32))
    g_vec_ref[6:8, :] = jnp.zeros((2, width), jnp.float32)
    d_ctx = dot(d_branch, wo_ref[...], ROWS).astype(jnp.bfloat16)
    for pair in range(d_c_ref.shape[0]):
        col, top = pair // 2 * HD, pair % 2 * rows
        mid = top + rows // 2
        d_c_ref[pair] = jnp.concatenate(
            [halves(d_ctx[top:mid], col), halves(d_ctx[mid : top + rows], col)], axis=1
        )
    begin_d()
    corner(0)
    begin(0, (1, 2, 3))
    g_out_ref[...] = dot(ctx[...], d_branch, COLS).astype(jnp.bfloat16)
    for copy in leave(1, down_left, out_sem) + leave(0, up_left, out_sem):
        copy.wait()
    sent()
    arrive_d()
    sent_c()
    sent_d()


def dense_call(c, tokens, cot, mixed, up, down, vec, up_bias, collective):
    micro, rows, width = tokens.shape
    ff = up.shape[1]
    both = micro * rows
    devices = c.shape[0]
    up_chunk, down_chunk = (width // devices, ff), (ff // devices, width)
    far = pl.BlockSpec(memory_space=pl.ANY)
    f32, bf16 = jnp.float32, jnp.bfloat16

    def full(shape):
        return pl.BlockSpec(memory_space=pltpu.VMEM)

    outs = (
        jax.ShapeDtypeStruct(tokens.shape, bf16),
        jax.ShapeDtypeStruct((both, width), f32),
        jax.ShapeDtypeStruct(c.shape, bf16),
        jax.ShapeDtypeStruct((width, width), bf16),
        jax.ShapeDtypeStruct((3, 4) + up_chunk, bf16),
        jax.ShapeDtypeStruct((4, width // devices, ff // 2), bf16),
        jax.ShapeDtypeStruct((4, width // devices, ff // 2), bf16),
        jax.ShapeDtypeStruct((3, 4) + down_chunk, bf16),
        jax.ShapeDtypeStruct((4, ff // devices, width // 2), bf16),
        jax.ShapeDtypeStruct((4, ff // devices, width // 2), bf16),
        jax.ShapeDtypeStruct((8, width), f32),
        jax.ShapeDtypeStruct((1, ff), f32),
    )
    return pl.pallas_call(
        dense_kernel,
        out_shape=outs,
        in_specs=[
            far,
            full(tokens.shape),
            full(cot.shape),
            far,
            far,
            far,
            full(vec.shape),
            full(up_bias.shape),
        ],
        out_specs=tuple(far if k == 2 or 4 <= k < 10 else full(o.shape) for k, o in enumerate(outs)),
        scratch_shapes=[
            pltpu.VMEM((both, width), bf16),
            pltpu.VMEM((both, width), f32),
            pltpu.VMEM((both, width), f32),
            pltpu.VMEM((both, width), bf16),
            pltpu.VMEM((width, both), bf16),
            pltpu.VMEM((both, ff), bf16),
            pltpu.VMEM((both, ff), f32),
            pltpu.VMEM((both, width), f32),
            pltpu.VMEM((width, width), bf16),
            pltpu.VMEM((width, ff), bf16),
            pltpu.VMEM((ff, width), bf16),
            pltpu.VMEM((devices,) + up_chunk, bf16),
            pltpu.VMEM((devices,) + down_chunk, bf16),
            pltpu.SemaphoreType.DMA((1 + 2 * (ff // WEIGHT_CHUNK),)),
            pltpu.SemaphoreType.DMA((2, 4)),
            pltpu.VMEM((HEADS * micro,) + c.shape[1:], bf16),
            pltpu.VMEM((HEADS * micro,) + c.shape[1:], bf16),
            pltpu.VMEM((4, 4) + up_chunk, bf16),
            pltpu.VMEM((4, 4) + up_chunk, bf16),
            pltpu.VMEM((4, 4) + down_chunk, bf16),
            pltpu.VMEM((4, 4) + down_chunk, bf16),
        ]
        + exchange_semaphores() * 2
        + scatter_semaphores(2),
        compiler_params=pltpu.CompilerParams(
            collective_id=collective, has_side_effects=True, vmem_limit_bytes=60 * 2**20
        ),
        name="dense",
    )(c, tokens, cot, mixed, up, down, vec, up_bias)


def near_body(inputs, cotangent, random_blocks, global_blocks, *shards):
    (
        query_weight, query_bias, key_weight, value_weight, value_bias, out_weight, out_bias, attn_gain,
        attn_shift, up_weight, up_bias, down_weight, down_bias, ffn_gain, ffn_shift,
    ) = shards
    devices = lax.axis_size("head") * lax.axis_size("blk")
    micro, rows, width = inputs.shape
    depth = query_weight.shape[0]
    ff = up_weight.shape[1]
    land, up, down, mixed, vec, up_bias_row = front_call(
        inputs,
        (query_weight, key_weight, value_weight, out_weight),
        up_weight,
        down_weight,
        (
            query_bias, value_bias, out_bias, attn_gain, attn_shift, down_bias, ffn_gain, ffn_shift, up_bias,
        ),
        1,
    )
    up = up.reshape(width, ff)
    down = down.reshape(ff, width)
    busy, pair = place_pair(lax.axis_index("blk"), lax.axis_index("head"))
    head, at = pair // micro, pair % micro
    table = jnp.concatenate(
        [
            lax.dynamic_slice(
                random_blocks, (at, 0, head, 0), (1, random_blocks.shape[1], 1, RAND)
            ).reshape(-1),
            lax.dynamic_slice(global_blocks, (at, 0), (1, GLOB)).reshape(-1),
            busy.astype(jnp.int32)[None],
        ]
    )
    land = land.reshape(devices, 3, rows // 2, 2 * HD)
    attended, lse = attend_call(table, land)
    layer_out, d_mix, d_context, g_out, *lefts, g_vec, g_up_bias = dense_call(
        attended, inputs, cotangent, mixed, up, down, vec, up_bias_row, 3
    )
    parts = attend_back_call(table, land, d_context, attended, lse)
    results = back_call(
        parts.reshape(devices, 3 * rows // 2, 2 * HD),
        lefts,
        inputs,
        mixed,
        d_mix,
        g_out,
        g_vec,
        g_up_bias,
        5,
    )
    (
        input_grad, grad_out, grad_query, grad_key, grad_value, grad_up, grad_down, *vector, grad_up_bias,
    ) = leave_call(*results)
    return (
        layer_out, input_grad, grad_query, vector[0], grad_key, grad_value, vector[1], grad_out,
        vector[2], vector[3], vector[4], grad_up, grad_up_bias, grad_down, vector[5], vector[6], vector[7],
    )


def with_halo(cells, sides, width):
    for axis, dim in sides:
        count = lax.axis_size(axis)
        ends = count - 1
        head = lax.slice_in_dim(cells, 0, width, axis=dim)
        tail = lax.slice_in_dim(cells, cells.shape[dim] - width, cells.shape[dim], axis=dim)
        cells = jnp.concatenate(
            [
                lax.ppermute(tail, axis, [(i, (i + 1) % count) for i in range(ends)]),
                cells,
                lax.ppermute(head, axis, [((i + 1) % count, i) for i in range(ends)]),
            ],
            axis=dim,
        )
    return cells


def combined_all(part, axis, combine):
    gathered = jax.tree.map(lambda a: lax.all_gather(a, axis), part)

    def take(source):
        return jax.tree.map(lambda a: lax.dynamic_index_in_dim(a, source, 0, False), gathered)

    return lax.fori_loop(
        1, lax.axis_size(axis), lambda source, state: combine(state, take(source)), take(0)
    )


def taken(table, rows):
    return lax.map(lambda row: lax.dynamic_index_in_dim(table, row, 0, False), rows)


def layer_norm(values, norm_gain, norm_shift):
    center = jnp.mean(values, axis=-1, keepdims=True)
    centred = values - center
    spread = jnp.mean(centred * centred, axis=-1, keepdims=True)
    return centred * lax.rsqrt(spread + 1e-12) * norm_gain + norm_shift


def gelu_exact(values):
    return jax.nn.gelu(values, approximate=False)


def matmul(left_side, right_side):
    return jnp.dot(left_side, right_side, preferred_element_type=jnp.float32)


def matmul_left(left_side, right_side):
    return lax.dot_general(
        left_side, right_side, (((0,), (0,)), ((), ())), preferred_element_type=jnp.float32
    )


def matmul_right(left_side, right_side):
    return lax.dot_general(
        left_side, right_side, (((1,), (1,)), ((), ())), preferred_element_type=jnp.float32
    )


def column_sum(values):
    return jnp.sum(values.astype(jnp.float32), axis=0)


def combine_parts(earlier, later_part):
    joint_top = jnp.maximum(earlier[0], later_part[0])
    first_factor = jnp.exp(earlier[0] - joint_top)
    second_factor = jnp.exp(later_part[0] - joint_top)
    return (
        joint_top,
        earlier[1] * first_factor + later_part[1] * second_factor,
        earlier[2] * first_factor[..., None] + later_part[2] * second_factor[..., None],
    )


def fetch_weights(
    query_weight,
    query_bias,
    key_weight,
    value_weight,
    value_bias,
    out_weight,
    out_bias,
    attn_gain,
    attn_shift,
    up_weight,
    up_bias,
    down_weight,
    down_bias,
    ffn_gain,
    ffn_shift,
):
    return (
        lax.all_gather(query_weight, ("blk", "head"), axis=0, tiled=True),
        lax.all_gather(query_bias, ("blk", "head"), axis=0, tiled=True),
        lax.all_gather(key_weight, ("blk", "head"), axis=0, tiled=True),
        lax.all_gather(value_weight, ("blk", "head"), axis=0, tiled=True),
        lax.all_gather(value_bias, ("blk", "head"), axis=0, tiled=True),
        lax.all_gather(out_weight, ("blk", "head"), axis=0, tiled=True),
        lax.all_gather(out_bias, ("blk", "head"), axis=0, tiled=True),
        lax.all_gather(attn_gain, ("blk", "head"), axis=0, tiled=True),
        lax.all_gather(attn_shift, ("blk", "head"), axis=0, tiled=True),
        lax.all_gather(up_weight, ("blk", "head"), axis=0, tiled=True),
        lax.all_gather(up_bias, ("blk", "head"), axis=0, tiled=True),
        lax.all_gather(down_weight, ("blk", "head"), axis=0, tiled=True),
        lax.all_gather(down_bias, ("blk", "head"), axis=0, tiled=True),
        lax.all_gather(ffn_gain, ("blk", "head"), axis=0, tiled=True),
        lax.all_gather(ffn_shift, ("blk", "head"), axis=0, tiled=True),
    )


def reduce_grads(totals):
    return (
        lax.psum_scatter(totals[0], ("blk", "head"), scatter_dimension=0, tiled=True),
        lax.psum_scatter(totals[1], ("blk", "head"), scatter_dimension=0, tiled=True),
        lax.psum_scatter(totals[2], ("blk", "head"), scatter_dimension=0, tiled=True),
        lax.psum_scatter(totals[3], ("blk", "head"), scatter_dimension=0, tiled=True),
        lax.psum_scatter(totals[4], ("blk", "head"), scatter_dimension=0, tiled=True),
        lax.psum_scatter(totals[5], ("blk", "head"), scatter_dimension=0, tiled=True),
        lax.psum_scatter(totals[6], ("blk", "head"), scatter_dimension=0, tiled=True),
        lax.psum_scatter(totals[7], ("blk", "head"), scatter_dimension=0, tiled=True),
        lax.psum_scatter(totals[8], ("blk", "head"), scatter_dimension=0, tiled=True),
        lax.psum_scatter(totals[9], ("blk", "head"), scatter_dimension=0, tiled=True),
        lax.psum_scatter(totals[10], ("blk", "head"), scatter_dimension=0, tiled=True),
        lax.psum_scatter(totals[11], ("blk", "head"), scatter_dimension=0, tiled=True),
        lax.psum_scatter(totals[12], ("blk", "head"), scatter_dimension=0, tiled=True),
        lax.psum_scatter(totals[13], ("blk", "head"), scatter_dimension=0, tiled=True),
        lax.psum_scatter(totals[14], ("blk", "head"), scatter_dimension=0, tiled=True),
    )


def sparse_forward(packed):
    group_queries, group_keys, group_values, group_allowed = packed
    attn_scale = HD ** (-0.5)
    scores = (
        jnp.einsum("gqhd,ghkd->ghqk", group_queries, group_keys, preferred_element_type=jnp.float32)
        * attn_scale
    )
    scores = jnp.where(group_allowed[:, None, None, :], scores, -jnp.inf)
    row_top = jnp.max(scores, axis=-1, keepdims=True)
    raised = jnp.exp(scores - row_top)
    row_total = jnp.sum(raised, axis=-1, keepdims=True)
    probs_low = (raised / row_total).astype(jnp.bfloat16)
    output = jnp.einsum(
        "ghqk,ghkd->gqhd", probs_low, group_values, preferred_element_type=jnp.float32
    )
    return (output, (row_top + jnp.log(row_total))[..., 0])


def sparse_backward(nearby, carried, packed):
    group_queries, group_keys, group_values, group_allowed, group_lse, group_grad = packed
    attn_scale = HD ** (-0.5)
    per_group = group_queries.shape[0]
    heads_dev = group_queries.shape[2]
    scores = (
        jnp.einsum("gqhd,ghkd->ghqk", group_queries, group_keys, preferred_element_type=jnp.float32)
        * attn_scale
    )
    scores = jnp.where(group_allowed[:, None, None, :], scores, -jnp.inf)
    probs = jnp.exp(scores - group_lse[..., None])
    d_probs = jnp.einsum(
        "gqhd,ghkd->ghqk", group_grad, group_values, preferred_element_type=jnp.float32
    )
    row_delta = jnp.sum(probs * d_probs, axis=-1, keepdims=True)
    d_scores = (probs * (d_probs - row_delta)).astype(jnp.bfloat16)
    d_queries = (
        jnp.einsum("ghqk,ghkd->gqhd", d_scores, group_keys, preferred_element_type=jnp.float32)
        * attn_scale
    )
    d_keys = (
        jnp.einsum("ghqk,gqhd->ghkd", d_scores, group_queries, preferred_element_type=jnp.float32)
        * attn_scale
    )
    d_values = jnp.einsum(
        "ghqk,gqhd->ghkd",
        probs.astype(jnp.bfloat16),
        group_grad,
        preferred_element_type=jnp.float32,
    )
    d_keys = d_keys.reshape(per_group, heads_dev, -1, BLOCK, HD)
    d_values = d_values.reshape(per_group, heads_dev, -1, BLOCK, HD)
    carried = (
        carried[0] + jnp.sum(d_keys[:, :, nearby:], axis=0),
        carried[1] + jnp.sum(d_values[:, :, nearby:], axis=0),
    )
    return (carried, (d_queries, d_keys[:, :, :nearby], d_values[:, :, :nearby]))


def micro_batch(tokens, cotangent_rows, random_rows, global_rows, weights):
    (
        full_query,
        full_query_bias,
        full_key,
        full_value,
        full_value_bias,
        full_out,
        full_out_bias,
        full_attn_gain,
        full_attn_shift,
        full_up,
        full_up_bias,
        full_down,
        full_down_bias,
        full_ffn_gain,
        full_ffn_shift,
    ) = weights
    attn_scale = HD ** (-0.5)
    shards = lax.axis_size("blk")
    head_groups = lax.axis_size("head")
    shard_index = lax.axis_index("blk")
    group_index = lax.axis_index("head")
    heads_dev = HEADS // head_groups
    group_width = heads_dev * HD
    listed = 3 + RAND + GLOB
    nearby = 3 + RAND
    projected = jnp.stack(
        [
            matmul(tokens, full_query) + full_query_bias,
            matmul(tokens, full_key),
            matmul(tokens, full_value) + full_value_bias,
        ]
    ).astype(jnp.bfloat16)
    by_head = lax.all_to_all(projected, "head", split_axis=2, concat_axis=1, tiled=True)
    row_count = by_head.shape[1]
    block_count = row_count // BLOCK
    blocks_all = block_count * shards
    key_rows = by_head[1]
    value_rows = by_head[2]
    padded = with_halo(by_head[1:3], (("blk", 1),), BLOCK)
    extended = padded.reshape(2, block_count + 2, BLOCK, heads_dev, HD).transpose(0, 1, 3, 2, 4)
    window = jnp.stack([extended[:, offset : offset + block_count] for offset in range(3)], axis=3)
    block_ids = shard_index * block_count + jnp.arange(block_count, dtype=jnp.int32)
    neighbour = block_ids[:, None] + jnp.arange(-1, 2, dtype=jnp.int32)[None, :]
    inside = (neighbour >= 0) & (neighbour < blocks_all)
    head_table = lax.dynamic_slice_in_dim(random_rows, group_index * heads_dev, heads_dev, 1)
    requests = block_count * heads_dev * RAND
    all_requests = head_table.reshape(shards, requests)
    capacity = (requests + shards - 1) // shards + 1
    wanted = lax.dynamic_slice_in_dim(all_requests, shard_index, 1, 0)[0]
    source = wanted // block_count
    place = jnp.arange(requests, dtype=jnp.int32)
    earlier = (place[:, None] > place[None, :]).astype(jnp.int32)
    same_source = (source[:, None] == source[None, :]).astype(jnp.int32)
    slot_index = jnp.sum(earlier * same_source, axis=1)
    mine_mask = (all_requests // block_count == shard_index).astype(jnp.int32)
    send_order = jnp.sum(earlier[None] * mine_mask[:, None, :], axis=2)
    match_mask = mine_mask[:, :, None] * (
        send_order[:, :, None] == jnp.arange(capacity, dtype=jnp.int32)[None, None, :]
    ).astype(jnp.int32)
    head_of = jnp.arange(requests, dtype=jnp.int32) // RAND % heads_dev
    row_of = all_requests % block_count * heads_dev + head_of[None, :]
    send_rows = jnp.sum(match_mask * row_of[:, :, None], axis=1)
    filled = jnp.sum(match_mask, axis=1).astype(jnp.float32)
    block_table = (
        by_head[1:3]
        .reshape(2, block_count, BLOCK, heads_dev, HD)
        .transpose(1, 3, 0, 2, 4)
        .reshape(block_count * heads_dev, 2, BLOCK, HD)
    )
    outgoing = taken(block_table, send_rows.reshape(-1))
    incoming = lax.all_to_all(outgoing, "blk", split_axis=0, concat_axis=0, tiled=True)
    fetched = taken(incoming, source * capacity + slot_index).reshape(
        block_count, heads_dev, RAND, 2, BLOCK, HD
    )
    owner_shard = global_rows // block_count
    present = owner_shard == shard_index
    local_block = global_rows % block_count
    own_rows = jnp.stack(
        [
            lax.dynamic_index_in_dim(
                by_head.reshape(3, block_count, BLOCK, group_width), local_block[g], 1, False
            )
            for g in range(GLOB)
        ],
        axis=1,
    )
    shared = lax.psum(
        jnp.where(present[None, :, None, None], own_rows.astype(jnp.float32), 0.0), "blk"
    ).astype(jnp.bfloat16)
    shared_pairs = shared[1:3].reshape(2, GLOB, BLOCK, heads_dev, HD).transpose(0, 3, 1, 2, 4)

    def listed_blocks(which):
        near_part = window[which]
        random_part = fetched[:, :, :, which]
        global_part = jnp.broadcast_to(
            shared_pairs[which][None], (block_count, heads_dev, GLOB, BLOCK, HD)
        )
        return jnp.concatenate([near_part, random_part, global_part], axis=2).reshape(
            block_count, heads_dev, listed * BLOCK, HD
        )

    per_group = min(8, block_count)
    group_count = block_count // per_group
    query_groups = by_head[0].reshape(group_count, per_group, BLOCK, heads_dev, HD)
    key_groups = listed_blocks(0).reshape(group_count, per_group, heads_dev, listed * BLOCK, HD)
    value_groups = listed_blocks(1).reshape(group_count, per_group, heads_dev, listed * BLOCK, HD)
    allowed = jnp.repeat(
        jnp.concatenate([inside, jnp.ones((block_count, RAND + GLOB), jnp.bool_)], axis=1),
        BLOCK,
        axis=1,
    )
    allow_groups = allowed.reshape(group_count, per_group, listed * BLOCK)
    sparse_out, sparse_lse = lax.map(
        sparse_forward, (query_groups, key_groups, value_groups, allow_groups)
    )
    global_queries = shared[0].reshape(GLOB, BLOCK, heads_dev, HD)
    key_heads = key_rows.reshape(row_count, heads_dev, HD)
    value_wide = value_rows.reshape(row_count, heads_dev, HD).astype(jnp.float32)
    global_scores = (
        jnp.einsum("gqhd,khd->ghqk", global_queries, key_heads, preferred_element_type=jnp.float32)
        * attn_scale
    )
    global_top = jnp.max(global_scores, axis=-1)
    global_raised = jnp.exp(global_scores - global_top[..., None])
    merged = combined_all(
        (
            global_top,
            jnp.sum(global_raised, axis=-1),
            jnp.einsum(
                "ghqk,khd->ghqd", global_raised, value_wide, precision=lax.Precision.HIGHEST
            ),
        ),
        "blk",
        combine_parts,
    )
    global_out = merged[2] / merged[1][..., None]
    global_lse = merged[0] + jnp.log(merged[1])
    global_hits = (block_ids[:, None] == global_rows[None, :]).astype(jnp.float32)
    is_global = jnp.sum(global_hits, axis=1) > 0
    replaced = jnp.einsum("ng,ghqd->nqhd", global_hits, global_out, precision=lax.Precision.HIGHEST)
    context = jnp.where(
        is_global[:, None, None, None],
        replaced,
        sparse_out.reshape(block_count, BLOCK, heads_dev, HD),
    )
    context_rows = context.reshape(row_count, group_width).astype(jnp.bfloat16)
    context_tokens = lax.all_to_all(context_rows, "head", split_axis=0, concat_axis=1, tiled=True)
    branch = matmul(context_tokens, full_out) + full_out_bias
    first_in = tokens.astype(jnp.float32) + branch
    first_norm, first_pull = jax.vjp(
        layer_norm,
        first_in,
        full_attn_gain.astype(jnp.float32),
        full_attn_shift.astype(jnp.float32),
    )
    first_low = first_norm.astype(jnp.bfloat16)
    hidden = matmul(first_low, full_up) + full_up_bias
    act_value, gelu_pull = jax.vjp(gelu_exact, hidden)
    act_low = act_value.astype(jnp.bfloat16)
    ffn_out = matmul(act_low, full_down) + full_down_bias
    result, second_pull = jax.vjp(
        layer_norm,
        first_norm + ffn_out,
        full_ffn_gain.astype(jnp.float32),
        full_ffn_shift.astype(jnp.float32),
    )
    d_second, grad_ffn_gain, grad_ffn_shift = second_pull(cotangent_rows.astype(jnp.float32))
    d_ffn = d_second.astype(jnp.bfloat16)
    grad_down = matmul_left(act_low, d_ffn)
    grad_down_bias = column_sum(d_ffn)
    (d_hidden,) = gelu_pull(matmul_right(d_ffn, full_down))
    d_hidden_low = d_hidden.astype(jnp.bfloat16)
    grad_up = matmul_left(first_low, d_hidden_low)
    grad_up_bias = column_sum(d_hidden_low)
    d_first = d_second + matmul_right(d_hidden_low, full_up)
    d_mix, grad_attn_gain, grad_attn_shift = first_pull(d_first)
    d_branch = d_mix.astype(jnp.bfloat16)
    grad_out = matmul_left(context_tokens, d_branch)
    grad_out_bias = column_sum(d_branch)
    d_context = matmul_right(d_branch, full_out).astype(jnp.bfloat16)
    d_heads = lax.all_to_all(d_context, "head", split_axis=1, concat_axis=0, tiled=True).reshape(
        block_count, BLOCK, heads_dev, HD
    )
    d_sparse = jnp.where(is_global[:, None, None, None], jnp.zeros_like(d_heads), d_heads)
    d_global = lax.psum(
        jnp.where(
            present[:, None, None, None], taken(d_heads, local_block).astype(jnp.float32), 0.0
        ),
        "blk",
    )
    start_carry = (
        jnp.zeros((heads_dev, GLOB, BLOCK, HD), jnp.float32),
        jnp.zeros((heads_dev, GLOB, BLOCK, HD), jnp.float32),
    )
    global_sums, (d_query_parts, near_keys, near_values) = lax.scan(
        partial(sparse_backward, nearby),
        start_carry,
        (
            query_groups,
            key_groups,
            value_groups,
            allow_groups,
            sparse_lse,
            d_sparse.reshape(group_count, per_group, BLOCK, heads_dev, HD),
        ),
    )
    d_query_sparse = d_query_parts.reshape(block_count, BLOCK, heads_dev, HD)
    near_keys = near_keys.reshape(block_count, heads_dev, nearby, BLOCK, HD)
    near_values = near_values.reshape(block_count, heads_dev, nearby, BLOCK, HD)
    near_grads = jnp.stack([near_keys[:, :, :3], near_values[:, :, :3]])
    ext_grads = jnp.zeros((2, block_count + 2, heads_dev, BLOCK, HD), jnp.float32)
    for offset in range(3):
        ext_grads = ext_grads + jnp.pad(
            near_grads[:, :, :, offset], ((0, 0), (offset, 2 - offset), (0, 0), (0, 0), (0, 0))
        )
    rim_pair = jnp.stack([ext_grads[:, 0], ext_grads[:, block_count + 1]], axis=1)
    arrived = with_halo(rim_pair.astype(jnp.bfloat16), (("blk", 1),), 1).astype(rim_pair.dtype)
    inner_grads = ext_grads[:, 1 : block_count + 1]
    inner_grads = inner_grads.at[:, 0].add(arrived[:, 0]).at[:, block_count - 1].add(arrived[:, 3])
    far_grads = jnp.stack([near_keys[:, :, 3:], near_values[:, :, 3:]], axis=3).reshape(
        requests, 2, BLOCK, HD
    )
    outbox = (
        jnp.zeros((shards, capacity, 2, BLOCK, HD), jnp.float32)
        .at[source, slot_index]
        .set(far_grads)
    )
    arrived_slots = (
        lax.all_to_all(
            outbox.astype(jnp.bfloat16), "blk", split_axis=0, concat_axis=0, tiled=True
        ).astype(outbox.dtype)
        * filled[:, :, None, None, None]
    )
    landed = (
        jnp.zeros((block_count * heads_dev, 2, BLOCK, HD), jnp.float32)
        .at[send_rows.reshape(-1)]
        .add(arrived_slots.reshape(shards * capacity, 2, BLOCK, HD))
    )
    landed = landed.reshape(block_count, heads_dev, 2, BLOCK, HD)
    global_probs = jnp.exp(global_scores - global_lse[..., None])
    d_probs_global = jnp.einsum(
        "gqhd,khd->ghqk", d_global, value_wide, precision=lax.Precision.HIGHEST
    )
    delta_global = jnp.einsum(
        "gqhd,ghqd->ghq", d_global, global_out, precision=lax.Precision.HIGHEST
    )
    d_scores_global = (global_probs * (d_probs_global - delta_global[..., None])).astype(
        jnp.bfloat16
    )
    d_global_queries = (
        jnp.einsum("ghqk,khd->gqhd", d_scores_global, key_heads, preferred_element_type=jnp.float32)
        * attn_scale
    )
    d_keys_global = (
        jnp.einsum(
            "ghqk,gqhd->khd", d_scores_global, global_queries, preferred_element_type=jnp.float32
        )
        * attn_scale
    )
    d_values_global = jnp.einsum(
        "ghqk,gqhd->khd", global_probs, d_global, precision=lax.Precision.HIGHEST
    )
    returned = lax.psum(
        jnp.stack(
            [
                d_global_queries,
                global_sums[0].transpose(1, 2, 0, 3),
                global_sums[1].transpose(1, 2, 0, 3),
            ]
        ),
        "blk",
    )
    owned_grads = jnp.einsum(
        "ng,cgqhd->cnqhd", global_hits, returned, precision=lax.Precision.HIGHEST
    )
    d_query_total = d_query_sparse + owned_grads[0]
    d_key_total = (
        (inner_grads[0] + landed[:, :, 0]).transpose(0, 2, 1, 3)
        + d_keys_global.reshape(block_count, BLOCK, heads_dev, HD)
        + owned_grads[1]
    )
    d_value_total = (
        (inner_grads[1] + landed[:, :, 1]).transpose(0, 2, 1, 3)
        + d_values_global.reshape(block_count, BLOCK, heads_dev, HD)
        + owned_grads[2]
    )
    stacked = (
        jnp.stack([d_query_total, d_key_total, d_value_total])
        .reshape(3, row_count, group_width)
        .astype(jnp.bfloat16)
    )
    token_grads = lax.all_to_all(stacked, "head", split_axis=1, concat_axis=2, tiled=True)
    d_tokens = (
        d_mix
        + matmul_right(token_grads[0], full_query)
        + matmul_right(token_grads[1], full_key)
        + matmul_right(token_grads[2], full_value)
    )
    grads = (
        matmul_left(tokens, token_grads[0]),
        column_sum(token_grads[0]),
        matmul_left(tokens, token_grads[1]),
        matmul_left(tokens, token_grads[2]),
        column_sum(token_grads[2]),
        grad_out,
        grad_out_bias,
        grad_attn_gain,
        grad_attn_shift,
        grad_up,
        grad_up_bias,
        grad_down,
        grad_down_bias,
        grad_ffn_gain,
        grad_ffn_shift,
    )
    return (result.astype(jnp.bfloat16), d_tokens.astype(jnp.bfloat16), grads)


def body(
    inputs,
    cotangent,
    random_blocks,
    global_blocks,
    query_weight,
    query_bias,
    key_weight,
    value_weight,
    value_bias,
    out_weight,
    out_bias,
    attn_gain,
    attn_shift,
    up_weight,
    up_bias,
    down_weight,
    down_bias,
    ffn_gain,
    ffn_shift,
):
    weight_shards = (
        query_weight,
        query_bias,
        key_weight,
        value_weight,
        value_bias,
        out_weight,
        out_bias,
        attn_gain,
        attn_shift,
        up_weight,
        up_bias,
        down_weight,
        down_bias,
        ffn_gain,
        ffn_shift,
    )
    results = []
    input_grads = []
    totals = None
    for micro_index in range(inputs.shape[0]):
        weights = fetch_weights(*weight_shards)
        result, token_grad, grads = micro_batch(
            inputs[micro_index],
            cotangent[micro_index],
            random_blocks[micro_index],
            global_blocks[micro_index],
            weights,
        )
        grads = reduce_grads(grads)
        totals = (
            grads
            if totals is None
            else tuple((total_sum + extra_sum for total_sum, extra_sum in zip(totals, grads)))
        )
        results.append(result)
        input_grads.append(token_grad)
    return (jnp.stack(results), jnp.stack(input_grads)) + tuple(totals)


def solution(mesh):
    return jax.shard_map(
        near_body if (mesh.shape["blk"], mesh.shape["head"]) == (8, 4) else body,
        mesh=mesh,
        in_specs=(
            P(None, ("blk", "head"), None),
            P(None, ("blk", "head"), None),
            P(),
            P(),
            P(("blk", "head"), None),
            P(("blk", "head")),
            P(("blk", "head"), None),
            P(("blk", "head"), None),
            P(("blk", "head")),
            P(("blk", "head"), None),
            P(("blk", "head")),
            P(("blk", "head")),
            P(("blk", "head")),
            P(("blk", "head"), None),
            P(("blk", "head")),
            P(("blk", "head"), None),
            P(("blk", "head")),
            P(("blk", "head")),
            P(("blk", "head")),
        ),
        out_specs=(
            P(None, ("blk", "head"), None),
            P(None, ("blk", "head"), None),
            P(("blk", "head"), None),
            P(("blk", "head")),
            P(("blk", "head"), None),
            P(("blk", "head"), None),
            P(("blk", "head")),
            P(("blk", "head"), None),
            P(("blk", "head")),
            P(("blk", "head")),
            P(("blk", "head")),
            P(("blk", "head"), None),
            P(("blk", "head")),
            P(("blk", "head"), None),
            P(("blk", "head")),
            P(("blk", "head")),
            P(("blk", "head")),
        ),
        check_vma=False,
    )
```

```python
from functools import partial

import jax
import jax.numpy as jnp
from jax import lax
from jax.experimental import pallas as pl
from jax.experimental.pallas import tpu as pltpu
from jax.sharding import PartitionSpec as P

HEADS = 12
HD = 64
BLOCK = 64
RAND = 3
GLOB = 2


MESH = pl.DeviceIdType.MESH


def places():
    b = lax.axis_index("blk")
    h = lax.axis_index("head")
    core = b % 2
    x = (b // 2) % 2
    y = b // 4
    across_x = b + 2 - 4 * x
    across_y = b + 4 - 8 * y
    partner = b + 1 - 2 * core
    pair = h // 2
    line = (h, h + 1 - 2 * (h % 2), 2 - pair, 3 - 3 * pair)
    return b, h, core, x, y, across_x, across_y, partner, line


def meet(b, h):
    barrier = pltpu.get_barrier_semaphore()
    count = lax.axis_size("blk") * lax.axis_size("head")

    def tell(k, carry):
        other = (b * 4 + h + k) % count
        pl.semaphore_signal(barrier, inc=1, device_id=(other // 4, other % 4), device_id_type=MESH)
        return carry

    lax.fori_loop(1, count, tell, 0)
    pl.semaphore_wait(barrier, count - 1)


def pair_place(pair):
    at, along = pair % 6, pair // 6
    place = at + at // 3 + jnp.where(at > 3, 1, 0)
    x = place // 2 % 2
    return place + along % 2 * (2 - 4 * x), along


def place_pair(b, h):
    x = b // 2 % 2
    place = b + h % 2 * (2 - 4 * x)
    busy = jnp.logical_and(place != 3, place != 5)
    at = place - jnp.where(place > 3, 1, 0) - jnp.where(place > 5, 1, 0)
    return busy, jnp.minimum(h * 6 + at, 23)


def exchange(to_pairs, src, dst, sems, rows=slice(None)):
    send, recv, own = sems
    b = lax.axis_index("blk")
    h = lax.axis_index("head")
    me = b * 4 + h
    devices = lax.axis_size("blk") * lax.axis_size("head")
    pairs = 24
    busy, mine = place_pair(b, h)

    def other(at):
        if to_pairs:
            return pair_place(at)
        return at // 4, at % 4

    def copy(at):
        slot = me if to_pairs else mine
        return remote(
            src.at[at, rows], dst.at[slot, rows], send.at[at], recv.at[slot], other(at)
        )

    def away(at):
        place, along = other(at)
        return jnp.logical_not(jnp.logical_and(place == b, along == h))

    count = pairs if to_pairs else devices
    first = me * count // devices
    kept = pltpu.make_async_copy(
        src.at[mine if to_pairs else me, rows], dst.at[me if to_pairs else mine, rows], own
    )

    def begin():
        def one(k, carry):
            at = (first + k) % count

            @pl.when(away(at))
            def _():
                copy(at).start()

            return carry

        def everything():
            lax.fori_loop(0, count, one, 0)

        if to_pairs:
            everything()
            pl.when(busy)(kept.start)
        else:

            @pl.when(busy)
            def _():
                everything()
                kept.start()

    def arrive():
        def one(at, carry):
            here = dst.at[at, rows]
            landed = remote(here, here, send.at[0], recv.at[at], (b, h))
            if to_pairs:
                pl.when(at != me)(landed.wait_recv)
            else:
                place, along = pair_place(at)
                own_pair = jnp.logical_and(place == b, along == h)
                pl.when(jnp.logical_not(own_pair))(landed.wait_recv)
            return carry

        def everything():
            lax.fori_loop(0, devices if to_pairs else pairs, one, 0)

        if to_pairs:

            @pl.when(busy)
            def _():
                everything()
                kept.wait()
        else:
            everything()
            pl.when(busy)(kept.wait)

    def sent():
        def one(at, carry):
            pl.when(away(at))(copy(at).wait_send)
            return carry

        def everything():
            lax.fori_loop(0, count, one, 0)

        if to_pairs:
            everything()
        else:
            pl.when(busy)(everything)

    return begin, arrive, sent


def exchange_semaphores():
    dma = pltpu.SemaphoreType.DMA
    return [dma((32,)), dma((32,)), dma]


def remote(src, dst, send_sem, recv_sem, device):
    return pltpu.make_async_remote_copy(
        src_ref=src,
        dst_ref=dst,
        send_sem=send_sem,
        recv_sem=recv_sem,
        device_id=device,
        device_id_type=MESH,
    )


def gather_steps(kinds, ins, outs, sems):
    own_sem, line_send, line_recv, send, recv = sems
    b, h, core, x, y, across_x, across_y, partner, line = places()
    far_corner = across_x + 4 - 8 * y
    partner_x = partner + 2 - 4 * x
    partner_y = partner + 4 - 8 * y
    partner_corner = partner_x + 4 - 8 * y
    inner = jnp.logical_or(h == 1, h == 2)
    seen = jnp.where(inner, 2, 3)
    started = []
    started_inner = []
    locals_ = []

    def enter():
        meet(b, h)

    def piece(i, place):
        return ins[i].at[place] if kinds[i][0] else ins[i]

    def slot(i, shard, place):
        return outs[i].at[shard * 4 + place] if kinds[i][1] else outs[i].at[place]

    def part(ref, cut_):
        axis, start, size = cut_
        return ref.at[(slice(None),) * axis + (pl.ds(start, size),)]

    def go(copy, only_inner=False):
        if only_inner:

            @pl.when(inner)
            def _():
                copy.start()

            started_inner.append(copy)
        else:
            copy.start()
            started.append(copy)

    def along(i, src, landing, sender_at, receiver_at, place, only_inner=False):
        go(
            remote(
                src, landing, line_send.at[i, sender_at], line_recv.at[i, receiver_at], (b, place)
            ),
            only_inner,
        )

    def plane(i, d):
        src = piece(i, h) if d == 0 else slot(i, b, line[d])
        for k, other in enumerate((across_x, across_y, partner)):
            go(
                remote(
                    src, slot(i, b, line[d]), send.at[i, d, k], recv.at[i, d, k], (other, h)
                )
            )

    def arrived(i, d, k, shard, cut_=None):
        here = slot(i, shard, line[d])
        if cut_ is not None:
            here = part(here, cut_)
        remote(here, here, send.at[i, d, k], recv.at[i, d, k], (partner, h)).wait_recv()
        return here

    def begin(i):
        if kinds[i][0]:
            for d in (2, 3, 1):
                along(i, piece(i, line[d]), slot(i, b, h), d, 1 if d == 1 else seen, line[d])
        else:
            along(i, piece(i, h), slot(i, b, h), 2, 2, 3 - h, True)
            along(i, piece(i, h), slot(i, b, h), 1, 1, line[1])
        if kinds[i][1]:
            plane(i, 0)
        own = pltpu.make_async_copy(piece(i, h), slot(i, b, h), own_sem.at[i])
        own.start()
        locals_.append(own)

    def along_done(i, d):
        here = slot(i, b, line[d])
        remote(
            here, here, line_send.at[i, d], line_recv.at[i, d], (b, line[d])
        ).wait_recv()
        if not kinds[i][0]:
            if d == 1:
                along(i, here, here, 3, 3, 3 - h, True)
            else:
                along(i, here, here, d + 2, d, line[1], True)
        if kinds[i][1]:
            plane(i, d)

    def pass_on(i, d):
        first, second = kinds[i][2]
        for k, shard, cut_, onward in (
            (0, across_x, first, across_y),
            (1, across_y, second, across_x),
        ):
            here = arrived(i, d, k, shard)
            if cut_ is not None:
                go(
                    remote(
                        part(here, cut_),
                        part(here, cut_),
                        send.at[i, d, 6 + k],
                        recv.at[i, d, 6 + k],
                        (onward, h),
                    )
                )
            go(remote(here, here, send.at[i, d, 3 + k], recv.at[i, d, 3 + k], (partner, h)))

    def corner(i, d):
        for k, cut_ in enumerate(kinds[i][2]):
            if cut_ is not None:
                arrived(i, d, 6 + k, far_corner, cut_)
        here = slot(i, far_corner, line[d])
        go(remote(here, here, send.at[i, d, 5], recv.at[i, d, 5], (partner, h)))

    def finish(i):
        for d in range(4):
            for k, shard in ((2, partner), (3, partner_x), (4, partner_y), (5, partner_corner)):
                arrived(i, d, k, shard)

    def kept():
        for own in locals_:
            own.wait()
        locals_.clear()

    def sent():
        for copy in started:
            copy.wait_send()
        if started_inner:

            @pl.when(inner)
            def _():
                for copy in started_inner:
                    copy.wait_send()

    return enter, begin, along_done, pass_on, corner, finish, kept, sent


def gather_semaphores(n):
    dma = pltpu.SemaphoreType.DMA
    return [dma((n,)), dma((n, 6)), dma((n, 4)), dma((n, 4, 8)), dma((n, 4, 8))]


def spread_of(rows, width):
    shards, n = rows.shape
    total = shards * width
    lane = lax.broadcasted_iota(jnp.int32, (n, total), 0)
    column = lax.broadcasted_iota(jnp.int32, (n, total), 1)
    repeat = jnp.where(column % width == lane, 1.0, 0.0).astype(jnp.bfloat16)
    shard = lax.broadcasted_iota(jnp.int32, (shards, total), 0)
    column = lax.broadcasted_iota(jnp.int32, (shards, total), 1)
    return rows_sum(jnp.where(column // width == shard, dot(rows.astype(jnp.bfloat16), repeat), 0.0))


def front_kernel(kinds, *refs):
    (
        x_ref, wq_in, wk_in, wv_in, wo_in, up_in, down_in, *vectors,
    ) = refs[:16]
    (
        land_out, up_out, down_out, w_out, vec_ref, up_bias_ref,
        tile, chunk, mixed, rows_wide, w_ref, parts, join_sem, w_sem,
    ) = refs[16:30]
    rows = x_ref.shape[1]
    width = x_ref.shape[2]
    shards, depth, _ = mixed.shape
    enter, begin, along_done, pass_on, corner, finish, kept, sent = gather_steps(
        kinds,
        [chunk, up_in, down_in],
        [mixed, up_out, down_out],
        refs[33:],
    )
    begin_pairs, arrive_pairs, sent_pairs = exchange(True, parts, land_out, refs[30:33])
    joins = [
        pltpu.make_async_copy(ref, chunk.at[:, pl.ds(k * width, width)], join_sem.at[k])
        for k, ref in enumerate((wq_in, wk_in, wv_in, wo_in))
    ]
    for copy in joins:
        copy.start()
    tile[...] = jnp.zeros(tile.shape, jnp.float32)
    for k, ref in enumerate(vectors):
        tile[k, : ref.shape[0]] = ref[...].astype(jnp.float32)
    chunk[:, 4 * width :] = tile[...].astype(jnp.bfloat16)
    for copy in joins:
        copy.wait()
    enter()
    begin(0)
    begin(1)
    begin(2)
    along_done(0, 1)
    pass_on(0, 0)
    along_done(0, 2)
    along_done(1, 1)
    along_done(2, 1)
    pass_on(0, 1)
    corner(0, 0)
    along_done(0, 3)
    pass_on(1, 0)
    pass_on(2, 0)
    pass_on(0, 2)
    corner(0, 1)
    pass_on(0, 3)
    corner(0, 2)
    along_done(1, 2)
    along_done(2, 2)
    corner(0, 3)
    finish(0)
    kept()
    for s in range(0, 4 * width, width):
        part = mixed[:, :, s : s + width].astype(jnp.float32).reshape(width, width)
        w_ref[:, s : s + width] = part.astype(jnp.bfloat16)
    leave = pltpu.make_async_copy(w_ref, w_out, w_sem)
    leave.start()
    rows_wide[...] = mixed[:, :, 4 * width :].astype(jnp.float32)
    for k in range(8):
        vec_ref[k : k + 1, :] = spread_of(rows_wide[:, k, :], depth)
    up_bias_ref[...] = spread_of(rows_wide[:, 8, :], up_bias_ref.shape[1] // shards)
    tokens = x_ref[...].reshape(2 * rows, width)
    made = []
    for k in range(3):
        part = dot(tokens, w_ref[:, k * width : (k + 1) * width])
        if k != 1:
            part = part + vec_ref[k // 2 : k // 2 + 1, :]
        made.append(part.astype(jnp.bfloat16))
    q, k, v = made
    for pair in range(parts.shape[0]):
        col, at = pair // 2 * HD, pair % 2 * rows
        mid = at + rows // 2
        parts[pair, :rows] = jnp.concatenate(
            [halves(k[at : at + rows], col), halves(v[at : at + rows], col)], axis=1
        )
        parts[pair, rows:] = jnp.concatenate(
            [halves(q[at:mid], col), halves(q[mid : at + rows], col)], axis=1
        )
    begin_pairs()
    for i in (1, 2):
        pass_on(i, 1)
        corner(i, 0)
    for i in (1, 2):
        along_done(i, 3)
    for i in (1, 2):
        pass_on(i, 2)
        corner(i, 1)
    for i in (1, 2):
        pass_on(i, 3)
        corner(i, 2)
    for i in (1, 2):
        corner(i, 3)
    arrive_pairs()
    finish(1)
    finish(2)
    kept()
    leave.wait()
    sent()
    sent_pairs()


def front_call(tokens, matrices, up, down, vectors, collective):
    micro, rows, width = tokens.shape
    depth, ff = up.shape
    groups = lax.axis_size("head")
    devices = groups * lax.axis_size("blk")
    f32, bf16 = jnp.float32, jnp.bfloat16
    half = 2 * width
    kinds = [
        (False, True, (cut(1, 0, half), cut(1, half, half + 128))),
        (False, True, weight_cuts(ff, width)[0]),
        (False, True, weight_cuts(ff, width)[1]),
    ]
    near = pl.BlockSpec(memory_space=pltpu.VMEM)
    far = pl.BlockSpec(memory_space=pl.ANY)
    return pl.pallas_call(
        partial(front_kernel, kinds),
        out_shape=(
            jax.ShapeDtypeStruct((devices, rows + rows // 2, 2 * HD), bf16),
            jax.ShapeDtypeStruct((devices,) + up.shape, bf16),
            jax.ShapeDtypeStruct((devices,) + down.shape, bf16),
            jax.ShapeDtypeStruct((width, 4 * width), bf16),
            jax.ShapeDtypeStruct((8, width), f32),
            jax.ShapeDtypeStruct((1, ff), f32),
        ),
        in_specs=[near] + [far] * 6 + [near] * 9,
        out_specs=(far,) * 4 + (near,) * 2,
        scratch_shapes=[
            pltpu.VMEM((depth, 128), f32),
            pltpu.VMEM((depth, 4 * width + 128), bf16),
            pltpu.VMEM((devices, depth, 4 * width + 128), bf16),
            pltpu.VMEM((devices, depth, 128), f32),
            pltpu.VMEM((width, 4 * width), bf16),
            pltpu.VMEM((HEADS * micro, rows + rows // 2, 2 * HD), bf16),
            pltpu.SemaphoreType.DMA((4,)),
            pltpu.SemaphoreType.DMA,
        ]
        + exchange_semaphores()
        + gather_semaphores(3),
        compiler_params=pltpu.CompilerParams(
            collective_id=collective, has_side_effects=True, vmem_limit_bytes=56 * 2**20
        ),
        name="front",
    )(tokens, *matrices, up, down, *vectors)


def scatter_steps(cuts, ins, bufs, sems, made=()):
    local_sem, line_send, line_recv, core_send, core_recv, send, recv = sems
    b, h, core, x, y, across_x, across_y, partner, line = places()
    seen = jnp.where(jnp.logical_or(h == 1, h == 2), 2, 3)
    chip = b // 2
    targets = (3 - chip, chip + 1 - 2 * x, chip + 2 - 4 * y, chip)
    started = []
    loads = {}
    order = (3, 2, 1, 0)

    def go(copy):
        copy.start()
        started.append(copy)

    def part(ref, cut):
        axis, start, size = cut
        return ref.at[(slice(None),) * axis + (pl.ds(start, size),)]

    def along(i, src, landing, d):
        go(
            remote(
                src, landing, line_send.at[i, d], line_recv.at[i, 1 if d == 1 else seen], (b, line[d])
            )
        )

    def fetch(i, at, src, dst):
        loads[i, at] = pltpu.make_async_copy(src, dst, local_sem.at[i, at])
        loads[i, at].start()

    def begin(i, some=(0, 1, 2, 3)):
        if i in made:
            fetch(i, 0, ins[i][0], bufs[i][1].at[pl.ds(1, 3)])
            fetch(i, 1, ins[i][1], bufs[i][2])
            fetch(i, 2, ins[i][2], bufs[i][3])
            return
        from_partner, total = bufs[i][0], bufs[i][1]
        for t in some:
            go(
                remote(
                    ins[i].at[pl.ds((targets[t] * 2 + 1 - core) * 4, 4)],
                    from_partner.at[t],
                    core_send.at[i, t],
                    core_recv.at[i, t],
                    (partner, h),
                )
            )
            fetch(i, t, ins[i].at[pl.ds((targets[t] * 2 + core) * 4, 4)], total.at[t])

    def wait_for(ref, i, d, k):
        remote(ref, ref, send.at[i, d, k], recv.at[i, d, k], (partner, h)).wait_recv()

    def ready(i, t):
        loads[i, t].wait()
        here = bufs[i][0].at[t]
        remote(here, here, core_send.at[i, t], core_recv.at[i, t], (partner, h)).wait_recv()

    def both_cores(i, t, d, extra=()):
        from_partner, total = bufs[i][0], bufs[i][1]
        place = line[d]
        value = total[t, place].astype(jnp.float32)
        if i not in made:
            value = value + from_partner[t, place].astype(jnp.float32)
        elif not extra:
            return
        for ref in extra:
            value = value + ref[d].astype(jnp.float32)
        total[t, place] = value.astype(total.dtype)

    def add_corner(i, t, d, ref, cut):
        total = bufs[i][1]
        axis, start, size = cut
        at = (t, line[d]) + (slice(None),) * axis + (pl.ds(start, size),)
        value = total[at].astype(jnp.float32) + ref[d].astype(jnp.float32)
        total[at] = value.astype(total.dtype)

    def corner(i):
        total = bufs[i][1]
        first, second = cuts[i]
        ready(i, 0)
        for d in order:
            both_cores(i, 0, d)
            mine = total.at[0, line[d]]
            if first is not None:
                go(remote(part(mine, first), bufs[i][2].at[d], send.at[i, d, 0], recv.at[i, d, 0], (across_x, h)))
            if second is not None:
                go(remote(part(mine, second), bufs[i][3].at[d], send.at[i, d, 1], recv.at[i, d, 1], (across_y, h)))

    def corner_arrived(i, d, at):
        if cuts[i][at] is not None and i not in made:
            wait_for(bufs[i][2 + at].at[d], i, d, at)

    def leave(i, left, sems_):
        copies = []
        for t in (1, 2, 3):
            ready(i, t)
            for d in order:
                both_cores(i, t, d)
            copies.append(pltpu.make_async_copy(bufs[i][1].at[t], left.at[t - 1], sems_.at[i, t]))
            copies[-1].start()
        for d in order:
            for at in range(2):
                corner_arrived(i, d, at)
        return copies

    def sides(i):
        total = bufs[i][1]
        first, second = cuts[i]
        if i in made:
            for at in range(3):
                loads[i, at].wait()
        else:
            ready(i, 1)
            ready(i, 2)
        for d in order:
            both_cores(i, 1, d)
            if second is not None:
                corner_arrived(i, d, 1)
                add_corner(i, 1, d, bufs[i][3], second)
            go(remote(total.at[1, line[d]], bufs[i][4].at[d], send.at[i, d, 2], recv.at[i, d, 2], (across_x, h)))
            both_cores(i, 2, d)
            if first is not None:
                corner_arrived(i, d, 0)
                add_corner(i, 2, d, bufs[i][2], first)
            go(remote(total.at[2, line[d]], bufs[i][5].at[d], send.at[i, d, 3], recv.at[i, d, 3], (across_y, h)))

    def own(i):
        total = bufs[i][1]
        if i not in made:
            ready(i, 3)
        for d in order:
            wait_for(bufs[i][4].at[d], i, d, 2)
            wait_for(bufs[i][5].at[d], i, d, 3)
            both_cores(i, 3, d, (bufs[i][4], bufs[i][5]))
            if d > 0:
                along(i, total.at[3, line[d]], bufs[i][6].at[1 if d == 1 else seen], d)

    def finish(i):
        value = bufs[i][1][3, h].astype(jnp.float32)
        for d in range(1, 4):
            landing = bufs[i][6].at[d]
            remote(
                landing, landing, line_send.at[i, d], line_recv.at[i, d], (b, line[d])
            ).wait_recv()
            value = value + bufs[i][6][d].astype(jnp.float32)
        return value

    def sent():
        for copy in started:
            copy.wait_send()

    def enter():
        meet(b, h)

    return enter, begin, corner, leave, sides, own, finish, sent


def weight_cuts(ff, width):
    return tuple((cut(1, 0, n // 2), cut(1, n // 2, n // 2)) for n in (ff, width))


def scatter_scratch(chunk, dtype, cuts, made=False):
    shapes = [(16, 128) if made else (4, 4) + chunk, (4, 4) + chunk]
    for cut_ in cuts:
        size = [16, 128]
        if cut_ is not None:
            size = list(chunk)
            size[cut_[0]] = cut_[2]
        shapes.append((4,) + tuple(size))
    shapes += [(4,) + chunk] * 3
    return [pltpu.VMEM(shape, dtype) for shape in shapes]


def scatter_semaphores(n):
    dma = pltpu.SemaphoreType.DMA
    return [dma((n, 4))] * 5 + [dma((n, 4, 4))] * 2


UP, DOWN, OUT, QUERY, KEY, VALUE, SMALL = range(7)


def back_kernel(cuts, *refs):
    (
        parts_in, up_left, up_first, up_second, down_left, down_first, down_second, x_ref, mixed_in, d_mix_ref, g_out_ref, g_vec_ref, g_up_bias_ref,
        d_x_ref, g_outw_ref, g_query_ref, g_key_ref, g_value_ref, g_up_ref, g_down_ref, g_small_ref,
        land, terms, small, w_ref, d_q, d_k, d_v, w_sem,
    ), rest = refs[:29], list(refs[29:])
    q_sems, kv_sems, rest = rest[:3], rest[3:6], rest[6:]
    bufs = [rest[7 * i : 7 * i + 7] for i in range(len(cuts))]
    rows = x_ref.shape[1]
    width = x_ref.shape[2]
    _, shards, depth, _ = terms.shape
    ins = ((up_left, up_first, up_second), (down_left, down_first, down_second), terms.at[0], terms.at[1], terms.at[2], terms.at[3], small)
    enter, begin, corner, _, sides, own, finish, sent = scatter_steps(
        cuts, ins, bufs, rest[7 * len(cuts) :], (UP, DOWN)
    )
    begin_q, arrive_q, sent_q = exchange(False, parts_in, land, q_sems, pl.ds(rows, rows // 2))
    begin_kv, arrive_kv, sent_kv = exchange(False, parts_in, land, kv_sems, pl.ds(0, rows))
    load = pltpu.make_async_copy(mixed_in.at[:, pl.ds(0, 3 * width)], w_ref, w_sem)
    load.start()
    def keep_term(at, value):
        terms[at] = value.reshape(shards, depth, width).astype(jnp.bfloat16)

    def keep_term(at, value):
        terms[at] = value.reshape(shards, depth, width).astype(jnp.bfloat16)

    begin(UP)
    begin(DOWN)
    enter()
    begin_q()
    begin_kv()
    keep_term(0, g_out_ref[...].astype(jnp.float32))
    small[...] = jnp.zeros(small.shape, jnp.float32)
    begin(OUT)
    sides(UP)
    sides(DOWN)
    corner(OUT)
    own(UP)
    arrive_q()
    arrive_kv()
    spans = []
    for m in range(2):
        top, mid = m * rows, m * rows + rows // 2
        spans.append((m, slice(top, top + rows), slice(top, mid), slice(mid, top + rows)))
    tokens = x_ref[...].reshape(2 * rows, width)
    for p in range(HEADS // 2):
        at = pl.ds(p * 2 * HD, 2 * HD)
        for m, _, early, late in spans:
            one, two = land[4 * p + m, rows:], land[4 * p + 2 + m, rows:]
            d_q[early, at] = jnp.concatenate([one[:, :HD], two[:, :HD]], axis=1)
            d_q[late, at] = jnp.concatenate([one[:, HD:], two[:, HD:]], axis=1)
    for p in range(HEADS // 2):
        at = pl.ds(p * 2 * HD, 2 * HD)
        for m, both, _, _ in spans:
            one, two = land[4 * p + m, :rows], land[4 * p + 2 + m, :rows]
            d_k[both, at] = jnp.concatenate([one[:, :HD], two[:, :HD]], axis=1)
            d_v[both, at] = jnp.concatenate([one[:, HD:], two[:, HD:]], axis=1)
    keep_term(1, dot(tokens, d_q[...], COLS))
    keep_term(2, dot(tokens, d_k[...], COLS))
    keep_term(3, dot(tokens, d_v[...], COLS))
    vectors = jnp.concatenate(
        [
            rows_sum(d_q[...].astype(jnp.float32)),
            rows_sum(d_v[...].astype(jnp.float32)),
            g_vec_ref[:6, :],
        ],
        axis=0,
    )
    up_bias = g_up_bias_ref[...]
    up_depth = up_bias.shape[1] // shards
    for s in range(shards):
        small[s, :8, :depth] = vectors[:, s * depth : (s + 1) * depth]
        small[s, 8:9, :up_depth] = up_bias[:, s * up_depth : (s + 1) * up_depth]
    begin(QUERY)
    begin(KEY)
    begin(VALUE)
    begin(SMALL)
    corner(QUERY)
    corner(KEY)
    corner(VALUE)
    corner(SMALL)
    own(DOWN)
    sides(OUT)
    sides(QUERY)
    sides(KEY)
    sides(VALUE)
    sides(SMALL)
    load.wait()
    d_x = d_mix_ref[...]
    for k, half_ref in enumerate((d_q, d_k, d_v)):
        d_x = d_x + dot(half_ref[...], w_ref[:, k * width : (k + 1) * width], ROWS)
    d_x_ref[...] = d_x.astype(jnp.bfloat16).reshape(2, rows, width)
    g_up_ref[...] = finish(UP)
    g_down_ref[...] = finish(DOWN)
    own(OUT)
    own(QUERY)
    own(KEY)
    own(VALUE)
    own(SMALL)
    g_outw_ref[...] = finish(OUT)
    g_query_ref[...] = finish(QUERY)
    g_key_ref[...] = finish(KEY)
    g_value_ref[...] = finish(VALUE)
    g_small_ref[...] = finish(SMALL)
    sent_q()
    sent()
    sent_kv()


def back_call(parts, lefts, tokens, mixed, d_mix, g_out, g_vec, g_up_bias, collective):
    micro, rows, width = tokens.shape
    devices = parts.shape[0]
    depth, ff = lefts[0].shape[2:]
    f32, bf16 = jnp.float32, jnp.bfloat16
    one_way, other_way = (cut(1, 0, width), None), (None, cut(1, 0, width))
    cuts = [*weight_cuts(ff, width), one_way, other_way, one_way, other_way, (cut(1, 0, 128), None)]
    square = (depth, width)
    chunks = [(lefts[0].shape[2:], bf16), (lefts[3].shape[2:], bf16)] + [(square, bf16)] * 4
    chunks += [((16, 128), f32)]
    scratch = [
        one
        for i, ((chunk, dtype), c) in enumerate(zip(chunks, cuts))
        for one in scatter_scratch(chunk, dtype, c, i < 2)
    ]
    near = pl.BlockSpec(memory_space=pltpu.VMEM)
    far = pl.BlockSpec(memory_space=pl.ANY)
    outs = [jax.ShapeDtypeStruct(tokens.shape, bf16)]
    outs += [jax.ShapeDtypeStruct(square, f32)] * 4
    outs += [
        jax.ShapeDtypeStruct((depth, ff), f32),
        jax.ShapeDtypeStruct(lefts[3].shape[2:], f32),
        jax.ShapeDtypeStruct((16, 128), f32),
    ]
    return pl.pallas_call(
        partial(back_kernel, cuts),
        out_shape=tuple(outs),
        in_specs=[far] * 7 + [near, far] + [near] * 4,
        out_specs=(near,) * len(outs),
        scratch_shapes=[
            pltpu.VMEM((HEADS * micro,) + parts.shape[1:], bf16),
            pltpu.VMEM((4, devices) + square, bf16),
            pltpu.VMEM((devices, 16, 128), f32),
            pltpu.VMEM((width, 3 * width), bf16),
        ]
        + [pltpu.VMEM((micro * rows, width), bf16)] * 3
        + [pltpu.SemaphoreType.DMA]
        + exchange_semaphores() * 2
        + scratch
        + scatter_semaphores(len(cuts)),
        compiler_params=pltpu.CompilerParams(
            collective_id=collective, has_side_effects=True, vmem_limit_bytes=61 * 2**20
        ),
        name="back",
    )(parts, *lefts, tokens, mixed, d_mix, g_out, g_vec, g_up_bias)


def leave_kernel(*refs):
    *wholes, small_in = refs[:8]
    outs = refs[8:]
    for from_ref, to_ref in zip(wholes, outs):
        to_ref[...] = from_ref[...]
    for k, ref in enumerate(outs[7:]):
        ref[...] = small_in[k, : ref.shape[0]]


def leave_call(*arrays):
    *wholes, _ = arrays
    depth, width = wholes[1].shape
    f32 = jnp.float32
    outs = [jax.ShapeDtypeStruct(a.shape, a.dtype) for a in wholes]
    outs += [jax.ShapeDtypeStruct((depth,), f32)] * 8
    outs += [jax.ShapeDtypeStruct((wholes[6].shape[0],), f32)]
    near = pl.BlockSpec(memory_space=pltpu.VMEM)
    return pl.pallas_call(
        leave_kernel,
        out_shape=tuple(outs),
        in_specs=[near] * 8,
        out_specs=(near,) * len(outs),
        name="leave",
    )(*arrays)


def cut(axis, start, size):
    return (axis, start, size)


def lanes_of(shape, low):
    lane = lax.broadcasted_iota(jnp.int32, shape, len(shape) - 1)
    if isinstance(low, bool):
        return lane < HD if low else lane >= HD
    return lane // HD == jnp.where(low, 0, 1)


def dot(left_side, right_side, contract=((1,), (0,))):
    return lax.dot_general(
        left_side, right_side, (contract, ((), ())), preferred_element_type=jnp.float32
    )


ROWS = ((1,), (1,))
COLS = ((0,), (0,))


def halves(array, col):
    return array[:, col : col + HD]


def listed_rows(table_ref, blocks, n):
    rows = [jnp.maximum(n - 1, 0), n, jnp.minimum(n + 1, blocks - 1)]
    rows += [table_ref[n * RAND + r] for r in range(RAND)]
    return rows + [table_ref[blocks * RAND + g] for g in range(GLOB)]


def outside(here, total, listed):
    lane = lax.broadcasted_iota(jnp.int32, (1, listed * BLOCK), 1)
    before = jnp.logical_and(lane < BLOCK, here == 0)
    after = jnp.logical_and(
        jnp.logical_and(lane >= 2 * BLOCK, lane < 3 * BLOCK), here == total - 1
    )
    return jnp.where(jnp.logical_or(before, after), -jnp.inf, 0.0)


def only(value, low):
    return jnp.where(lanes_of(value.shape, low), value, jnp.zeros_like(value))


def turned(value):
    return jnp.concatenate([value[:, HD:], value[:, :HD]], axis=1)


def to_side(value, odd, low):
    if isinstance(odd, bool):
        return only(turned(value) if odd == low else value, low)
    return only(jnp.where((odd == 1) == low, turned(value), value), low)


def key_rows(ref, spot, step):
    return ref[pl.ds(spot, step), :2].reshape(step * 2 * BLOCK, 2 * HD)


GROUP = 16
STEP = 8


def attend_kernel(table_ref, land_ref, out_ref, lse_ref):
    devices = land_ref.shape[0]
    blocks = 2 * devices
    scale = jnp.bfloat16(HD ** (-0.5))

    def query_blocks(group, carry):
        kvs, scores = [], []
        for u in range(GROUP):
            n = group * GROUP + u
            rows = listed_rows(table_ref, blocks, n)
            kvs.append(jnp.concatenate([land_ref[r // 2, r % 2] for r in rows], axis=0))
            q = to_side(land_ref[group * (GROUP // 2) + u // 2, 2], u % 2 == 1, True) * scale
            scores.append(dot(q, kvs[-1], ROWS) + outside(n, blocks, len(rows)))
        raised = []
        for u, score in enumerate(scores):
            top = jnp.max(score, axis=1, keepdims=True)
            probs = jnp.exp(score - top)
            total_sum = jnp.sum(probs, axis=1, keepdims=True)
            raised.append((probs * (1.0 / total_sum)).astype(jnp.bfloat16))
            lse_ref[group * GROUP + u] = jnp.broadcast_to(
                top + jnp.log(total_sum), lse_ref.shape[1:]
            )
        outs = [dot(r, kv) for r, kv in zip(raised, kvs)]
        for u in range(0, GROUP, 2):
            out_ref[group * (GROUP // 2) + u // 2] = jnp.where(
                lanes_of(outs[u].shape, True), turned(outs[u]), outs[u + 1]
            ).astype(jnp.bfloat16)
        return carry

    def everything():
        lax.fori_loop(0, blocks // GROUP, query_blocks, 0)
        spots = range(0, devices, STEP)
        chosen = [table_ref[blocks * RAND + g] for g in range(GLOB)]
        q = jnp.concatenate(
            [to_side(land_ref[row // 2, 2], row % 2, True) for row in chosen], axis=0
        )
        scores = [dot(q * scale, key_rows(land_ref, spot, STEP), ROWS) for spot in spots]
        top = scores[0].max(axis=1, keepdims=True)
        for score in scores[1:]:
            top = jnp.maximum(top, score.max(axis=1, keepdims=True))
        raised = [jnp.exp(score - top) for score in scores]
        total_sum = sum(jnp.sum(r, axis=1, keepdims=True) for r in raised)
        out = sum(
            dot(r.astype(jnp.bfloat16), key_rows(land_ref, spot, STEP))
            for r, spot in zip(raised, spots)
        )
        out = out / total_sum
        lse = jnp.broadcast_to(top + jnp.log(total_sum), out.shape)
        for g, row in enumerate(chosen):
            at = slice(g * BLOCK, (g + 1) * BLOCK)
            lse_ref[row] = lse[at]
            new = jnp.where(row % 2 == 0, turned(out[at]), out[at]).astype(jnp.bfloat16)
            old = out_ref[row // 2]
            out_ref[row // 2] = jnp.where(lanes_of(old.shape, row % 2 == 0), new, old)

    pl.when(table_ref[blocks * RAND + GLOB] == 1)(everything)


def attend_call(table, land):
    spec = pl.BlockSpec(memory_space=pltpu.VMEM)
    devices, _, block, lanes = land.shape
    return pl.pallas_call(
        attend_kernel,
        out_shape=(
            jax.ShapeDtypeStruct((devices, block, lanes), jnp.bfloat16),
            jax.ShapeDtypeStruct((2 * devices, block, lanes), jnp.float32),
        ),
        in_specs=[pl.BlockSpec(memory_space=pltpu.SMEM), spec],
        out_specs=(spec, spec),
        compiler_params=pltpu.CompilerParams(vmem_limit_bytes=56 * 2**20),
        name="attend",
    )(table, land)


def attend_back_kernel(table_ref, land_ref, d_ref, out_ref, lse_ref, parts_ref, total_ref):
    devices = land_ref.shape[0]
    blocks = 2 * devices
    scale = jnp.bfloat16(HD ** (-0.5))

    def wide(column, width):
        return jnp.concatenate([column] * (width // column.shape[1]), axis=1)

    def pair_of(place, odd, keep):
        q = to_side(land_ref[place, 2], odd, True) * scale
        d = to_side(d_ref[place], odd, False)
        if keep is not None:
            d = d * keep
        out = to_side(out_ref[place], odd, False)
        delta = jnp.sum(d.astype(jnp.float32) * out.astype(jnp.float32), axis=1, keepdims=True)
        return q, d, delta

    def query_blocks(group, carry):
        listed, kvs, pairs, deltas, boths = [], [], [], [], []
        for u in range(GROUP):
            n = group * GROUP + u
            rows = listed_rows(table_ref, blocks, n)
            is_global = jnp.logical_or(n == rows[-1], n == rows[-2])
            keep = jnp.where(is_global, 0.0, 1.0).astype(jnp.bfloat16)
            kv = jnp.concatenate([land_ref[r // 2, r % 2] for r in rows], axis=0)
            q, d, delta = pair_of(group * (GROUP // 2) + u // 2, u % 2 == 1, keep)
            listed.append(rows)
            kvs.append(kv)
            pairs.append(jnp.concatenate([q, d], axis=0))
            deltas.append(delta)
            boths.append(dot(pairs[-1], kv, ROWS))
        weights = []
        for u, both in enumerate(boths):
            n = group * GROUP + u
            width = both.shape[1]
            scores = both[:BLOCK] + outside(n, blocks, width // BLOCK)
            probs = jnp.exp(scores - wide(lse_ref[n], width))
            d_scores = probs * (both[BLOCK:] - deltas[u])
            weights.append(
                jnp.concatenate(
                    [d_scores.astype(jnp.bfloat16), probs.astype(jnp.bfloat16)], axis=0
                )
            )
        outs = []
        for u, weight in enumerate(weights):
            d_kv = dot(weight, pairs[u], COLS)
            for at, r in enumerate(listed[u]):
                total_ref[r // 2, r % 2] += d_kv[at * BLOCK : (at + 1) * BLOCK]
            outs.append(dot(weight[:BLOCK], kvs[u]) * HD ** (-0.5))
        for u in range(0, GROUP, 2):
            parts_ref[group * (GROUP // 2) + u // 2, 2] = jnp.where(
                lanes_of(outs[u].shape, True), outs[u], turned(outs[u + 1])
            ).astype(jnp.bfloat16)
        return carry

    def everything():
        def clear(i, carry):
            total_ref[i] = jnp.zeros(total_ref.shape[1:], jnp.float32)
            return carry

        lax.fori_loop(0, devices, clear, 0)
        lax.fori_loop(0, blocks // GROUP, query_blocks, 0)
        chosen = [table_ref[blocks * RAND + g] for g in range(GLOB)]
        found = [pair_of(row // 2, row % 2, None) for row in chosen]
        both_rows = GLOB * BLOCK
        pairs = jnp.concatenate([f[0] for f in found] + [f[1] for f in found], axis=0)
        delta = jnp.concatenate([f[2] for f in found], axis=0)
        lse = jnp.concatenate([lse_ref[row] for row in chosen], axis=0)

        def some_keys(spot, d_q):
            kv = key_rows(land_ref, spot * STEP, STEP)
            both = dot(pairs, kv, ROWS)
            probs = jnp.exp(both[:both_rows] - wide(lse, both.shape[1]))
            d_scores = probs * (both[both_rows:] - delta)
            weight = jnp.concatenate(
                [d_scores.astype(jnp.bfloat16), probs.astype(jnp.bfloat16)], axis=0
            )
            total_ref[pl.ds(spot * STEP, STEP)] += dot(weight, pairs, COLS).reshape(
                STEP, 2, BLOCK, 2 * HD
            )
            return d_q + dot(weight[:both_rows], kv)

        d_q = lax.fori_loop(
            0, devices // STEP, some_keys, jnp.zeros((both_rows, 2 * HD), jnp.float32)
        )
        d_q = d_q * HD ** (-0.5)
        for g, row in enumerate(chosen):
            part = d_q[g * BLOCK : (g + 1) * BLOCK]
            new = jnp.where(row % 2 == 0, part, turned(part)).astype(jnp.bfloat16)
            old = parts_ref[row // 2, 2]
            parts_ref[row // 2, 2] = jnp.where(lanes_of(old.shape, row % 2 == 0), new, old)

        def give(i, carry):
            parts_ref[i, :2] = total_ref[i].astype(jnp.bfloat16)
            return carry

        lax.fori_loop(0, devices, give, 0)

    pl.when(table_ref[blocks * RAND + GLOB] == 1)(everything)


def attend_back_call(table, land, d, out, lse):
    spec = pl.BlockSpec(memory_space=pltpu.VMEM)
    devices, _, block, lanes = land.shape
    return pl.pallas_call(
        attend_back_kernel,
        out_shape=jax.ShapeDtypeStruct(land.shape, jnp.bfloat16),
        in_specs=[pl.BlockSpec(memory_space=pltpu.SMEM)] + [spec] * 4,
        out_specs=spec,
        scratch_shapes=[pltpu.VMEM((devices, 2, block, lanes), jnp.float32)],
        compiler_params=pltpu.CompilerParams(vmem_limit_bytes=60 * 2**20),
        name="attend_back",
    )(table, land, d, out, lse)


def centre(values):
    center = jnp.mean(values, axis=1, keepdims=True)
    centred = values - center
    spread = jnp.mean(centred * centred, axis=1, keepdims=True)
    inverse = lax.rsqrt(spread + 1e-12)
    return centred * inverse, inverse


def centre_back(hat, inverse, grad):
    return inverse * (
        grad
        - jnp.mean(grad, axis=1, keepdims=True)
        - hat * jnp.mean(grad * hat, axis=1, keepdims=True)
    )


def rows_sum(values):
    return jnp.sum(values, axis=0, keepdims=True)


WEIGHT_CHUNK = 1024


def dense_kernel(
    c_in, x_ref, cot_ref, wo_in, up_in, down_in, vec_ref, up_bias_ref,
    out_ref, d_mix_ref, d_land, g_out_ref, up_left, up_first, up_second, down_left, down_first, down_second, g_vec_ref, g_up_bias_ref,
    ctx, first, hat, low, low_t, act, slope, ffn, wo_ref, up_ref, down_ref, g_up_ref, g_down_ref, in_sem, out_sem,
    c_ref, d_c_ref, up_other, up_total, down_other, down_total, *sems,
):
    rows = x_ref.shape[1]
    width = x_ref.shape[2]
    ff = up_ref.shape[1]
    chunk = WEIGHT_CHUNK
    fetches = [
        pltpu.make_async_copy(wo_in.at[:, pl.ds(3 * width, width)], wo_ref, in_sem.at[0]),
    ]
    for i in range(ff // chunk):
        at = pl.ds(i * chunk, chunk)
        fetches.append(pltpu.make_async_copy(up_in.at[:, at], up_ref.at[:, at], in_sem.at[2 * i + 1]))
        fetches.append(pltpu.make_async_copy(down_in.at[at], down_ref.at[at], in_sem.at[2 * i + 2]))
    for copy in fetches:
        copy.start()
    begin_c, arrive_c, sent_c = exchange(False, c_in, c_ref, sems[:3])
    begin_d, arrive_d, sent_d = exchange(True, d_c_ref, d_land, sems[3:6])
    enter, begin, corner, leave, _, _, _, sent = scatter_steps(
        weight_cuts(ff, width),
        (g_up_ref, g_down_ref),
        ((up_other, up_total, up_first, up_second), (down_other, down_total, down_first, down_second)),
        sems[6:],
    )
    enter()
    begin_c()
    arrive_c()
    out_bias, attn_gain, attn_shift, down_bias, ffn_gain, ffn_shift = (
        vec_ref[k : k + 1, :] for k in range(2, 8)
    )
    for p in range(HEADS // 2):
        at = pl.ds(p * 2 * HD, 2 * HD)
        for m in range(2):
            one, two = c_ref[4 * p + m], c_ref[4 * p + 2 + m]
            top, mid = m * rows, m * rows + rows // 2
            ctx[top:mid, at] = jnp.concatenate([one[:, :HD], two[:, :HD]], axis=1)
            ctx[mid : top + rows, at] = jnp.concatenate([one[:, HD:], two[:, HD:]], axis=1)
    tokens = x_ref[...].reshape(2 * rows, width).astype(jnp.float32)
    fetches[0].wait()
    hat_first, inverse_first = centre(tokens + dot(ctx[...], wo_ref[...]) + out_bias)
    hat[...] = hat_first
    first[...] = hat_first * attn_gain + attn_shift
    low[...] = first[...].astype(jnp.bfloat16)
    low_t[...] = first[...].T.astype(jnp.bfloat16)
    ffn[...] = first[...] + down_bias

    def forward(i):
        at = pl.ds(i * chunk, chunk)
        fetches[2 * i + 1].wait()
        fetches[2 * i + 2].wait()
        hidden = dot(low[...], up_ref[:, at]) + up_bias_ref[:, at]
        share = 0.5 * (1.0 + lax.erf(hidden * 0.7071067811865476))
        bell = jnp.exp(-0.5 * hidden * hidden) * 0.3989422804014327
        slope[:, at] = share + hidden * bell
        act_low = (hidden * share).astype(jnp.bfloat16)
        act[:, at] = act_low
        ffn[...] += dot(act_low, down_ref[at, :])

    for i in range(ff // chunk):
        forward(i)
    hat_second, inverse_second = centre(ffn[...])
    out_ref[...] = (
        (hat_second * ffn_gain + ffn_shift).astype(jnp.bfloat16).reshape(2, rows, width)
    )
    cot = cot_ref[...].reshape(2 * rows, width).astype(jnp.float32)
    g_vec_ref[4:5, :] = rows_sum(cot * hat_second)
    g_vec_ref[5:6, :] = rows_sum(cot)
    d_second = centre_back(hat_second, inverse_second, cot * ffn_gain)
    d_ffn = d_second.astype(jnp.bfloat16)
    g_vec_ref[3:4, :] = rows_sum(d_ffn.astype(jnp.float32))
    ffn[...] = d_second

    shards, depth, _ = g_up_ref.shape
    down_depth = g_down_ref.shape[1]
    half = ff // 2
    for i in range(2):
        at = pl.ds(i * half, half)
        g_down_ref[pl.ds(i * (shards // 2), shards // 2)] = (
            dot(act[:, at], d_ffn, COLS)
            .reshape(shards // 2, down_depth, width)
            .astype(jnp.bfloat16)
        )
    begin(1, (0,))
    for i in range(2):
        at = pl.ds(i * half, half)
        d_act = dot(d_ffn, down_ref[at, :], ROWS)
        d_hidden = (d_act * slope[:, at]).astype(jnp.bfloat16)
        g_up_bias_ref[:, at] = rows_sum(d_hidden.astype(jnp.float32))
        g_up_ref[:, :, at] = (
            dot(low_t[...], d_hidden).reshape(shards, depth, half).astype(jnp.bfloat16)
        )
        ffn[...] += dot(d_hidden, up_ref[:, at], ROWS)
        if i == 0:
            corner(1)
            begin(1, (1, 2, 3))
    begin(0, (0,))
    d_first = ffn[...]
    g_vec_ref[1:2, :] = rows_sum(d_first * hat[...])
    g_vec_ref[2:3, :] = rows_sum(d_first)
    d_mix = centre_back(hat[...], inverse_first, d_first * attn_gain)
    d_mix_ref[...] = d_mix
    d_branch = d_mix.astype(jnp.bfloat16)
    g_vec_ref[0:1, :] = rows_sum(d_branch.astype(jnp.float32))
    g_vec_ref[6:8, :] = jnp.zeros((2, width), jnp.float32)
    d_ctx = dot(d_branch, wo_ref[...], ROWS).astype(jnp.bfloat16)
    for pair in range(d_c_ref.shape[0]):
        col, top = pair // 2 * HD, pair % 2 * rows
        mid = top + rows // 2
        d_c_ref[pair] = jnp.concatenate(
            [halves(d_ctx[top:mid], col), halves(d_ctx[mid : top + rows], col)], axis=1
        )
    begin_d()
    corner(0)
    begin(0, (1, 2, 3))
    g_out_ref[...] = dot(ctx[...], d_branch, COLS).astype(jnp.bfloat16)
    for copy in leave(1, down_left, out_sem) + leave(0, up_left, out_sem):
        copy.wait()
    sent()
    arrive_d()
    sent_c()
    sent_d()


def dense_call(c, tokens, cot, mixed, up, down, vec, up_bias, collective):
    micro, rows, width = tokens.shape
    ff = up.shape[1]
    both = micro * rows
    devices = c.shape[0]
    up_chunk, down_chunk = (width // devices, ff), (ff // devices, width)
    far = pl.BlockSpec(memory_space=pl.ANY)
    f32, bf16 = jnp.float32, jnp.bfloat16

    def full(shape):
        return pl.BlockSpec(memory_space=pltpu.VMEM)

    outs = (
        jax.ShapeDtypeStruct(tokens.shape, bf16),
        jax.ShapeDtypeStruct((both, width), f32),
        jax.ShapeDtypeStruct(c.shape, bf16),
        jax.ShapeDtypeStruct((width, width), bf16),
        jax.ShapeDtypeStruct((3, 4) + up_chunk, bf16),
        jax.ShapeDtypeStruct((4, width // devices, ff // 2), bf16),
        jax.ShapeDtypeStruct((4, width // devices, ff // 2), bf16),
        jax.ShapeDtypeStruct((3, 4) + down_chunk, bf16),
        jax.ShapeDtypeStruct((4, ff // devices, width // 2), bf16),
        jax.ShapeDtypeStruct((4, ff // devices, width // 2), bf16),
        jax.ShapeDtypeStruct((8, width), f32),
        jax.ShapeDtypeStruct((1, ff), f32),
    )
    return pl.pallas_call(
        dense_kernel,
        out_shape=outs,
        in_specs=[
            far,
            full(tokens.shape),
            full(cot.shape),
            far,
            far,
            far,
            full(vec.shape),
            full(up_bias.shape),
        ],
        out_specs=tuple(far if k == 2 or 4 <= k < 10 else full(o.shape) for k, o in enumerate(outs)),
        scratch_shapes=[
            pltpu.VMEM((both, width), bf16),
            pltpu.VMEM((both, width), f32),
            pltpu.VMEM((both, width), f32),
            pltpu.VMEM((both, width), bf16),
            pltpu.VMEM((width, both), bf16),
            pltpu.VMEM((both, ff), bf16),
            pltpu.VMEM((both, ff), f32),
            pltpu.VMEM((both, width), f32),
            pltpu.VMEM((width, width), bf16),
            pltpu.VMEM((width, ff), bf16),
            pltpu.VMEM((ff, width), bf16),
            pltpu.VMEM((devices,) + up_chunk, bf16),
            pltpu.VMEM((devices,) + down_chunk, bf16),
            pltpu.SemaphoreType.DMA((1 + 2 * (ff // WEIGHT_CHUNK),)),
            pltpu.SemaphoreType.DMA((2, 4)),
            pltpu.VMEM((HEADS * micro,) + c.shape[1:], bf16),
            pltpu.VMEM((HEADS * micro,) + c.shape[1:], bf16),
            pltpu.VMEM((4, 4) + up_chunk, bf16),
            pltpu.VMEM((4, 4) + up_chunk, bf16),
            pltpu.VMEM((4, 4) + down_chunk, bf16),
            pltpu.VMEM((4, 4) + down_chunk, bf16),
        ]
        + exchange_semaphores() * 2
        + scatter_semaphores(2),
        compiler_params=pltpu.CompilerParams(
            collective_id=collective, has_side_effects=True, vmem_limit_bytes=60 * 2**20
        ),
        name="dense",
    )(c, tokens, cot, mixed, up, down, vec, up_bias)


def near_body(inputs, cotangent, random_blocks, global_blocks, *shards):
    (
        query_weight, query_bias, key_weight, value_weight, value_bias, out_weight, out_bias, attn_gain,
        attn_shift, up_weight, up_bias, down_weight, down_bias, ffn_gain, ffn_shift,
    ) = shards
    devices = lax.axis_size("head") * lax.axis_size("blk")
    micro, rows, width = inputs.shape
    depth = query_weight.shape[0]
    ff = up_weight.shape[1]
    land, up, down, mixed, vec, up_bias_row = front_call(
        inputs,
        (query_weight, key_weight, value_weight, out_weight),
        up_weight,
        down_weight,
        (
            query_bias, value_bias, out_bias, attn_gain, attn_shift, down_bias, ffn_gain, ffn_shift, up_bias,
        ),
        1,
    )
    up = up.reshape(width, ff)
    down = down.reshape(ff, width)
    busy, pair = place_pair(lax.axis_index("blk"), lax.axis_index("head"))
    head, at = pair // micro, pair % micro
    table = jnp.concatenate(
        [
            lax.dynamic_slice(
                random_blocks, (at, 0, head, 0), (1, random_blocks.shape[1], 1, RAND)
            ).reshape(-1),
            lax.dynamic_slice(global_blocks, (at, 0), (1, GLOB)).reshape(-1),
            busy.astype(jnp.int32)[None],
        ]
    )
    land = land.reshape(devices, 3, rows // 2, 2 * HD)
    attended, lse = attend_call(table, land)
    layer_out, d_mix, d_context, g_out, *lefts, g_vec, g_up_bias = dense_call(
        attended, inputs, cotangent, mixed, up, down, vec, up_bias_row, 3
    )
    parts = attend_back_call(table, land, d_context, attended, lse)
    results = back_call(
        parts.reshape(devices, 3 * rows // 2, 2 * HD),
        lefts,
        inputs,
        mixed,
        d_mix,
        g_out,
        g_vec,
        g_up_bias,
        5,
    )
    (
        input_grad, grad_out, grad_query, grad_key, grad_value, grad_up, grad_down, *vector, grad_up_bias,
    ) = leave_call(*results)
    return (
        layer_out, input_grad, grad_query, vector[0], grad_key, grad_value, vector[1], grad_out,
        vector[2], vector[3], vector[4], grad_up, grad_up_bias, grad_down, vector[5], vector[6], vector[7],
    )


def with_halo(cells, sides, width):
    for axis, dim in sides:
        count = lax.axis_size(axis)
        ends = count - 1
        head = lax.slice_in_dim(cells, 0, width, axis=dim)
        tail = lax.slice_in_dim(cells, cells.shape[dim] - width, cells.shape[dim], axis=dim)
        cells = jnp.concatenate(
            [
                lax.ppermute(tail, axis, [(i, (i + 1) % count) for i in range(ends)]),
                cells,
                lax.ppermute(head, axis, [((i + 1) % count, i) for i in range(ends)]),
            ],
            axis=dim,
        )
    return cells


def combined_all(part, axis, combine):
    gathered = jax.tree.map(lambda a: lax.all_gather(a, axis), part)

    def take(source):
        return jax.tree.map(lambda a: lax.dynamic_index_in_dim(a, source, 0, False), gathered)

    return lax.fori_loop(
        1, lax.axis_size(axis), lambda source, state: combine(state, take(source)), take(0)
    )


def taken(table, rows):
    return lax.map(lambda row: lax.dynamic_index_in_dim(table, row, 0, False), rows)


def layer_norm(values, norm_gain, norm_shift):
    center = jnp.mean(values, axis=-1, keepdims=True)
    centred = values - center
    spread = jnp.mean(centred * centred, axis=-1, keepdims=True)
    return centred * lax.rsqrt(spread + 1e-12) * norm_gain + norm_shift


def gelu_exact(values):
    return jax.nn.gelu(values, approximate=False)


def matmul(left_side, right_side):
    return jnp.dot(left_side, right_side, preferred_element_type=jnp.float32)


def matmul_left(left_side, right_side):
    return lax.dot_general(
        left_side, right_side, (((0,), (0,)), ((), ())), preferred_element_type=jnp.float32
    )


def matmul_right(left_side, right_side):
    return lax.dot_general(
        left_side, right_side, (((1,), (1,)), ((), ())), preferred_element_type=jnp.float32
    )


def column_sum(values):
    return jnp.sum(values.astype(jnp.float32), axis=0)


def combine_parts(earlier, later_part):
    joint_top = jnp.maximum(earlier[0], later_part[0])
    first_factor = jnp.exp(earlier[0] - joint_top)
    second_factor = jnp.exp(later_part[0] - joint_top)
    return (
        joint_top,
        earlier[1] * first_factor + later_part[1] * second_factor,
        earlier[2] * first_factor[..., None] + later_part[2] * second_factor[..., None],
    )


def fetch_weights(
    query_weight,
    query_bias,
    key_weight,
    value_weight,
    value_bias,
    out_weight,
    out_bias,
    attn_gain,
    attn_shift,
    up_weight,
    up_bias,
    down_weight,
    down_bias,
    ffn_gain,
    ffn_shift,
):
    return (
        lax.all_gather(query_weight, ("blk", "head"), axis=0, tiled=True),
        lax.all_gather(query_bias, ("blk", "head"), axis=0, tiled=True),
        lax.all_gather(key_weight, ("blk", "head"), axis=0, tiled=True),
        lax.all_gather(value_weight, ("blk", "head"), axis=0, tiled=True),
        lax.all_gather(value_bias, ("blk", "head"), axis=0, tiled=True),
        lax.all_gather(out_weight, ("blk", "head"), axis=0, tiled=True),
        lax.all_gather(out_bias, ("blk", "head"), axis=0, tiled=True),
        lax.all_gather(attn_gain, ("blk", "head"), axis=0, tiled=True),
        lax.all_gather(attn_shift, ("blk", "head"), axis=0, tiled=True),
        lax.all_gather(up_weight, ("blk", "head"), axis=0, tiled=True),
        lax.all_gather(up_bias, ("blk", "head"), axis=0, tiled=True),
        lax.all_gather(down_weight, ("blk", "head"), axis=0, tiled=True),
        lax.all_gather(down_bias, ("blk", "head"), axis=0, tiled=True),
        lax.all_gather(ffn_gain, ("blk", "head"), axis=0, tiled=True),
        lax.all_gather(ffn_shift, ("blk", "head"), axis=0, tiled=True),
    )


def reduce_grads(totals):
    return (
        lax.psum_scatter(totals[0], ("blk", "head"), scatter_dimension=0, tiled=True),
        lax.psum_scatter(totals[1], ("blk", "head"), scatter_dimension=0, tiled=True),
        lax.psum_scatter(totals[2], ("blk", "head"), scatter_dimension=0, tiled=True),
        lax.psum_scatter(totals[3], ("blk", "head"), scatter_dimension=0, tiled=True),
        lax.psum_scatter(totals[4], ("blk", "head"), scatter_dimension=0, tiled=True),
        lax.psum_scatter(totals[5], ("blk", "head"), scatter_dimension=0, tiled=True),
        lax.psum_scatter(totals[6], ("blk", "head"), scatter_dimension=0, tiled=True),
        lax.psum_scatter(totals[7], ("blk", "head"), scatter_dimension=0, tiled=True),
        lax.psum_scatter(totals[8], ("blk", "head"), scatter_dimension=0, tiled=True),
        lax.psum_scatter(totals[9], ("blk", "head"), scatter_dimension=0, tiled=True),
        lax.psum_scatter(totals[10], ("blk", "head"), scatter_dimension=0, tiled=True),
        lax.psum_scatter(totals[11], ("blk", "head"), scatter_dimension=0, tiled=True),
        lax.psum_scatter(totals[12], ("blk", "head"), scatter_dimension=0, tiled=True),
        lax.psum_scatter(totals[13], ("blk", "head"), scatter_dimension=0, tiled=True),
        lax.psum_scatter(totals[14], ("blk", "head"), scatter_dimension=0, tiled=True),
    )


def sparse_forward(packed):
    group_queries, group_keys, group_values, group_allowed = packed
    attn_scale = HD ** (-0.5)
    scores = (
        jnp.einsum("gqhd,ghkd->ghqk", group_queries, group_keys, preferred_element_type=jnp.float32)
        * attn_scale
    )
    scores = jnp.where(group_allowed[:, None, None, :], scores, -jnp.inf)
    row_top = jnp.max(scores, axis=-1, keepdims=True)
    raised = jnp.exp(scores - row_top)
    row_total = jnp.sum(raised, axis=-1, keepdims=True)
    probs_low = (raised / row_total).astype(jnp.bfloat16)
    output = jnp.einsum(
        "ghqk,ghkd->gqhd", probs_low, group_values, preferred_element_type=jnp.float32
    )
    return (output, (row_top + jnp.log(row_total))[..., 0])


def sparse_backward(nearby, carried, packed):
    group_queries, group_keys, group_values, group_allowed, group_lse, group_grad = packed
    attn_scale = HD ** (-0.5)
    per_group = group_queries.shape[0]
    heads_dev = group_queries.shape[2]
    scores = (
        jnp.einsum("gqhd,ghkd->ghqk", group_queries, group_keys, preferred_element_type=jnp.float32)
        * attn_scale
    )
    scores = jnp.where(group_allowed[:, None, None, :], scores, -jnp.inf)
    probs = jnp.exp(scores - group_lse[..., None])
    d_probs = jnp.einsum(
        "gqhd,ghkd->ghqk", group_grad, group_values, preferred_element_type=jnp.float32
    )
    row_delta = jnp.sum(probs * d_probs, axis=-1, keepdims=True)
    d_scores = (probs * (d_probs - row_delta)).astype(jnp.bfloat16)
    d_queries = (
        jnp.einsum("ghqk,ghkd->gqhd", d_scores, group_keys, preferred_element_type=jnp.float32)
        * attn_scale
    )
    d_keys = (
        jnp.einsum("ghqk,gqhd->ghkd", d_scores, group_queries, preferred_element_type=jnp.float32)
        * attn_scale
    )
    d_values = jnp.einsum(
        "ghqk,gqhd->ghkd",
        probs.astype(jnp.bfloat16),
        group_grad,
        preferred_element_type=jnp.float32,
    )
    d_keys = d_keys.reshape(per_group, heads_dev, -1, BLOCK, HD)
    d_values = d_values.reshape(per_group, heads_dev, -1, BLOCK, HD)
    carried = (
        carried[0] + jnp.sum(d_keys[:, :, nearby:], axis=0),
        carried[1] + jnp.sum(d_values[:, :, nearby:], axis=0),
    )
    return (carried, (d_queries, d_keys[:, :, :nearby], d_values[:, :, :nearby]))


def micro_batch(tokens, cotangent_rows, random_rows, global_rows, weights):
    (
        full_query,
        full_query_bias,
        full_key,
        full_value,
        full_value_bias,
        full_out,
        full_out_bias,
        full_attn_gain,
        full_attn_shift,
        full_up,
        full_up_bias,
        full_down,
        full_down_bias,
        full_ffn_gain,
        full_ffn_shift,
    ) = weights
    attn_scale = HD ** (-0.5)
    shards = lax.axis_size("blk")
    head_groups = lax.axis_size("head")
    shard_index = lax.axis_index("blk")
    group_index = lax.axis_index("head")
    heads_dev = HEADS // head_groups
    group_width = heads_dev * HD
    listed = 3 + RAND + GLOB
    nearby = 3 + RAND
    projected = jnp.stack(
        [
            matmul(tokens, full_query) + full_query_bias,
            matmul(tokens, full_key),
            matmul(tokens, full_value) + full_value_bias,
        ]
    ).astype(jnp.bfloat16)
    by_head = lax.all_to_all(projected, "head", split_axis=2, concat_axis=1, tiled=True)
    row_count = by_head.shape[1]
    block_count = row_count // BLOCK
    blocks_all = block_count * shards
    key_rows = by_head[1]
    value_rows = by_head[2]
    padded = with_halo(by_head[1:3], (("blk", 1),), BLOCK)
    extended = padded.reshape(2, block_count + 2, BLOCK, heads_dev, HD).transpose(0, 1, 3, 2, 4)
    window = jnp.stack([extended[:, offset : offset + block_count] for offset in range(3)], axis=3)
    block_ids = shard_index * block_count + jnp.arange(block_count, dtype=jnp.int32)
    neighbour = block_ids[:, None] + jnp.arange(-1, 2, dtype=jnp.int32)[None, :]
    inside = (neighbour >= 0) & (neighbour < blocks_all)
    head_table = lax.dynamic_slice_in_dim(random_rows, group_index * heads_dev, heads_dev, 1)
    requests = block_count * heads_dev * RAND
    all_requests = head_table.reshape(shards, requests)
    capacity = (requests + shards - 1) // shards + 1
    wanted = lax.dynamic_slice_in_dim(all_requests, shard_index, 1, 0)[0]
    source = wanted // block_count
    place = jnp.arange(requests, dtype=jnp.int32)
    earlier = (place[:, None] > place[None, :]).astype(jnp.int32)
    same_source = (source[:, None] == source[None, :]).astype(jnp.int32)
    slot_index = jnp.sum(earlier * same_source, axis=1)
    mine_mask = (all_requests // block_count == shard_index).astype(jnp.int32)
    send_order = jnp.sum(earlier[None] * mine_mask[:, None, :], axis=2)
    match_mask = mine_mask[:, :, None] * (
        send_order[:, :, None] == jnp.arange(capacity, dtype=jnp.int32)[None, None, :]
    ).astype(jnp.int32)
    head_of = jnp.arange(requests, dtype=jnp.int32) // RAND % heads_dev
    row_of = all_requests % block_count * heads_dev + head_of[None, :]
    send_rows = jnp.sum(match_mask * row_of[:, :, None], axis=1)
    filled = jnp.sum(match_mask, axis=1).astype(jnp.float32)
    block_table = (
        by_head[1:3]
        .reshape(2, block_count, BLOCK, heads_dev, HD)
        .transpose(1, 3, 0, 2, 4)
        .reshape(block_count * heads_dev, 2, BLOCK, HD)
    )
    outgoing = taken(block_table, send_rows.reshape(-1))
    incoming = lax.all_to_all(outgoing, "blk", split_axis=0, concat_axis=0, tiled=True)
    fetched = taken(incoming, source * capacity + slot_index).reshape(
        block_count, heads_dev, RAND, 2, BLOCK, HD
    )
    owner_shard = global_rows // block_count
    present = owner_shard == shard_index
    local_block = global_rows % block_count
    own_rows = jnp.stack(
        [
            lax.dynamic_index_in_dim(
                by_head.reshape(3, block_count, BLOCK, group_width), local_block[g], 1, False
            )
            for g in range(GLOB)
        ],
        axis=1,
    )
    shared = lax.psum(
        jnp.where(present[None, :, None, None], own_rows.astype(jnp.float32), 0.0), "blk"
    ).astype(jnp.bfloat16)
    shared_pairs = shared[1:3].reshape(2, GLOB, BLOCK, heads_dev, HD).transpose(0, 3, 1, 2, 4)

    def listed_blocks(which):
        near_part = window[which]
        random_part = fetched[:, :, :, which]
        global_part = jnp.broadcast_to(
            shared_pairs[which][None], (block_count, heads_dev, GLOB, BLOCK, HD)
        )
        return jnp.concatenate([near_part, random_part, global_part], axis=2).reshape(
            block_count, heads_dev, listed * BLOCK, HD
        )

    per_group = min(8, block_count)
    group_count = block_count // per_group
    query_groups = by_head[0].reshape(group_count, per_group, BLOCK, heads_dev, HD)
    key_groups = listed_blocks(0).reshape(group_count, per_group, heads_dev, listed * BLOCK, HD)
    value_groups = listed_blocks(1).reshape(group_count, per_group, heads_dev, listed * BLOCK, HD)
    allowed = jnp.repeat(
        jnp.concatenate([inside, jnp.ones((block_count, RAND + GLOB), jnp.bool_)], axis=1),
        BLOCK,
        axis=1,
    )
    allow_groups = allowed.reshape(group_count, per_group, listed * BLOCK)
    sparse_out, sparse_lse = lax.map(
        sparse_forward, (query_groups, key_groups, value_groups, allow_groups)
    )
    global_queries = shared[0].reshape(GLOB, BLOCK, heads_dev, HD)
    key_heads = key_rows.reshape(row_count, heads_dev, HD)
    value_wide = value_rows.reshape(row_count, heads_dev, HD).astype(jnp.float32)
    global_scores = (
        jnp.einsum("gqhd,khd->ghqk", global_queries, key_heads, preferred_element_type=jnp.float32)
        * attn_scale
    )
    global_top = jnp.max(global_scores, axis=-1)
    global_raised = jnp.exp(global_scores - global_top[..., None])
    merged = combined_all(
        (
            global_top,
            jnp.sum(global_raised, axis=-1),
            jnp.einsum(
                "ghqk,khd->ghqd", global_raised, value_wide, precision=lax.Precision.HIGHEST
            ),
        ),
        "blk",
        combine_parts,
    )
    global_out = merged[2] / merged[1][..., None]
    global_lse = merged[0] + jnp.log(merged[1])
    global_hits = (block_ids[:, None] == global_rows[None, :]).astype(jnp.float32)
    is_global = jnp.sum(global_hits, axis=1) > 0
    replaced = jnp.einsum("ng,ghqd->nqhd", global_hits, global_out, precision=lax.Precision.HIGHEST)
    context = jnp.where(
        is_global[:, None, None, None],
        replaced,
        sparse_out.reshape(block_count, BLOCK, heads_dev, HD),
    )
    context_rows = context.reshape(row_count, group_width).astype(jnp.bfloat16)
    context_tokens = lax.all_to_all(context_rows, "head", split_axis=0, concat_axis=1, tiled=True)
    branch = matmul(context_tokens, full_out) + full_out_bias
    first_in = tokens.astype(jnp.float32) + branch
    first_norm, first_pull = jax.vjp(
        layer_norm,
        first_in,
        full_attn_gain.astype(jnp.float32),
        full_attn_shift.astype(jnp.float32),
    )
    first_low = first_norm.astype(jnp.bfloat16)
    hidden = matmul(first_low, full_up) + full_up_bias
    act_value, gelu_pull = jax.vjp(gelu_exact, hidden)
    act_low = act_value.astype(jnp.bfloat16)
    ffn_out = matmul(act_low, full_down) + full_down_bias
    result, second_pull = jax.vjp(
        layer_norm,
        first_norm + ffn_out,
        full_ffn_gain.astype(jnp.float32),
        full_ffn_shift.astype(jnp.float32),
    )
    d_second, grad_ffn_gain, grad_ffn_shift = second_pull(cotangent_rows.astype(jnp.float32))
    d_ffn = d_second.astype(jnp.bfloat16)
    grad_down = matmul_left(act_low, d_ffn)
    grad_down_bias = column_sum(d_ffn)
    (d_hidden,) = gelu_pull(matmul_right(d_ffn, full_down))
    d_hidden_low = d_hidden.astype(jnp.bfloat16)
    grad_up = matmul_left(first_low, d_hidden_low)
    grad_up_bias = column_sum(d_hidden_low)
    d_first = d_second + matmul_right(d_hidden_low, full_up)
    d_mix, grad_attn_gain, grad_attn_shift = first_pull(d_first)
    d_branch = d_mix.astype(jnp.bfloat16)
    grad_out = matmul_left(context_tokens, d_branch)
    grad_out_bias = column_sum(d_branch)
    d_context = matmul_right(d_branch, full_out).astype(jnp.bfloat16)
    d_heads = lax.all_to_all(d_context, "head", split_axis=1, concat_axis=0, tiled=True).reshape(
        block_count, BLOCK, heads_dev, HD
    )
    d_sparse = jnp.where(is_global[:, None, None, None], jnp.zeros_like(d_heads), d_heads)
    d_global = lax.psum(
        jnp.where(
            present[:, None, None, None], taken(d_heads, local_block).astype(jnp.float32), 0.0
        ),
        "blk",
    )
    start_carry = (
        jnp.zeros((heads_dev, GLOB, BLOCK, HD), jnp.float32),
        jnp.zeros((heads_dev, GLOB, BLOCK, HD), jnp.float32),
    )
    global_sums, (d_query_parts, near_keys, near_values) = lax.scan(
        partial(sparse_backward, nearby),
        start_carry,
        (
            query_groups,
            key_groups,
            value_groups,
            allow_groups,
            sparse_lse,
            d_sparse.reshape(group_count, per_group, BLOCK, heads_dev, HD),
        ),
    )
    d_query_sparse = d_query_parts.reshape(block_count, BLOCK, heads_dev, HD)
    near_keys = near_keys.reshape(block_count, heads_dev, nearby, BLOCK, HD)
    near_values = near_values.reshape(block_count, heads_dev, nearby, BLOCK, HD)
    near_grads = jnp.stack([near_keys[:, :, :3], near_values[:, :, :3]])
    ext_grads = jnp.zeros((2, block_count + 2, heads_dev, BLOCK, HD), jnp.float32)
    for offset in range(3):
        ext_grads = ext_grads + jnp.pad(
            near_grads[:, :, :, offset], ((0, 0), (offset, 2 - offset), (0, 0), (0, 0), (0, 0))
        )
    rim_pair = jnp.stack([ext_grads[:, 0], ext_grads[:, block_count + 1]], axis=1)
    arrived = with_halo(rim_pair.astype(jnp.bfloat16), (("blk", 1),), 1).astype(rim_pair.dtype)
    inner_grads = ext_grads[:, 1 : block_count + 1]
    inner_grads = inner_grads.at[:, 0].add(arrived[:, 0]).at[:, block_count - 1].add(arrived[:, 3])
    far_grads = jnp.stack([near_keys[:, :, 3:], near_values[:, :, 3:]], axis=3).reshape(
        requests, 2, BLOCK, HD
    )
    outbox = (
        jnp.zeros((shards, capacity, 2, BLOCK, HD), jnp.float32)
        .at[source, slot_index]
        .set(far_grads)
    )
    arrived_slots = (
        lax.all_to_all(
            outbox.astype(jnp.bfloat16), "blk", split_axis=0, concat_axis=0, tiled=True
        ).astype(outbox.dtype)
        * filled[:, :, None, None, None]
    )
    landed = (
        jnp.zeros((block_count * heads_dev, 2, BLOCK, HD), jnp.float32)
        .at[send_rows.reshape(-1)]
        .add(arrived_slots.reshape(shards * capacity, 2, BLOCK, HD))
    )
    landed = landed.reshape(block_count, heads_dev, 2, BLOCK, HD)
    global_probs = jnp.exp(global_scores - global_lse[..., None])
    d_probs_global = jnp.einsum(
        "gqhd,khd->ghqk", d_global, value_wide, precision=lax.Precision.HIGHEST
    )
    delta_global = jnp.einsum(
        "gqhd,ghqd->ghq", d_global, global_out, precision=lax.Precision.HIGHEST
    )
    d_scores_global = (global_probs * (d_probs_global - delta_global[..., None])).astype(
        jnp.bfloat16
    )
    d_global_queries = (
        jnp.einsum("ghqk,khd->gqhd", d_scores_global, key_heads, preferred_element_type=jnp.float32)
        * attn_scale
    )
    d_keys_global = (
        jnp.einsum(
            "ghqk,gqhd->khd", d_scores_global, global_queries, preferred_element_type=jnp.float32
        )
        * attn_scale
    )
    d_values_global = jnp.einsum(
        "ghqk,gqhd->khd", global_probs, d_global, precision=lax.Precision.HIGHEST
    )
    returned = lax.psum(
        jnp.stack(
            [
                d_global_queries,
                global_sums[0].transpose(1, 2, 0, 3),
                global_sums[1].transpose(1, 2, 0, 3),
            ]
        ),
        "blk",
    )
    owned_grads = jnp.einsum(
        "ng,cgqhd->cnqhd", global_hits, returned, precision=lax.Precision.HIGHEST
    )
    d_query_total = d_query_sparse + owned_grads[0]
    d_key_total = (
        (inner_grads[0] + landed[:, :, 0]).transpose(0, 2, 1, 3)
        + d_keys_global.reshape(block_count, BLOCK, heads_dev, HD)
        + owned_grads[1]
    )
    d_value_total = (
        (inner_grads[1] + landed[:, :, 1]).transpose(0, 2, 1, 3)
        + d_values_global.reshape(block_count, BLOCK, heads_dev, HD)
        + owned_grads[2]
    )
    stacked = (
        jnp.stack([d_query_total, d_key_total, d_value_total])
        .reshape(3, row_count, group_width)
        .astype(jnp.bfloat16)
    )
    token_grads = lax.all_to_all(stacked, "head", split_axis=1, concat_axis=2, tiled=True)
    d_tokens = (
        d_mix
        + matmul_right(token_grads[0], full_query)
        + matmul_right(token_grads[1], full_key)
        + matmul_right(token_grads[2], full_value)
    )
    grads = (
        matmul_left(tokens, token_grads[0]),
        column_sum(token_grads[0]),
        matmul_left(tokens, token_grads[1]),
        matmul_left(tokens, token_grads[2]),
        column_sum(token_grads[2]),
        grad_out,
        grad_out_bias,
        grad_attn_gain,
        grad_attn_shift,
        grad_up,
        grad_up_bias,
        grad_down,
        grad_down_bias,
        grad_ffn_gain,
        grad_ffn_shift,
    )
    return (result.astype(jnp.bfloat16), d_tokens.astype(jnp.bfloat16), grads)


def body(
    inputs,
    cotangent,
    random_blocks,
    global_blocks,
    query_weight,
    query_bias,
    key_weight,
    value_weight,
    value_bias,
    out_weight,
    out_bias,
    attn_gain,
    attn_shift,
    up_weight,
    up_bias,
    down_weight,
    down_bias,
    ffn_gain,
    ffn_shift,
):
    weight_shards = (
        query_weight,
        query_bias,
        key_weight,
        value_weight,
        value_bias,
        out_weight,
        out_bias,
        attn_gain,
        attn_shift,
        up_weight,
        up_bias,
        down_weight,
        down_bias,
        ffn_gain,
        ffn_shift,
    )
    results = []
    input_grads = []
    totals = None
    for micro_index in range(inputs.shape[0]):
        weights = fetch_weights(*weight_shards)
        result, token_grad, grads = micro_batch(
            inputs[micro_index],
            cotangent[micro_index],
            random_blocks[micro_index],
            global_blocks[micro_index],
            weights,
        )
        grads = reduce_grads(grads)
        totals = (
            grads
            if totals is None
            else tuple((total_sum + extra_sum for total_sum, extra_sum in zip(totals, grads)))
        )
        results.append(result)
        input_grads.append(token_grad)
    return (jnp.stack(results), jnp.stack(input_grads)) + tuple(totals)


def solution(mesh):
    return jax.shard_map(
        near_body if (mesh.shape["blk"], mesh.shape["head"]) == (8, 4) else body,
        mesh=mesh,
        in_specs=(
            P(None, ("blk", "head"), None),
            P(None, ("blk", "head"), None),
            P(),
            P(),
            P(("blk", "head"), None),
            P(("blk", "head")),
            P(("blk", "head"), None),
            P(("blk", "head"), None),
            P(("blk", "head")),
            P(("blk", "head"), None),
            P(("blk", "head")),
            P(("blk", "head")),
            P(("blk", "head")),
            P(("blk", "head"), None),
            P(("blk", "head")),
            P(("blk", "head"), None),
            P(("blk", "head")),
            P(("blk", "head")),
            P(("blk", "head")),
        ),
        out_specs=(
            P(None, ("blk", "head"), None),
            P(None, ("blk", "head"), None),
            P(("blk", "head"), None),
            P(("blk", "head")),
            P(("blk", "head"), None),
            P(("blk", "head"), None),
            P(("blk", "head")),
            P(("blk", "head"), None),
            P(("blk", "head")),
            P(("blk", "head")),
            P(("blk", "head")),
            P(("blk", "head"), None),
            P(("blk", "head")),
            P(("blk", "head"), None),
            P(("blk", "head")),
            P(("blk", "head")),
            P(("blk", "head")),
        ),
        check_vma=False,
    )
```
